32 devices in a mesh: grp: 4 (over x, core), gx: 2 (over y), gy: 4 (over z).
Axes of the slice: x: 2, y: 2, z: 4, core: 2. Of those that a mesh axis runs over, the one named last changes fastest.
Arguments:
- fields: float32 [4, 5, 32, 128, 384], P('grp', None, 'gx', 'gy'), may hold values from -6 to 6
- closure_in: float32 [64, 5], replicated, may hold values from -2.5 to 2.5
- closure_bias: float32 [64], replicated, may hold values from -4 to 4
- closure_out: float32 [64], replicated, may hold values from -0.75 to 0.75
- master: float32 [17280], replicated, may hold values from -0.6 to 0.6
- momentum: float32 [17280], replicated, may hold values from -3 to 3
- sample_block: int32 [24], replicated, may hold values from 0 to 47
- sample_trainer: int32 [24], replicated, may hold values from 0 to 7, as said below
Outputs:
- new_fields: float32 [4, 5, 32, 128, 384], P('grp', None, 'gx', 'gy')
- new_master: float32 [17280], P(('grp', 'gx', 'gy'))
- new_momentum: float32 [17280], P(('grp', 'gx', 'gy'))
The draws below stay inside these ranges and needn't reach their ends.
Inputs may be any that keep to these rules, and one draw needn't show every extreme that they name: `sample_trainer`: entry o names the trainer c = gx * 4 + gy of the last group that receives the cube of evolution device o. Every trainer receives at least 2 and at most 6 cubes, at most 4 from one evolution group; in every draw some trainer receives 6, 4 of them from one group.
All inputs are finite; a program needn't handle non-finite values.
Results may differ from the reference program's by a relative error of at most 0.0026.
The reference program's roundings to bfloat16 on the way (of `samples`, `hidden`, `error_grad` and `pre_grad`) count: a program that leaves them out, or rounds other values in their place, can miss the bound.
Values may be sent and summed in bfloat16 or wider, within the bound.
No kernel may reach another device: no remote copies, remote signals or barrier semaphores. Data moves between devices by JAX's collectives and lax.ppermute only.
A program may use at most 192 MiB of HBM per device.

```python
import jax
import jax.numpy as jnp
from jax import lax

F = 5
CH = 64
HID = 64
SUB = 16
CX = 16
CY = 32
CZ = 384
TCAP = 6
INNER = 3
TRAINERS = 8
OWNERS = 24
NX = 32
NY = 128
CELLS = 4096
BLOCKS = 48
NPARAM = 17280
N_GRP = 4
N_GX = 2
N_GY = 4


def draw_master(key, part):
    first_count = CH * 27 * F
    position = jnp.arange(NPARAM)
    scales = jnp.where(position < first_count, (27.0 * F) ** (-0.5), (27.0 * CH) ** (-0.5))
    normal_draw = jax.random.truncated_normal(key, -6.0, 6.0, (NPARAM,), jnp.float32)
    return (normal_draw * scales).astype(jnp.float32)


def draw_sample_trainer(key, part):
    first_group = jax.random.permutation(jax.random.fold_in(key, 1), TRAINERS)
    busy_list = jax.random.permutation(jax.random.fold_in(key, 2), TRAINERS)
    spread = jax.random.permutation(jax.random.fold_in(key, 3), TRAINERS)
    third_group = jax.random.permutation(jax.random.fold_in(key, 4), TRAINERS)
    second_group = busy_list[spread // 4]
    return jnp.concatenate([first_group, second_group, third_group]).astype(jnp.int32)


def set_ends(values, key, smallest, high):
    longest = values.shape.index(max(values.shape))
    spots = []
    for shift in (0, 1):
        where = [jax.random.randint(jax.random.fold_in(key, axis), (), 0, length) for axis, length in enumerate(values.shape)]
        where[longest] = (where[longest] + shift) % values.shape[longest]
        spots.append(tuple(where))
    return values.at[spots[0]].set(smallest).at[spots[1]].set(high)


def steps_of(own_key, dims, pieces, least, top_value):
    loudness, own = 1.0, jax.random.fold_in(own_key, 6)
    for dim, shards_of in pieces:
        draws = jnp.exp(jax.random.uniform(jax.random.fold_in(own, dim), (shards_of,), jnp.float32, least / len(pieces), top_value / len(pieces)))
        loudness = loudness * jnp.repeat(draws, dims[dim] // shards_of).reshape([-1 if axis == dim else 1 for axis in range(len(dims))])
    return loudness


def bell_draw(stream_key, shape, width, reach, pieces=(), kind=jnp.bfloat16):
    loudness = steps_of(stream_key, shape, pieces, -0.22, 0.18) if pieces else 1.0
    drawn = jax.random.normal(stream_key, shape, jnp.float32) * width * loudness
    return jnp.minimum(jnp.maximum(drawn, -reach), reach).astype(kind)


def setup_inputs(seed: int = 0) -> dict:
    arg_keys = jax.random.split(jax.random.key(seed), 9)
    fields = bell_draw(arg_keys[0], (N_GRP, F, NX, NY, CZ), 1.0, 6.0, ((0, 4), (2, 2), (3, 4)), jnp.float32)
    closure_in = bell_draw(arg_keys[1], (HID, F), F ** -0.5, 2.5, (), jnp.float32)
    closure_bias = bell_draw(arg_keys[2], (HID,), 1.0, 4.0, (), jnp.float32)
    closure_out = bell_draw(arg_keys[3], (HID,), HID ** -0.5, 0.75, (), jnp.float32)
    master = draw_master(jax.random.fold_in(arg_keys[8], 71), 0)
    momentum = bell_draw(arg_keys[5], (NPARAM,), 0.5, 3.0, (), jnp.float32)
    sample_block = set_ends(jax.random.randint(arg_keys[6], (OWNERS,), 0, BLOCKS), jax.random.fold_in(arg_keys[6], 1), 0, BLOCKS - 1).astype(jnp.int32)
    sample_trainer = draw_sample_trainer(jax.random.fold_in(arg_keys[8], 71), 0)
    return {"fields": fields, "closure_in": closure_in, "closure_bias": closure_bias, "closure_out": closure_out, "master": master, "momentum": momentum, "sample_block": sample_block, "sample_trainer": sample_trainer}


time_step = 0.1
base_viscosity = 0.02
viscosity_gain = 0.2
buoyancy = 0.5
inner_rate = 0.02
outer_rate = 0.01
momentum_decay = 0.9
norm_epsilon = 1e-06
highest = lax.Precision.HIGHEST

def eddy_viscosity(center, closure_in, closure_bias, closure_out):
    channels, x_cells, y_cells, z_cells = center.shape
    flattened = center.reshape(channels, x_cells * y_cells * z_cells)
    block_size = 4 * y_cells * z_cells
    block_count = x_cells // 4

    def viscosity_block(block_index):
        columns = lax.dynamic_slice_in_dim(flattened, block_index * block_size, block_size, 1)
        hidden = jax.nn.silu(jnp.dot(closure_in, columns, precision=highest) + closure_bias[:, None])
        return viscosity_gain * jax.nn.softplus(jnp.dot(closure_out, hidden, precision=highest))
    blocks = lax.map(viscosity_block, jnp.arange(block_count, dtype=jnp.int32))
    return blocks.reshape(x_cells, y_cells, z_cells)

def field_tendency(padded, closure_in, closure_bias, closure_out):
    walled = jnp.pad(padded, ((0, 0), (0, 0), (0, 0), (1, 1)))
    center = walled[:, 1:-1, 1:-1, 1:-1]
    east_side = walled[:, 2:, 1:-1, 1:-1]
    west_side = walled[:, :-2, 1:-1, 1:-1]
    north_side = walled[:, 1:-1, 2:, 1:-1]
    south_side = walled[:, 1:-1, :-2, 1:-1]
    upper_side = walled[:, 1:-1, 1:-1, 2:]
    lower_side = walled[:, 1:-1, 1:-1, :-2]
    laplacian = east_side + west_side + north_side + south_side + upper_side + lower_side - 6.0 * center
    advection = center[0] * (east_side - west_side) + center[1] * (north_side - south_side) + center[2] * (upper_side - lower_side)
    viscosity = base_viscosity + eddy_viscosity(center, closure_in, closure_bias, closure_out)
    tendency = viscosity * laplacian - 0.5 * advection
    return tendency.at[2].add(buoyancy * center[3])

def shift_tables(edge_cells, slot_count):
    cube_cells = edge_cells * edge_cells * edge_cells
    position = jnp.arange(slot_count * cube_cells, dtype=jnp.int32) % cube_cells
    x_coord = position // (edge_cells * edge_cells)
    y_coord = position // edge_cells % edge_cells
    z_coord = position % edge_cells
    tables = []
    for x_step in (-1, 0, 1):
        for y_step in (-1, 0, 1):
            for z_step in (-1, 0, 1):
                offset = x_step * edge_cells * edge_cells + y_step * edge_cells + z_step
                inside = (x_coord + x_step >= 0) & (x_coord + x_step < edge_cells)
                inside = inside & (y_coord + y_step >= 0) & (y_coord + y_step < edge_cells)
                inside = inside & (z_coord + z_step >= 0) & (z_coord + z_step < edge_cells)
                tables.append((offset, inside))
    return tables

def shift_from(values, offset, inside):
    return jnp.where(inside, jnp.roll(values, -offset, axis=1), jnp.zeros((), values.dtype))

def shift_back(values, offset, inside):
    return jnp.roll(jnp.where(inside, values, jnp.zeros((), values.dtype)), offset, axis=1)

def stacked_from(values, tables):
    return jnp.concatenate([shift_from(values, offset, inside) for offset, inside in tables], axis=0)

def stacked_back(values, tables):
    return jnp.concatenate([shift_back(values, offset, inside) for offset, inside in tables], axis=0)

def silu_slope(values):
    sigmoid_value = jax.nn.sigmoid(values)
    return sigmoid_value * (1.0 + values * (1.0 - sigmoid_value))

def batch_gradient(flat_weights, inputs, targets, cell_weight, tables):
    first_count = CH * 27 * F
    first_weight = flat_weights[:first_count].reshape(CH, 27 * F)
    last_weight = flat_weights[first_count:].reshape(F, 27, CH)
    stacked_last = jnp.transpose(last_weight, (1, 0, 2)).reshape(27 * F, CH)
    input_stack = stacked_from(inputs, tables)
    first_pre = jnp.dot(first_weight, input_stack, preferred_element_type=jnp.float32)
    hidden = jax.nn.silu(first_pre).astype(jnp.bfloat16)
    partial_out = jnp.dot(stacked_last, hidden, preferred_element_type=jnp.float32)
    predicted = jnp.zeros((F, inputs.shape[1]), jnp.float32)
    for slot_index, (offset, inside) in enumerate(tables):
        predicted = predicted + shift_from(partial_out[slot_index * F:(slot_index + 1) * F], offset, inside)
    error_grad = (2.0 * cell_weight[None, :] * (predicted - targets.astype(jnp.float32))).astype(jnp.bfloat16)
    grad_stack = stacked_back(error_grad, tables)
    last_grad = lax.dot_general(grad_stack, hidden, (((1,), (1,)), ((), ())), preferred_element_type=jnp.float32)
    last_grad = jnp.transpose(last_grad.reshape(27, F, CH), (1, 0, 2)).reshape(F * 27 * CH)
    hidden_grad = lax.dot_general(stacked_last, grad_stack, (((0,), (0,)), ((), ())), preferred_element_type=jnp.float32)
    pre_grad = (hidden_grad * silu_slope(first_pre)).astype(jnp.bfloat16)
    first_grad = lax.dot_general(pre_grad, input_stack, (((1,), (1,)), ((), ())), preferred_element_type=jnp.float32)
    return jnp.concatenate([first_grad.reshape(CH * 27 * F), last_grad])

def local_train(flat_weights, inputs, targets, cell_weight, tables):
    start_weights = flat_weights.astype(jnp.float32)
    current = start_weights
    for inner_index in range(INNER):
        gradient = batch_gradient(current.astype(jnp.bfloat16), inputs, targets, cell_weight, tables)
        current = current - inner_rate * gradient
    return start_weights - current

def slot_lists(sample_trainer, trainers, column):
    owner_ids = jnp.arange(sample_trainer.shape[0], dtype=jnp.int32)
    same_trainer = sample_trainer[:, None] == sample_trainer[None, :]
    earlier = owner_ids[None, :] < owner_ids[:, None]
    rank_all = lax.optimization_barrier(jnp.sum((same_trainer & earlier).astype(jnp.int32), axis=1))
    mine_mask = sample_trainer == column
    slot_ids = jnp.arange(TCAP, dtype=jnp.int32)
    chosen = mine_mask[None, :] & (rank_all[None, :] == slot_ids[:, None])
    slot_owner = lax.optimization_barrier(jnp.sum(jnp.where(chosen, owner_ids[None, :], 0), axis=1)).astype(jnp.int32)
    slot_valid = jnp.any(chosen, axis=1)
    sample_count = jnp.maximum(jnp.sum(mine_mask.astype(jnp.int32)), 1)
    return (slot_owner, slot_valid, sample_count)

def train_batch(batch_cubes, slot_valid, sample_count, flat_weights, tables):
    inputs = jnp.transpose(batch_cubes[:, :F], (1, 0, 2)).reshape(F, TCAP * CELLS)
    targets = jnp.transpose(batch_cubes[:, F:], (1, 0, 2)).reshape(F, TCAP * CELLS)
    slot_weight = jnp.where(slot_valid, 1.0 / (sample_count.astype(jnp.float32) * CELLS), 0.0).astype(jnp.float32)
    cell_weight = jnp.repeat(slot_weight, CELLS)
    return local_train(flat_weights, inputs, targets, cell_weight, tables)

def reference(fields, closure_in, closure_bias, closure_out, master, momentum, sample_block, sample_trainer):
    trainers = N_GX * N_GY
    sim_groups = N_GRP - 1
    updated = []
    tendencies = []
    for group_index in range(sim_groups):
        slab_fields = fields[group_index]
        padded = jnp.pad(slab_fields, ((0, 0), (1, 1), (1, 1), (0, 0)), mode='wrap')
        tendency = field_tendency(padded, closure_in, closure_bias, closure_out)
        tendencies.append(tendency)
        updated.append(slab_fields + time_step * tendency)
    updated.append(fields[sim_groups])
    new_fields = jnp.stack(updated)
    tendency_all = jnp.stack(tendencies)
    y_blocks = CY // SUB
    z_blocks = CZ // SUB

    def cut_sample(owner_id):
        group_index = owner_id // trainers
        column = owner_id % trainers
        block_id = sample_block[owner_id]
        x_start = column // N_GY * CX + block_id // (y_blocks * z_blocks) * SUB
        y_start = column % N_GY * CY + block_id // z_blocks % y_blocks * SUB
        z_start = block_id % z_blocks * SUB
        corner = (group_index.astype(jnp.int32), jnp.int32(0), x_start.astype(jnp.int32), y_start.astype(jnp.int32), z_start.astype(jnp.int32))
        old_cube = lax.dynamic_slice(fields, corner, (1, F, SUB, SUB, SUB)).reshape(F, CELLS)
        new_cube = lax.dynamic_slice(tendency_all, corner, (1, F, SUB, SUB, SUB)).reshape(F, CELLS)
        return jnp.concatenate([old_cube.astype(jnp.bfloat16), new_cube.astype(jnp.bfloat16)], axis=0)
    samples = lax.map(cut_sample, jnp.arange(OWNERS, dtype=jnp.int32))
    tables = shift_tables(SUB, TCAP)
    flat_weights = master.astype(jnp.bfloat16)

    def trainer_delta(running, column):
        slot_owner, slot_valid, sample_count = slot_lists(sample_trainer, trainers, column)
        batch_cubes = jnp.where(slot_valid[:, None, None], jnp.take(samples, slot_owner, axis=0), jnp.zeros((), jnp.bfloat16))
        return (running + train_batch(batch_cubes, slot_valid, sample_count, flat_weights, tables), None)
    weight_delta, unused = lax.scan(trainer_delta, jnp.zeros((NPARAM,), jnp.float32), jnp.arange(trainers, dtype=jnp.int32))
    inverse = 1.0 / jnp.sqrt(jnp.sum(weight_delta * weight_delta) / NPARAM + norm_epsilon)
    new_momentum = momentum_decay * momentum + weight_delta * inverse
    new_master = master - outer_rate * new_momentum
    return (new_fields, new_master, new_momentum)
```

```python
import functools

import jax
import jax.numpy as jnp
import numpy as np
from jax import lax
from jax.experimental import pallas as pl
from jax.experimental.pallas import tpu as pltpu
from jax.sharding import PartitionSpec as P

F = 5
CH = 64
HID = 64
SUB = 16
TCAP = 6
INNER = 3
CELLS = 4096
NPARAM = 17280
TAPS = 27
PAIRS = TCAP // 2
COLS = (SUB + 2) * 128
PATCH = 16 * F
STACK = 3 * PATCH

time_step = 0.1
base_viscosity = 0.02
viscosity_gain = 0.2
buoyancy = 0.5
inner_rate = 0.02
outer_rate = 0.01
momentum_decay = 0.9
norm_epsilon = 1e-06
highest = lax.Precision.HIGHEST


def patch_position(row):
    group, py, pz = row // 4, row // 2 % 2, row % 2
    ypos = py + 1 if group in (0, 1) else (3 if py == 0 else 0)
    zpos = pz + 1 if group in (0, 2) else (3 if pz == 0 else 0)
    return ypos - 1, zpos - 1


def selections():
    first = np.zeros((4, 256, STACK), np.float32)
    last = np.zeros((4, 256, STACK), np.float32)
    for cell in range(4):
        py, pz = cell // 2, cell % 2
        for kx in range(3):
            for channel in range(F):
                for row in range(16):
                    ypos, zpos = patch_position(row)
                    column = kx * PATCH + channel * 16 + row
                    dy, dz = ypos - py, zpos - pz
                    if abs(dy) <= 1 and abs(dz) <= 1:
                        tap = 9 * kx + 3 * (dy + 1) + dz + 1
                        first[cell, tap * F + channel, column] = 1.0
                        last[cell, channel * TAPS + 26 - tap, column] = 1.0
    return first, last


SELECT_FIRST, SELECT_LAST = selections()


def dot_rows(left, right):
    return jnp.dot(left, right, preferred_element_type=jnp.float32)


def dot_lanes(left, right):
    return lax.dot_general(left, right, (((1,), (1,)), ((), ())), preferred_element_type=jnp.float32)


def patch_masks():
    row = lax.broadcasted_iota(jnp.int32, (8, 128), 0)
    lane = lax.broadcasted_iota(jnp.int32, (8, 128), 1)
    return {
        "pz0": row % 2 == 0,
        "py0": row // 2 % 2 == 0,
        "centre": row < 4,
        "z_first": lane % 8 == 0,
        "z_last": lane % 8 == 7,
        "y_first": lane // 8 % 8 == 0,
        "y_last": lane // 8 % 8 == 7,
    }


def edge_shift(values, step, parity_zero, first, last, forward):
    before = jnp.where(first, 0.0, pltpu.roll(values, step, 1))
    after = jnp.where(last, 0.0, pltpu.roll(values, 128 - step, 1))
    if forward:
        return jnp.where(parity_zero, after, before)
    return jnp.where(parity_zero, before, after)


def patch_stack(rows, masks):
    both = rows + pltpu.roll(rows, 4, 0)
    z_edge = edge_shift(both, 1, masks["pz0"], masks["z_first"], masks["z_last"], True)
    upper = jnp.where(masks["centre"], both, z_edge)
    lower = edge_shift(upper, 8, masks["py0"], masks["y_first"], masks["y_last"], True)
    return upper, lower


def patch_fold(upper, lower, masks):
    def fold_z(values):
        moved = edge_shift(values, 1, masks["pz0"], masks["z_first"], masks["z_last"], False)
        return values + pltpu.roll(moved, 4, 0)

    shifted = edge_shift(fold_z(lower), 8, masks["py0"], masks["y_first"], masks["y_last"], False)
    return fold_z(upper) + shifted


def store_planes(ref, pair, x, channels):
    stacked = jnp.concatenate([part for both in channels for part in both], axis=0).astype(jnp.bfloat16)
    for kx in range(3):
        start = pl.multiple_of((x + 2 - kx) * 128, 128)
        ref[pair, kx * PATCH : (kx + 1) * PATCH, pl.ds(start, 128)] = stacked


def train_kernel(sources, *refs):
    (slots, first_ref, last_ref, weight_ref, select_first, select_last) = refs[:6]
    arrived = refs[6 : 6 + sources]
    fields_ref = refs[6 + sources]
    delta_first, delta_last, new_fields_ref = refs[7 + sources : 10 + sources]
    (
        cubes,
        table,
        targets,
        inputs,
        errors,
        hiddens,
        slopes,
        partial_out,
        big_first,
        big_last,
        big_last_t,
        grad_first,
        grad_last,
        now_first,
        now_last,
        slot_sems,
        field_sem,
    ) = refs[10 + sources :]

    field_copy = pltpu.make_async_copy(fields_ref, new_fields_ref, field_sem)
    field_copy.start()
    for slot in range(TCAP):
        for source in range(sources):

            @pl.when((slots[2, slot] == 1) & (slots[0, slot] == source))
            def _():
                pltpu.make_async_copy(
                    arrived[source].at[slots[1, slot]], cubes.at[slot], slot_sems.at[slot]
                ).start()

        @pl.when(slots[2, slot] == 0)
        def _():
            cubes[slot] = jnp.zeros((2 * SUB * F, 256), jnp.bfloat16)

    masks = patch_masks()
    errors[...] = jnp.zeros(errors.shape, errors.dtype)
    inputs[...] = jnp.zeros(inputs.shape, inputs.dtype)
    partial_out[:, :, :128] = jnp.zeros((PAIRS, STACK, 128), jnp.float32)
    partial_out[:, :, COLS - 128 :] = jnp.zeros((PAIRS, STACK, 128), jnp.float32)
    table[...] = jnp.zeros(table.shape, table.dtype)
    targets[...] = jnp.zeros(targets.shape, targets.dtype)
    start_first = first_ref[...].astype(jnp.bfloat16).astype(jnp.float32)
    start_last = last_ref[...].astype(jnp.bfloat16).astype(jnp.float32)
    now_first[...] = start_first
    now_last[...] = start_last

    for slot in range(TCAP):

        @pl.when(slots[2, slot] == 1)
        def _():
            pltpu.make_async_copy(arrived[0].at[0], cubes.at[slot], slot_sems.at[slot]).wait()

    low_lanes = lax.broadcasted_iota(jnp.int32, (SUB * F, 128), 1) < 64

    def spread_rows(pair, start, put):
        even = cubes[2 * pair, start : start + SUB * F, :].astype(jnp.float32)
        odd = cubes[2 * pair + 1, start : start + SUB * F, :].astype(jnp.float32)
        for half in range(2):
            left = even[:, half * 128 : (half + 1) * 128]
            right = odd[:, half * 128 : (half + 1) * 128]
            put(2 * half, jnp.where(low_lanes, left, pltpu.roll(right, 64, 1)))
            put(2 * half + 1, jnp.where(low_lanes, pltpu.roll(left, 64, 1), right))

    for pair in range(PAIRS):

        def put_input(cell, values):
            table[pl.ds(cell, SUB * F, 8), :] = values

        def put_target(cell, values):
            targets[pl.ds(pair * SUB * F * 8 + cell, SUB * F, 8), :] = values

        spread_rows(pair, 0, put_input)
        spread_rows(pair, SUB * F, put_target)

        def stack_plane(x, carry):
            base = pl.multiple_of(x * (F * 8), 8)
            rows = table[pl.ds(base, F * 8), :]
            channels = [patch_stack(rows[8 * c : 8 * c + 8], masks) for c in range(F)]
            store_planes(inputs, pair, x, channels)
            return carry

        lax.fori_loop(0, SUB, stack_plane, 0)

    def train_step(step, step_carry):
        first_now = now_first[...].astype(jnp.bfloat16)
        last_now = now_last[...].astype(jnp.bfloat16)
        for cell in range(4):
            rows = slice(cell * CH, (cell + 1) * CH)
            big_first[rows, :] = dot_rows(first_now, select_first[cell]).astype(jnp.bfloat16)
            big_last[rows, :] = dot_rows(last_now, select_last[cell]).astype(jnp.bfloat16)
        big_last_t[...] = big_last[...].T
        grad_first[...] = jnp.zeros(grad_first.shape, jnp.float32)
        grad_last[...] = jnp.zeros(grad_last.shape, jnp.float32)

        def forward(index, carry):
            pair = index // 8
            column = pl.multiple_of((index % 8) * 256 + 128, 128)
            pre = dot_rows(big_first[...], inputs[pair, :, pl.ds(column, 256)])
            sigmoid = 0.5 * jnp.tanh(0.5 * pre) + 0.5
            value = pre * sigmoid
            hidden = value.astype(jnp.bfloat16)
            hiddens[pair, :, pl.ds(column, 256)] = hidden
            slopes[pair, :, pl.ds(column, 256)] = sigmoid + value * (1.0 - sigmoid)
            partial_out[pair, :, pl.ds(column, 256)] = dot_rows(big_last_t[...], hidden)
            return carry

        lax.fori_loop(0, 8 * PAIRS, forward, 0)

        def error_plane(index, carry):
            pair = index // SUB
            x = index % SUB
            column = pl.multiple_of((x + 1) * 128, 128)
            total = (
                partial_out[pair, 0:PATCH, pl.ds(pl.multiple_of(column + 128, 128), 128)]
                + partial_out[pair, PATCH : 2 * PATCH, pl.ds(column, 128)]
                + partial_out[pair, 2 * PATCH :, pl.ds(pl.multiple_of(column - 128, 128), 128)]
            )
            wanted = targets[pl.ds(pl.multiple_of(index * (F * 8), 8), F * 8), :]
            weight = weight_ref[pair]
            channels = []
            for c in range(F):
                predicted = patch_fold(
                    total[16 * c : 16 * c + 8], total[16 * c + 8 : 16 * c + 16], masks
                )
                error = weight * (predicted - wanted[8 * c : 8 * c + 8])
                error = jnp.where(masks["centre"], error, 0.0)
                error = error.astype(jnp.bfloat16).astype(jnp.float32)
                channels.append(patch_stack(error, masks))
            store_planes(errors, pair, x, channels)
            return carry

        lax.fori_loop(0, SUB * PAIRS, error_plane, 0)

        def backward(index, carry):
            pair = index // 4
            column = pl.multiple_of((index % 4) * 512 + 128, 128)
            error_stack = errors[pair, :, pl.ds(column, 512)]
            hidden_grad = dot_rows(big_last[...], error_stack)
            pre_grad = (hidden_grad * slopes[pair, :, pl.ds(column, 512)]).astype(jnp.bfloat16)
            grad_first[...] += dot_lanes(pre_grad, inputs[pair, :, pl.ds(column, 512)])
            grad_last[...] += dot_lanes(hiddens[pair, :, pl.ds(column, 512)], error_stack)
            return carry

        lax.fori_loop(0, 4 * PAIRS, backward, 0)

        def folded(grad_ref, select_ref):
            total = jnp.zeros((CH, 256), jnp.float32)
            for cell in range(4):
                rest = grad_ref[cell * CH : (cell + 1) * CH, :]
                for _ in range(3):
                    part = rest.astype(jnp.bfloat16)
                    total = total + dot_lanes(part, select_ref[cell])
                    rest = rest - part.astype(jnp.float32)
            return total

        now_first[...] = now_first[...] - inner_rate * folded(grad_first, select_first)
        now_last[...] = now_last[...] - inner_rate * folded(grad_last, select_last)
        return step_carry

    lax.fori_loop(0, INNER, train_step, 0)
    delta_first[...] = start_first - now_first[...]
    delta_last[...] = start_last - now_last[...]
    field_copy.wait()


def train_cubes(slots, first, last, weights, arrived, fields):
    sources = len(arrived)
    vmem = pl.BlockSpec(memory_space=pltpu.VMEM)
    anywhere = pl.BlockSpec(memory_space=pl.ANY)
    return pl.pallas_call(
        functools.partial(train_kernel, sources),
        out_shape=(
            jax.ShapeDtypeStruct((CH, 256), jnp.float32),
            jax.ShapeDtypeStruct((CH, 256), jnp.float32),
            jax.ShapeDtypeStruct(fields.shape, fields.dtype),
        ),
        in_specs=[pl.BlockSpec(memory_space=pltpu.SMEM)] + [vmem] * 5 + [anywhere] * (sources + 1),
        out_specs=(vmem, vmem, anywhere),
        scratch_shapes=[
            pltpu.VMEM((TCAP, 2 * SUB * F, 256), jnp.bfloat16),
            pltpu.VMEM((SUB * F * 8, 128), jnp.float32),
            pltpu.VMEM((PAIRS * SUB * F * 8, 128), jnp.float32),
            pltpu.VMEM((PAIRS, STACK, COLS), jnp.bfloat16),
            pltpu.VMEM((PAIRS, STACK, COLS), jnp.bfloat16),
            pltpu.VMEM((PAIRS, 4 * CH, COLS), jnp.bfloat16),
            pltpu.VMEM((PAIRS, 4 * CH, COLS), jnp.float32),
            pltpu.VMEM((PAIRS, STACK, COLS), jnp.float32),
            pltpu.VMEM((4 * CH, STACK), jnp.bfloat16),
            pltpu.VMEM((4 * CH, STACK), jnp.bfloat16),
            pltpu.VMEM((STACK, 4 * CH), jnp.bfloat16),
            pltpu.VMEM((4 * CH, STACK), jnp.float32),
            pltpu.VMEM((4 * CH, STACK), jnp.float32),
            pltpu.VMEM((CH, 256), jnp.float32),
            pltpu.VMEM((CH, 256), jnp.float32),
            pltpu.SemaphoreType.DMA((TCAP,)),
            pltpu.SemaphoreType.DMA,
        ],
        compiler_params=pltpu.CompilerParams(vmem_limit_bytes=48 * 1024 * 1024),
        name="train_cubes",
    )(
        slots,
        first,
        last,
        weights,
        jnp.asarray(SELECT_FIRST, jnp.bfloat16),
        jnp.asarray(SELECT_LAST, jnp.bfloat16),
        *arrived,
        fields,
    )


def evolve_kernel(closure, fields, x_low, x_high, y_low, y_high, new_fields):
    x_cells, y_cells, z_cells = fields.shape[1:]
    row = lax.broadcasted_iota(jnp.int32, (y_cells, z_cells), 0)
    lane = lax.broadcasted_iota(jnp.int32, (y_cells, z_cells), 1)
    part = y_cells // 2

    def plane(x, carry):
        eddies = []
        for half in range(2):
            rows = pl.ds(half * part, part)
            cells = [fields[f, x, rows, :] for f in range(F)]

            def unit(h, total):
                pre = closure[F, h] + closure[0, h] * cells[0]
                for f in range(1, F):
                    pre = pre + closure[f, h] * cells[f]
                return total + closure[F + 1, h] * (pre + pre * jnp.tanh(pre))

            total = lax.fori_loop(0, HID, unit, jnp.zeros((part, z_cells), jnp.float32), unroll=4)
            soft = jnp.maximum(total, 0.0) + jnp.log1p(jnp.exp(-jnp.abs(total)))
            eddies.append(base_viscosity + viscosity_gain * soft)
        viscosity = jnp.concatenate(eddies, axis=0)
        centre = [fields[f, x] for f in range(F)]
        below = jnp.maximum(x - 1, 0)
        above = jnp.minimum(x + 1, x_cells - 1)
        for f in range(F):
            value = centre[f]
            west = jnp.where(x == 0, x_low[f, 0], fields[f, below])
            east = jnp.where(x == x_cells - 1, x_high[f, 0], fields[f, above])
            south = jnp.where(row == 0, y_low[f, pl.ds(x, 1), :], pltpu.roll(value, 1, 0))
            north = jnp.where(
                row == y_cells - 1, y_high[f, pl.ds(x, 1), :], pltpu.roll(value, y_cells - 1, 0)
            )
            lower = jnp.where(lane == 0, 0.0, pltpu.roll(value, 1, 1))
            upper = jnp.where(lane == z_cells - 1, 0.0, pltpu.roll(value, z_cells - 1, 1))
            laplacian = east + west + north + south + upper + lower - 6.0 * value
            advection = (
                centre[0] * (east - west) + centre[1] * (north - south) + centre[2] * (upper - lower)
            )
            tendency = viscosity * laplacian - 0.5 * advection
            if f == 2:
                tendency = tendency + buoyancy * centre[3]
            new_fields[f, x] = value + time_step * tendency
        return carry

    lax.fori_loop(0, x_cells, plane, 0)


def evolve(closure, fields, x_low, x_high, y_low, y_high):
    vmem = pl.BlockSpec(memory_space=pltpu.VMEM)
    return pl.pallas_call(
        evolve_kernel,
        out_shape=jax.ShapeDtypeStruct(fields.shape, fields.dtype),
        in_specs=[pl.BlockSpec(memory_space=pltpu.SMEM)] + [vmem] * 5,
        out_specs=vmem,
        compiler_params=pltpu.CompilerParams(vmem_limit_bytes=48 * 1024 * 1024),
        name="evolve_brick",
    )(closure, fields, x_low, x_high, y_low, y_high)


def cube_tendency(padded, closure_in, closure_bias, closure_out):
    centre = padded[:, 1:-1, 1:-1, 1:-1]
    east, west = padded[:, 2:, 1:-1, 1:-1], padded[:, :-2, 1:-1, 1:-1]
    north, south = padded[:, 1:-1, 2:, 1:-1], padded[:, 1:-1, :-2, 1:-1]
    upper, lower = padded[:, 1:-1, 1:-1, 2:], padded[:, 1:-1, 1:-1, :-2]
    laplacian = east + west + north + south + upper + lower - 6.0 * centre
    advection = centre[0] * (east - west) + centre[1] * (north - south) + centre[2] * (upper - lower)
    columns = centre.reshape(F, CELLS)
    hidden = jax.nn.silu(jnp.dot(closure_in, columns, precision=highest) + closure_bias[:, None])
    soft = jax.nn.softplus(jnp.dot(closure_out, hidden, precision=highest))
    viscosity = base_viscosity + viscosity_gain * soft.reshape(SUB, SUB, SUB)
    tendency = viscosity * laplacian - 0.5 * advection
    return tendency.at[2].add(buoyancy * centre[3])


def patch_rows(cube):
    half = SUB // 2
    split = cube.astype(jnp.bfloat16).reshape(F, SUB, half, 2, half, 2)
    return jnp.transpose(split, (1, 0, 3, 5, 2, 4)).reshape(SUB * F, 256)


def slot_lists(sample_trainer, column, trainers):
    owner_ids = jnp.arange(sample_trainer.shape[0], dtype=jnp.int32)
    same_trainer = sample_trainer[:, None] == sample_trainer[None, :]
    earlier = owner_ids[None, :] < owner_ids[:, None]
    rank_all = jnp.sum((same_trainer & earlier).astype(jnp.int32), axis=1)
    mine_mask = sample_trainer == column
    slot_ids = jnp.arange(TCAP, dtype=jnp.int32)
    chosen = mine_mask[None, :] & (rank_all[None, :] == slot_ids[:, None])
    slot_owner = jnp.sum(jnp.where(chosen, owner_ids[None, :], 0), axis=1)
    slot_valid = jnp.any(chosen, axis=1)
    sample_count = jnp.maximum(jnp.sum(mine_mask.astype(jnp.int32)), 1)
    shift = jnp.mod(column - slot_owner % trainers, trainers)
    table = jnp.stack([shift, slot_owner // trainers, slot_valid.astype(jnp.int32)])
    slot_weight = jnp.where(slot_valid, 1.0 / (sample_count.astype(jnp.float32) * CELLS), 0.0)
    weights = jnp.repeat(2.0 * slot_weight, 64).reshape(PAIRS, 1, 128)
    return table.astype(jnp.int32), jnp.broadcast_to(weights, (PAIRS, 8, 128))


def on_device(
    fields, closure_in, closure_bias, closure_out, master, momentum, sample_block, sample_trainer
):
    group_count = lax.axis_size("grp")
    x_devices = lax.axis_size("gx")
    y_devices = lax.axis_size("gy")
    trainers = x_devices * y_devices
    my_group = lax.axis_index("grp")
    my_column = lax.axis_index("gx") * y_devices + lax.axis_index("gy")
    is_trainer = my_group == group_count - 1
    everyone = ("grp", "gx", "gy")
    first_trainer = (group_count - 1) * trainers
    brick = fields[0]
    x_cells, y_cells, z_cells = brick.shape[1:]

    def neighbours(values_low, values_high, axis):
        count = lax.axis_size(axis)
        from_low = lax.ppermute(values_high, axis, [(i, (i + 1) % count) for i in range(count)])
        from_high = lax.ppermute(values_low, axis, [((i + 1) % count, i) for i in range(count)])
        return from_low, from_high

    x_low, x_high = neighbours(brick[:, :1], brick[:, -1:], "gx")
    y_low, y_high = neighbours(brick[:, :, 0], brick[:, :, -1], "gy")

    sim_group = jnp.minimum(my_group, group_count - 2)
    block_id = sample_block[sim_group * trainers + my_column]
    y_blocks = y_cells // SUB
    z_blocks = z_cells // SUB
    x_start = block_id // (y_blocks * z_blocks) * SUB
    y_start = block_id // z_blocks % y_blocks * SUB
    z_start = block_id % z_blocks * SUB
    walled = jnp.pad(brick, ((0, 0), (1, 1), (1, 1), (1, 1)))
    core = lax.dynamic_slice(walled, (0, x_start, y_start, z_start), (F, SUB + 2, SUB + 2, SUB + 2))

    def side(values, starts, shape):
        pads = [(0, 0)] + [(1, 1)] * (values.ndim - 1)
        return lax.dynamic_slice(jnp.pad(values, pads), (0,) + starts, (F,) + shape)

    span = SUB + 2
    place = lax.broadcasted_iota(jnp.int32, (1, span, span, span), 1) + x_start
    across = lax.broadcasted_iota(jnp.int32, (1, span, span, span), 2) + y_start
    core = jnp.where(
        place == 0, side(x_low[:, 0], (y_start, z_start), (span, span))[:, None], core
    )
    core = jnp.where(
        place == x_cells + 1, side(x_high[:, 0], (y_start, z_start), (span, span))[:, None], core
    )
    core = jnp.where(
        across == 0, side(y_low, (x_start, z_start), (span, span))[:, :, None], core
    )
    core = jnp.where(
        across == y_cells + 1, side(y_high, (x_start, z_start), (span, span))[:, :, None], core
    )
    change = cube_tendency(core, closure_in, closure_bias, closure_out)
    payload = jnp.concatenate([patch_rows(core[:, 1:-1, 1:-1, 1:-1]), patch_rows(change)], axis=0)

    landed = jnp.stack(
        [
            lax.ppermute(
                payload,
                everyone,
                [(g * trainers + c, first_trainer + c) for c in range(trainers)],
            )
            for g in range(group_count - 1)
        ]
    )
    arrived = [landed]
    for shift in range(1, trainers):
        pairs = [
            (first_trainer + c, first_trainer + (c + shift) % trainers) for c in range(trainers)
        ]
        arrived.append(lax.ppermute(landed, everyone, pairs))

    slots, weights = slot_lists(sample_trainer, my_column, trainers)
    first_count = CH * TAPS * F
    first = jnp.pad(master[:first_count].reshape(CH, TAPS * F), ((0, 0), (0, 256 - TAPS * F)))
    last = jnp.pad(master[first_count:].reshape(TAPS * F, CH).T, ((0, 0), (0, 256 - TAPS * F)))
    closure = jnp.concatenate(
        [0.5 * closure_in.T, 0.5 * closure_bias[None], closure_out[None]], axis=0
    )

    def train_here():
        delta_first, delta_last, new_brick = train_cubes(
            slots, first, last, weights, arrived, brick
        )
        delta = jnp.concatenate(
            [delta_first[:, : TAPS * F].reshape(-1), delta_last[:, : TAPS * F].T.reshape(-1)]
        )
        return delta, new_brick

    def evolve_here():
        new_brick = evolve(closure, brick, x_low, x_high, y_low, y_high)
        return jnp.zeros((NPARAM,), jnp.float32), new_brick

    delta, new_brick = lax.cond(is_trainer, train_here, evolve_here)

    part_size = NPARAM // trainers
    total = jnp.zeros((NPARAM,), jnp.float32)
    mine = lax.dynamic_slice_in_dim(delta, my_column * part_size, part_size)
    for shift in range(1, trainers):
        pairs = [
            (first_trainer + c, first_trainer + (c + shift) % trainers) for c in range(trainers)
        ]
        target = (my_column + shift) % trainers
        piece = lax.dynamic_slice_in_dim(delta, target * part_size, part_size)
        mine = mine + lax.ppermute(piece, everyone, pairs)
    total = lax.dynamic_update_slice_in_dim(total, mine, my_column * part_size, 0)
    for shift in range(1, trainers):
        pairs = [
            (first_trainer + c, first_trainer + (c + shift) % trainers) for c in range(trainers)
        ]
        source = (my_column - shift) % trainers
        total = lax.dynamic_update_slice_in_dim(
            total, lax.ppermute(mine, everyone, pairs), source * part_size, 0
        )
    final = jnp.where(is_trainer, total, 0.0)
    for g in range(group_count - 1):
        pairs = [(first_trainer + c, g * trainers + c) for c in range(trainers)]
        final = final + lax.ppermute(total, everyone, pairs)

    share_size = NPARAM // (group_count * trainers)
    share_start = (my_group * trainers + my_column) * share_size
    momentum_share = lax.dynamic_slice_in_dim(momentum, share_start, share_size)
    master_share = lax.dynamic_slice_in_dim(master, share_start, share_size)
    inverse = 1.0 / jnp.sqrt(jnp.sum(final * final) / NPARAM + norm_epsilon)
    delta_share = lax.dynamic_slice_in_dim(final, share_start, share_size)
    new_momentum = momentum_decay * momentum_share + delta_share * inverse
    new_master = master_share - outer_rate * new_momentum
    return (new_brick[None], new_master, new_momentum)


def solution(mesh):
    in_specs = (P("grp", None, "gx", "gy", None), P(), P(), P(), P(), P(), P(), P())
    out_specs = (P("grp", None, "gx", "gy", None), P(("grp", "gx", "gy")), P(("grp", "gx", "gy")))
    return jax.shard_map(
        on_device, mesh=mesh, in_specs=in_specs, out_specs=out_specs, check_vma=False
    )
```

```python
import functools

import jax
import jax.numpy as jnp
import numpy as np
from jax import lax
from jax.experimental import pallas as pl
from jax.experimental.pallas import tpu as pltpu
from jax.sharding import PartitionSpec as P

F = 5
CH = 64
HID = 64
SUB = 16
TCAP = 6
INNER = 3
CELLS = 4096
NPARAM = 17280
TAPS = 27
PAIRS = TCAP // 2
COLS = (SUB + 2) * 128
PATCH = 16 * F
STACK = 3 * PATCH

time_step = 0.1
base_viscosity = 0.02
viscosity_gain = 0.2
buoyancy = 0.5
inner_rate = 0.02
outer_rate = 0.01
momentum_decay = 0.9
norm_epsilon = 1e-06
highest = lax.Precision.HIGHEST


def patch_position(row):
    group, py, pz = row // 4, row // 2 % 2, row % 2
    ypos = py + 1 if group in (0, 1) else (3 if py == 0 else 0)
    zpos = pz + 1 if group in (0, 2) else (3 if pz == 0 else 0)
    return ypos - 1, zpos - 1


def selections():
    first = np.zeros((4, 256, STACK), np.float32)
    last = np.zeros((4, 256, STACK), np.float32)
    for cell in range(4):
        py, pz = cell // 2, cell % 2
        for kx in range(3):
            for channel in range(F):
                for row in range(16):
                    ypos, zpos = patch_position(row)
                    column = kx * PATCH + channel * 16 + row
                    dy, dz = ypos - py, zpos - pz
                    if abs(dy) <= 1 and abs(dz) <= 1:
                        tap = 9 * kx + 3 * (dy + 1) + dz + 1
                        first[cell, tap * F + channel, column] = 1.0
                        last[cell, channel * TAPS + 26 - tap, column] = 1.0
    return first, last


SELECT_FIRST, SELECT_LAST = selections()


def dot_rows(left, right):
    return jnp.dot(left, right, preferred_element_type=jnp.float32)


def dot_lanes(left, right):
    return lax.dot_general(left, right, (((1,), (1,)), ((), ())), preferred_element_type=jnp.float32)


def patch_masks():
    row = lax.broadcasted_iota(jnp.int32, (8, 128), 0)
    lane = lax.broadcasted_iota(jnp.int32, (8, 128), 1)
    return {
        "pz0": row % 2 == 0,
        "py0": row // 2 % 2 == 0,
        "centre": row < 4,
        "z_first": lane % 8 == 0,
        "z_last": lane % 8 == 7,
        "y_first": lane // 8 % 8 == 0,
        "y_last": lane // 8 % 8 == 7,
    }


def edge_shift(values, step, parity_zero, first, last, forward):
    before = jnp.where(first, 0.0, pltpu.roll(values, step, 1))
    after = jnp.where(last, 0.0, pltpu.roll(values, 128 - step, 1))
    if forward:
        return jnp.where(parity_zero, after, before)
    return jnp.where(parity_zero, before, after)


def patch_stack(rows, masks):
    both = rows + pltpu.roll(rows, 4, 0)
    z_edge = edge_shift(both, 1, masks["pz0"], masks["z_first"], masks["z_last"], True)
    upper = jnp.where(masks["centre"], both, z_edge)
    lower = edge_shift(upper, 8, masks["py0"], masks["y_first"], masks["y_last"], True)
    return upper, lower


def patch_fold(upper, lower, masks):
    def fold_z(values):
        moved = edge_shift(values, 1, masks["pz0"], masks["z_first"], masks["z_last"], False)
        return values + pltpu.roll(moved, 4, 0)

    shifted = edge_shift(fold_z(lower), 8, masks["py0"], masks["y_first"], masks["y_last"], False)
    return fold_z(upper) + shifted


def store_planes(ref, pair, x, channels):
    stacked = jnp.concatenate([part for both in channels for part in both], axis=0).astype(jnp.bfloat16)
    for kx in range(3):
        start = pl.multiple_of((x + 2 - kx) * 128, 128)
        ref[pair, kx * PATCH : (kx + 1) * PATCH, pl.ds(start, 128)] = stacked


def train_kernel(sources, *refs):
    (slots, first_ref, last_ref, weight_ref, select_first, select_last) = refs[:6]
    arrived = refs[6 : 6 + sources]
    fields_ref = refs[6 + sources]
    delta_first, delta_last, new_fields_ref = refs[7 + sources : 10 + sources]
    (
        cubes,
        table,
        targets,
        inputs,
        errors,
        hiddens,
        slopes,
        partial_out,
        big_first,
        big_last,
        big_last_t,
        grad_first,
        grad_last,
        now_first,
        now_last,
        slot_sems,
        field_sem,
    ) = refs[10 + sources :]

    field_copy = pltpu.make_async_copy(fields_ref, new_fields_ref, field_sem)
    field_copy.start()
    for slot in range(TCAP):
        for source in range(sources):

            @pl.when((slots[2, slot] == 1) & (slots[0, slot] == source))
            def _():
                pltpu.make_async_copy(
                    arrived[source].at[slots[1, slot]], cubes.at[slot], slot_sems.at[slot]
                ).start()

        @pl.when(slots[2, slot] == 0)
        def _():
            cubes[slot] = jnp.zeros((2 * SUB * F, 256), jnp.bfloat16)

    masks = patch_masks()
    errors[...] = jnp.zeros(errors.shape, errors.dtype)
    inputs[...] = jnp.zeros(inputs.shape, inputs.dtype)
    partial_out[:, :, :128] = jnp.zeros((PAIRS, STACK, 128), jnp.float32)
    partial_out[:, :, COLS - 128 :] = jnp.zeros((PAIRS, STACK, 128), jnp.float32)
    table[...] = jnp.zeros(table.shape, table.dtype)
    targets[...] = jnp.zeros(targets.shape, targets.dtype)
    start_first = first_ref[...].astype(jnp.bfloat16).astype(jnp.float32)
    start_last = last_ref[...].astype(jnp.bfloat16).astype(jnp.float32)
    now_first[...] = start_first
    now_last[...] = start_last

    for slot in range(TCAP):

        @pl.when(slots[2, slot] == 1)
        def _():
            pltpu.make_async_copy(arrived[0].at[0], cubes.at[slot], slot_sems.at[slot]).wait()

    low_lanes = lax.broadcasted_iota(jnp.int32, (SUB * F, 128), 1) < 64

    def spread_rows(pair, start, put):
        even = cubes[2 * pair, start : start + SUB * F, :].astype(jnp.float32)
        odd = cubes[2 * pair + 1, start : start + SUB * F, :].astype(jnp.float32)
        for half in range(2):
            left = even[:, half * 128 : (half + 1) * 128]
            right = odd[:, half * 128 : (half + 1) * 128]
            put(2 * half, jnp.where(low_lanes, left, pltpu.roll(right, 64, 1)))
            put(2 * half + 1, jnp.where(low_lanes, pltpu.roll(left, 64, 1), right))

    for pair in range(PAIRS):

        def put_input(cell, values):
            table[pl.ds(cell, SUB * F, 8), :] = values

        def put_target(cell, values):
            targets[pl.ds(pair * SUB * F * 8 + cell, SUB * F, 8), :] = values

        spread_rows(pair, 0, put_input)
        spread_rows(pair, SUB * F, put_target)

        def stack_plane(x, carry):
            base = pl.multiple_of(x * (F * 8), 8)
            rows = table[pl.ds(base, F * 8), :]
            channels = [patch_stack(rows[8 * c : 8 * c + 8], masks) for c in range(F)]
            store_planes(inputs, pair, x, channels)
            return carry

        lax.fori_loop(0, SUB, stack_plane, 0, unroll=8)

    def train_step(step, step_carry):
        first_now = now_first[...].astype(jnp.bfloat16)
        last_now = now_last[...].astype(jnp.bfloat16)
        for cell in range(4):
            rows = slice(cell * CH, (cell + 1) * CH)
            big_first[rows, :] = dot_rows(first_now, select_first[cell]).astype(jnp.bfloat16)
            big_last[rows, :] = dot_rows(last_now, select_last[cell]).astype(jnp.bfloat16)
        big_last_t[...] = big_last[...].T
        grad_first[...] = jnp.zeros(grad_first.shape, jnp.float32)
        grad_last[...] = jnp.zeros(grad_last.shape, jnp.float32)

        def forward(index, carry):
            pair = index // 8
            column = pl.multiple_of((index % 8) * 256 + 128, 128)
            pre = dot_rows(big_first[...], inputs[pair, :, pl.ds(column, 256)])
            sigmoid = 0.5 * jnp.tanh(0.5 * pre) + 0.5
            value = pre * sigmoid
            hidden = value.astype(jnp.bfloat16)
            hiddens[pair, :, pl.ds(column, 256)] = hidden
            slopes[pair, :, pl.ds(column, 256)] = sigmoid + value * (1.0 - sigmoid)
            partial_out[pair, :, pl.ds(column, 256)] = dot_rows(big_last_t[...], hidden)
            return carry

        lax.fori_loop(0, 8 * PAIRS, forward, 0, unroll=2)

        def error_plane(index, carry):
            pair = index // SUB
            x = index % SUB
            column = pl.multiple_of((x + 1) * 128, 128)
            total = (
                partial_out[pair, 0:PATCH, pl.ds(pl.multiple_of(column + 128, 128), 128)]
                + partial_out[pair, PATCH : 2 * PATCH, pl.ds(column, 128)]
                + partial_out[pair, 2 * PATCH :, pl.ds(pl.multiple_of(column - 128, 128), 128)]
            )
            wanted = targets[pl.ds(pl.multiple_of(index * (F * 8), 8), F * 8), :]
            weight = weight_ref[pair]
            channels = []
            for c in range(F):
                predicted = patch_fold(
                    total[16 * c : 16 * c + 8], total[16 * c + 8 : 16 * c + 16], masks
                )
                error = weight * (predicted - wanted[8 * c : 8 * c + 8])
                error = jnp.where(masks["centre"], error, 0.0)
                error = error.astype(jnp.bfloat16).astype(jnp.float32)
                channels.append(patch_stack(error, masks))
            store_planes(errors, pair, x, channels)
            return carry

        lax.fori_loop(0, SUB * PAIRS, error_plane, 0, unroll=8)

        def backward(index, carry):
            pair = index // 4
            column = pl.multiple_of((index % 4) * 512 + 128, 128)
            error_stack = errors[pair, :, pl.ds(column, 512)]
            hidden_grad = dot_rows(big_last[...], error_stack)
            pre_grad = (hidden_grad * slopes[pair, :, pl.ds(column, 512)]).astype(jnp.bfloat16)
            grad_first[...] += dot_lanes(pre_grad, inputs[pair, :, pl.ds(column, 512)])
            grad_last[...] += dot_lanes(hiddens[pair, :, pl.ds(column, 512)], error_stack)
            return carry

        lax.fori_loop(0, 4 * PAIRS, backward, 0)

        def folded(grad_ref, select_ref):
            total = jnp.zeros((3 * CH, 256), jnp.float32)
            for cell in range(4):
                rest = grad_ref[cell * CH : (cell + 1) * CH, :]
                parts = []
                for _ in range(3):
                    parts.append(rest.astype(jnp.bfloat16))
                    rest = rest - parts[-1].astype(jnp.float32)
                total = total + dot_lanes(jnp.concatenate(parts, axis=0), select_ref[cell])
            return total[:CH] + total[CH : 2 * CH] + total[2 * CH :]

        now_first[...] = now_first[...] - inner_rate * folded(grad_first, select_first)
        now_last[...] = now_last[...] - inner_rate * folded(grad_last, select_last)
        return step_carry

    lax.fori_loop(0, INNER, train_step, 0)
    delta_first[...] = start_first - now_first[...]
    delta_last[...] = start_last - now_last[...]
    field_copy.wait()


def train_cubes(slots, first, last, weights, arrived, fields):
    sources = len(arrived)
    vmem = pl.BlockSpec(memory_space=pltpu.VMEM)
    anywhere = pl.BlockSpec(memory_space=pl.ANY)
    return pl.pallas_call(
        functools.partial(train_kernel, sources),
        out_shape=(
            jax.ShapeDtypeStruct((CH, 256), jnp.float32),
            jax.ShapeDtypeStruct((CH, 256), jnp.float32),
            jax.ShapeDtypeStruct(fields.shape, fields.dtype),
        ),
        in_specs=[pl.BlockSpec(memory_space=pltpu.SMEM)] + [vmem] * 5 + [anywhere] * (sources + 1),
        out_specs=(vmem, vmem, anywhere),
        scratch_shapes=[
            pltpu.VMEM((TCAP, 2 * SUB * F, 256), jnp.bfloat16),
            pltpu.VMEM((SUB * F * 8, 128), jnp.float32),
            pltpu.VMEM((PAIRS * SUB * F * 8, 128), jnp.float32),
            pltpu.VMEM((PAIRS, STACK, COLS), jnp.bfloat16),
            pltpu.VMEM((PAIRS, STACK, COLS), jnp.bfloat16),
            pltpu.VMEM((PAIRS, 4 * CH, COLS), jnp.bfloat16),
            pltpu.VMEM((PAIRS, 4 * CH, COLS), jnp.float32),
            pltpu.VMEM((PAIRS, STACK, COLS), jnp.float32),
            pltpu.VMEM((4 * CH, STACK), jnp.bfloat16),
            pltpu.VMEM((4 * CH, STACK), jnp.bfloat16),
            pltpu.VMEM((STACK, 4 * CH), jnp.bfloat16),
            pltpu.VMEM((4 * CH, STACK), jnp.float32),
            pltpu.VMEM((4 * CH, STACK), jnp.float32),
            pltpu.VMEM((CH, 256), jnp.float32),
            pltpu.VMEM((CH, 256), jnp.float32),
            pltpu.SemaphoreType.DMA((TCAP,)),
            pltpu.SemaphoreType.DMA,
        ],
        compiler_params=pltpu.CompilerParams(vmem_limit_bytes=48 * 1024 * 1024),
        name="train_cubes",
    )(
        slots,
        first,
        last,
        weights,
        jnp.asarray(SELECT_FIRST, jnp.bfloat16),
        jnp.asarray(SELECT_LAST, jnp.bfloat16),
        *arrived,
        fields,
    )


def evolve_kernel(closure, fields, x_low, x_high, y_low, y_high, new_fields):
    x_cells, y_cells, z_cells = fields.shape[1:]
    row = lax.broadcasted_iota(jnp.int32, (y_cells, z_cells), 0)
    lane = lax.broadcasted_iota(jnp.int32, (y_cells, z_cells), 1)
    part = y_cells // 2

    def plane(x, carry):
        eddies = []
        for half in range(2):
            rows = pl.ds(half * part, part)
            cells = [fields[f, x, rows, :] for f in range(F)]

            def unit(h, total):
                pre = closure[F, h] + closure[0, h] * cells[0]
                for f in range(1, F):
                    pre = pre + closure[f, h] * cells[f]
                return total + closure[F + 1, h] * (pre + pre * jnp.tanh(pre))

            total = lax.fori_loop(0, HID, unit, jnp.zeros((part, z_cells), jnp.float32), unroll=4)
            soft = jnp.maximum(total, 0.0) + jnp.log1p(jnp.exp(-jnp.abs(total)))
            eddies.append(base_viscosity + viscosity_gain * soft)
        viscosity = jnp.concatenate(eddies, axis=0)
        centre = [fields[f, x] for f in range(F)]
        below = jnp.maximum(x - 1, 0)
        above = jnp.minimum(x + 1, x_cells - 1)
        for f in range(F):
            value = centre[f]
            west = jnp.where(x == 0, x_low[f, 0], fields[f, below])
            east = jnp.where(x == x_cells - 1, x_high[f, 0], fields[f, above])
            south = jnp.where(row == 0, y_low[f, pl.ds(x, 1), :], pltpu.roll(value, 1, 0))
            north = jnp.where(
                row == y_cells - 1, y_high[f, pl.ds(x, 1), :], pltpu.roll(value, y_cells - 1, 0)
            )
            lower = jnp.where(lane == 0, 0.0, pltpu.roll(value, 1, 1))
            upper = jnp.where(lane == z_cells - 1, 0.0, pltpu.roll(value, z_cells - 1, 1))
            laplacian = east + west + north + south + upper + lower - 6.0 * value
            advection = (
                centre[0] * (east - west) + centre[1] * (north - south) + centre[2] * (upper - lower)
            )
            tendency = viscosity * laplacian - 0.5 * advection
            if f == 2:
                tendency = tendency + buoyancy * centre[3]
            new_fields[f, x] = value + time_step * tendency
        return carry

    lax.fori_loop(0, x_cells, plane, 0)


def evolve(closure, fields, x_low, x_high, y_low, y_high):
    vmem = pl.BlockSpec(memory_space=pltpu.VMEM)
    return pl.pallas_call(
        evolve_kernel,
        out_shape=jax.ShapeDtypeStruct(fields.shape, fields.dtype),
        in_specs=[pl.BlockSpec(memory_space=pltpu.SMEM)] + [vmem] * 5,
        out_specs=vmem,
        compiler_params=pltpu.CompilerParams(vmem_limit_bytes=48 * 1024 * 1024),
        name="evolve_brick",
    )(closure, fields, x_low, x_high, y_low, y_high)


def cube_tendency(padded, closure_in, closure_bias, closure_out):
    centre = padded[:, 1:-1, 1:-1, 1:-1]
    east, west = padded[:, 2:, 1:-1, 1:-1], padded[:, :-2, 1:-1, 1:-1]
    north, south = padded[:, 1:-1, 2:, 1:-1], padded[:, 1:-1, :-2, 1:-1]
    upper, lower = padded[:, 1:-1, 1:-1, 2:], padded[:, 1:-1, 1:-1, :-2]
    laplacian = east + west + north + south + upper + lower - 6.0 * centre
    advection = centre[0] * (east - west) + centre[1] * (north - south) + centre[2] * (upper - lower)
    columns = centre.reshape(F, CELLS)
    hidden = jax.nn.silu(jnp.dot(closure_in, columns, precision=highest) + closure_bias[:, None])
    soft = jax.nn.softplus(jnp.dot(closure_out, hidden, precision=highest))
    viscosity = base_viscosity + viscosity_gain * soft.reshape(SUB, SUB, SUB)
    tendency = viscosity * laplacian - 0.5 * advection
    return tendency.at[2].add(buoyancy * centre[3])


def patch_rows(cube):
    half = SUB // 2
    split = cube.astype(jnp.bfloat16).reshape(F, SUB, half, 2, half, 2)
    return jnp.transpose(split, (1, 0, 3, 5, 2, 4)).reshape(SUB * F, 256)


def doubling_steps(x_devices, y_devices):
    along_y = [1 << bit for bit in reversed(range(y_devices.bit_length() - 1))]
    along_x = [y_devices << bit for bit in reversed(range(x_devices.bit_length() - 1))]
    return along_y + along_x


def slot_lists(sample_trainer, column, trainers, groups, steps):
    owner_ids = jnp.arange(sample_trainer.shape[0], dtype=jnp.int32)
    same_trainer = sample_trainer[:, None] == sample_trainer[None, :]
    earlier = owner_ids[None, :] < owner_ids[:, None]
    rank_all = jnp.sum((same_trainer & earlier).astype(jnp.int32), axis=1)
    mine_mask = sample_trainer == column
    slot_ids = jnp.arange(TCAP, dtype=jnp.int32)
    chosen = mine_mask[None, :] & (rank_all[None, :] == slot_ids[:, None])
    slot_owner = jnp.sum(jnp.where(chosen, owner_ids[None, :], 0), axis=1)
    slot_valid = jnp.any(chosen, axis=1)
    sample_count = jnp.maximum(jnp.sum(mine_mask.astype(jnp.int32)), 1)
    apart = jnp.bitwise_xor(slot_owner % trainers, column)
    place = jnp.zeros_like(apart)
    for order, distance in enumerate(steps[:-1]):
        place = place + (apart // distance % 2) * (1 << order)
    half = apart // steps[-1] % 2
    table = jnp.stack([half, place * groups + slot_owner // trainers, slot_valid.astype(jnp.int32)])
    slot_weight = jnp.where(slot_valid, 1.0 / (sample_count.astype(jnp.float32) * CELLS), 0.0)
    weights = jnp.repeat(2.0 * slot_weight, 64).reshape(PAIRS, 1, 128)
    return table.astype(jnp.int32), jnp.broadcast_to(weights, (PAIRS, 8, 128))


def on_device(
    fields, closure_in, closure_bias, closure_out, master, momentum, sample_block, sample_trainer
):
    group_count = lax.axis_size("grp")
    x_devices = lax.axis_size("gx")
    y_devices = lax.axis_size("gy")
    trainers = x_devices * y_devices
    my_group = lax.axis_index("grp")
    my_column = lax.axis_index("gx") * y_devices + lax.axis_index("gy")
    is_trainer = my_group == group_count - 1
    everyone = ("grp", "gx", "gy")
    first_trainer = (group_count - 1) * trainers
    brick = fields[0]
    x_cells, y_cells, z_cells = brick.shape[1:]

    def neighbours(values_low, values_high, axis):
        count = lax.axis_size(axis)
        from_low = lax.ppermute(values_high, axis, [(i, (i + 1) % count) for i in range(count)])
        from_high = lax.ppermute(values_low, axis, [((i + 1) % count, i) for i in range(count)])
        return from_low, from_high

    x_low, x_high = neighbours(brick[:, :1], brick[:, -1:], "gx")
    y_low, y_high = neighbours(brick[:, :, 0], brick[:, :, -1], "gy")

    sim_group = jnp.minimum(my_group, group_count - 2)
    block_id = sample_block[sim_group * trainers + my_column]
    y_blocks = y_cells // SUB
    z_blocks = z_cells // SUB
    x_start = block_id // (y_blocks * z_blocks) * SUB
    y_start = block_id // z_blocks % y_blocks * SUB
    z_start = block_id % z_blocks * SUB
    walled = jnp.pad(brick, ((0, 0), (1, 1), (1, 1), (1, 1)))
    core = lax.dynamic_slice(walled, (0, x_start, y_start, z_start), (F, SUB + 2, SUB + 2, SUB + 2))

    def side(values, starts, shape):
        pads = [(0, 0)] + [(1, 1)] * (values.ndim - 1)
        return lax.dynamic_slice(jnp.pad(values, pads), (0,) + starts, (F,) + shape)

    span = SUB + 2
    place = lax.broadcasted_iota(jnp.int32, (1, span, span, span), 1) + x_start
    across = lax.broadcasted_iota(jnp.int32, (1, span, span, span), 2) + y_start
    core = jnp.where(
        place == 0, side(x_low[:, 0], (y_start, z_start), (span, span))[:, None], core
    )
    core = jnp.where(
        place == x_cells + 1, side(x_high[:, 0], (y_start, z_start), (span, span))[:, None], core
    )
    core = jnp.where(
        across == 0, side(y_low, (x_start, z_start), (span, span))[:, :, None], core
    )
    core = jnp.where(
        across == y_cells + 1, side(y_high, (x_start, z_start), (span, span))[:, :, None], core
    )
    change = cube_tendency(core, closure_in, closure_bias, closure_out)
    payload = jnp.concatenate([patch_rows(core[:, 1:-1, 1:-1, 1:-1]), patch_rows(change)], axis=0)

    def swap(distance):
        return [(first_trainer + c, first_trainer + (c ^ distance)) for c in range(trainers)]

    landed = jnp.stack(
        [
            lax.ppermute(
                payload,
                everyone,
                [(g * trainers + c, first_trainer + c) for c in range(trainers)],
            )
            for g in range(group_count - 1)
        ]
    )
    steps = doubling_steps(x_devices, y_devices)
    held = landed
    for distance in steps[:-1]:
        held = jnp.concatenate([held, lax.ppermute(held, everyone, swap(distance))], axis=0)
    arrived = [held, lax.ppermute(held, everyone, swap(steps[-1]))]

    slots, weights = slot_lists(sample_trainer, my_column, trainers, group_count - 1, steps)
    first_count = CH * TAPS * F
    first = jnp.pad(master[:first_count].reshape(CH, TAPS * F), ((0, 0), (0, 256 - TAPS * F)))
    last = jnp.pad(master[first_count:].reshape(TAPS * F, CH).T, ((0, 0), (0, 256 - TAPS * F)))
    closure = jnp.concatenate(
        [0.5 * closure_in.T, 0.5 * closure_bias[None], closure_out[None]], axis=0
    )

    def train_here():
        delta_first, delta_last, new_brick = train_cubes(
            slots, first, last, weights, arrived, brick
        )
        delta = jnp.concatenate(
            [delta_first[:, : TAPS * F].reshape(-1), delta_last[:, : TAPS * F].T.reshape(-1)]
        )
        return delta, new_brick

    def evolve_here():
        new_brick = evolve(closure, brick, x_low, x_high, y_low, y_high)
        return jnp.zeros((NPARAM,), jnp.float32), new_brick

    delta, new_brick = lax.cond(is_trainer, train_here, evolve_here)

    total = delta
    for distance in steps:
        total = total + lax.ppermute(total, everyone, swap(distance))
    final = jnp.where(is_trainer, total, 0.0)
    for g in range(group_count - 1):
        pairs = [(first_trainer + c, g * trainers + c) for c in range(trainers)]
        final = final + lax.ppermute(total, everyone, pairs)

    share_size = NPARAM // (group_count * trainers)
    share_start = (my_group * trainers + my_column) * share_size
    momentum_share = lax.dynamic_slice_in_dim(momentum, share_start, share_size)
    master_share = lax.dynamic_slice_in_dim(master, share_start, share_size)
    inverse = 1.0 / jnp.sqrt(jnp.sum(final * final) / NPARAM + norm_epsilon)
    delta_share = lax.dynamic_slice_in_dim(final, share_start, share_size)
    new_momentum = momentum_decay * momentum_share + delta_share * inverse
    new_master = master_share - outer_rate * new_momentum
    return (new_brick[None], new_master, new_momentum)


def solution(mesh):
    in_specs = (P("grp", None, "gx", "gy", None), P(), P(), P(), P(), P(), P(), P())
    out_specs = (P("grp", None, "gx", "gy", None), P(("grp", "gx", "gy")), P(("grp", "gx", "gy")))
    return jax.shard_map(
        on_device, mesh=mesh, in_specs=in_specs, out_specs=out_specs, check_vma=False
    )
```

```python
import functools

import jax
import jax.numpy as jnp
import numpy as np
from jax import lax
from jax.experimental import pallas as pl
from jax.experimental.pallas import tpu as pltpu
from jax.sharding import PartitionSpec as P

F = 5
CH = 64
HID = 64
SUB = 16
TCAP = 6
INNER = 3
CELLS = 4096
NPARAM = 17280
TAPS = 27
PAIRS = TCAP // 2
COLS = (SUB + 2) * 128
PATCH = 16 * F
STACK = 3 * PATCH

time_step = 0.1
base_viscosity = 0.02
viscosity_gain = 0.2
buoyancy = 0.5
inner_rate = 0.02
outer_rate = 0.01
momentum_decay = 0.9
norm_epsilon = 1e-06


def patch_position(row):
    group, py, pz = row // 4, row // 2 % 2, row % 2
    ypos = py + 1 if group in (0, 1) else (3 if py == 0 else 0)
    zpos = pz + 1 if group in (0, 2) else (3 if pz == 0 else 0)
    return ypos - 1, zpos - 1


def selections():
    first = np.zeros((4, 256, STACK), np.float32)
    last = np.zeros((4, 256, STACK), np.float32)
    for cell in range(4):
        py, pz = cell // 2, cell % 2
        for kx in range(3):
            for channel in range(F):
                for row in range(16):
                    ypos, zpos = patch_position(row)
                    column = kx * PATCH + channel * 16 + row
                    dy, dz = ypos - py, zpos - pz
                    if abs(dy) <= 1 and abs(dz) <= 1:
                        tap = 9 * kx + 3 * (dy + 1) + dz + 1
                        first[cell, tap * F + channel, column] = 1.0
                        last[cell, channel * TAPS + 26 - tap, column] = 1.0
    return first, last


SELECT_FIRST, SELECT_LAST = selections()


def dot_rows(left, right):
    return jnp.dot(left, right, preferred_element_type=jnp.float32)


def dot_lanes(left, right):
    return lax.dot_general(left, right, (((1,), (1,)), ((), ())), preferred_element_type=jnp.float32)


def patch_masks():
    row = lax.broadcasted_iota(jnp.int32, (8, 128), 0)
    lane = lax.broadcasted_iota(jnp.int32, (8, 128), 1)
    return {
        "pz0": row % 2 == 0,
        "py0": row // 2 % 2 == 0,
        "centre": row < 4,
        "z_first": lane % 8 == 0,
        "z_last": lane % 8 == 7,
        "y_first": lane // 8 % 8 == 0,
        "y_last": lane // 8 % 8 == 7,
    }


def edge_shift(values, step, parity_zero, first, last, forward):
    before = jnp.where(first, 0.0, pltpu.roll(values, step, 1))
    after = jnp.where(last, 0.0, pltpu.roll(values, 128 - step, 1))
    if forward:
        return jnp.where(parity_zero, after, before)
    return jnp.where(parity_zero, before, after)


def patch_stack(rows, masks):
    both = rows + pltpu.roll(rows, 4, 0)
    z_edge = edge_shift(both, 1, masks["pz0"], masks["z_first"], masks["z_last"], True)
    upper = jnp.where(masks["centre"], both, z_edge)
    lower = edge_shift(upper, 8, masks["py0"], masks["y_first"], masks["y_last"], True)
    return upper, lower


def patch_fold(upper, lower, masks):
    def fold_z(values):
        moved = edge_shift(values, 1, masks["pz0"], masks["z_first"], masks["z_last"], False)
        return values + pltpu.roll(moved, 4, 0)

    shifted = edge_shift(fold_z(lower), 8, masks["py0"], masks["y_first"], masks["y_last"], False)
    return fold_z(upper) + shifted


def store_planes(ref, pair, x, channels):
    stacked = jnp.concatenate([part for both in channels for part in both], axis=0).astype(jnp.bfloat16)
    for kx in range(3):
        start = pl.multiple_of((x + 2 - kx) * 128, 128)
        ref[pair, kx * PATCH : (kx + 1) * PATCH, pl.ds(start, 128)] = stacked


def train_kernel(steps, *refs):
    (trainer_of, place, first_ref, last_ref, select_first, select_last) = refs[:6]
    arrived_inputs, arrived_targets = refs[6:8], refs[8:10]
    fields_ref = refs[10]
    delta_first, delta_last, new_fields_ref = refs[11:14]
    (
        slots,
        cubes,
        table,
        targets,
        inputs,
        errors,
        hiddens,
        pre_grads,
        slopes,
        partial_out,
        big_first,
        big_last,
        big_last_t,
        now_first,
        now_last,
        slot_sems,
        field_sem,
    ) = refs[14:]

    field_copy = pltpu.make_async_copy(fields_ref, new_fields_ref, field_sem)
    field_copy.start()

    groups = place[3]
    trainers = trainer_of.shape[0] // groups
    column = place[1] * place[4] + place[2]

    def visit(owner, count):
        mine = trainer_of[owner] == column

        @pl.when(mine)
        def _():
            source = lax.rem(owner, trainers)
            entry = jnp.int32(0)
            for order, distance in enumerate(steps[:-1]):
                entry = entry + apart(source, column, distance) * (1 << order)
            slots[0, count] = apart(source, column, steps[-1])
            slots[1, count] = entry * groups + lax.div(owner, trainers)

        return count + jnp.where(mine, 1, 0)

    count = lax.fori_loop(0, trainer_of.shape[0], visit, jnp.int32(0))

    def fetch(slot, wait):
        for kind, arrived in enumerate((arrived_inputs, arrived_targets)):
            for half in range(2):

                @pl.when((slot < count) & (slots[0, slot] == half))
                def _():
                    copy = pltpu.make_async_copy(
                        arrived[half].at[slots[1, slot]], cubes.at[kind, slot], slot_sems.at[kind, slot]
                    )
                    copy.wait() if wait else copy.start()

    for slot in range(TCAP):
        fetch(slot, False)

        @pl.when(slot >= count)
        def _():
            cubes[:, slot] = jnp.zeros((2, SUB * F, 256), jnp.bfloat16)

    masks = patch_masks()
    for ref in (errors, inputs):
        ref[:, :PATCH, 128:256] = jnp.zeros((PAIRS, PATCH, 128), jnp.bfloat16)
        ref[:, 2 * PATCH :, COLS - 256 : COLS - 128] = jnp.zeros((PAIRS, PATCH, 128), jnp.bfloat16)
    partial_out[:, :, :128] = jnp.zeros((PAIRS, STACK, 128), jnp.float32)
    partial_out[:, :, COLS - 128 :] = jnp.zeros((PAIRS, STACK, 128), jnp.float32)
    table[...] = jnp.zeros(table.shape, table.dtype)
    targets[...] = jnp.zeros(targets.shape, targets.dtype)
    lane = lax.broadcasted_iota(jnp.int32, (8, 128), 1)
    full_weight = 2.0 * (1.0 / (jnp.full((8, 128), count, jnp.int32).astype(jnp.float32) * CELLS))
    weights = [
        jnp.where(lane // 64 + 2 * pair < count, full_weight, 0.0) for pair in range(PAIRS)
    ]
    start_first = first_ref[...].astype(jnp.bfloat16).astype(jnp.float32)
    start_last = last_ref[...].astype(jnp.bfloat16).astype(jnp.float32)
    now_first[...] = start_first
    now_last[...] = start_last

    for slot in range(TCAP):
        fetch(slot, True)

    low_lanes = lax.broadcasted_iota(jnp.int32, (SUB * F, 128), 1) < 64

    def spread_rows(pair, kind, put):
        even = cubes[kind, 2 * pair].astype(jnp.float32)
        odd = cubes[kind, 2 * pair + 1].astype(jnp.float32)
        for half in range(2):
            left = even[:, half * 128 : (half + 1) * 128]
            right = odd[:, half * 128 : (half + 1) * 128]
            put(2 * half, jnp.where(low_lanes, left, pltpu.roll(right, 64, 1)))
            put(2 * half + 1, jnp.where(low_lanes, pltpu.roll(left, 64, 1), right))

    for pair in range(PAIRS):

        def put_input(cell, values):
            table[pl.ds(cell, SUB * F, 8), :] = values

        def put_target(cell, values):
            targets[pl.ds(pair * SUB * F * 8 + cell, SUB * F, 8), :] = values

        spread_rows(pair, 0, put_input)
        spread_rows(pair, 1, put_target)

        def stack_plane(x, carry):
            channels = [
                patch_stack(table[pl.ds(pl.multiple_of((c * SUB + x) * 8, 8), 8), :], masks)
                for c in range(F)
            ]
            store_planes(inputs, pair, x, channels)
            return carry

        lax.fori_loop(0, SUB, stack_plane, 0, unroll=8)

    def train_step(step, step_carry):
        first_now = now_first[...].astype(jnp.bfloat16)
        last_now = now_last[...].astype(jnp.bfloat16)
        for cell in range(4):
            rows = slice(cell * CH, (cell + 1) * CH)
            big_first[rows, :] = dot_rows(first_now, select_first[cell]).astype(jnp.bfloat16)
            big_last[rows, :] = dot_rows(last_now, select_last[cell]).astype(jnp.bfloat16)
        big_last_t[...] = big_last[...].T
        def forward(index, carry):
            pair = index // 4
            column = pl.multiple_of((index % 4) * 512 + 128, 128)
            pre = dot_rows(big_first[...], inputs[pair, :, pl.ds(column, 512)])
            sigmoid = 0.5 * jnp.tanh(0.5 * pre) + 0.5
            value = pre * sigmoid
            hidden = value.astype(jnp.bfloat16)
            hiddens[pair, :, pl.ds(column, 512)] = hidden
            slopes[pair, :, pl.ds(column, 512)] = sigmoid + value * (1.0 - sigmoid)
            partial_out[pair, :, pl.ds(column, 512)] = dot_rows(big_last_t[...], hidden)
            return carry

        lax.fori_loop(0, 4 * PAIRS, forward, 0, unroll=2)

        def error_plane(index, carry):
            pair = index // SUB
            x = index % SUB
            column = pl.multiple_of((x + 1) * 128, 128)
            total = (
                partial_out[pair, 0:PATCH, pl.ds(pl.multiple_of(column + 128, 128), 128)]
                + partial_out[pair, PATCH : 2 * PATCH, pl.ds(column, 128)]
                + partial_out[pair, 2 * PATCH :, pl.ds(pl.multiple_of(column - 128, 128), 128)]
            )
            weight = jnp.where(pair == 0, weights[0], jnp.where(pair == 1, weights[1], weights[2]))
            channels = []
            for c in range(F):
                predicted = patch_fold(
                    total[16 * c : 16 * c + 8], total[16 * c + 8 : 16 * c + 16], masks
                )
                row = pl.multiple_of(((pair * F + c) * SUB + x) * 8, 8)
                error = weight * (predicted - targets[pl.ds(row, 8), :])
                error = jnp.where(masks["centre"], error, 0.0)
                error = error.astype(jnp.bfloat16).astype(jnp.float32)
                channels.append(patch_stack(error, masks))
            store_planes(errors, pair, x, channels)
            return carry

        lax.fori_loop(0, SUB * PAIRS, error_plane, 0, unroll=8)

        def backward(index, carry):
            pair = index // 4
            column = pl.multiple_of((index % 4) * 512 + 128, 128)
            hidden_grad = dot_rows(big_last[...], errors[pair, :, pl.ds(column, 512)])
            slope = slopes[pair, :, pl.ds(column, 512)]
            pre_grads[pair, :, pl.ds(column, 512)] = (hidden_grad * slope).astype(jnp.bfloat16)
            return carry

        lax.fori_loop(0, 4 * PAIRS, backward, 0, unroll=2)
        body = slice(128, COLS - 128)
        grad_first = jnp.zeros((4 * CH, STACK), jnp.float32)
        grad_last = jnp.zeros((4 * CH, STACK), jnp.float32)
        for pair in range(PAIRS):
            grad_first += dot_lanes(pre_grads[pair, :, body], inputs[pair, :, body])
            grad_last += dot_lanes(hiddens[pair, :, body], errors[pair, :, body])

        def folded(grad, select_ref):
            total = jnp.zeros((3 * CH, 256), jnp.float32)
            for cell in range(4):
                rest = grad[cell * CH : (cell + 1) * CH, :]
                parts = []
                for _ in range(3):
                    parts.append(rest.astype(jnp.bfloat16))
                    rest = rest - parts[-1].astype(jnp.float32)
                total = total + dot_lanes(jnp.concatenate(parts, axis=0), select_ref[cell])
            return total[:CH] + total[CH : 2 * CH] + total[2 * CH :]

        now_first[...] = now_first[...] - inner_rate * folded(grad_first, select_first)
        now_last[...] = now_last[...] - inner_rate * folded(grad_last, select_last)
        return step_carry

    lax.fori_loop(0, INNER, train_step, 0)
    delta_first[...] = start_first - now_first[...]
    delta_last[...] = start_last - now_last[...]
    field_copy.wait()


def apart(left, right, distance):
    return jnp.where(lax.rem(lax.div(left, distance), 2) == lax.rem(lax.div(right, distance), 2), 0, 1)


def train_cubes(trainer_of, place, first, last, arrived_inputs, arrived_targets, fields, steps):
    vmem = pl.BlockSpec(memory_space=pltpu.VMEM)
    smem = pl.BlockSpec(memory_space=pltpu.SMEM)
    anywhere = pl.BlockSpec(memory_space=pl.ANY)
    hbm = pl.BlockSpec(memory_space=pltpu.HBM)
    return pl.pallas_call(
        functools.partial(train_kernel, steps),
        out_shape=(
            jax.ShapeDtypeStruct((CH, 256), jnp.float32),
            jax.ShapeDtypeStruct((CH, 256), jnp.float32),
            jax.ShapeDtypeStruct(fields.shape, fields.dtype),
        ),
        in_specs=[smem] * 2 + [vmem] * 4 + [anywhere] * 4 + [hbm],
        out_specs=(vmem, vmem, hbm),
        scratch_shapes=[
            pltpu.SMEM((2, TCAP), jnp.int32),
            pltpu.VMEM((2, TCAP, SUB * F, 256), jnp.bfloat16),
            pltpu.VMEM((SUB * F * 8, 128), jnp.float32),
            pltpu.VMEM((PAIRS * SUB * F * 8, 128), jnp.float32),
            pltpu.VMEM((PAIRS, STACK, COLS), jnp.bfloat16),
            pltpu.VMEM((PAIRS, STACK, COLS), jnp.bfloat16),
            pltpu.VMEM((PAIRS, 4 * CH, COLS), jnp.bfloat16),
            pltpu.VMEM((PAIRS, 4 * CH, COLS), jnp.bfloat16),
            pltpu.VMEM((PAIRS, 4 * CH, COLS), jnp.float32),
            pltpu.VMEM((PAIRS, STACK, COLS), jnp.float32),
            pltpu.VMEM((4 * CH, STACK), jnp.bfloat16),
            pltpu.VMEM((4 * CH, STACK), jnp.bfloat16),
            pltpu.VMEM((STACK, 4 * CH), jnp.bfloat16),
            pltpu.VMEM((CH, 256), jnp.float32),
            pltpu.VMEM((CH, 256), jnp.float32),
            pltpu.SemaphoreType.DMA((2, TCAP)),
            pltpu.SemaphoreType.DMA,
        ],
        compiler_params=pltpu.CompilerParams(vmem_limit_bytes=48 * 1024 * 1024),
        name="train_cubes",
    )(
        trainer_of,
        place,
        first,
        last,
        jnp.asarray(SELECT_FIRST, jnp.bfloat16),
        jnp.asarray(SELECT_LAST, jnp.bfloat16),
        *arrived_inputs,
        *arrived_targets,
        fields,
    )


def viscosity_of(cells, closure_in, closure_bias, closure_out):
    halves = [0.5 * value for value in cells]

    def unit(h, total):
        half = 0.5 * closure_bias[h] + closure_in[h, 0] * halves[0]
        for f in range(1, F):
            half = half + closure_in[h, f] * halves[f]
        return total + closure_out[h] * (half + half * jnp.tanh(half))

    total = lax.fori_loop(0, HID, unit, jnp.zeros(cells[0].shape, jnp.float32), unroll=4)
    soft = jnp.maximum(total, 0.0) + jnp.log1p(jnp.exp(-jnp.abs(total)))
    return base_viscosity + viscosity_gain * soft


def evolve_kernel(
    closure_in, closure_bias, closure_out, fields, x_low, x_high, y_low, y_high, new_fields
):
    x_cells, y_cells, z_cells = fields.shape[1:]
    row = lax.broadcasted_iota(jnp.int32, (y_cells, z_cells), 0)
    lane = lax.broadcasted_iota(jnp.int32, (y_cells, z_cells), 1)
    part = y_cells // 2

    def plane(x, carry):
        eddies = []
        for half in range(2):
            rows = pl.ds(half * part, part)
            cells = [fields[f, x, rows, :] for f in range(F)]
            eddies.append(viscosity_of(cells, closure_in, closure_bias, closure_out))
        viscosity = jnp.concatenate(eddies, axis=0)
        centre = [fields[f, x] for f in range(F)]
        below = jnp.maximum(x - 1, 0)
        above = jnp.minimum(x + 1, x_cells - 1)
        for f in range(F):
            value = centre[f]
            west = jnp.where(x == 0, x_low[f], fields[f, below])
            east = jnp.where(x == x_cells - 1, x_high[f], fields[f, above])
            south = jnp.where(row == 0, y_low[f, pl.ds(x, 1), :], pltpu.roll(value, 1, 0))
            north = jnp.where(
                row == y_cells - 1, y_high[f, pl.ds(x, 1), :], pltpu.roll(value, y_cells - 1, 0)
            )
            lower = jnp.where(lane == 0, 0.0, pltpu.roll(value, 1, 1))
            upper = jnp.where(lane == z_cells - 1, 0.0, pltpu.roll(value, z_cells - 1, 1))
            laplacian = east + west + north + south + upper + lower - 6.0 * value
            advection = (
                centre[0] * (east - west) + centre[1] * (north - south) + centre[2] * (upper - lower)
            )
            tendency = viscosity * laplacian - 0.5 * advection
            if f == 2:
                tendency = tendency + buoyancy * centre[3]
            new_fields[f, x] = value + time_step * tendency
        return carry

    lax.fori_loop(0, x_cells, plane, 0)


def evolve(closure_in, closure_bias, closure_out, fields, x_low, x_high, y_low, y_high):
    vmem = pl.BlockSpec(memory_space=pltpu.VMEM)
    return pl.pallas_call(
        evolve_kernel,
        out_shape=jax.ShapeDtypeStruct(fields.shape, fields.dtype),
        in_specs=[pl.BlockSpec(memory_space=pltpu.SMEM)] * 3 + [vmem] * 5,
        out_specs=vmem,
        compiler_params=pltpu.CompilerParams(vmem_limit_bytes=48 * 1024 * 1024),
        name="evolve_brick",
    )(closure_in, closure_bias, closure_out, fields, x_low, x_high, y_low, y_high)


def cell_order():
    order = np.zeros((256, 256), np.float32)
    for y in range(SUB):
        for z in range(SUB):
            order[y * SUB + z, (y % 2 * 2 + z % 2) * 64 + y // 2 * 8 + z // 2] = 1.0
    return order


CELL_ORDER = cell_order()


def corner_of(sample_block, place, x_step, y_step, y_cells, z_cells):
    x_devices, y_devices = place[5], place[4]
    gx = lax.rem(place[1] + x_step + x_devices, x_devices)
    gy = lax.rem(place[2] + y_step + y_devices, y_devices)
    group = jnp.minimum(place[0], place[3] - 1)
    block = sample_block[(group * x_devices + gx) * y_devices + gy]
    z_blocks = z_cells // SUB
    return lax.rem(lax.div(block, z_blocks), y_cells // SUB) * SUB, lax.rem(block, z_blocks) * SUB


def sample_kernel(
    y_cells,
    z_cells,
    sample_block,
    place,
    order,
    brick,
    centre,
    lower,
    upper,
    own_rows,
    faces,
    row_for_low,
    row_for_high,
    payload,
    windows,
    sems,
):
    rows_of_x = y_cells
    rows_of_field = SUB * y_cells
    window_rows = F * rows_of_field
    copies = [
        pltpu.make_async_copy(
            brick.at[:, pl.ds(w * 128, 128)], windows.at[pl.ds(w * window_rows, window_rows)], sems.at[w]
        )
        for w in range(z_cells // 128)
    ]
    for copy in copies:
        copy.start()
    for copy in copies:
        copy.wait()

    def corner(x_step, y_step):
        return corner_of(sample_block, place, x_step, y_step, y_cells, z_cells)

    def piece(row, count, stride, z, lane_start):
        values = windows[pl.ds(lax.div(z, 128) * window_rows + row, count, stride), :]
        return pltpu.roll(values, lax.rem(lane_start - lax.rem(z, 128) + 256, 128), 1)

    lane = lax.broadcasted_iota(jnp.int32, (SUB, 128), 1)
    y_start, z_start = corner(0, 0)
    z_below = jnp.maximum(z_start - 1, 0)
    z_above = jnp.minimum(z_start + SUB, z_cells - 1)
    for field in range(F):
        for half in range(2):
            inside = jnp.zeros((SUB, 128), jnp.float32)
            below = jnp.zeros((SUB, 128), jnp.float32)
            above = jnp.zeros((SUB, 128), jnp.float32)
            for step in range(8):
                row = field * rows_of_field + y_start + half * 8 + step
                first = step * SUB
                inside = jnp.where(lane // SUB == step, piece(row, SUB, rows_of_x, z_start, first), inside)
                below = jnp.where(lane == first, piece(row, SUB, rows_of_x, z_below, first), below)
                last = first + SUB - 1
                above = jnp.where(lane == last, piece(row, SUB, rows_of_x, z_above, last), above)
            below = jnp.where(z_start == 0, 0.0, below)
            above = jnp.where(z_start + SUB == z_cells, 0.0, above)
            at = (slice(field * SUB, (field + 1) * SUB), slice(half * 128, (half + 1) * 128))
            centre[at] = inside
            lower[at] = jnp.where(lane % SUB == 0, below, pltpu.roll(inside, 1, 1))
            upper[at] = jnp.where(lane % SUB == SUB - 1, above, pltpu.roll(inside, 127, 1))

    def y_row(y, z):
        total = jnp.zeros((SUB, 128), jnp.float32)
        for field in range(F):
            part = piece(field * rows_of_field + y, SUB, rows_of_x, z, field * SUB)
            total = jnp.where(lane // SUB == field, part, total)
        return total

    own_rows[0] = y_row(jnp.maximum(y_start - 1, 0), z_start)
    own_rows[1] = y_row(jnp.minimum(y_start + SUB, y_cells - 1), z_start)
    row_for_low[...] = y_row(0, corner(0, -1)[1])
    row_for_high[...] = y_row(y_cells - 1, corner(0, 1)[1])
    lane = lane[:8]
    for face, (x, step) in enumerate(((0, -1), (SUB - 1, 1))):
        y_there, z_there = corner(step, 0)
        for half in range(2):
            total = jnp.zeros((8, 128), jnp.float32)
            for step in range(8):
                row = x * rows_of_x + y_there + half * 8 + step
                part = piece(row, 8, rows_of_field, z_there, step * SUB)
                total = jnp.where(lane // SUB == step, part, total)
            faces[face, :, half * 128 : (half + 1) * 128] = total
    payload[...] = dot_rows(centre[...].astype(jnp.bfloat16), order[...]).astype(jnp.bfloat16)


def sample_cube(sample_block, place, brick):
    fields, x_cells, y_cells, z_cells = brick.shape
    vmem = pl.BlockSpec(memory_space=pltpu.VMEM)
    smem = pl.BlockSpec(memory_space=pltpu.SMEM)
    rows = fields * x_cells * y_cells
    cube = jax.ShapeDtypeStruct((F * SUB, 256), jnp.float32)
    line = jax.ShapeDtypeStruct((SUB, 128), jnp.float32)
    return pl.pallas_call(
        functools.partial(sample_kernel, y_cells, z_cells),
        out_shape=(
            cube,
            cube,
            cube,
            jax.ShapeDtypeStruct((2, SUB, 128), jnp.float32),
            jax.ShapeDtypeStruct((2, 8, 256), jnp.float32),
            line,
            line,
            jax.ShapeDtypeStruct((F * SUB, 256), jnp.bfloat16),
        ),
        in_specs=[smem, smem, vmem, pl.BlockSpec(memory_space=pltpu.HBM)],
        out_specs=(vmem,) * 8,
        scratch_shapes=[
            pltpu.VMEM((z_cells // 128 * rows + 4 * x_cells * y_cells, 128), jnp.float32),
            pltpu.SemaphoreType.DMA((z_cells // 128,)),
        ],
        compiler_params=pltpu.CompilerParams(vmem_limit_bytes=48 * 1024 * 1024),
        name="sample_cube",
    )(sample_block, place, jnp.asarray(CELL_ORDER, jnp.bfloat16), brick.reshape(rows, z_cells))


def change_kernel(
    y_cells,
    z_cells,
    sample_block,
    place,
    closure_in,
    closure_bias,
    closure_out,
    order,
    centre,
    lower,
    upper,
    own_rows,
    face_low,
    face_high,
    row_low,
    row_high,
    payload,
):
    y_start = corner_of(sample_block, place, 0, 0, y_cells, z_cells)[0]
    row = lax.broadcasted_iota(jnp.int32, (SUB, 256), 0)
    lane = lax.broadcasted_iota(jnp.int32, (SUB, 256), 1)
    south_row = jnp.where(y_start == 0, row_low[...], own_rows[0])
    north_row = jnp.where(y_start + SUB == y_cells, row_high[...], own_rows[1])
    cells = [centre[f * SUB : (f + 1) * SUB, :] for f in range(F)]
    viscosity = viscosity_of(cells, closure_in, closure_bias, closure_out)
    changes = []
    for f in range(F):
        value = cells[f]
        west = jnp.where(row == 0, face_low[f : f + 1, :], pltpu.roll(value, 1, 0))
        east = jnp.where(row == SUB - 1, face_high[f : f + 1, :], pltpu.roll(value, SUB - 1, 0))
        edge = pltpu.roll(south_row, (128 - f * SUB) % 128, 1)
        south = jnp.where(lane < SUB, jnp.concatenate([edge, edge], 1), pltpu.roll(value, SUB, 1))
        edge = pltpu.roll(north_row, 112 - f * SUB, 1)
        north = jnp.where(
            lane >= 256 - SUB, jnp.concatenate([edge, edge], 1), pltpu.roll(value, 256 - SUB, 1)
        )
        down = lower[f * SUB : (f + 1) * SUB, :]
        up = upper[f * SUB : (f + 1) * SUB, :]
        laplacian = east + west + north + south + up + down - 6.0 * value
        advection = cells[0] * (east - west) + cells[1] * (north - south) + cells[2] * (up - down)
        change = viscosity * laplacian - 0.5 * advection
        if f == 2:
            change = change + buoyancy * cells[3]
        changes.append(change)
    changes = jnp.concatenate(changes, axis=0).astype(jnp.bfloat16)
    payload[...] = dot_rows(changes, order[...]).astype(jnp.bfloat16)


def cube_change(sample_block, place, closure, cube, halo, y_cells, z_cells):
    vmem = pl.BlockSpec(memory_space=pltpu.VMEM)
    smem = pl.BlockSpec(memory_space=pltpu.SMEM)
    return pl.pallas_call(
        functools.partial(change_kernel, y_cells, z_cells),
        out_shape=jax.ShapeDtypeStruct((F * SUB, 256), jnp.bfloat16),
        in_specs=[smem] * 5 + [vmem] * 9,
        out_specs=vmem,
        name="cube_change",
    )(sample_block, place, *closure, jnp.asarray(CELL_ORDER, jnp.bfloat16), *cube, *halo)


def doubling_steps(x_devices, y_devices):
    along_y = [1 << bit for bit in reversed(range(y_devices.bit_length() - 1))]
    along_x = [y_devices << bit for bit in reversed(range(x_devices.bit_length() - 1))]
    return along_y + along_x


def on_device(
    fields, closure_in, closure_bias, closure_out, master, momentum, sample_block, sample_trainer
):
    group_count = lax.axis_size("grp")
    x_devices = lax.axis_size("gx")
    y_devices = lax.axis_size("gy")
    trainers = x_devices * y_devices
    my_group = lax.axis_index("grp")
    my_column = lax.axis_index("gx") * y_devices + lax.axis_index("gy")
    is_trainer = my_group == group_count - 1
    everyone = ("grp", "gx", "gy")
    sim_groups = group_count - 1
    first_trainer = sim_groups * trainers
    brick = fields[0]
    y_cells, z_cells = brick.shape[2:]
    closure = (closure_in, closure_bias, closure_out)
    place = jnp.stack(
        [
            my_group,
            lax.axis_index("gx"),
            lax.axis_index("gy"),
            jnp.int32(sim_groups),
            jnp.int32(y_devices),
            jnp.int32(x_devices),
        ]
    ).astype(jnp.int32)

    def neighbours(for_low, for_high, along_x):
        def pairs(step):
            found = []
            for g in range(sim_groups):
                for c in range(trainers):
                    gx, gy = c // y_devices, c % y_devices
                    if along_x:
                        gx = (gx + step) % x_devices
                    else:
                        gy = (gy + step) % y_devices
                    found.append((g * trainers + c, (g * x_devices + gx) * y_devices + gy))
            return found

        if (x_devices if along_x else y_devices) == 2:
            both = lax.ppermute(jnp.stack([for_high, for_low]), everyone, pairs(1))
            return both[0], both[1]
        from_low = lax.ppermute(for_high, everyone, pairs(1))
        return from_low, lax.ppermute(for_low, everyone, pairs(-1))

    def swap(distance):
        return [(first_trainer + c, first_trainer + (c ^ distance)) for c in range(trainers)]

    steps = doubling_steps(x_devices, y_devices)

    def to_trainers(payload):
        return jnp.stack(
            [
                lax.ppermute(
                    payload,
                    everyone,
                    [(g * trainers + c, first_trainer + c) for c in range(trainers)],
                )
                for g in range(sim_groups)
            ]
        )

    def among_trainers(held):
        for distance in steps[:-1]:
            held = jnp.concatenate([held, lax.ppermute(held, everyone, swap(distance))], axis=0)
        return [held, lax.ppermute(held, everyone, swap(steps[-1]))]

    *cube, faces, row_for_low, row_for_high, sent_inputs = sample_cube(sample_block, place, brick)
    face_halo = neighbours(faces[0], faces[1], True)
    row_halo = neighbours(row_for_low, row_for_high, False)
    landed_inputs = to_trainers(sent_inputs)
    sent_targets = cube_change(
        sample_block, place, closure, cube, (*face_halo, *row_halo), y_cells, z_cells
    )
    landed_targets = to_trainers(sent_targets)
    edges = (brick[:, 0], brick[:, -1], brick[:, :, 0], brick[:, :, -1])
    *edges, landed_targets = lax.optimization_barrier((*edges, landed_targets))
    halo = (*neighbours(edges[0], edges[1], True), *neighbours(edges[2], edges[3], False))
    arrived_inputs = among_trainers(landed_inputs)
    arrived_targets = among_trainers(landed_targets)

    first_count = CH * TAPS * F
    first = jnp.pad(master[:first_count].reshape(CH, TAPS * F), ((0, 0), (0, 256 - TAPS * F)))
    last = jnp.pad(master[first_count:].reshape(TAPS * F, CH).T, ((0, 0), (0, 256 - TAPS * F)))

    def train_here():
        delta_first, delta_last, new_brick = train_cubes(
            sample_trainer, place, first, last, arrived_inputs, arrived_targets, brick, steps
        )
        delta = jnp.concatenate(
            [delta_first[:, : TAPS * F].reshape(-1), delta_last[:, : TAPS * F].T.reshape(-1)]
        )
        return delta, new_brick

    def evolve_here():
        new_brick = evolve(*closure, brick, *halo)
        return jnp.zeros((NPARAM,), jnp.float32), new_brick

    delta, new_brick = lax.cond(is_trainer, train_here, evolve_here)

    total = delta
    for distance in steps:
        total = total + lax.ppermute(total, everyone, swap(distance))
    final = jnp.where(is_trainer, total, 0.0)
    for g in range(sim_groups):
        pairs = [(first_trainer + c, g * trainers + c) for c in range(trainers)]
        final = final + lax.ppermute(total, everyone, pairs)

    share_size = NPARAM // (group_count * trainers)
    share_start = (my_group * trainers + my_column) * share_size
    momentum_share = lax.dynamic_slice_in_dim(momentum, share_start, share_size)
    master_share = lax.dynamic_slice_in_dim(master, share_start, share_size)
    inverse = 1.0 / jnp.sqrt(jnp.sum(final * final) / NPARAM + norm_epsilon)
    delta_share = lax.dynamic_slice_in_dim(final, share_start, share_size)
    new_momentum = momentum_decay * momentum_share + delta_share * inverse
    new_master = master_share - outer_rate * new_momentum
    return (new_brick[None], new_master, new_momentum)


def solution(mesh):
    in_specs = (P("grp", None, "gx", "gy", None), P(), P(), P(), P(), P(), P(), P())
    out_specs = (P("grp", None, "gx", "gy", None), P(("grp", "gx", "gy")), P(("grp", "gx", "gy")))
    return jax.shard_map(
        on_device, mesh=mesh, in_specs=in_specs, out_specs=out_specs, check_vma=False
    )
```

```python
import functools

import jax
import jax.numpy as jnp
import numpy as np
from jax import lax
from jax.experimental import pallas as pl
from jax.experimental.pallas import tpu as pltpu
from jax.sharding import PartitionSpec as P

F = 5
CH = 64
HID = 64
SUB = 16
TCAP = 6
INNER = 3
CELLS = 4096
NPARAM = 17280
TAPS = 27
PAIRS = TCAP // 2
COLS = (SUB + 2) * 128
PATCH = 16 * F
STACK = 3 * PATCH

time_step = 0.1
base_viscosity = 0.02
viscosity_gain = 0.2
buoyancy = 0.5
inner_rate = 0.02
outer_rate = 0.01
momentum_decay = 0.9
norm_epsilon = 1e-06


def patch_position(row):
    group, py, pz = row // 4, row // 2 % 2, row % 2
    ypos = py + 1 if group in (0, 1) else (3 if py == 0 else 0)
    zpos = pz + 1 if group in (0, 2) else (3 if pz == 0 else 0)
    return ypos - 1, zpos - 1


def selections():
    first = np.zeros((4, 256, STACK), np.float32)
    last = np.zeros((4, 256, STACK), np.float32)
    for cell in range(4):
        py, pz = cell // 2, cell % 2
        for kx in range(3):
            for channel in range(F):
                for row in range(16):
                    ypos, zpos = patch_position(row)
                    column = kx * PATCH + channel * 16 + row
                    dy, dz = ypos - py, zpos - pz
                    if abs(dy) <= 1 and abs(dz) <= 1:
                        tap = 9 * kx + 3 * (dy + 1) + dz + 1
                        first[cell, tap * F + channel, column] = 1.0
                        last[cell, channel * TAPS + 26 - tap, column] = 1.0
    return first, last


SELECT_FIRST, SELECT_LAST = selections()


def dot_rows(left, right):
    return jnp.dot(left, right, preferred_element_type=jnp.float32)


def dot_lanes(left, right):
    return lax.dot_general(left, right, (((1,), (1,)), ((), ())), preferred_element_type=jnp.float32)


def patch_masks():
    row = lax.broadcasted_iota(jnp.int32, (8, 128), 0)
    lane = lax.broadcasted_iota(jnp.int32, (8, 128), 1)
    return {
        "pz0": row % 2 == 0,
        "py0": row // 2 % 2 == 0,
        "centre": row < 4,
        "z_first": lane % 8 == 0,
        "z_last": lane % 8 == 7,
        "y_first": lane // 8 % 8 == 0,
        "y_last": lane // 8 % 8 == 7,
    }


def edge_shift(values, step, parity_zero, first, last, forward):
    before = jnp.where(first, 0.0, pltpu.roll(values, step, 1))
    after = jnp.where(last, 0.0, pltpu.roll(values, 128 - step, 1))
    if forward:
        return jnp.where(parity_zero, after, before)
    return jnp.where(parity_zero, before, after)


def patch_stack(rows, masks):
    both = rows + pltpu.roll(rows, 4, 0)
    z_edge = edge_shift(both, 1, masks["pz0"], masks["z_first"], masks["z_last"], True)
    upper = jnp.where(masks["centre"], both, z_edge)
    lower = edge_shift(upper, 8, masks["py0"], masks["y_first"], masks["y_last"], True)
    return upper, lower


def patch_fold(upper, lower, masks):
    def fold_z(values):
        moved = edge_shift(values, 1, masks["pz0"], masks["z_first"], masks["z_last"], False)
        return values + pltpu.roll(moved, 4, 0)

    shifted = edge_shift(fold_z(lower), 8, masks["py0"], masks["y_first"], masks["y_last"], False)
    return fold_z(upper) + shifted


def store_planes(ref, pair, x, channels):
    stacked = jnp.concatenate([part for both in channels for part in both], axis=0).astype(jnp.bfloat16)
    for kx in range(3):
        start = pl.multiple_of((x + 2 - kx) * 128, 128)
        ref[pair, kx * PATCH : (kx + 1) * PATCH, pl.ds(start, 128)] = stacked


def train_kernel(steps, *refs):
    (trainer_of, place, first_ref, last_ref, select_first, select_last) = refs[:6]
    arrived = refs[6:8]
    fields_ref = refs[8]
    delta_first, delta_last, new_fields_ref = refs[9:12]
    (
        slots,
        cubes,
        table,
        targets,
        inputs,
        errors,
        hiddens,
        pre_grads,
        slopes,
        partial_out,
        big_first,
        big_last,
        big_last_t,
        raw,
        grad_first,
        grad_last,
        now_first,
        now_last,
        slot_sems,
        field_sem,
    ) = refs[12:]

    field_copy = pltpu.make_async_copy(fields_ref, new_fields_ref, field_sem)
    field_copy.start()

    groups = place[3]
    trainers = trainer_of.shape[0] // groups
    column = place[1] * place[4] + place[2]

    def visit(owner, count):
        mine = trainer_of[owner] == column

        @pl.when(mine)
        def _():
            source = lax.rem(owner, trainers)
            entry = jnp.int32(0)
            for order, distance in enumerate(steps[:-1]):
                entry = entry + apart(source, column, distance) * (1 << order)
            slots[0, count] = apart(source, column, steps[-1])
            slots[1, count] = entry * groups + lax.div(owner, trainers)

        return count + jnp.where(mine, 1, 0)

    count = lax.fori_loop(0, trainer_of.shape[0], visit, jnp.int32(0))

    def fetch(slot, wait):
        for half in range(2):

            @pl.when((slot < count) & (slots[0, slot] == half))
            def _():
                copy = pltpu.make_async_copy(
                    arrived[half].at[slots[1, slot]], cubes.at[slot], slot_sems.at[slot]
                )
                copy.wait() if wait else copy.start()

    for slot in range(TCAP):
        fetch(slot, False)

        @pl.when(slot >= count)
        def _():
            cubes[slot] = jnp.zeros((2 * SUB * F, 256), jnp.bfloat16)

    masks = patch_masks()
    for ref in (errors, inputs):
        ref[:, :PATCH, 128:256] = jnp.zeros((PAIRS, PATCH, 128), jnp.bfloat16)
        ref[:, 2 * PATCH :, COLS - 256 : COLS - 128] = jnp.zeros((PAIRS, PATCH, 128), jnp.bfloat16)
    partial_out[:, :, :128] = jnp.zeros((PAIRS, STACK, 128), jnp.float32)
    partial_out[:, :, COLS - 128 :] = jnp.zeros((PAIRS, STACK, 128), jnp.float32)
    table[...] = jnp.zeros(table.shape, table.dtype)
    targets[...] = jnp.zeros(targets.shape, targets.dtype)
    lane = lax.broadcasted_iota(jnp.int32, (8, 128), 1)
    full_weight = 2.0 * (1.0 / (jnp.full((8, 128), count, jnp.int32).astype(jnp.float32) * CELLS))
    weights = [
        jnp.where(lane // 64 + 2 * pair < count, full_weight, 0.0) for pair in range(PAIRS)
    ]
    start_first = first_ref[...].astype(jnp.bfloat16).astype(jnp.float32)
    start_last = last_ref[...].astype(jnp.bfloat16).astype(jnp.float32)
    now_first[...] = start_first
    now_last[...] = start_last

    for slot in range(TCAP):
        fetch(slot, True)

    low_lanes = lax.broadcasted_iota(jnp.int32, (SUB * F, 128), 1) < 64

    def spread_rows(pair, kind, put):
        rows = slice(kind * SUB * F, (kind + 1) * SUB * F)
        even = cubes[2 * pair, rows, :].astype(jnp.float32)
        odd = cubes[2 * pair + 1, rows, :].astype(jnp.float32)
        for half in range(2):
            left = even[:, half * 128 : (half + 1) * 128]
            right = odd[:, half * 128 : (half + 1) * 128]
            put(2 * half, jnp.where(low_lanes, left, pltpu.roll(right, 64, 1)))
            put(2 * half + 1, jnp.where(low_lanes, pltpu.roll(left, 64, 1), right))

    for pair in range(PAIRS):

        def put_input(cell, values):
            table[pl.ds(cell, SUB * F, 8), :] = values

        def put_target(cell, values):
            targets[pl.ds(pair * SUB * F * 8 + cell, SUB * F, 8), :] = values

        spread_rows(pair, 0, put_input)
        spread_rows(pair, 1, put_target)

        def stack_plane(x, carry):
            channels = [
                patch_stack(table[pl.ds(pl.multiple_of((c * SUB + x) * 8, 8), 8), :], masks)
                for c in range(F)
            ]
            store_planes(inputs, pair, x, channels)
            return carry

        lax.fori_loop(0, SUB, stack_plane, 0, unroll=8)

    def train_step(step, step_carry):
        first_now = now_first[...].astype(jnp.bfloat16)
        last_now = now_last[...].astype(jnp.bfloat16)
        for cell in range(4):
            rows = slice(cell * CH, (cell + 1) * CH)
            big_first[rows, :] = dot_rows(first_now, select_first[cell]).astype(jnp.bfloat16)
            big_last[rows, :] = dot_rows(last_now, select_last[cell]).astype(jnp.bfloat16)
        big_last_t[...] = big_last[...].T
        def tile_of(index):
            return index // 8, pl.ds(pl.multiple_of((index % 8) * 256 + 128, 128), 256)

        def first_layer(index):
            pair, columns = tile_of(index)
            raw[index % 2] = dot_rows(big_first[...], inputs[pair, :, columns])

        def activate(index):
            pair, columns = tile_of(index)
            for part in range(8):
                rows = slice(part * 32, (part + 1) * 32)
                half = 0.5 * raw[index % 2, rows, :]
                curve = jnp.tanh(half)
                value = half + half * curve
                hiddens[pair, rows, columns] = value.astype(jnp.bfloat16)
                slopes[pair, rows, columns] = (0.5 + 0.5 * curve) + value * (0.5 - 0.5 * curve)

        def last_layer(index):
            pair, columns = tile_of(index)
            partial_out[pair, :, columns] = dot_rows(big_last_t[...], hiddens[pair, :, columns])

        def forward(index, carry):
            last_layer(index - 2)
            activate(index - 1)
            first_layer(index)
            return carry

        tiles = 8 * PAIRS
        first_layer(0)
        activate(0)
        first_layer(1)
        lax.fori_loop(2, tiles, forward, 0)
        last_layer(tiles - 2)
        activate(tiles - 1)
        last_layer(tiles - 1)

        def error_plane(index, carry):
            pair = index // SUB
            x = index % SUB
            column = pl.multiple_of((x + 1) * 128, 128)
            total = (
                partial_out[pair, 0:PATCH, pl.ds(pl.multiple_of(column + 128, 128), 128)]
                + partial_out[pair, PATCH : 2 * PATCH, pl.ds(column, 128)]
                + partial_out[pair, 2 * PATCH :, pl.ds(pl.multiple_of(column - 128, 128), 128)]
            )
            weight = jnp.where(pair == 0, weights[0], jnp.where(pair == 1, weights[1], weights[2]))
            channels = []
            for c in range(F):
                predicted = patch_fold(
                    total[16 * c : 16 * c + 8], total[16 * c + 8 : 16 * c + 16], masks
                )
                row = pl.multiple_of(((pair * F + c) * SUB + x) * 8, 8)
                error = weight * (predicted - targets[pl.ds(row, 8), :])
                error = jnp.where(masks["centre"], error, 0.0)
                error = error.astype(jnp.bfloat16).astype(jnp.float32)
                channels.append(patch_stack(error, masks))
            store_planes(errors, pair, x, channels)
            return carry

        lax.fori_loop(0, SUB * PAIRS, error_plane, 0, unroll=8)

        grad_first[...] = jnp.zeros(grad_first.shape, jnp.float32)
        grad_last[...] = jnp.zeros(grad_last.shape, jnp.float32)

        def hidden_layer(index):
            pair, columns = tile_of(index)
            raw[index % 2] = dot_rows(big_last[...], errors[pair, :, columns])

        def scale(index):
            pair, columns = tile_of(index)
            for part in range(8):
                rows = slice(part * 32, (part + 1) * 32)
                product = raw[index % 2, rows, :] * slopes[pair, rows, columns]
                pre_grads[pair, rows, columns] = product.astype(jnp.bfloat16)

        def gradients(index):
            pair, columns = tile_of(index)
            grad_first[...] += dot_lanes(pre_grads[pair, :, columns], inputs[pair, :, columns])
            grad_last[...] += dot_lanes(hiddens[pair, :, columns], errors[pair, :, columns])

        def backward(index, carry):
            gradients(index - 2)
            scale(index - 1)
            hidden_layer(index)
            return carry

        hidden_layer(0)
        scale(0)
        hidden_layer(1)
        lax.fori_loop(2, tiles, backward, 0)
        gradients(tiles - 2)
        scale(tiles - 1)
        gradients(tiles - 1)

        def folded(grad, select_ref):
            total = jnp.zeros((3 * CH, 256), jnp.float32)
            for cell in range(4):
                rest = grad[cell * CH : (cell + 1) * CH, :]
                parts = []
                for _ in range(3):
                    parts.append(rest.astype(jnp.bfloat16))
                    rest = rest - parts[-1].astype(jnp.float32)
                total = total + dot_lanes(jnp.concatenate(parts, axis=0), select_ref[cell])
            return total[:CH] + total[CH : 2 * CH] + total[2 * CH :]

        now_first[...] = now_first[...] - inner_rate * folded(grad_first, select_first)
        now_last[...] = now_last[...] - inner_rate * folded(grad_last, select_last)
        return step_carry

    lax.fori_loop(0, INNER, train_step, 0)
    delta_first[...] = start_first - now_first[...]
    delta_last[...] = start_last - now_last[...]
    field_copy.wait()


def apart(left, right, distance):
    return jnp.where(lax.rem(lax.div(left, distance), 2) == lax.rem(lax.div(right, distance), 2), 0, 1)


def train_cubes(trainer_of, place, first, last, arrived, fields, steps):
    vmem = pl.BlockSpec(memory_space=pltpu.VMEM)
    smem = pl.BlockSpec(memory_space=pltpu.SMEM)
    anywhere = pl.BlockSpec(memory_space=pl.ANY)
    hbm = pl.BlockSpec(memory_space=pltpu.HBM)
    return pl.pallas_call(
        functools.partial(train_kernel, steps),
        out_shape=(
            jax.ShapeDtypeStruct((CH, 256), jnp.float32),
            jax.ShapeDtypeStruct((CH, 256), jnp.float32),
            jax.ShapeDtypeStruct(fields.shape, fields.dtype),
        ),
        in_specs=[smem] * 2 + [vmem] * 4 + [anywhere] * 2 + [hbm],
        out_specs=(vmem, vmem, hbm),
        scratch_shapes=[
            pltpu.SMEM((2, TCAP), jnp.int32),
            pltpu.VMEM((TCAP, 2 * SUB * F, 256), jnp.bfloat16),
            pltpu.VMEM((SUB * F * 8, 128), jnp.float32),
            pltpu.VMEM((PAIRS * SUB * F * 8, 128), jnp.float32),
            pltpu.VMEM((PAIRS, STACK, COLS), jnp.bfloat16),
            pltpu.VMEM((PAIRS, STACK, COLS), jnp.bfloat16),
            pltpu.VMEM((PAIRS, 4 * CH, COLS), jnp.bfloat16),
            pltpu.VMEM((PAIRS, 4 * CH, COLS), jnp.bfloat16),
            pltpu.VMEM((PAIRS, 4 * CH, COLS), jnp.float32),
            pltpu.VMEM((PAIRS, STACK, COLS), jnp.float32),
            pltpu.VMEM((4 * CH, STACK), jnp.bfloat16),
            pltpu.VMEM((4 * CH, STACK), jnp.bfloat16),
            pltpu.VMEM((STACK, 4 * CH), jnp.bfloat16),
            pltpu.VMEM((2, 4 * CH, 256), jnp.float32),
            pltpu.VMEM((4 * CH, STACK), jnp.float32),
            pltpu.VMEM((4 * CH, STACK), jnp.float32),
            pltpu.VMEM((CH, 256), jnp.float32),
            pltpu.VMEM((CH, 256), jnp.float32),
            pltpu.SemaphoreType.DMA((TCAP,)),
            pltpu.SemaphoreType.DMA,
        ],
        compiler_params=pltpu.CompilerParams(vmem_limit_bytes=48 * 1024 * 1024),
        name="train_cubes",
    )(
        trainer_of,
        place,
        first,
        last,
        jnp.asarray(SELECT_FIRST, jnp.bfloat16),
        jnp.asarray(SELECT_LAST, jnp.bfloat16),
        *arrived,
        fields,
    )


def viscosity_of(cells, closure):
    def unit(h, total):
        half = closure[F, h] + closure[0, h] * cells[0]
        for f in range(1, F):
            half = half + closure[f, h] * cells[f]
        return total + closure[F + 1, h] * (half + half * jnp.tanh(half))

    total = lax.fori_loop(0, HID, unit, jnp.zeros(cells[0].shape, jnp.float32), unroll=4)
    soft = jnp.maximum(total, 0.0) + jnp.log1p(jnp.exp(-jnp.abs(total)))
    return base_viscosity + viscosity_gain * soft


def evolve_kernel(closure, fields, x_halo, y_low, y_high, new_fields):
    x_cells, y_cells, z_cells = fields.shape[1:]
    row = lax.broadcasted_iota(jnp.int32, (y_cells, z_cells), 0)
    lane = lax.broadcasted_iota(jnp.int32, (y_cells, z_cells), 1)
    part = y_cells // 2

    def plane(x, carry):
        eddies = []
        for half in range(2):
            rows = pl.ds(half * part, part)
            cells = [fields[f, x, rows, :] for f in range(F)]
            eddies.append(viscosity_of(cells, closure))
        viscosity = jnp.concatenate(eddies, axis=0)
        centre = [fields[f, x] for f in range(F)]
        below = jnp.maximum(x - 1, 0)
        above = jnp.minimum(x + 1, x_cells - 1)
        for f in range(F):
            value = centre[f]
            west = jnp.where(x == 0, x_halo[1, f], fields[f, below])
            east = jnp.where(x == x_cells - 1, x_halo[0, f], fields[f, above])
            south = jnp.where(row == 0, y_low[f, pl.ds(x, 1), :], pltpu.roll(value, 1, 0))
            north = jnp.where(
                row == y_cells - 1, y_high[f, pl.ds(x, 1), :], pltpu.roll(value, y_cells - 1, 0)
            )
            lower = jnp.where(lane == 0, 0.0, pltpu.roll(value, 1, 1))
            upper = jnp.where(lane == z_cells - 1, 0.0, pltpu.roll(value, z_cells - 1, 1))
            laplacian = east + west + north + south + upper + lower - 6.0 * value
            advection = (
                centre[0] * (east - west) + centre[1] * (north - south) + centre[2] * (upper - lower)
            )
            tendency = viscosity * laplacian - 0.5 * advection
            if f == 2:
                tendency = tendency + buoyancy * centre[3]
            new_fields[f, x] = value + time_step * tendency
        return carry

    lax.fori_loop(0, x_cells, plane, 0)


def evolve(closure, fields, x_halo, y_low, y_high):
    vmem = pl.BlockSpec(memory_space=pltpu.VMEM)
    return pl.pallas_call(
        evolve_kernel,
        out_shape=jax.ShapeDtypeStruct(fields.shape, fields.dtype),
        in_specs=[pl.BlockSpec(memory_space=pltpu.SMEM)] + [vmem] * 4,
        out_specs=vmem,
        compiler_params=pltpu.CompilerParams(vmem_limit_bytes=16 * 1024 * 1024),
        name="evolve_brick",
    )(closure, fields, x_halo, y_low, y_high)


def cell_order():
    order = np.zeros((256, 256), np.float32)
    for y in range(SUB):
        for z in range(SUB):
            order[y * SUB + z, (y % 2 * 2 + z % 2) * 64 + y // 2 * 8 + z // 2] = 1.0
    return order


CELL_ORDER = cell_order()


def corner_of(sample_block, place, x_step, y_step, y_cells, z_cells):
    x_devices, y_devices = place[5], place[4]
    gx = lax.rem(place[1] + x_step + x_devices, x_devices)
    gy = lax.rem(place[2] + y_step + y_devices, y_devices)
    group = jnp.minimum(place[0], place[3] - 1)
    block = sample_block[(group * x_devices + gx) * y_devices + gy]
    z_blocks = z_cells // SUB
    return lax.rem(lax.div(block, z_blocks), y_cells // SUB) * SUB, lax.rem(block, z_blocks) * SUB


def sample_kernel(
    y_cells,
    z_cells,
    sample_block,
    place,
    brick,
    centre,
    lower,
    upper,
    own_rows,
    faces,
    row_for_low,
    row_for_high,
    x_edges,
    y_edges,
    windows,
    sems,
    edge_sems,
):
    rows_of_x = y_cells
    rows_of_field = SUB * y_cells
    window_rows = F * rows_of_field
    copies = [
        pltpu.make_async_copy(
            brick.at[:, pl.ds(w * 128, 128)], windows.at[pl.ds(w * window_rows, window_rows)], sems.at[w]
        )
        for w in range(z_cells // 128)
    ]
    edge_copies = [
        pltpu.make_async_copy(
            brick.at[pl.ds(f * rows_of_field + x * rows_of_x, rows_of_x)],
            x_edges.at[side, f],
            edge_sems.at[side, f],
        )
        for side, x in enumerate((0, SUB - 1))
        for f in range(F)
    ]
    for copy in copies + edge_copies:
        copy.start()
    for copy in copies:
        copy.wait()

    def corner(x_step, y_step):
        return corner_of(sample_block, place, x_step, y_step, y_cells, z_cells)

    def piece(row, count, stride, z, lane_start):
        values = windows[pl.ds(lax.div(z, 128) * window_rows + row, count, stride), :]
        return pltpu.roll(values, lax.rem(lane_start - lax.rem(z, 128) + 256, 128), 1)

    lane = lax.broadcasted_iota(jnp.int32, (SUB, 128), 1)
    y_start, z_start = corner(0, 0)
    z_below = jnp.maximum(z_start - 1, 0)
    z_above = jnp.minimum(z_start + SUB, z_cells - 1)
    for field in range(F):
        for half in range(2):
            inside = jnp.zeros((SUB, 128), jnp.float32)
            below = jnp.zeros((SUB, 128), jnp.float32)
            above = jnp.zeros((SUB, 128), jnp.float32)
            for step in range(8):
                row = field * rows_of_field + y_start + half * 8 + step
                first = step * SUB
                inside = jnp.where(lane // SUB == step, piece(row, SUB, rows_of_x, z_start, first), inside)
                below = jnp.where(lane == first, piece(row, SUB, rows_of_x, z_below, first), below)
                last = first + SUB - 1
                above = jnp.where(lane == last, piece(row, SUB, rows_of_x, z_above, last), above)
            below = jnp.where(z_start == 0, 0.0, below)
            above = jnp.where(z_start + SUB == z_cells, 0.0, above)
            at = (slice(field * SUB, (field + 1) * SUB), slice(half * 128, (half + 1) * 128))
            centre[at] = inside
            lower[at] = jnp.where(lane % SUB == 0, below, pltpu.roll(inside, 1, 1))
            upper[at] = jnp.where(lane % SUB == SUB - 1, above, pltpu.roll(inside, 127, 1))

    def y_row(y, z):
        total = jnp.zeros((SUB, 128), jnp.float32)
        for field in range(F):
            part = piece(field * rows_of_field + y, SUB, rows_of_x, z, field * SUB)
            total = jnp.where(lane // SUB == field, part, total)
        return total

    own_rows[0] = y_row(jnp.maximum(y_start - 1, 0), z_start)
    own_rows[1] = y_row(jnp.minimum(y_start + SUB, y_cells - 1), z_start)
    row_for_low[...] = y_row(0, corner(0, -1)[1])
    row_for_high[...] = y_row(y_cells - 1, corner(0, 1)[1])
    lane = lane[:8]
    for face, (x, step) in enumerate(((0, -1), (SUB - 1, 1))):
        y_there, z_there = corner(step, 0)
        for half in range(2):
            total = jnp.zeros((8, 128), jnp.float32)
            for step in range(8):
                row = x * rows_of_x + y_there + half * 8 + step
                part = piece(row, 8, rows_of_field, z_there, step * SUB)
                total = jnp.where(lane // SUB == step, part, total)
            faces[face, :, half * 128 : (half + 1) * 128] = total
    for side, y in enumerate((0, y_cells - 1)):
        for field in range(F):
            for w in range(z_cells // 128):
                start = w * window_rows + field * rows_of_field + y
                y_edges[side, field, :, w * 128 : (w + 1) * 128] = windows[
                    pl.ds(start, SUB, rows_of_x), :
                ]
    for copy in edge_copies:
        copy.wait()


def sample_cube(sample_block, place, brick):
    fields, x_cells, y_cells, z_cells = brick.shape
    vmem = pl.BlockSpec(memory_space=pltpu.VMEM)
    smem = pl.BlockSpec(memory_space=pltpu.SMEM)
    hbm = pl.BlockSpec(memory_space=pltpu.HBM)
    rows = fields * x_cells * y_cells
    cube = jax.ShapeDtypeStruct((F * SUB, 256), jnp.float32)
    line = jax.ShapeDtypeStruct((SUB, 128), jnp.float32)
    return pl.pallas_call(
        functools.partial(sample_kernel, y_cells, z_cells),
        out_shape=(
            cube,
            cube,
            cube,
            jax.ShapeDtypeStruct((2, SUB, 128), jnp.float32),
            jax.ShapeDtypeStruct((2, 8, 256), jnp.float32),
            line,
            line,
            jax.ShapeDtypeStruct((2, fields, y_cells, z_cells), jnp.float32),
            jax.ShapeDtypeStruct((2, fields, x_cells, z_cells), jnp.float32),
        ),
        in_specs=[smem, smem, hbm],
        out_specs=(vmem,) * 7 + (hbm, vmem),
        scratch_shapes=[
            pltpu.VMEM((z_cells // 128 * rows + 4 * x_cells * y_cells, 128), jnp.float32),
            pltpu.SemaphoreType.DMA((z_cells // 128,)),
            pltpu.SemaphoreType.DMA((2, fields)),
        ],
        compiler_params=pltpu.CompilerParams(vmem_limit_bytes=16 * 1024 * 1024),
        name="sample_cube",
    )(sample_block, place, brick.reshape(rows, z_cells))


def change_kernel(
    y_cells,
    z_cells,
    sample_block,
    place,
    closure,
    order,
    centre,
    lower,
    upper,
    own_rows,
    face_halo,
    row_low,
    row_high,
    payload,
):
    y_start = corner_of(sample_block, place, 0, 0, y_cells, z_cells)[0]
    row = lax.broadcasted_iota(jnp.int32, (SUB, 256), 0)
    lane = lax.broadcasted_iota(jnp.int32, (SUB, 256), 1)
    south_row = jnp.where(y_start == 0, row_low[...], own_rows[0])
    north_row = jnp.where(y_start + SUB == y_cells, row_high[...], own_rows[1])
    cells = [centre[f * SUB : (f + 1) * SUB, :] for f in range(F)]
    viscosity = viscosity_of(cells, closure)
    changes = []
    for f in range(F):
        value = cells[f]
        west = jnp.where(row == 0, face_halo[1, f : f + 1, :], pltpu.roll(value, 1, 0))
        east = jnp.where(row == SUB - 1, face_halo[0, f : f + 1, :], pltpu.roll(value, SUB - 1, 0))
        edge = pltpu.roll(south_row, (128 - f * SUB) % 128, 1)
        south = jnp.where(lane < SUB, jnp.concatenate([edge, edge], 1), pltpu.roll(value, SUB, 1))
        edge = pltpu.roll(north_row, 112 - f * SUB, 1)
        north = jnp.where(
            lane >= 256 - SUB, jnp.concatenate([edge, edge], 1), pltpu.roll(value, 256 - SUB, 1)
        )
        down = lower[f * SUB : (f + 1) * SUB, :]
        up = upper[f * SUB : (f + 1) * SUB, :]
        laplacian = east + west + north + south + up + down - 6.0 * value
        advection = cells[0] * (east - west) + cells[1] * (north - south) + cells[2] * (up - down)
        change = viscosity * laplacian - 0.5 * advection
        if f == 2:
            change = change + buoyancy * cells[3]
        changes.append(change)
    both = jnp.concatenate(cells + changes, axis=0).astype(jnp.bfloat16)
    payload[...] = dot_rows(both, order[...]).astype(jnp.bfloat16)


def cube_change(sample_block, place, closure, cube, halo, y_cells, z_cells):
    vmem = pl.BlockSpec(memory_space=pltpu.VMEM)
    smem = pl.BlockSpec(memory_space=pltpu.SMEM)
    return pl.pallas_call(
        functools.partial(change_kernel, y_cells, z_cells),
        out_shape=jax.ShapeDtypeStruct((2 * F * SUB, 256), jnp.bfloat16),
        in_specs=[smem] * 3 + [vmem] * 8,
        out_specs=vmem,
        compiler_params=pltpu.CompilerParams(vmem_limit_bytes=16 * 1024 * 1024),
        name="cube_change",
    )(sample_block, place, closure, jnp.asarray(CELL_ORDER, jnp.bfloat16), *cube, *halo)


def doubling_steps(x_devices, y_devices):
    along_y = [1 << bit for bit in reversed(range(y_devices.bit_length() - 1))]
    along_x = [y_devices << bit for bit in reversed(range(x_devices.bit_length() - 1))]
    return along_y + along_x


def on_device(
    fields, closure_in, closure_bias, closure_out, master, momentum, sample_block, sample_trainer
):
    group_count = lax.axis_size("grp")
    x_devices = lax.axis_size("gx")
    y_devices = lax.axis_size("gy")
    trainers = x_devices * y_devices
    my_group = lax.axis_index("grp")
    my_column = lax.axis_index("gx") * y_devices + lax.axis_index("gy")
    is_trainer = my_group == group_count - 1
    everyone = ("grp", "gx", "gy")
    sim_groups = group_count - 1
    first_trainer = sim_groups * trainers
    brick = fields[0]
    y_cells, z_cells = brick.shape[2:]
    closure = jnp.concatenate(
        [0.5 * closure_in.T, 0.5 * closure_bias[None], closure_out[None]], axis=0
    )
    place = jnp.stack(
        [
            my_group,
            lax.axis_index("gx"),
            lax.axis_index("gy"),
            jnp.int32(sim_groups),
            jnp.int32(y_devices),
            jnp.int32(x_devices),
        ]
    ).astype(jnp.int32)

    def pairs(along_x, step):
        found = []
        for g in range(sim_groups):
            for c in range(trainers):
                gx, gy = c // y_devices, c % y_devices
                if along_x:
                    gx = (gx + step) % x_devices
                else:
                    gy = (gy + step) % y_devices
                found.append((g * trainers + c, (g * x_devices + gx) * y_devices + gy))
        return found

    def x_neighbours(edges):
        if x_devices == 2:
            return lax.ppermute(edges, everyone, pairs(True, 1))
        from_high = lax.ppermute(edges[0], everyone, pairs(True, -1))
        return jnp.stack([from_high, lax.ppermute(edges[1], everyone, pairs(True, 1))])

    def y_neighbours(for_low, for_high):
        from_low = lax.ppermute(for_high, everyone, pairs(False, 1))
        return from_low, lax.ppermute(for_low, everyone, pairs(False, -1))

    def swap(distance):
        return [(first_trainer + c, first_trainer + (c ^ distance)) for c in range(trainers)]

    steps = doubling_steps(x_devices, y_devices)

    def to_trainers(payload):
        return jnp.stack(
            [
                lax.ppermute(
                    payload,
                    everyone,
                    [(g * trainers + c, first_trainer + c) for c in range(trainers)],
                )
                for g in range(sim_groups)
            ]
        )

    def among_trainers(held):
        for distance in steps[:-1]:
            held = jnp.concatenate([held, lax.ppermute(held, everyone, swap(distance))], axis=0)
        return [held, lax.ppermute(held, everyone, swap(steps[-1]))]

    *cube, faces, row_for_low, row_for_high, x_edges, y_edges = sample_cube(
        sample_block, place, brick
    )
    thin_halo = (x_neighbours(faces), *y_neighbours(row_for_low, row_for_high))
    payload = cube_change(sample_block, place, closure, cube, thin_halo, y_cells, z_cells)
    landed = to_trainers(payload)
    x_edges, y_edges, landed = lax.optimization_barrier((x_edges, y_edges, landed))
    halo = (x_neighbours(x_edges), *y_neighbours(y_edges[0], y_edges[1]))
    arrived = among_trainers(landed)

    first_count = CH * TAPS * F
    first = jnp.pad(master[:first_count].reshape(CH, TAPS * F), ((0, 0), (0, 256 - TAPS * F)))
    last = jnp.pad(master[first_count:].reshape(TAPS * F, CH).T, ((0, 0), (0, 256 - TAPS * F)))

    def train_here():
        delta_first, delta_last, new_brick = train_cubes(
            sample_trainer, place, first, last, arrived, brick, steps
        )
        delta = jnp.concatenate(
            [delta_first[:, : TAPS * F].reshape(-1), delta_last[:, : TAPS * F].T.reshape(-1)]
        )
        return delta, new_brick

    def evolve_here():
        new_brick = evolve(closure, brick, *halo)
        return jnp.zeros((NPARAM,), jnp.float32), new_brick

    delta, new_brick = lax.cond(is_trainer, train_here, evolve_here)

    total = delta
    for distance in steps:
        total = total + lax.ppermute(total, everyone, swap(distance))
    final = jnp.where(is_trainer, total, 0.0)
    for g in range(sim_groups):
        pairs = [(first_trainer + c, g * trainers + c) for c in range(trainers)]
        final = final + lax.ppermute(total, everyone, pairs)

    share_size = NPARAM // (group_count * trainers)
    share_start = (my_group * trainers + my_column) * share_size
    momentum_share = lax.dynamic_slice_in_dim(momentum, share_start, share_size)
    master_share = lax.dynamic_slice_in_dim(master, share_start, share_size)
    inverse = 1.0 / jnp.sqrt(jnp.sum(final * final) / NPARAM + norm_epsilon)
    delta_share = lax.dynamic_slice_in_dim(final, share_start, share_size)
    new_momentum = momentum_decay * momentum_share + delta_share * inverse
    new_master = master_share - outer_rate * new_momentum
    return (new_brick[None], new_master, new_momentum)


def solution(mesh):
    in_specs = (P("grp", None, "gx", "gy", None), P(), P(), P(), P(), P(), P(), P())
    out_specs = (P("grp", None, "gx", "gy", None), P(("grp", "gx", "gy")), P(("grp", "gx", "gy")))
    return jax.shard_map(
        on_device, mesh=mesh, in_specs=in_specs, out_specs=out_specs, check_vma=False
    )
```

```python
import functools

import jax
import jax.numpy as jnp
import numpy as np
from jax import lax
from jax.experimental import pallas as pl
from jax.experimental.pallas import tpu as pltpu
from jax.sharding import PartitionSpec as P

F = 5
CH = 64
HID = 64
SUB = 16
TCAP = 6
INNER = 3
CELLS = 4096
NPARAM = 17280
TAPS = 27
PAIRS = TCAP // 2
COLS = (SUB + 2) * 128
PATCH = 16 * F
STACK = 3 * PATCH

time_step = 0.1
base_viscosity = 0.02
viscosity_gain = 0.2
buoyancy = 0.5
inner_rate = 0.02
outer_rate = 0.01
momentum_decay = 0.9
norm_epsilon = 1e-06


def patch_position(row):
    group, py, pz = row // 4, row // 2 % 2, row % 2
    ypos = py + 1 if group in (0, 1) else (3 if py == 0 else 0)
    zpos = pz + 1 if group in (0, 2) else (3 if pz == 0 else 0)
    return ypos - 1, zpos - 1


def selections():
    first = np.zeros((4, 256, STACK), np.float32)
    last = np.zeros((4, 256, STACK), np.float32)
    for cell in range(4):
        py, pz = cell // 2, cell % 2
        for kx in range(3):
            for channel in range(F):
                for row in range(16):
                    ypos, zpos = patch_position(row)
                    column = kx * PATCH + channel * 16 + row
                    dy, dz = ypos - py, zpos - pz
                    if abs(dy) <= 1 and abs(dz) <= 1:
                        tap = 9 * kx + 3 * (dy + 1) + dz + 1
                        first[cell, tap * F + channel, column] = 1.0
                        last[cell, channel * TAPS + 26 - tap, column] = 1.0
    return first, last


SELECT_FIRST, SELECT_LAST = selections()


def dot_rows(left, right):
    return jnp.dot(left, right, preferred_element_type=jnp.float32)


def dot_lanes(left, right):
    return lax.dot_general(left, right, (((1,), (1,)), ((), ())), preferred_element_type=jnp.float32)


def patch_masks():
    row = lax.broadcasted_iota(jnp.int32, (8, 128), 0)
    lane = lax.broadcasted_iota(jnp.int32, (8, 128), 1)
    return {
        "pz0": row % 2 == 0,
        "py0": row // 2 % 2 == 0,
        "centre": row < 4,
        "z_first": lane % 8 == 0,
        "z_last": lane % 8 == 7,
        "y_first": lane // 8 % 8 == 0,
        "y_last": lane // 8 % 8 == 7,
    }


def edge_shift(values, step, parity_zero, first, last, forward):
    before = jnp.where(first, 0.0, pltpu.roll(values, step, 1))
    after = jnp.where(last, 0.0, pltpu.roll(values, 128 - step, 1))
    if forward:
        return jnp.where(parity_zero, after, before)
    return jnp.where(parity_zero, before, after)


def patch_stack(rows, masks):
    both = rows + pltpu.roll(rows, 4, 0)
    z_edge = edge_shift(both, 1, masks["pz0"], masks["z_first"], masks["z_last"], True)
    upper = jnp.where(masks["centre"], both, z_edge)
    lower = edge_shift(upper, 8, masks["py0"], masks["y_first"], masks["y_last"], True)
    return upper, lower


def patch_fold(upper, lower, masks):
    def fold_z(values):
        moved = edge_shift(values, 1, masks["pz0"], masks["z_first"], masks["z_last"], False)
        return values + pltpu.roll(moved, 4, 0)

    shifted = edge_shift(fold_z(lower), 8, masks["py0"], masks["y_first"], masks["y_last"], False)
    return fold_z(upper) + shifted


def store_planes(ref, pair, x, channels):
    stacked = jnp.concatenate([part for both in channels for part in both], axis=0).astype(jnp.bfloat16)
    for kx in range(3):
        start = pl.multiple_of((x + 2 - kx) * 128, 128)
        ref[pair, kx * PATCH : (kx + 1) * PATCH, pl.ds(start, 128)] = stacked


def train_kernel(steps, *refs):
    (trainer_of, place, first_ref, last_ref, select_first, select_last) = refs[:6]
    arrived = refs[6:8]
    fields_ref = refs[8]
    delta_first, delta_last, new_fields_ref = refs[9:12]
    (
        slots,
        cubes,
        table,
        targets,
        inputs,
        errors,
        hiddens,
        pre_grads,
        slopes,
        partial_out,
        big_first,
        big_last,
        big_last_t,
        raw,
        grad_first,
        grad_last,
        now_first,
        now_last,
        brick,
        slot_sems,
        field_sem,
    ) = refs[12:]

    field_in = pltpu.make_async_copy(fields_ref, brick, field_sem)
    field_out = pltpu.make_async_copy(brick, new_fields_ref, field_sem)
    field_in.start()

    groups = place[3]
    trainers = trainer_of.shape[0] // groups
    column = place[1] * place[4] + place[2]

    def visit(owner, count):
        mine = trainer_of[owner] == column

        @pl.when(mine)
        def _():
            source = lax.rem(owner, trainers)
            entry = jnp.int32(0)
            for order, distance in enumerate(steps[:-1]):
                entry = entry + apart(source, column, distance) * (1 << order)
            slots[0, count] = apart(source, column, steps[-1])
            slots[1, count] = entry * groups + lax.div(owner, trainers)

        return count + jnp.where(mine, 1, 0)

    count = lax.fori_loop(0, trainer_of.shape[0], visit, jnp.int32(0))

    def fetch(slot, wait):
        for half in range(2):

            @pl.when((slot < count) & (slots[0, slot] == half))
            def _():
                copy = pltpu.make_async_copy(
                    arrived[half].at[slots[1, slot]], cubes.at[slot], slot_sems.at[slot]
                )
                copy.wait() if wait else copy.start()

    for slot in range(TCAP):
        fetch(slot, False)

        @pl.when(slot >= count)
        def _():
            cubes[slot] = jnp.zeros((2 * SUB * F, 256), jnp.bfloat16)

    masks = patch_masks()
    for ref in (errors, inputs):
        ref[:, :PATCH, 128:256] = jnp.zeros((PAIRS, PATCH, 128), jnp.bfloat16)
        ref[:, 2 * PATCH :, COLS - 256 : COLS - 128] = jnp.zeros((PAIRS, PATCH, 128), jnp.bfloat16)
    partial_out[:, :, :128] = jnp.zeros((PAIRS, STACK, 128), jnp.float32)
    partial_out[:, :, COLS - 128 :] = jnp.zeros((PAIRS, STACK, 128), jnp.float32)
    table[...] = jnp.zeros(table.shape, table.dtype)
    targets[...] = jnp.zeros(targets.shape, targets.dtype)
    lane = lax.broadcasted_iota(jnp.int32, (8, 128), 1)
    full_weight = 2.0 * (1.0 / (jnp.full((8, 128), count, jnp.int32).astype(jnp.float32) * CELLS))
    weights = [
        jnp.where(lane // 64 + 2 * pair < count, full_weight, 0.0) for pair in range(PAIRS)
    ]
    start_first = first_ref[...].astype(jnp.bfloat16).astype(jnp.float32)
    start_last = last_ref[...].astype(jnp.bfloat16).astype(jnp.float32)
    now_first[...] = start_first
    now_last[...] = start_last

    for slot in range(TCAP):
        fetch(slot, True)

    low_lanes = lax.broadcasted_iota(jnp.int32, (SUB * F, 128), 1) < 64

    def spread_rows(pair, kind, put):
        rows = slice(kind * SUB * F, (kind + 1) * SUB * F)
        even = cubes[2 * pair, rows, :].astype(jnp.float32)
        odd = cubes[2 * pair + 1, rows, :].astype(jnp.float32)
        for half in range(2):
            left = even[:, half * 128 : (half + 1) * 128]
            right = odd[:, half * 128 : (half + 1) * 128]
            put(2 * half, jnp.where(low_lanes, left, pltpu.roll(right, 64, 1)))
            put(2 * half + 1, jnp.where(low_lanes, pltpu.roll(left, 64, 1), right))

    for pair in range(PAIRS):

        def put_input(cell, values):
            table[pl.ds(cell, SUB * F, 8), :] = values

        def put_target(cell, values):
            targets[pl.ds(pair * SUB * F * 8 + cell, SUB * F, 8), :] = values

        spread_rows(pair, 0, put_input)
        spread_rows(pair, 1, put_target)

        def stack_plane(x, carry):
            channels = [
                patch_stack(table[pl.ds(pl.multiple_of((c * SUB + x) * 8, 8), 8), :], masks)
                for c in range(F)
            ]
            store_planes(inputs, pair, x, channels)
            return carry

        lax.fori_loop(0, SUB, stack_plane, 0, unroll=8)

    field_in.wait()
    field_out.start()

    def train_step(step, step_carry):
        first_now = now_first[...].astype(jnp.bfloat16)
        last_now = now_last[...].astype(jnp.bfloat16)
        for cell in range(4):
            rows = slice(cell * CH, (cell + 1) * CH)
            big_first[rows, :] = dot_rows(first_now, select_first[cell]).astype(jnp.bfloat16)
            big_last[rows, :] = dot_rows(last_now, select_last[cell]).astype(jnp.bfloat16)
        big_last_t[...] = big_last[...].T
        def tile_of(index):
            return index // 8, pl.ds(pl.multiple_of((index % 8) * 256 + 128, 128), 256)

        def first_layer(index):
            pair, columns = tile_of(index)
            raw[index % 2] = dot_rows(big_first[...], inputs[pair, :, columns])

        def activate(index):
            pair, columns = tile_of(index)
            for part in range(8):
                rows = slice(part * 32, (part + 1) * 32)
                half = 0.5 * raw[index % 2, rows, :]
                curve = jnp.tanh(half)
                value = half + half * curve
                hiddens[pair, rows, columns] = value.astype(jnp.bfloat16)
                slopes[pair, rows, columns] = (0.5 + 0.5 * curve) + value * (0.5 - 0.5 * curve)

        def last_layer(index):
            pair, columns = tile_of(index)
            partial_out[pair, :, columns] = dot_rows(big_last_t[...], hiddens[pair, :, columns])

        def forward(index, carry):
            last_layer(index - 2)
            activate(index - 1)
            first_layer(index)
            return carry

        tiles = 8 * PAIRS
        first_layer(0)
        activate(0)
        first_layer(1)
        lax.fori_loop(2, tiles, forward, 0)
        last_layer(tiles - 2)
        activate(tiles - 1)
        last_layer(tiles - 1)

        def error_plane(index, carry):
            pair = index // SUB
            x = index % SUB
            column = pl.multiple_of((x + 1) * 128, 128)
            total = (
                partial_out[pair, 0:PATCH, pl.ds(pl.multiple_of(column + 128, 128), 128)]
                + partial_out[pair, PATCH : 2 * PATCH, pl.ds(column, 128)]
                + partial_out[pair, 2 * PATCH :, pl.ds(pl.multiple_of(column - 128, 128), 128)]
            )
            weight = jnp.where(pair == 0, weights[0], jnp.where(pair == 1, weights[1], weights[2]))
            channels = []
            for c in range(F):
                predicted = patch_fold(
                    total[16 * c : 16 * c + 8], total[16 * c + 8 : 16 * c + 16], masks
                )
                row = pl.multiple_of(((pair * F + c) * SUB + x) * 8, 8)
                error = weight * (predicted - targets[pl.ds(row, 8), :])
                error = jnp.where(masks["centre"], error, 0.0)
                error = error.astype(jnp.bfloat16).astype(jnp.float32)
                channels.append(patch_stack(error, masks))
            store_planes(errors, pair, x, channels)
            return carry

        lax.fori_loop(0, SUB * PAIRS, error_plane, 0, unroll=8)

        grad_first[...] = jnp.zeros(grad_first.shape, jnp.float32)
        grad_last[...] = jnp.zeros(grad_last.shape, jnp.float32)

        def hidden_layer(index):
            pair, columns = tile_of(index)
            raw[index % 2] = dot_rows(big_last[...], errors[pair, :, columns])

        def scale(index):
            pair, columns = tile_of(index)
            for part in range(8):
                rows = slice(part * 32, (part + 1) * 32)
                product = raw[index % 2, rows, :] * slopes[pair, rows, columns]
                pre_grads[pair, rows, columns] = product.astype(jnp.bfloat16)

        def gradients(index):
            pair, columns = tile_of(index)
            grad_first[...] += dot_lanes(pre_grads[pair, :, columns], inputs[pair, :, columns])
            grad_last[...] += dot_lanes(hiddens[pair, :, columns], errors[pair, :, columns])

        def backward(index, carry):
            gradients(index - 2)
            scale(index - 1)
            hidden_layer(index)
            return carry

        hidden_layer(0)
        scale(0)
        hidden_layer(1)
        lax.fori_loop(2, tiles, backward, 0)
        gradients(tiles - 2)
        scale(tiles - 1)
        gradients(tiles - 1)

        def folded(grad, select_ref):
            total = jnp.zeros((3 * CH, 256), jnp.float32)
            for cell in range(4):
                rest = grad[cell * CH : (cell + 1) * CH, :]
                parts = []
                for _ in range(3):
                    parts.append(rest.astype(jnp.bfloat16))
                    rest = rest - parts[-1].astype(jnp.float32)
                total = total + dot_lanes(jnp.concatenate(parts, axis=0), select_ref[cell])
            return total[:CH] + total[CH : 2 * CH] + total[2 * CH :]

        now_first[...] = now_first[...] - inner_rate * folded(grad_first, select_first)
        now_last[...] = now_last[...] - inner_rate * folded(grad_last, select_last)
        return step_carry

    lax.fori_loop(0, INNER, train_step, 0)
    delta_first[...] = start_first - now_first[...]
    delta_last[...] = start_last - now_last[...]
    field_out.wait()


def apart(left, right, distance):
    return jnp.where(lax.rem(lax.div(left, distance), 2) == lax.rem(lax.div(right, distance), 2), 0, 1)


def train_cubes(trainer_of, place, first, last, arrived, fields, steps):
    vmem = pl.BlockSpec(memory_space=pltpu.VMEM)
    smem = pl.BlockSpec(memory_space=pltpu.SMEM)
    anywhere = pl.BlockSpec(memory_space=pl.ANY)
    hbm = pl.BlockSpec(memory_space=pltpu.HBM)
    return pl.pallas_call(
        functools.partial(train_kernel, steps),
        out_shape=(
            jax.ShapeDtypeStruct((CH, 256), jnp.float32),
            jax.ShapeDtypeStruct((CH, 256), jnp.float32),
            jax.ShapeDtypeStruct(fields.shape, fields.dtype),
        ),
        in_specs=[smem] * 2 + [vmem] * 4 + [anywhere] * 2 + [hbm],
        out_specs=(vmem, vmem, hbm),
        scratch_shapes=[
            pltpu.SMEM((2, TCAP), jnp.int32),
            pltpu.VMEM((TCAP, 2 * SUB * F, 256), jnp.bfloat16),
            pltpu.VMEM((SUB * F * 8, 128), jnp.float32),
            pltpu.VMEM((PAIRS * SUB * F * 8, 128), jnp.float32),
            pltpu.VMEM((PAIRS, STACK, COLS), jnp.bfloat16),
            pltpu.VMEM((PAIRS, STACK, COLS), jnp.bfloat16),
            pltpu.VMEM((PAIRS, 4 * CH, COLS), jnp.bfloat16),
            pltpu.VMEM((PAIRS, 4 * CH, COLS), jnp.bfloat16),
            pltpu.VMEM((PAIRS, 4 * CH, COLS), jnp.float32),
            pltpu.VMEM((PAIRS, STACK, COLS), jnp.float32),
            pltpu.VMEM((4 * CH, STACK), jnp.bfloat16),
            pltpu.VMEM((4 * CH, STACK), jnp.bfloat16),
            pltpu.VMEM((STACK, 4 * CH), jnp.bfloat16),
            pltpu.VMEM((2, 4 * CH, 256), jnp.float32),
            pltpu.VMEM((4 * CH, STACK), jnp.float32),
            pltpu.VMEM((4 * CH, STACK), jnp.float32),
            pltpu.VMEM((CH, 256), jnp.float32),
            pltpu.VMEM((CH, 256), jnp.float32),
            pltpu.VMEM(fields.shape, fields.dtype),
            pltpu.SemaphoreType.DMA((TCAP,)),
            pltpu.SemaphoreType.DMA,
        ],
        compiler_params=pltpu.CompilerParams(vmem_limit_bytes=48 * 1024 * 1024),
        name="train_cubes",
    )(
        trainer_of,
        place,
        first,
        last,
        jnp.asarray(SELECT_FIRST, jnp.bfloat16),
        jnp.asarray(SELECT_LAST, jnp.bfloat16),
        *arrived,
        fields,
    )


def viscosity_of(cells, closure):
    def unit(h, total):
        half = closure[F, h] + closure[0, h] * cells[0]
        for f in range(1, F):
            half = half + closure[f, h] * cells[f]
        return total + closure[F + 1, h] * (half + half * jnp.tanh(half))

    total = lax.fori_loop(0, HID, unit, jnp.zeros(cells[0].shape, jnp.float32), unroll=4)
    soft = jnp.maximum(total, 0.0) + jnp.log1p(jnp.exp(-jnp.abs(total)))
    return base_viscosity + viscosity_gain * soft


def evolve_kernel(closure, place, fields, x_halo, y_first, y_second, new_fields):
    up_first = lax.rem(place[2], 2) == 0
    x_cells, y_cells, z_cells = fields.shape[1:]
    row = lax.broadcasted_iota(jnp.int32, (y_cells, z_cells), 0)
    lane = lax.broadcasted_iota(jnp.int32, (y_cells, z_cells), 1)
    part = y_cells // 2

    def plane(x, carry):
        eddies = []
        for half in range(2):
            rows = pl.ds(half * part, part)
            cells = [fields[f, x, rows, :] for f in range(F)]
            eddies.append(viscosity_of(cells, closure))
        viscosity = jnp.concatenate(eddies, axis=0)
        centre = [fields[f, x] for f in range(F)]
        below = jnp.maximum(x - 1, 0)
        above = jnp.minimum(x + 1, x_cells - 1)
        for f in range(F):
            value = centre[f]
            west = jnp.where(x == 0, x_halo[1, f], fields[f, below])
            east = jnp.where(x == x_cells - 1, x_halo[0, f], fields[f, above])
            first, second = y_first[f, pl.ds(x, 1), :], y_second[f, pl.ds(x, 1), :]
            south = jnp.where(
                row == 0, jnp.where(up_first, second, first), pltpu.roll(value, 1, 0)
            )
            north = jnp.where(
                row == y_cells - 1,
                jnp.where(up_first, first, second),
                pltpu.roll(value, y_cells - 1, 0),
            )
            lower = jnp.where(lane == 0, 0.0, pltpu.roll(value, 1, 1))
            upper = jnp.where(lane == z_cells - 1, 0.0, pltpu.roll(value, z_cells - 1, 1))
            laplacian = east + west + north + south + upper + lower - 6.0 * value
            advection = (
                centre[0] * (east - west) + centre[1] * (north - south) + centre[2] * (upper - lower)
            )
            tendency = viscosity * laplacian - 0.5 * advection
            if f == 2:
                tendency = tendency + buoyancy * centre[3]
            new_fields[f, x] = value + time_step * tendency
        return carry

    lax.fori_loop(0, x_cells, plane, 0)


def evolve(closure, place, fields, x_halo, y_first, y_second):
    vmem = pl.BlockSpec(memory_space=pltpu.VMEM)
    return pl.pallas_call(
        evolve_kernel,
        out_shape=jax.ShapeDtypeStruct(fields.shape, fields.dtype),
        in_specs=[pl.BlockSpec(memory_space=pltpu.SMEM)] * 2 + [vmem] * 4,
        out_specs=vmem,
        compiler_params=pltpu.CompilerParams(vmem_limit_bytes=16 * 1024 * 1024),
        name="evolve_brick",
    )(closure, place, fields, x_halo, y_first, y_second)


def cell_order():
    order = np.zeros((256, 256), np.float32)
    for y in range(SUB):
        for z in range(SUB):
            order[y * SUB + z, (y % 2 * 2 + z % 2) * 64 + y // 2 * 8 + z // 2] = 1.0
    return order


CELL_ORDER = cell_order()


def corner_of(sample_block, place, x_step, y_step, y_cells, z_cells):
    x_devices, y_devices = place[5], place[4]
    gx = lax.rem(place[1] + x_step + x_devices, x_devices)
    gy = lax.rem(place[2] + y_step + y_devices, y_devices)
    group = jnp.minimum(place[0], place[3] - 1)
    block = sample_block[(group * x_devices + gx) * y_devices + gy]
    z_blocks = z_cells // SUB
    return lax.rem(lax.div(block, z_blocks), y_cells // SUB) * SUB, lax.rem(block, z_blocks) * SUB


def sample_kernel(
    y_cells,
    z_cells,
    sample_block,
    place,
    brick,
    centre,
    lower,
    upper,
    own_rows,
    faces,
    row_for_first,
    row_for_second,
    x_edges,
    y_edges,
    windows,
    sems,
):
    rows_of_x = y_cells
    rows_of_field = SUB * y_cells
    window_rows = F * rows_of_field
    copies = [
        pltpu.make_async_copy(
            brick.at[:, pl.ds(w * 128, 128)], windows.at[pl.ds(w * window_rows, window_rows)], sems.at[w]
        )
        for w in range(z_cells // 128)
    ]
    for copy in copies:
        copy.start()
    for copy in copies:
        copy.wait()

    def corner(x_step, y_step):
        return corner_of(sample_block, place, x_step, y_step, y_cells, z_cells)

    def piece(row, count, stride, z, lane_start):
        values = windows[pl.ds(lax.div(z, 128) * window_rows + row, count, stride), :]
        return pltpu.roll(values, lax.rem(lane_start - lax.rem(z, 128) + 256, 128), 1)

    lane = lax.broadcasted_iota(jnp.int32, (SUB, 128), 1)
    y_start, z_start = corner(0, 0)
    z_below = jnp.maximum(z_start - 1, 0)
    z_above = jnp.minimum(z_start + SUB, z_cells - 1)
    for field in range(F):
        for half in range(2):
            inside = jnp.zeros((SUB, 128), jnp.float32)
            below = jnp.zeros((SUB, 128), jnp.float32)
            above = jnp.zeros((SUB, 128), jnp.float32)
            for step in range(8):
                row = field * rows_of_field + y_start + half * 8 + step
                first = step * SUB
                inside = jnp.where(lane // SUB == step, piece(row, SUB, rows_of_x, z_start, first), inside)
                below = jnp.where(lane == first, piece(row, SUB, rows_of_x, z_below, first), below)
                last = first + SUB - 1
                above = jnp.where(lane == last, piece(row, SUB, rows_of_x, z_above, last), above)
            below = jnp.where(z_start == 0, 0.0, below)
            above = jnp.where(z_start + SUB == z_cells, 0.0, above)
            at = (slice(field * SUB, (field + 1) * SUB), slice(half * 128, (half + 1) * 128))
            centre[at] = inside
            lower[at] = jnp.where(lane % SUB == 0, below, pltpu.roll(inside, 1, 1))
            upper[at] = jnp.where(lane % SUB == SUB - 1, above, pltpu.roll(inside, 127, 1))

    def y_row(y, z):
        total = jnp.zeros((SUB, 128), jnp.float32)
        for field in range(F):
            part = piece(field * rows_of_field + y, SUB, rows_of_x, z, field * SUB)
            total = jnp.where(lane // SUB == field, part, total)
        return total

    own_rows[0] = y_row(jnp.maximum(y_start - 1, 0), z_start)
    own_rows[1] = y_row(jnp.minimum(y_start + SUB, y_cells - 1), z_start)
    up_first = lax.rem(place[2], 2) == 0
    z_first = corner(0, jnp.where(up_first, 1, -1))[1]
    z_second = corner(0, jnp.where(up_first, -1, 1))[1]
    row_for_first[...] = y_row(jnp.where(up_first, y_cells - 1, 0), z_first)
    row_for_second[...] = y_row(jnp.where(up_first, 0, y_cells - 1), z_second)
    lane = lane[:8]
    for face, (x, step) in enumerate(((0, -1), (SUB - 1, 1))):
        y_there, z_there = corner(step, 0)
        for half in range(2):
            total = jnp.zeros((8, 128), jnp.float32)
            for step in range(8):
                row = x * rows_of_x + y_there + half * 8 + step
                part = piece(row, 8, rows_of_field, z_there, step * SUB)
                total = jnp.where(lane // SUB == step, part, total)
            faces[face, :, half * 128 : (half + 1) * 128] = total
    for side in range(2):
        y = jnp.where(up_first == (side == 0), y_cells - 1, 0)
        for field in range(F):
            for w in range(z_cells // 128):
                start = w * window_rows + field * rows_of_field + y
                y_edges[side, field, :, w * 128 : (w + 1) * 128] = windows[
                    pl.ds(start, SUB, rows_of_x), :
                ]
    for side, x in enumerate((0, SUB - 1)):
        for field in range(F):
            for w in range(z_cells // 128):
                start = w * window_rows + field * rows_of_field + x * rows_of_x
                x_edges[side, field, :, w * 128 : (w + 1) * 128] = windows[pl.ds(start, rows_of_x), :]


def sample_cube(sample_block, place, brick):
    fields, x_cells, y_cells, z_cells = brick.shape
    vmem = pl.BlockSpec(memory_space=pltpu.VMEM)
    smem = pl.BlockSpec(memory_space=pltpu.SMEM)
    hbm = pl.BlockSpec(memory_space=pltpu.HBM)
    rows = fields * x_cells * y_cells
    cube = jax.ShapeDtypeStruct((F * SUB, 256), jnp.float32)
    line = jax.ShapeDtypeStruct((SUB, 128), jnp.float32)
    return pl.pallas_call(
        functools.partial(sample_kernel, y_cells, z_cells),
        out_shape=(
            cube,
            cube,
            cube,
            jax.ShapeDtypeStruct((2, SUB, 128), jnp.float32),
            jax.ShapeDtypeStruct((2, 8, 256), jnp.float32),
            line,
            line,
            jax.ShapeDtypeStruct((2, fields, y_cells, z_cells), jnp.float32),
            jax.ShapeDtypeStruct((2, fields, x_cells, z_cells), jnp.float32),
        ),
        in_specs=[smem, smem, hbm],
        out_specs=(vmem,) * 9,
        scratch_shapes=[
            pltpu.VMEM((z_cells // 128 * rows + 4 * x_cells * y_cells, 128), jnp.float32),
            pltpu.SemaphoreType.DMA((z_cells // 128,)),
        ],
        compiler_params=pltpu.CompilerParams(vmem_limit_bytes=16 * 1024 * 1024),
        name="sample_cube",
    )(sample_block, place, brick.reshape(rows, z_cells))


def change_kernel(
    y_cells,
    z_cells,
    sample_block,
    place,
    closure,
    order,
    centre,
    lower,
    upper,
    own_rows,
    face_halo,
    row_first,
    row_second,
    payload,
):
    y_start = corner_of(sample_block, place, 0, 0, y_cells, z_cells)[0]
    row = lax.broadcasted_iota(jnp.int32, (SUB, 256), 0)
    lane = lax.broadcasted_iota(jnp.int32, (SUB, 256), 1)
    up_first = lax.rem(place[2], 2) == 0
    row_low = jnp.where(up_first, row_second[...], row_first[...])
    row_high = jnp.where(up_first, row_first[...], row_second[...])
    south_row = jnp.where(y_start == 0, row_low, own_rows[0])
    north_row = jnp.where(y_start + SUB == y_cells, row_high, own_rows[1])
    cells = [centre[f * SUB : (f + 1) * SUB, :] for f in range(F)]
    viscosity = viscosity_of(cells, closure)
    changes = []
    for f in range(F):
        value = cells[f]
        west = jnp.where(row == 0, face_halo[1, f : f + 1, :], pltpu.roll(value, 1, 0))
        east = jnp.where(row == SUB - 1, face_halo[0, f : f + 1, :], pltpu.roll(value, SUB - 1, 0))
        edge = pltpu.roll(south_row, (128 - f * SUB) % 128, 1)
        south = jnp.where(lane < SUB, jnp.concatenate([edge, edge], 1), pltpu.roll(value, SUB, 1))
        edge = pltpu.roll(north_row, 112 - f * SUB, 1)
        north = jnp.where(
            lane >= 256 - SUB, jnp.concatenate([edge, edge], 1), pltpu.roll(value, 256 - SUB, 1)
        )
        down = lower[f * SUB : (f + 1) * SUB, :]
        up = upper[f * SUB : (f + 1) * SUB, :]
        laplacian = east + west + north + south + up + down - 6.0 * value
        advection = cells[0] * (east - west) + cells[1] * (north - south) + cells[2] * (up - down)
        change = viscosity * laplacian - 0.5 * advection
        if f == 2:
            change = change + buoyancy * cells[3]
        changes.append(change)
    both = jnp.concatenate(cells + changes, axis=0).astype(jnp.bfloat16)
    payload[...] = dot_rows(both, order[...]).astype(jnp.bfloat16)


def cube_change(sample_block, place, closure, cube, halo, y_cells, z_cells):
    vmem = pl.BlockSpec(memory_space=pltpu.VMEM)
    smem = pl.BlockSpec(memory_space=pltpu.SMEM)
    return pl.pallas_call(
        functools.partial(change_kernel, y_cells, z_cells),
        out_shape=jax.ShapeDtypeStruct((2 * F * SUB, 256), jnp.bfloat16),
        in_specs=[smem] * 3 + [vmem] * 8,
        out_specs=vmem,
        compiler_params=pltpu.CompilerParams(vmem_limit_bytes=16 * 1024 * 1024),
        name="cube_change",
    )(sample_block, place, closure, jnp.asarray(CELL_ORDER, jnp.bfloat16), *cube, *halo)


def doubling_steps(x_devices, y_devices):
    along_y = [1 << bit for bit in reversed(range(y_devices.bit_length() - 1))]
    along_x = [y_devices << bit for bit in reversed(range(x_devices.bit_length() - 1))]
    return along_y + along_x


def on_device(
    fields, closure_in, closure_bias, closure_out, master, momentum, sample_block, sample_trainer
):
    group_count = lax.axis_size("grp")
    x_devices = lax.axis_size("gx")
    y_devices = lax.axis_size("gy")
    trainers = x_devices * y_devices
    my_group = lax.axis_index("grp")
    my_column = lax.axis_index("gx") * y_devices + lax.axis_index("gy")
    is_trainer = my_group == group_count - 1
    everyone = ("grp", "gx", "gy")
    sim_groups = group_count - 1
    first_trainer = sim_groups * trainers
    brick = fields[0]
    y_cells, z_cells = brick.shape[2:]
    closure = jnp.concatenate(
        [0.5 * closure_in.T, 0.5 * closure_bias[None], closure_out[None]], axis=0
    )
    place = jnp.stack(
        [
            my_group,
            lax.axis_index("gx"),
            lax.axis_index("gy"),
            jnp.int32(sim_groups),
            jnp.int32(y_devices),
            jnp.int32(x_devices),
        ]
    ).astype(jnp.int32)

    def pairs(x_step, even_step):
        found = []
        for g in range(sim_groups):
            for c in range(trainers):
                gx, gy = c // y_devices, c % y_devices
                gx = (gx + x_step) % x_devices
                gy = (gy + (even_step if gy % 2 == 0 else -even_step)) % y_devices
                found.append((g * trainers + c, (g * x_devices + gx) * y_devices + gy))
        return found

    def x_neighbours(edges):
        if x_devices == 2:
            return lax.ppermute(edges, everyone, pairs(1, 0))
        from_high = lax.ppermute(edges[0], everyone, pairs(-1, 0))
        return jnp.stack([from_high, lax.ppermute(edges[1], everyone, pairs(1, 0))])

    def y_neighbours(for_first, for_second):
        return (
            lax.ppermute(for_first, everyone, pairs(0, 1)),
            lax.ppermute(for_second, everyone, pairs(0, -1)),
        )

    def swap(distance):
        return [(first_trainer + c, first_trainer + (c ^ distance)) for c in range(trainers)]

    steps = doubling_steps(x_devices, y_devices)

    def to_trainers(payload):
        return jnp.stack(
            [
                lax.ppermute(
                    payload,
                    everyone,
                    [(g * trainers + c, first_trainer + c) for c in range(trainers)],
                )
                for g in range(sim_groups)
            ]
        )

    def among_trainers(held):
        for distance in steps[:-1]:
            held = jnp.concatenate([held, lax.ppermute(held, everyone, swap(distance))], axis=0)
        return [held, lax.ppermute(held, everyone, swap(steps[-1]))]

    *cube, faces, row_for_first, row_for_second, x_edges, y_edges = sample_cube(
        sample_block, place, brick
    )
    thin_halo = (x_neighbours(faces), *y_neighbours(row_for_first, row_for_second))
    payload = cube_change(sample_block, place, closure, cube, thin_halo, y_cells, z_cells)
    landed = to_trainers(payload)
    x_edges, y_edges, landed = lax.optimization_barrier((x_edges, y_edges, landed))
    halo = (x_neighbours(x_edges), *y_neighbours(y_edges[0], y_edges[1]))
    arrived = among_trainers(landed)

    first_count = CH * TAPS * F
    first = jnp.pad(master[:first_count].reshape(CH, TAPS * F), ((0, 0), (0, 256 - TAPS * F)))
    last = jnp.pad(master[first_count:].reshape(TAPS * F, CH).T, ((0, 0), (0, 256 - TAPS * F)))

    def train_here():
        delta_first, delta_last, new_brick = train_cubes(
            sample_trainer, place, first, last, arrived, brick, steps
        )
        delta = jnp.concatenate(
            [delta_first[:, : TAPS * F].reshape(-1), delta_last[:, : TAPS * F].T.reshape(-1)]
        )
        return delta, new_brick

    def evolve_here():
        new_brick = evolve(closure, place, brick, *halo)
        return jnp.zeros((NPARAM,), jnp.float32), new_brick

    delta, new_brick = lax.cond(is_trainer, train_here, evolve_here)

    total = delta
    for distance in steps:
        total = total + lax.ppermute(total, everyone, swap(distance))
    final = jnp.where(is_trainer, total, 0.0)
    for g in range(sim_groups):
        pairs = [(first_trainer + c, g * trainers + c) for c in range(trainers)]
        final = final + lax.ppermute(total, everyone, pairs)

    share_size = NPARAM // (group_count * trainers)
    share_start = (my_group * trainers + my_column) * share_size
    momentum_share = lax.dynamic_slice_in_dim(momentum, share_start, share_size)
    master_share = lax.dynamic_slice_in_dim(master, share_start, share_size)
    inverse = 1.0 / jnp.sqrt(jnp.sum(final * final) / NPARAM + norm_epsilon)
    delta_share = lax.dynamic_slice_in_dim(final, share_start, share_size)
    new_momentum = momentum_decay * momentum_share + delta_share * inverse
    new_master = master_share - outer_rate * new_momentum
    return (new_brick[None], new_master, new_momentum)


def solution(mesh):
    in_specs = (P("grp", None, "gx", "gy", None), P(), P(), P(), P(), P(), P(), P())
    out_specs = (P("grp", None, "gx", "gy", None), P(("grp", "gx", "gy")), P(("grp", "gx", "gy")))
    return jax.shard_map(
        on_device, mesh=mesh, in_specs=in_specs, out_specs=out_specs, check_vma=False
    )
```

```python
import functools

import jax
import jax.numpy as jnp
import numpy as np
from jax import lax
from jax.experimental import pallas as pl
from jax.experimental.pallas import tpu as pltpu
from jax.sharding import PartitionSpec as P

F = 5
CH = 64
HID = 64
SUB = 16
TCAP = 6
INNER = 3
CELLS = 4096
NPARAM = 17280
TAPS = 27
PAIRS = TCAP // 2
COLS = (SUB + 2) * 128
PATCH = 16 * F
STACK = 3 * PATCH

time_step = 0.1
base_viscosity = 0.02
viscosity_gain = 0.2
buoyancy = 0.5
inner_rate = 0.02
outer_rate = 0.01
momentum_decay = 0.9
norm_epsilon = 1e-06


def patch_position(row):
    group, py, pz = row // 4, row // 2 % 2, row % 2
    ypos = py + 1 if group in (0, 1) else (3 if py == 0 else 0)
    zpos = pz + 1 if group in (0, 2) else (3 if pz == 0 else 0)
    return ypos - 1, zpos - 1


def selections():
    first = np.zeros((4, 256, STACK), np.float32)
    last = np.zeros((4, 256, STACK), np.float32)
    for cell in range(4):
        py, pz = cell // 2, cell % 2
        for kx in range(3):
            for channel in range(F):
                for row in range(16):
                    ypos, zpos = patch_position(row)
                    column = kx * PATCH + channel * 16 + row
                    dy, dz = ypos - py, zpos - pz
                    if abs(dy) <= 1 and abs(dz) <= 1:
                        tap = 9 * kx + 3 * (dy + 1) + dz + 1
                        first[cell, tap * F + channel, column] = 1.0
                        last[cell, channel * TAPS + 26 - tap, column] = 1.0
    return first, last


SELECT_FIRST, SELECT_LAST = selections()


def dot_rows(left, right):
    return jnp.dot(left, right, preferred_element_type=jnp.float32)


def dot_lanes(left, right):
    return lax.dot_general(left, right, (((1,), (1,)), ((), ())), preferred_element_type=jnp.float32)


def patch_masks():
    row = lax.broadcasted_iota(jnp.int32, (8, 128), 0)
    lane = lax.broadcasted_iota(jnp.int32, (8, 128), 1)
    return {
        "pz0": row % 2 == 0,
        "py0": row // 2 % 2 == 0,
        "centre": row < 4,
        "z_first": lane % 8 == 0,
        "z_last": lane % 8 == 7,
        "y_first": lane // 8 % 8 == 0,
        "y_last": lane // 8 % 8 == 7,
    }


def edge_shift(values, step, parity_zero, first, last, forward):
    before = jnp.where(first, 0.0, pltpu.roll(values, step, 1))
    after = jnp.where(last, 0.0, pltpu.roll(values, 128 - step, 1))
    if forward:
        return jnp.where(parity_zero, after, before)
    return jnp.where(parity_zero, before, after)


def patch_stack(rows, masks):
    both = rows + pltpu.roll(rows, 4, 0)
    z_edge = edge_shift(both, 1, masks["pz0"], masks["z_first"], masks["z_last"], True)
    upper = jnp.where(masks["centre"], both, z_edge)
    lower = edge_shift(upper, 8, masks["py0"], masks["y_first"], masks["y_last"], True)
    return upper, lower


def patch_fold(upper, lower, masks):
    def fold_z(values):
        moved = edge_shift(values, 1, masks["pz0"], masks["z_first"], masks["z_last"], False)
        return values + pltpu.roll(moved, 4, 0)

    shifted = edge_shift(fold_z(lower), 8, masks["py0"], masks["y_first"], masks["y_last"], False)
    return fold_z(upper) + shifted


def store_planes(ref, pair, x, channels):
    stacked = jnp.concatenate([part for both in channels for part in both], axis=0).astype(jnp.bfloat16)
    for kx in range(3):
        start = pl.multiple_of((x + 2 - kx) * 128, 128)
        ref[pair, kx * PATCH : (kx + 1) * PATCH, pl.ds(start, 128)] = stacked


def train_kernel(steps, *refs):
    (trainer_of, place, first_ref, last_ref, far_first, far_last) = refs[:6]
    arrived = refs[6:8]
    fields_ref = refs[8]
    delta_first, delta_last, new_fields_ref = refs[9:12]
    (
        slots,
        cubes,
        table,
        targets,
        inputs,
        errors,
        hiddens,
        pre_grads,
        slopes,
        partial_out,
        big_first,
        big_last,
        big_last_t,
        now_first,
        now_last,
        brick,
        select_first,
        select_last,
        slot_sems,
        field_sem,
        select_sems,
    ) = refs[12:]

    field_in = pltpu.make_async_copy(fields_ref, brick, field_sem)
    field_out = pltpu.make_async_copy(brick, new_fields_ref, field_sem)
    select_copies = [
        pltpu.make_async_copy(far_first, select_first, select_sems.at[0]),
        pltpu.make_async_copy(far_last, select_last, select_sems.at[1]),
    ]

    groups = place[3]
    trainers = trainer_of.shape[0] // groups
    column = place[1] * place[4] + place[2]

    def visit(owner, count):
        mine = trainer_of[owner] == column

        @pl.when(mine)
        def _():
            source = lax.rem(owner, trainers)
            entry = jnp.int32(0)
            for order, distance in enumerate(steps[:-1]):
                entry = entry + apart(source, column, distance) * (1 << order)
            slots[0, count] = apart(source, column, steps[-1])
            slots[1, count] = entry * groups + lax.div(owner, trainers)

        return count + jnp.where(mine, 1, 0)

    count = lax.fori_loop(0, trainer_of.shape[0], visit, jnp.int32(0))

    def fetch(slot, wait):
        for half in range(2):

            @pl.when((slot < count) & (slots[0, slot] == half))
            def _():
                copy = pltpu.make_async_copy(
                    arrived[half].at[slots[1, slot]], cubes.at[slot], slot_sems.at[slot]
                )
                copy.wait() if wait else copy.start()

    for slot in range(TCAP):
        fetch(slot, False)

    for copy in select_copies:
        copy.start()
    field_in.start()
    for slot in range(TCAP):

        @pl.when(slot >= count)
        def _():
            cubes[slot] = jnp.zeros((2 * SUB * F, 256), jnp.bfloat16)

    masks = patch_masks()
    for ref in (errors, inputs):
        ref[:, :PATCH, 128:256] = jnp.zeros((PAIRS, PATCH, 128), jnp.bfloat16)
        ref[:, 2 * PATCH :, COLS - 256 : COLS - 128] = jnp.zeros((PAIRS, PATCH, 128), jnp.bfloat16)
    partial_out[:, :, :128] = jnp.zeros((PAIRS, STACK, 128), jnp.float32)
    partial_out[:, :, COLS - 128 :] = jnp.zeros((PAIRS, STACK, 128), jnp.float32)
    table[...] = jnp.zeros(table.shape, table.dtype)
    targets[...] = jnp.zeros(targets.shape, targets.dtype)
    lane = lax.broadcasted_iota(jnp.int32, (8, 128), 1)
    full_weight = 2.0 * (1.0 / (jnp.full((8, 128), count, jnp.int32).astype(jnp.float32) * CELLS))
    weights = [
        jnp.where(lane // 64 + 2 * pair < count, full_weight, 0.0) for pair in range(PAIRS)
    ]
    start_first = first_ref[...].astype(jnp.bfloat16).astype(jnp.float32)
    start_last = last_ref[...].astype(jnp.bfloat16).astype(jnp.float32)
    now_first[...] = start_first
    now_last[...] = start_last

    for slot in range(TCAP):
        fetch(slot, True)

    low_lanes = lax.broadcasted_iota(jnp.int32, (SUB * F, 128), 1) < 64

    def spread_rows(pair, kind, put):
        rows = slice(kind * SUB * F, (kind + 1) * SUB * F)
        even = cubes[2 * pair, rows, :].astype(jnp.float32)
        odd = cubes[2 * pair + 1, rows, :].astype(jnp.float32)
        for half in range(2):
            left = even[:, half * 128 : (half + 1) * 128]
            right = odd[:, half * 128 : (half + 1) * 128]
            put(2 * half, jnp.where(low_lanes, left, pltpu.roll(right, 64, 1)))
            put(2 * half + 1, jnp.where(low_lanes, pltpu.roll(left, 64, 1), right))

    for pair in range(PAIRS):

        def put_input(cell, values):
            table[pl.ds(cell, SUB * F, 8), :] = values

        def put_target(cell, values):
            targets[pl.ds(pair * SUB * F * 8 + cell, SUB * F, 8), :] = values

        spread_rows(pair, 0, put_input)
        spread_rows(pair, 1, put_target)

        def stack_plane(x, carry):
            channels = [
                patch_stack(table[pl.ds(pl.multiple_of((c * SUB + x) * 8, 8), 8), :], masks)
                for c in range(F)
            ]
            store_planes(inputs, pair, x, channels)
            return carry

        lax.fori_loop(0, SUB, stack_plane, 0, unroll=8)

    for copy in select_copies:
        copy.wait()
    field_in.wait()
    field_out.start()

    def train_step(step, step_carry):
        first_now = now_first[...].astype(jnp.bfloat16)
        last_now = now_last[...].astype(jnp.bfloat16)
        for cell in range(4):
            rows = slice(cell * CH, (cell + 1) * CH)
            big_first[rows, :] = dot_rows(first_now, select_first[cell]).astype(jnp.bfloat16)
            big_last[rows, :] = dot_rows(last_now, select_last[cell]).astype(jnp.bfloat16)
        big_last_t[...] = big_last[...].T
        def tile_of(index):
            return index // 8, pl.ds(pl.multiple_of((index % 8) * 256 + 128, 128), 256)

        def forward(index, carry):
            pair, columns = tile_of(index)
            half = 0.5 * dot_rows(big_first[...], inputs[pair, :, columns])
            curve = jnp.tanh(half)
            value = half + half * curve
            hidden = value.astype(jnp.bfloat16)
            hiddens[pair, :, columns] = hidden
            slopes[pair, :, columns] = (0.5 + 0.5 * curve) + value * (0.5 - 0.5 * curve)
            partial_out[pair, :, columns] = dot_rows(big_last_t[...], hidden)
            return carry

        lax.fori_loop(0, 8 * PAIRS, forward, 0, unroll=8)

        def error_plane(index, carry):
            pair = index // SUB
            x = index % SUB
            column = pl.multiple_of((x + 1) * 128, 128)
            total = (
                partial_out[pair, 0:PATCH, pl.ds(pl.multiple_of(column + 128, 128), 128)]
                + partial_out[pair, PATCH : 2 * PATCH, pl.ds(column, 128)]
                + partial_out[pair, 2 * PATCH :, pl.ds(pl.multiple_of(column - 128, 128), 128)]
            )
            weight = jnp.where(pair == 0, weights[0], jnp.where(pair == 1, weights[1], weights[2]))
            channels = []
            for c in range(F):
                predicted = patch_fold(
                    total[16 * c : 16 * c + 8], total[16 * c + 8 : 16 * c + 16], masks
                )
                row = pl.multiple_of(((pair * F + c) * SUB + x) * 8, 8)
                error = weight * (predicted - targets[pl.ds(row, 8), :])
                error = jnp.where(masks["centre"], error, 0.0)
                error = error.astype(jnp.bfloat16).astype(jnp.float32)
                channels.append(patch_stack(error, masks))
            store_planes(errors, pair, x, channels)
            return carry

        lax.fori_loop(0, SUB * PAIRS, error_plane, 0, unroll=8)

        def backward(index, carry):
            pair, columns = tile_of(index)
            hidden_grad = dot_rows(big_last[...], errors[pair, :, columns])
            pre_grads[pair, :, columns] = (hidden_grad * slopes[pair, :, columns]).astype(jnp.bfloat16)
            return carry

        lax.fori_loop(0, 8 * PAIRS, backward, 0, unroll=8)
        body = slice(128, COLS - 128)
        grad_first = jnp.zeros((4 * CH, STACK), jnp.float32)
        grad_last = jnp.zeros((4 * CH, STACK), jnp.float32)
        for pair in range(PAIRS):
            grad_first += dot_lanes(pre_grads[pair, :, body], inputs[pair, :, body])
            grad_last += dot_lanes(hiddens[pair, :, body], errors[pair, :, body])

        def folded(grad, select_ref):
            total = jnp.zeros((3 * CH, 256), jnp.float32)
            for cell in range(4):
                rest = grad[cell * CH : (cell + 1) * CH, :]
                parts = []
                for _ in range(3):
                    parts.append(rest.astype(jnp.bfloat16))
                    rest = rest - parts[-1].astype(jnp.float32)
                total = total + dot_lanes(jnp.concatenate(parts, axis=0), select_ref[cell])
            return total[:CH] + total[CH : 2 * CH] + total[2 * CH :]

        now_first[...] = now_first[...] - inner_rate * folded(grad_first, select_first)
        now_last[...] = now_last[...] - inner_rate * folded(grad_last, select_last)
        return step_carry

    lax.fori_loop(0, INNER, train_step, 0)
    delta_first[...] = start_first - now_first[...]
    delta_last[...] = start_last - now_last[...]
    field_out.wait()


def apart(left, right, distance):
    return jnp.where(lax.rem(lax.div(left, distance), 2) == lax.rem(lax.div(right, distance), 2), 0, 1)


def train_cubes(trainer_of, place, first, last, arrived, fields, steps):
    vmem = pl.BlockSpec(memory_space=pltpu.VMEM)
    smem = pl.BlockSpec(memory_space=pltpu.SMEM)
    anywhere = pl.BlockSpec(memory_space=pl.ANY)
    hbm = pl.BlockSpec(memory_space=pltpu.HBM)
    return pl.pallas_call(
        functools.partial(train_kernel, steps),
        out_shape=(
            jax.ShapeDtypeStruct((CH, 256), jnp.float32),
            jax.ShapeDtypeStruct((CH, 256), jnp.float32),
            jax.ShapeDtypeStruct(fields.shape, fields.dtype),
        ),
        in_specs=[smem] * 2 + [vmem] * 2 + [hbm] * 2 + [anywhere] * 2 + [hbm],
        out_specs=(vmem, vmem, hbm),
        scratch_shapes=[
            pltpu.SMEM((2, TCAP), jnp.int32),
            pltpu.VMEM((TCAP, 2 * SUB * F, 256), jnp.bfloat16),
            pltpu.VMEM((SUB * F * 8, 128), jnp.float32),
            pltpu.VMEM((PAIRS * SUB * F * 8, 128), jnp.float32),
            pltpu.VMEM((PAIRS, STACK, COLS), jnp.bfloat16),
            pltpu.VMEM((PAIRS, STACK, COLS), jnp.bfloat16),
            pltpu.VMEM((PAIRS, 4 * CH, COLS), jnp.bfloat16),
            pltpu.VMEM((PAIRS, 4 * CH, COLS), jnp.bfloat16),
            pltpu.VMEM((PAIRS, 4 * CH, COLS), jnp.float32),
            pltpu.VMEM((PAIRS, STACK, COLS), jnp.float32),
            pltpu.VMEM((4 * CH, STACK), jnp.bfloat16),
            pltpu.VMEM((4 * CH, STACK), jnp.bfloat16),
            pltpu.VMEM((STACK, 4 * CH), jnp.bfloat16),
            pltpu.VMEM((CH, 256), jnp.float32),
            pltpu.VMEM((CH, 256), jnp.float32),
            pltpu.VMEM(fields.shape, fields.dtype),
            pltpu.VMEM((4, 256, STACK), jnp.bfloat16),
            pltpu.VMEM((4, 256, STACK), jnp.bfloat16),
            pltpu.SemaphoreType.DMA((TCAP,)),
            pltpu.SemaphoreType.DMA,
            pltpu.SemaphoreType.DMA((2,)),
        ],
        compiler_params=pltpu.CompilerParams(vmem_limit_bytes=48 * 1024 * 1024),
        name="train_cubes",
    )(
        trainer_of,
        place,
        first,
        last,
        jnp.asarray(SELECT_FIRST, jnp.bfloat16),
        jnp.asarray(SELECT_LAST, jnp.bfloat16),
        *arrived,
        fields,
    )


def viscosity_of(cells, closure):
    def unit(h, total):
        half = closure[F, h] + closure[0, h] * cells[0]
        for f in range(1, F):
            half = half + closure[f, h] * cells[f]
        return total + closure[F + 1, h] * (half + half * jnp.tanh(half))

    total = lax.fori_loop(0, HID, unit, jnp.zeros(cells[0].shape, jnp.float32), unroll=4)
    soft = jnp.maximum(total, 0.0) + jnp.log1p(jnp.exp(-jnp.abs(total)))
    return base_viscosity + viscosity_gain * soft


def evolve_kernel(closure, place, fields, x_halo, y_first, y_second, new_fields):
    up_first = lax.rem(place[2], 2) == 0
    x_cells, y_cells, z_cells = fields.shape[1:]
    row = lax.broadcasted_iota(jnp.int32, (y_cells, z_cells), 0)
    lane = lax.broadcasted_iota(jnp.int32, (y_cells, z_cells), 1)
    part = y_cells // 2

    def plane(x, carry):
        eddies = []
        for half in range(2):
            rows = pl.ds(half * part, part)
            cells = [fields[f, x, rows, :] for f in range(F)]
            eddies.append(viscosity_of(cells, closure))
        viscosity = jnp.concatenate(eddies, axis=0)
        centre = [fields[f, x] for f in range(F)]
        below = jnp.maximum(x - 1, 0)
        above = jnp.minimum(x + 1, x_cells - 1)
        for f in range(F):
            value = centre[f]
            west = jnp.where(x == 0, x_halo[1, f], fields[f, below])
            east = jnp.where(x == x_cells - 1, x_halo[0, f], fields[f, above])
            first, second = y_first[f, pl.ds(x, 1), :], y_second[f, pl.ds(x, 1), :]
            south = jnp.where(
                row == 0, jnp.where(up_first, second, first), pltpu.roll(value, 1, 0)
            )
            north = jnp.where(
                row == y_cells - 1,
                jnp.where(up_first, first, second),
                pltpu.roll(value, y_cells - 1, 0),
            )
            lower = jnp.where(lane == 0, 0.0, pltpu.roll(value, 1, 1))
            upper = jnp.where(lane == z_cells - 1, 0.0, pltpu.roll(value, z_cells - 1, 1))
            laplacian = east + west + north + south + upper + lower - 6.0 * value
            advection = (
                centre[0] * (east - west) + centre[1] * (north - south) + centre[2] * (upper - lower)
            )
            tendency = viscosity * laplacian - 0.5 * advection
            if f == 2:
                tendency = tendency + buoyancy * centre[3]
            new_fields[f, x] = value + time_step * tendency
        return carry

    lax.fori_loop(0, x_cells, plane, 0)


def evolve(closure, place, fields, x_halo, y_first, y_second):
    vmem = pl.BlockSpec(memory_space=pltpu.VMEM)
    return pl.pallas_call(
        evolve_kernel,
        out_shape=jax.ShapeDtypeStruct(fields.shape, fields.dtype),
        in_specs=[pl.BlockSpec(memory_space=pltpu.SMEM)] * 2 + [vmem] * 4,
        out_specs=vmem,
        compiler_params=pltpu.CompilerParams(vmem_limit_bytes=16 * 1024 * 1024),
        name="evolve_brick",
    )(closure, place, fields, x_halo, y_first, y_second)


def cell_order():
    order = np.zeros((256, 256), np.float32)
    for y in range(SUB):
        for z in range(SUB):
            order[y * SUB + z, (y % 2 * 2 + z % 2) * 64 + y // 2 * 8 + z // 2] = 1.0
    return order


CELL_ORDER = cell_order()


def corner_of(sample_block, place, x_step, y_step, y_cells, z_cells):
    x_devices, y_devices = place[5], place[4]
    gx = lax.rem(place[1] + x_step + x_devices, x_devices)
    gy = lax.rem(place[2] + y_step + y_devices, y_devices)
    group = jnp.minimum(place[0], place[3] - 1)
    block = sample_block[(group * x_devices + gx) * y_devices + gy]
    z_blocks = z_cells // SUB
    return lax.rem(lax.div(block, z_blocks), y_cells // SUB) * SUB, lax.rem(block, z_blocks) * SUB


def column_of(place, x_step, y_step):
    gx = lax.rem(place[1] + x_step + place[5], place[5])
    gy = lax.rem(place[2] + y_step + place[4], place[4])
    return gx * place[4] + gy


def sample_kernel(
    y_cells,
    z_cells,
    sample_block,
    place,
    brick,
    centre,
    lower,
    upper,
    own_rows,
    thin,
    x_edges,
    y_edges,
    windows,
    sems,
):
    rows_of_x = y_cells
    rows_of_field = SUB * y_cells
    window_rows = F * rows_of_field
    copies = [
        pltpu.make_async_copy(
            brick.at[:, pl.ds(w * 128, 128)], windows.at[pl.ds(w * window_rows, window_rows)], sems.at[w]
        )
        for w in range(z_cells // 128)
    ]
    for copy in copies:
        copy.start()
    for copy in copies:
        copy.wait()

    def corner(x_step, y_step):
        return corner_of(sample_block, place, x_step, y_step, y_cells, z_cells)

    def piece(row, count, stride, z, lane_start):
        values = windows[pl.ds(lax.div(z, 128) * window_rows + row, count, stride), :]
        return pltpu.roll(values, lax.rem(lane_start - lax.rem(z, 128) + 256, 128), 1)

    lane = lax.broadcasted_iota(jnp.int32, (SUB, 128), 1)
    y_start, z_start = corner(0, 0)
    z_below = jnp.maximum(z_start - 1, 0)
    z_above = jnp.minimum(z_start + SUB, z_cells - 1)
    for field in range(F):
        for half in range(2):
            inside = jnp.zeros((SUB, 128), jnp.float32)
            below = jnp.zeros((SUB, 128), jnp.float32)
            above = jnp.zeros((SUB, 128), jnp.float32)
            for step in range(8):
                row = field * rows_of_field + y_start + half * 8 + step
                first = step * SUB
                inside = jnp.where(lane // SUB == step, piece(row, SUB, rows_of_x, z_start, first), inside)
                below = jnp.where(lane == first, piece(row, SUB, rows_of_x, z_below, first), below)
                last = first + SUB - 1
                above = jnp.where(lane == last, piece(row, SUB, rows_of_x, z_above, last), above)
            below = jnp.where(z_start == 0, 0.0, below)
            above = jnp.where(z_start + SUB == z_cells, 0.0, above)
            at = (slice(field * SUB, (field + 1) * SUB), slice(half * 128, (half + 1) * 128))
            centre[at] = inside
            lower[at] = jnp.where(lane % SUB == 0, below, pltpu.roll(inside, 1, 1))
            upper[at] = jnp.where(lane % SUB == SUB - 1, above, pltpu.roll(inside, 127, 1))

    def y_row(y, z):
        total = jnp.zeros((SUB, 128), jnp.float32)
        for field in range(F):
            part = piece(field * rows_of_field + y, SUB, rows_of_x, z, field * SUB)
            total = jnp.where(lane // SUB == field, part, total)
        return total

    own_rows[0] = y_row(jnp.maximum(y_start - 1, 0), z_start)
    own_rows[1] = y_row(jnp.minimum(y_start + SUB, y_cells - 1), z_start)
    thin[...] = jnp.zeros(thin.shape, thin.dtype)
    thin[column_of(place, 0, -1), :, :128] = y_row(0, corner(0, -1)[1])
    thin[column_of(place, 0, 1), :, 128:] = y_row(y_cells - 1, corner(0, 1)[1])
    lane = lane[:8]
    for face, (x, sign) in enumerate(((0, -1), (SUB - 1, 1))):
        y_there, z_there = corner(sign, 0)
        for half in range(2):
            total = jnp.zeros((8, 128), jnp.float32)
            for step in range(8):
                row = x * rows_of_x + y_there + half * 8 + step
                part = piece(row, 8, rows_of_field, z_there, step * SUB)
                total = jnp.where(lane // SUB == step, part, total)
            at = (column_of(place, sign, 0), slice(face * 8, face * 8 + 8), slice(half * 128, half * 128 + 128))
            thin[at] = total
    up_first = lax.rem(place[2], 2) == 0
    for side in range(2):
        y = jnp.where(up_first == (side == 0), y_cells - 1, 0)
        for field in range(F):
            for w in range(z_cells // 128):
                start = w * window_rows + field * rows_of_field + y
                y_edges[side, field, :, w * 128 : (w + 1) * 128] = windows[
                    pl.ds(start, SUB, rows_of_x), :
                ]
    for side, x in enumerate((0, SUB - 1)):
        for field in range(F):
            for w in range(z_cells // 128):
                start = w * window_rows + field * rows_of_field + x * rows_of_x
                x_edges[side, field, :, w * 128 : (w + 1) * 128] = windows[pl.ds(start, rows_of_x), :]


def sample_cube(sample_block, place, brick, columns):
    fields, x_cells, y_cells, z_cells = brick.shape
    vmem = pl.BlockSpec(memory_space=pltpu.VMEM)
    smem = pl.BlockSpec(memory_space=pltpu.SMEM)
    hbm = pl.BlockSpec(memory_space=pltpu.HBM)
    rows = fields * x_cells * y_cells
    cube = jax.ShapeDtypeStruct((F * SUB, 256), jnp.float32)
    return pl.pallas_call(
        functools.partial(sample_kernel, y_cells, z_cells),
        out_shape=(
            cube,
            cube,
            cube,
            jax.ShapeDtypeStruct((2, SUB, 128), jnp.float32),
            jax.ShapeDtypeStruct((columns, SUB, 256), jnp.float32),
            jax.ShapeDtypeStruct((2, fields, y_cells, z_cells), jnp.float32),
            jax.ShapeDtypeStruct((2, fields, x_cells, z_cells), jnp.float32),
        ),
        in_specs=[smem, smem, hbm],
        out_specs=(vmem,) * 7,
        scratch_shapes=[
            pltpu.VMEM((z_cells // 128 * rows + 4 * x_cells * y_cells, 128), jnp.float32),
            pltpu.SemaphoreType.DMA((z_cells // 128,)),
        ],
        compiler_params=pltpu.CompilerParams(vmem_limit_bytes=16 * 1024 * 1024),
        name="sample_cube",
    )(sample_block, place, brick.reshape(rows, z_cells))


def change_kernel(
    y_cells,
    z_cells,
    sample_block,
    place,
    closure,
    order,
    centre,
    lower,
    upper,
    own_rows,
    thin,
    payload,
):
    y_start = corner_of(sample_block, place, 0, 0, y_cells, z_cells)[0]
    row = lax.broadcasted_iota(jnp.int32, (SUB, 256), 0)
    lane = lax.broadcasted_iota(jnp.int32, (SUB, 256), 1)
    south_row = jnp.where(y_start == 0, thin[column_of(place, 0, -1), :, 128:], own_rows[0])
    north_row = jnp.where(y_start + SUB == y_cells, thin[column_of(place, 0, 1), :, :128], own_rows[1])
    face_low = thin[column_of(place, -1, 0), 8:, :]
    face_high = thin[column_of(place, 1, 0), :8, :]
    cells = [centre[f * SUB : (f + 1) * SUB, :] for f in range(F)]
    viscosity = viscosity_of(cells, closure)
    changes = []
    for f in range(F):
        value = cells[f]
        west = jnp.where(row == 0, face_low[f : f + 1, :], pltpu.roll(value, 1, 0))
        east = jnp.where(row == SUB - 1, face_high[f : f + 1, :], pltpu.roll(value, SUB - 1, 0))
        edge = pltpu.roll(south_row, (128 - f * SUB) % 128, 1)
        south = jnp.where(lane < SUB, jnp.concatenate([edge, edge], 1), pltpu.roll(value, SUB, 1))
        edge = pltpu.roll(north_row, 112 - f * SUB, 1)
        north = jnp.where(
            lane >= 256 - SUB, jnp.concatenate([edge, edge], 1), pltpu.roll(value, 256 - SUB, 1)
        )
        down = lower[f * SUB : (f + 1) * SUB, :]
        up = upper[f * SUB : (f + 1) * SUB, :]
        laplacian = east + west + north + south + up + down - 6.0 * value
        advection = cells[0] * (east - west) + cells[1] * (north - south) + cells[2] * (up - down)
        change = viscosity * laplacian - 0.5 * advection
        if f == 2:
            change = change + buoyancy * cells[3]
        changes.append(change)
    both = jnp.concatenate(cells + changes, axis=0).astype(jnp.bfloat16)
    payload[...] = dot_rows(both, order[...]).astype(jnp.bfloat16)


def cube_change(sample_block, place, closure, cube, thin, y_cells, z_cells):
    vmem = pl.BlockSpec(memory_space=pltpu.VMEM)
    smem = pl.BlockSpec(memory_space=pltpu.SMEM)
    return pl.pallas_call(
        functools.partial(change_kernel, y_cells, z_cells),
        out_shape=jax.ShapeDtypeStruct((2 * F * SUB, 256), jnp.bfloat16),
        in_specs=[smem] * 3 + [vmem] * 6,
        out_specs=vmem,
        compiler_params=pltpu.CompilerParams(vmem_limit_bytes=16 * 1024 * 1024),
        name="cube_change",
    )(sample_block, place, closure, jnp.asarray(CELL_ORDER, jnp.bfloat16), *cube, thin)


def doubling_steps(x_devices, y_devices):
    along_y = [1 << bit for bit in reversed(range(y_devices.bit_length() - 1))]
    along_x = [y_devices << bit for bit in reversed(range(x_devices.bit_length() - 1))]
    return along_y + along_x


def on_device(
    fields, closure_in, closure_bias, closure_out, master, momentum, sample_block, sample_trainer
):
    group_count = lax.axis_size("grp")
    x_devices = lax.axis_size("gx")
    y_devices = lax.axis_size("gy")
    trainers = x_devices * y_devices
    my_group = lax.axis_index("grp")
    my_column = lax.axis_index("gx") * y_devices + lax.axis_index("gy")
    is_trainer = my_group == group_count - 1
    everyone = ("grp", "gx", "gy")
    sim_groups = group_count - 1
    first_trainer = sim_groups * trainers
    brick = fields[0]
    y_cells, z_cells = brick.shape[2:]
    closure = jnp.concatenate(
        [0.5 * closure_in.T, 0.5 * closure_bias[None], closure_out[None]], axis=0
    )
    place = jnp.stack(
        [
            my_group,
            lax.axis_index("gx"),
            lax.axis_index("gy"),
            jnp.int32(sim_groups),
            jnp.int32(y_devices),
            jnp.int32(x_devices),
        ]
    ).astype(jnp.int32)

    def pairs(x_step, even_step):
        found = []
        for g in range(sim_groups):
            for c in range(trainers):
                gx, gy = c // y_devices, c % y_devices
                gx = (gx + x_step) % x_devices
                gy = (gy + (even_step if gy % 2 == 0 else -even_step)) % y_devices
                found.append((g * trainers + c, (g * x_devices + gx) * y_devices + gy))
        return found

    def x_neighbours(edges):
        if x_devices == 2:
            return lax.ppermute(edges, everyone, pairs(1, 0))
        from_high = lax.ppermute(edges[0], everyone, pairs(-1, 0))
        return jnp.stack([from_high, lax.ppermute(edges[1], everyone, pairs(1, 0))])

    def y_neighbours(for_first, for_second):
        return (
            lax.ppermute(for_first, everyone, pairs(0, 1)),
            lax.ppermute(for_second, everyone, pairs(0, -1)),
        )

    def swap(distance):
        return [(first_trainer + c, first_trainer + (c ^ distance)) for c in range(trainers)]

    steps = doubling_steps(x_devices, y_devices)

    def to_trainers(payload):
        return jnp.stack(
            [
                lax.ppermute(
                    payload,
                    everyone,
                    [(g * trainers + c, first_trainer + c) for c in range(trainers)],
                )
                for g in range(sim_groups)
            ]
        )

    def among_trainers(held):
        for distance in steps[:-1]:
            held = jnp.concatenate([held, lax.ppermute(held, everyone, swap(distance))], axis=0)
        return [held, lax.ppermute(held, everyone, swap(steps[-1]))]

    *cube, thin, x_edges, y_edges = sample_cube(sample_block, place, brick, trainers)
    thin = lax.all_to_all(thin, ("gx", "gy"), split_axis=0, concat_axis=0, tiled=True)
    payload = cube_change(sample_block, place, closure, cube, thin, y_cells, z_cells)
    landed = to_trainers(payload)
    x_edges, y_edges, landed = lax.optimization_barrier((x_edges, y_edges, landed))
    halo = (x_neighbours(x_edges), *y_neighbours(y_edges[0], y_edges[1]))
    arrived = among_trainers(landed)

    first_count = CH * TAPS * F
    first = jnp.pad(master[:first_count].reshape(CH, TAPS * F), ((0, 0), (0, 256 - TAPS * F)))
    last = jnp.pad(master[first_count:].reshape(TAPS * F, CH).T, ((0, 0), (0, 256 - TAPS * F)))

    first, last = lax.optimization_barrier((first, last))

    def train_here():
        delta_first, delta_last, new_brick = train_cubes(
            sample_trainer, place, first, last, arrived, brick, steps
        )
        delta = jnp.concatenate(
            [delta_first[:, : TAPS * F].reshape(-1), delta_last[:, : TAPS * F].T.reshape(-1)]
        )
        return delta, new_brick

    def evolve_here():
        new_brick = evolve(closure, place, brick, *halo)
        return jnp.zeros((NPARAM,), jnp.float32), new_brick

    delta, new_brick = lax.cond(is_trainer, train_here, evolve_here)

    total = delta
    for distance in steps:
        total = total + lax.ppermute(total, everyone, swap(distance))
    final = jnp.where(is_trainer, total, 0.0)
    for g in range(sim_groups):
        pairs = [(first_trainer + c, g * trainers + c) for c in range(trainers)]
        final = final + lax.ppermute(total, everyone, pairs)

    share_size = NPARAM // (group_count * trainers)
    share_start = (my_group * trainers + my_column) * share_size
    momentum_share = lax.dynamic_slice_in_dim(momentum, share_start, share_size)
    master_share = lax.dynamic_slice_in_dim(master, share_start, share_size)
    inverse = 1.0 / jnp.sqrt(jnp.sum(final * final) / NPARAM + norm_epsilon)
    delta_share = lax.dynamic_slice_in_dim(final, share_start, share_size)
    new_momentum = momentum_decay * momentum_share + delta_share * inverse
    new_master = master_share - outer_rate * new_momentum
    return (new_brick[None], new_master, new_momentum)


def solution(mesh):
    in_specs = (P("grp", None, "gx", "gy", None), P(), P(), P(), P(), P(), P(), P())
    out_specs = (P("grp", None, "gx", "gy", None), P(("grp", "gx", "gy")), P(("grp", "gx", "gy")))
    return jax.shard_map(
        on_device, mesh=mesh, in_specs=in_specs, out_specs=out_specs, check_vma=False
    )
```

```python
import functools

import jax
import jax.numpy as jnp
import numpy as np
from jax import lax
from jax.experimental import pallas as pl
from jax.experimental.pallas import tpu as pltpu
from jax.sharding import PartitionSpec as P

F = 5
CH = 64
HID = 64
SUB = 16
TCAP = 6
INNER = 3
CELLS = 4096
NPARAM = 17280
TAPS = 27
PAIRS = TCAP // 2
COLS = (SUB + 2) * 128
PATCH = 16 * F
STACK = 3 * PATCH

time_step = 0.1
base_viscosity = 0.02
viscosity_gain = 0.2
buoyancy = 0.5
inner_rate = 0.02
outer_rate = 0.01
momentum_decay = 0.9
norm_epsilon = 1e-06


def patch_position(row):
    group, py, pz = row // 4, row // 2 % 2, row % 2
    ypos = py + 1 if group in (0, 1) else (3 if py == 0 else 0)
    zpos = pz + 1 if group in (0, 2) else (3 if pz == 0 else 0)
    return ypos - 1, zpos - 1


def selections():
    first = np.zeros((4, 256, STACK), np.float32)
    last = np.zeros((4, 256, STACK), np.float32)
    for cell in range(4):
        py, pz = cell // 2, cell % 2
        for kx in range(3):
            for channel in range(F):
                for row in range(16):
                    ypos, zpos = patch_position(row)
                    column = kx * PATCH + channel * 16 + row
                    dy, dz = ypos - py, zpos - pz
                    if abs(dy) <= 1 and abs(dz) <= 1:
                        tap = 9 * kx + 3 * (dy + 1) + dz + 1
                        first[cell, tap * F + channel, column] = 1.0
                        last[cell, channel * TAPS + 26 - tap, column] = 1.0
    return first, last


SELECT_FIRST, SELECT_LAST = selections()


def column_of(place, x_step, y_step):
    gx = lax.rem(place[1] + x_step + place[5], place[5])
    gy = lax.rem(place[2] + y_step + place[4], place[4])
    return gx * place[4] + gy


def xor_of(left, right, size):
    total = jnp.int32(0)
    for bit in range(size.bit_length() - 1):
        one, other = lax.rem(lax.div(left, 1 << bit), 2), lax.rem(lax.div(right, 1 << bit), 2)
        total = total + jnp.where(one == other, 0, 1 << bit)
    return total


def owner_apart(owner, place, y_devices, x_devices):
    trainers = x_devices * y_devices
    column = lax.rem(owner, trainers)
    y_apart = xor_of(lax.rem(column, y_devices), place[2], y_devices)
    x_apart = xor_of(lax.div(column, y_devices), place[1], x_devices)
    return lax.div(owner, trainers), y_apart, x_apart


def pick_kernel(y_devices, x_devices, apart, trainer_of, place, *refs):
    near, chosen = refs[:y_devices], refs[y_devices]
    wanted = xor_of(place[1], apart, x_devices) * y_devices + place[2]

    def visit(owner, count):
        group, y_apart, x_apart = owner_apart(owner, place, y_devices, x_devices)
        mine = (trainer_of[owner] == wanted) & (x_apart == 0)
        for source in range(y_devices):

            @pl.when(mine & (y_apart == source))
            def _():
                chosen[count] = near[source][group]

        return count + jnp.where(mine, 1, 0)

    lax.fori_loop(0, trainer_of.shape[0], visit, jnp.int32(0))


def pick_cubes(trainer_of, place, near, y_devices, x_devices, apart):
    vmem = pl.BlockSpec(memory_space=pltpu.VMEM)
    smem = pl.BlockSpec(memory_space=pltpu.SMEM)
    return pl.pallas_call(
        functools.partial(pick_kernel, y_devices, x_devices, apart),
        out_shape=jax.ShapeDtypeStruct((TCAP, *near[0].shape[1:]), near[0].dtype),
        in_specs=[smem, smem] + [vmem] * len(near),
        out_specs=vmem,
        compiler_params=pltpu.CompilerParams(vmem_limit_bytes=16 * 1024 * 1024),
        name="pick_cubes",
    )(trainer_of, place, *near)


def dot_rows(left, right):
    return jnp.dot(left, right, preferred_element_type=jnp.float32)


def dot_lanes(left, right):
    return lax.dot_general(left, right, (((1,), (1,)), ((), ())), preferred_element_type=jnp.float32)


def patch_masks():
    row = lax.broadcasted_iota(jnp.int32, (8, 128), 0)
    lane = lax.broadcasted_iota(jnp.int32, (8, 128), 1)
    return {
        "pz0": row % 2 == 0,
        "py0": row // 2 % 2 == 0,
        "centre": row < 4,
        "z_first": lane % 8 == 0,
        "z_last": lane % 8 == 7,
        "y_first": lane // 8 % 8 == 0,
        "y_last": lane // 8 % 8 == 7,
    }


def edge_shift(values, step, parity_zero, first, last, forward):
    before = jnp.where(first, 0.0, pltpu.roll(values, step, 1))
    after = jnp.where(last, 0.0, pltpu.roll(values, 128 - step, 1))
    if forward:
        return jnp.where(parity_zero, after, before)
    return jnp.where(parity_zero, before, after)


def patch_stack(rows, masks):
    both = rows + pltpu.roll(rows, 4, 0)
    z_edge = edge_shift(both, 1, masks["pz0"], masks["z_first"], masks["z_last"], True)
    upper = jnp.where(masks["centre"], both, z_edge)
    lower = edge_shift(upper, 8, masks["py0"], masks["y_first"], masks["y_last"], True)
    return upper, lower


def patch_fold(upper, lower, masks):
    def fold_z(values):
        moved = edge_shift(values, 1, masks["pz0"], masks["z_first"], masks["z_last"], False)
        return values + pltpu.roll(moved, 4, 0)

    shifted = edge_shift(fold_z(lower), 8, masks["py0"], masks["y_first"], masks["y_last"], False)
    return fold_z(upper) + shifted


def store_planes(ref, pair, x, channels):
    stacked = jnp.concatenate([part for both in channels for part in both], axis=0).astype(jnp.bfloat16)
    for kx in range(3):
        start = pl.multiple_of((x + 2 - kx) * 128, 128)
        ref[pair, kx * PATCH : (kx + 1) * PATCH, pl.ds(start, 128)] = stacked


def train_kernel(y_devices, x_devices, *refs):
    sources = y_devices + x_devices - 1
    (trainer_of, place, first_ref, last_ref, far_first, far_last) = refs[:6]
    arrived = refs[6 : 6 + sources]
    fields_ref = refs[6 + sources]
    delta_first, delta_last, new_fields_ref = refs[7 + sources : 10 + sources]
    (
        slots,
        picked,
        cubes,
        table,
        targets,
        inputs,
        errors,
        hiddens,
        pre_grads,
        slopes,
        partial_out,
        big_first,
        big_last,
        big_last_t,
        raw,
        grad_first,
        grad_last,
        now_first,
        now_last,
        brick,
        select_first,
        select_last,
        slot_sems,
        field_sem,
        select_sems,
    ) = refs[10 + sources :]

    field_in = pltpu.make_async_copy(fields_ref, brick, field_sem)
    field_out = pltpu.make_async_copy(brick, new_fields_ref, field_sem)
    select_copies = [
        pltpu.make_async_copy(far_first, select_first, select_sems.at[0]),
        pltpu.make_async_copy(far_last, select_last, select_sems.at[1]),
    ]

    groups = place[3]
    for other in range(x_devices):
        picked[other] = 0

    def visit(owner, count):
        mine = trainer_of[owner] == column_of(place, 0, 0)

        @pl.when(mine)
        def _():
            group, y_apart, x_apart = owner_apart(owner, place, y_devices, x_devices)
            near = x_apart == 0
            slots[0, count] = jnp.where(near, y_apart, y_devices - 1 + x_apart)
            slots[1, count] = jnp.where(near, group, picked[x_apart])
            picked[x_apart] = picked[x_apart] + 1

        return count + jnp.where(mine, 1, 0)

    count = lax.fori_loop(0, trainer_of.shape[0], visit, jnp.int32(0))

    def fetch(slot, wait):
        for source in range(sources):

            @pl.when((slot < count) & (slots[0, slot] == source))
            def _():
                copy = pltpu.make_async_copy(
                    arrived[source].at[slots[1, slot]], cubes.at[slot], slot_sems.at[slot]
                )
                copy.wait() if wait else copy.start()

    for slot in range(TCAP):
        fetch(slot, False)

    for copy in select_copies:
        copy.start()
    field_in.start()
    for slot in range(TCAP):

        @pl.when(slot >= count)
        def _():
            cubes[slot] = jnp.zeros((2 * SUB * F, 256), jnp.bfloat16)

    masks = patch_masks()
    for ref in (errors, inputs):
        ref[:, :PATCH, 128:256] = jnp.zeros((PAIRS, PATCH, 128), jnp.bfloat16)
        ref[:, 2 * PATCH :, COLS - 256 : COLS - 128] = jnp.zeros((PAIRS, PATCH, 128), jnp.bfloat16)
    partial_out[:, :, :128] = jnp.zeros((PAIRS, STACK, 128), jnp.float32)
    partial_out[:, :, COLS - 128 :] = jnp.zeros((PAIRS, STACK, 128), jnp.float32)
    table[...] = jnp.zeros(table.shape, table.dtype)
    targets[...] = jnp.zeros(targets.shape, targets.dtype)
    lane = lax.broadcasted_iota(jnp.int32, (8, 128), 1)
    full_weight = 2.0 * (1.0 / (jnp.full((8, 128), count, jnp.int32).astype(jnp.float32) * CELLS))
    weights = [
        jnp.where(lane // 64 + 2 * pair < count, full_weight, 0.0) for pair in range(PAIRS)
    ]
    start_first = first_ref[...].astype(jnp.bfloat16).astype(jnp.float32)
    start_last = last_ref[...].astype(jnp.bfloat16).astype(jnp.float32)
    now_first[...] = start_first
    now_last[...] = start_last

    for slot in range(TCAP):
        fetch(slot, True)

    low_lanes = lax.broadcasted_iota(jnp.int32, (SUB * F, 128), 1) < 64

    def spread_rows(pair, kind, put):
        rows = slice(kind * SUB * F, (kind + 1) * SUB * F)
        even = cubes[2 * pair, rows, :].astype(jnp.float32)
        odd = cubes[2 * pair + 1, rows, :].astype(jnp.float32)
        for half in range(2):
            left = even[:, half * 128 : (half + 1) * 128]
            right = odd[:, half * 128 : (half + 1) * 128]
            put(2 * half, jnp.where(low_lanes, left, pltpu.roll(right, 64, 1)))
            put(2 * half + 1, jnp.where(low_lanes, pltpu.roll(left, 64, 1), right))

    for pair in range(PAIRS):

        def put_input(cell, values):
            table[pl.ds(cell, SUB * F, 8), :] = values

        def put_target(cell, values):
            targets[pl.ds(pair * SUB * F * 8 + cell, SUB * F, 8), :] = values

        spread_rows(pair, 0, put_input)
        spread_rows(pair, 1, put_target)

        def stack_plane(x, carry):
            channels = [
                patch_stack(table[pl.ds(pl.multiple_of((c * SUB + x) * 8, 8), 8), :], masks)
                for c in range(F)
            ]
            store_planes(inputs, pair, x, channels)
            return carry

        lax.fori_loop(0, SUB, stack_plane, 0, unroll=8)

    for copy in select_copies:
        copy.wait()
    field_in.wait()
    field_out.start()

    def train_step(step, step_carry):
        first_now = now_first[...].astype(jnp.bfloat16)
        last_now = now_last[...].astype(jnp.bfloat16)
        for cell in range(4):
            rows = slice(cell * CH, (cell + 1) * CH)
            big_first[rows, :] = dot_rows(first_now, select_first[cell]).astype(jnp.bfloat16)
            big_last[rows, :] = dot_rows(last_now, select_last[cell]).astype(jnp.bfloat16)
        big_last_t[...] = big_last[...].T
        def tile_of(index):
            return index // 8, pl.ds(pl.multiple_of((index % 8) * 256 + 128, 128), 256)

        def first_layer(index, carry):
            pair, columns = tile_of(index)
            raw[pair, :, columns] = dot_rows(big_first[...], inputs[pair, :, columns])
            return carry

        def activate(index, carry):
            pair, columns = tile_of(index)
            for part in range(4):
                rows = slice(part * 64, (part + 1) * 64)
                half = 0.5 * raw[pair, rows, columns]
                curve = jnp.tanh(half)
                value = half + half * curve
                hiddens[pair, rows, columns] = value.astype(jnp.bfloat16)
                slopes[pair, rows, columns] = (0.5 + 0.5 * curve) + value * (0.5 - 0.5 * curve)
            return carry

        def last_layer(index, carry):
            pair, columns = tile_of(index)
            partial_out[pair, :, columns] = dot_rows(big_last_t[...], hiddens[pair, :, columns])
            return carry

        lax.fori_loop(0, 8 * PAIRS, first_layer, 0, unroll=4)
        lax.fori_loop(0, 8 * PAIRS, activate, 0, unroll=2)
        lax.fori_loop(0, 8 * PAIRS, last_layer, 0, unroll=4)

        def error_plane(index, carry):
            pair = index // SUB
            x = index % SUB
            column = pl.multiple_of((x + 1) * 128, 128)
            total = (
                partial_out[pair, 0:PATCH, pl.ds(pl.multiple_of(column + 128, 128), 128)]
                + partial_out[pair, PATCH : 2 * PATCH, pl.ds(column, 128)]
                + partial_out[pair, 2 * PATCH :, pl.ds(pl.multiple_of(column - 128, 128), 128)]
            )
            weight = jnp.where(pair == 0, weights[0], jnp.where(pair == 1, weights[1], weights[2]))
            channels = []
            for c in range(F):
                predicted = patch_fold(
                    total[16 * c : 16 * c + 8], total[16 * c + 8 : 16 * c + 16], masks
                )
                row = pl.multiple_of(((pair * F + c) * SUB + x) * 8, 8)
                error = weight * (predicted - targets[pl.ds(row, 8), :])
                error = jnp.where(masks["centre"], error, 0.0)
                error = error.astype(jnp.bfloat16).astype(jnp.float32)
                channels.append(patch_stack(error, masks))
            store_planes(errors, pair, x, channels)
            return carry

        lax.fori_loop(0, SUB * PAIRS, error_plane, 0, unroll=8)

        def hidden_layer(index, carry):
            pair, columns = tile_of(index)
            raw[pair, :, columns] = dot_rows(big_last[...], errors[pair, :, columns])
            return carry

        def scale(index, carry):
            pair, columns = tile_of(index)
            for part in range(4):
                rows = slice(part * 64, (part + 1) * 64)
                product = raw[pair, rows, columns] * slopes[pair, rows, columns]
                pre_grads[pair, rows, columns] = product.astype(jnp.bfloat16)
            return carry

        lax.fori_loop(0, 8 * PAIRS, hidden_layer, 0, unroll=4)
        lax.fori_loop(0, 8 * PAIRS, scale, 0, unroll=2)
        body = slice(128, COLS - 128)
        grad_first[...] = jnp.zeros(grad_first.shape, jnp.float32)
        grad_last[...] = jnp.zeros(grad_last.shape, jnp.float32)

        def gradients(pair, carry):
            grad_first[...] += dot_lanes(pre_grads[pair, :, body], inputs[pair, :, body])
            grad_last[...] += dot_lanes(hiddens[pair, :, body], errors[pair, :, body])
            return carry

        lax.fori_loop(0, PAIRS, gradients, 0)

        def folded(grad, select_ref):
            total = jnp.zeros((3 * CH, 256), jnp.float32)
            for cell in range(4):
                rest = grad[cell * CH : (cell + 1) * CH, :]
                parts = []
                for _ in range(3):
                    parts.append(rest.astype(jnp.bfloat16))
                    rest = rest - parts[-1].astype(jnp.float32)
                total = total + dot_lanes(jnp.concatenate(parts, axis=0), select_ref[cell])
            return total[:CH] + total[CH : 2 * CH] + total[2 * CH :]

        now_first[...] = now_first[...] - inner_rate * folded(grad_first, select_first)
        now_last[...] = now_last[...] - inner_rate * folded(grad_last, select_last)
        return step_carry

    lax.fori_loop(0, INNER, train_step, 0)
    delta_first[...] = start_first - now_first[...]
    delta_last[...] = start_last - now_last[...]
    field_out.wait()


def train_cubes(trainer_of, place, first, last, arrived, fields, y_devices, x_devices):
    vmem = pl.BlockSpec(memory_space=pltpu.VMEM)
    smem = pl.BlockSpec(memory_space=pltpu.SMEM)
    anywhere = pl.BlockSpec(memory_space=pl.ANY)
    hbm = pl.BlockSpec(memory_space=pltpu.HBM)
    return pl.pallas_call(
        functools.partial(train_kernel, y_devices, x_devices),
        out_shape=(
            jax.ShapeDtypeStruct((CH, 256), jnp.float32),
            jax.ShapeDtypeStruct((CH, 256), jnp.float32),
            jax.ShapeDtypeStruct(fields.shape, fields.dtype),
        ),
        in_specs=[smem] * 2 + [vmem] * 2 + [hbm] * 2 + [anywhere] * len(arrived) + [hbm],
        out_specs=(vmem, vmem, hbm),
        scratch_shapes=[
            pltpu.SMEM((2, TCAP), jnp.int32),
            pltpu.SMEM((x_devices,), jnp.int32),
            pltpu.VMEM((TCAP, 2 * SUB * F, 256), jnp.bfloat16),
            pltpu.VMEM((SUB * F * 8, 128), jnp.float32),
            pltpu.VMEM((PAIRS * SUB * F * 8, 128), jnp.float32),
            pltpu.VMEM((PAIRS, STACK, COLS), jnp.bfloat16),
            pltpu.VMEM((PAIRS, STACK, COLS), jnp.bfloat16),
            pltpu.VMEM((PAIRS, 4 * CH, COLS), jnp.bfloat16),
            pltpu.VMEM((PAIRS, 4 * CH, COLS), jnp.bfloat16),
            pltpu.VMEM((PAIRS, 4 * CH, COLS), jnp.float32),
            pltpu.VMEM((PAIRS, STACK, COLS), jnp.float32),
            pltpu.VMEM((4 * CH, STACK), jnp.bfloat16),
            pltpu.VMEM((4 * CH, STACK), jnp.bfloat16),
            pltpu.VMEM((STACK, 4 * CH), jnp.bfloat16),
            pltpu.VMEM((PAIRS, 4 * CH, COLS), jnp.float32),
            pltpu.VMEM((4 * CH, STACK), jnp.float32),
            pltpu.VMEM((4 * CH, STACK), jnp.float32),
            pltpu.VMEM((CH, 256), jnp.float32),
            pltpu.VMEM((CH, 256), jnp.float32),
            pltpu.VMEM(fields.shape, fields.dtype),
            pltpu.VMEM((4, 256, STACK), jnp.bfloat16),
            pltpu.VMEM((4, 256, STACK), jnp.bfloat16),
            pltpu.SemaphoreType.DMA((TCAP,)),
            pltpu.SemaphoreType.DMA,
            pltpu.SemaphoreType.DMA((2,)),
        ],
        compiler_params=pltpu.CompilerParams(vmem_limit_bytes=48 * 1024 * 1024),
        name="train_cubes",
    )(
        trainer_of,
        place,
        first,
        last,
        jnp.asarray(SELECT_FIRST, jnp.bfloat16),
        jnp.asarray(SELECT_LAST, jnp.bfloat16),
        *arrived,
        fields,
    )


def viscosity_of(cells, closure):
    def unit(h, total):
        half = closure[F, h] + closure[0, h] * cells[0]
        for f in range(1, F):
            half = half + closure[f, h] * cells[f]
        return total + closure[F + 1, h] * (half + half * jnp.tanh(half))

    total = lax.fori_loop(0, HID, unit, jnp.zeros(cells[0].shape, jnp.float32), unroll=4)
    soft = jnp.maximum(total, 0.0) + jnp.log1p(jnp.exp(-jnp.abs(total)))
    return base_viscosity + viscosity_gain * soft


def evolve_kernel(closure, place, fields, x_halo, y_first, y_second, new_fields):
    up_first = lax.rem(place[2], 2) == 0
    x_cells, y_cells, z_cells = fields.shape[1:]
    row = lax.broadcasted_iota(jnp.int32, (y_cells, z_cells), 0)
    lane = lax.broadcasted_iota(jnp.int32, (y_cells, z_cells), 1)
    part = y_cells // 2

    def plane(x, carry):
        eddies = []
        for half in range(2):
            rows = pl.ds(half * part, part)
            cells = [fields[f, x, rows, :] for f in range(F)]
            eddies.append(viscosity_of(cells, closure))
        viscosity = jnp.concatenate(eddies, axis=0)
        centre = [fields[f, x] for f in range(F)]
        below = jnp.maximum(x - 1, 0)
        above = jnp.minimum(x + 1, x_cells - 1)
        for f in range(F):
            value = centre[f]
            west = jnp.where(x == 0, x_halo[1, f], fields[f, below])
            east = jnp.where(x == x_cells - 1, x_halo[0, f], fields[f, above])
            first, second = y_first[f, pl.ds(x, 1), :], y_second[f, pl.ds(x, 1), :]
            south = jnp.where(
                row == 0, jnp.where(up_first, second, first), pltpu.roll(value, 1, 0)
            )
            north = jnp.where(
                row == y_cells - 1,
                jnp.where(up_first, first, second),
                pltpu.roll(value, y_cells - 1, 0),
            )
            lower = jnp.where(lane == 0, 0.0, pltpu.roll(value, 1, 1))
            upper = jnp.where(lane == z_cells - 1, 0.0, pltpu.roll(value, z_cells - 1, 1))
            laplacian = east + west + north + south + upper + lower - 6.0 * value
            advection = (
                centre[0] * (east - west) + centre[1] * (north - south) + centre[2] * (upper - lower)
            )
            tendency = viscosity * laplacian - 0.5 * advection
            if f == 2:
                tendency = tendency + buoyancy * centre[3]
            new_fields[f, x] = value + time_step * tendency
        return carry

    lax.fori_loop(0, x_cells, plane, 0)


def evolve(closure, place, fields, x_halo, y_first, y_second):
    vmem = pl.BlockSpec(memory_space=pltpu.VMEM)
    return pl.pallas_call(
        evolve_kernel,
        out_shape=jax.ShapeDtypeStruct(fields.shape, fields.dtype),
        in_specs=[pl.BlockSpec(memory_space=pltpu.SMEM)] * 2 + [vmem] * 4,
        out_specs=vmem,
        compiler_params=pltpu.CompilerParams(vmem_limit_bytes=16 * 1024 * 1024),
        name="evolve_brick",
    )(closure, place, fields, x_halo, y_first, y_second)


def cell_order():
    order = np.zeros((256, 256), np.float32)
    for y in range(SUB):
        for z in range(SUB):
            order[y * SUB + z, (y % 2 * 2 + z % 2) * 64 + y // 2 * 8 + z // 2] = 1.0
    return order


CELL_ORDER = cell_order()


def corner_of(sample_block, place, x_step, y_step, y_cells, z_cells):
    x_devices, y_devices = place[5], place[4]
    gx = lax.rem(place[1] + x_step + x_devices, x_devices)
    gy = lax.rem(place[2] + y_step + y_devices, y_devices)
    group = jnp.minimum(place[0], place[3] - 1)
    block = sample_block[(group * x_devices + gx) * y_devices + gy]
    z_blocks = z_cells // SUB
    return lax.rem(lax.div(block, z_blocks), y_cells // SUB) * SUB, lax.rem(block, z_blocks) * SUB


def sample_kernel(
    y_cells,
    z_cells,
    sample_block,
    place,
    brick,
    centre,
    lower,
    upper,
    own_rows,
    thin,
    x_edges,
    y_edges,
    windows,
    sems,
):
    rows_of_x = y_cells
    rows_of_field = SUB * y_cells
    window_rows = F * rows_of_field
    copies = [
        pltpu.make_async_copy(
            brick.at[:, pl.ds(w * 128, 128)], windows.at[pl.ds(w * window_rows, window_rows)], sems.at[w]
        )
        for w in range(z_cells // 128)
    ]
    for copy in copies:
        copy.start()
    for copy in copies:
        copy.wait()

    def corner(x_step, y_step):
        return corner_of(sample_block, place, x_step, y_step, y_cells, z_cells)

    def piece(row, count, stride, z, lane_start):
        values = windows[pl.ds(lax.div(z, 128) * window_rows + row, count, stride), :]
        return pltpu.roll(values, lax.rem(lane_start - lax.rem(z, 128) + 256, 128), 1)

    lane = lax.broadcasted_iota(jnp.int32, (SUB, 128), 1)
    y_start, z_start = corner(0, 0)
    z_below = jnp.maximum(z_start - 1, 0)
    z_above = jnp.minimum(z_start + SUB, z_cells - 1)
    for field in range(F):
        for half in range(2):
            inside = jnp.zeros((SUB, 128), jnp.float32)
            below = jnp.zeros((SUB, 128), jnp.float32)
            above = jnp.zeros((SUB, 128), jnp.float32)
            for step in range(8):
                row = field * rows_of_field + y_start + half * 8 + step
                first = step * SUB
                inside = jnp.where(lane // SUB == step, piece(row, SUB, rows_of_x, z_start, first), inside)
                below = jnp.where(lane == first, piece(row, SUB, rows_of_x, z_below, first), below)
                last = first + SUB - 1
                above = jnp.where(lane == last, piece(row, SUB, rows_of_x, z_above, last), above)
            below = jnp.where(z_start == 0, 0.0, below)
            above = jnp.where(z_start + SUB == z_cells, 0.0, above)
            at = (slice(field * SUB, (field + 1) * SUB), slice(half * 128, (half + 1) * 128))
            centre[at] = inside
            lower[at] = jnp.where(lane % SUB == 0, below, pltpu.roll(inside, 1, 1))
            upper[at] = jnp.where(lane % SUB == SUB - 1, above, pltpu.roll(inside, 127, 1))

    def y_row(y, z):
        total = jnp.zeros((SUB, 128), jnp.float32)
        for field in range(F):
            part = piece(field * rows_of_field + y, SUB, rows_of_x, z, field * SUB)
            total = jnp.where(lane // SUB == field, part, total)
        return total

    own_rows[0] = y_row(jnp.maximum(y_start - 1, 0), z_start)
    own_rows[1] = y_row(jnp.minimum(y_start + SUB, y_cells - 1), z_start)
    thin[...] = jnp.zeros(thin.shape, thin.dtype)
    thin[column_of(place, 0, -1), :, :128] = y_row(0, corner(0, -1)[1])
    thin[column_of(place, 0, 1), :, 128:] = y_row(y_cells - 1, corner(0, 1)[1])
    lane = lane[:8]
    for face, (x, sign) in enumerate(((0, -1), (SUB - 1, 1))):
        y_there, z_there = corner(sign, 0)
        for half in range(2):
            total = jnp.zeros((8, 128), jnp.float32)
            for step in range(8):
                row = x * rows_of_x + y_there + half * 8 + step
                part = piece(row, 8, rows_of_field, z_there, step * SUB)
                total = jnp.where(lane // SUB == step, part, total)
            at = (column_of(place, sign, 0), slice(face * 8, face * 8 + 8), slice(half * 128, half * 128 + 128))
            thin[at] = total
    up_first = lax.rem(place[2], 2) == 0
    for side in range(2):
        y = jnp.where(up_first == (side == 0), y_cells - 1, 0)
        for field in range(F):
            for w in range(z_cells // 128):
                start = w * window_rows + field * rows_of_field + y
                y_edges[side, field, :, w * 128 : (w + 1) * 128] = windows[
                    pl.ds(start, SUB, rows_of_x), :
                ]
    for side, x in enumerate((0, SUB - 1)):
        for field in range(F):
            for w in range(z_cells // 128):
                start = w * window_rows + field * rows_of_field + x * rows_of_x
                x_edges[side, field, :, w * 128 : (w + 1) * 128] = windows[pl.ds(start, rows_of_x), :]


def sample_cube(sample_block, place, brick, columns):
    fields, x_cells, y_cells, z_cells = brick.shape
    vmem = pl.BlockSpec(memory_space=pltpu.VMEM)
    smem = pl.BlockSpec(memory_space=pltpu.SMEM)
    hbm = pl.BlockSpec(memory_space=pltpu.HBM)
    rows = fields * x_cells * y_cells
    cube = jax.ShapeDtypeStruct((F * SUB, 256), jnp.float32)
    return pl.pallas_call(
        functools.partial(sample_kernel, y_cells, z_cells),
        out_shape=(
            cube,
            cube,
            cube,
            jax.ShapeDtypeStruct((2, SUB, 128), jnp.float32),
            jax.ShapeDtypeStruct((columns, SUB, 256), jnp.float32),
            jax.ShapeDtypeStruct((2, fields, y_cells, z_cells), jnp.float32),
            jax.ShapeDtypeStruct((2, fields, x_cells, z_cells), jnp.float32),
        ),
        in_specs=[smem, smem, hbm],
        out_specs=(vmem,) * 7,
        scratch_shapes=[
            pltpu.VMEM((z_cells // 128 * rows + 4 * x_cells * y_cells, 128), jnp.float32),
            pltpu.SemaphoreType.DMA((z_cells // 128,)),
        ],
        compiler_params=pltpu.CompilerParams(vmem_limit_bytes=16 * 1024 * 1024),
        name="sample_cube",
    )(sample_block, place, brick.reshape(rows, z_cells))


def change_kernel(
    y_cells,
    z_cells,
    sample_block,
    place,
    closure,
    order,
    centre,
    lower,
    upper,
    own_rows,
    thin,
    payload,
):
    y_start = corner_of(sample_block, place, 0, 0, y_cells, z_cells)[0]
    row = lax.broadcasted_iota(jnp.int32, (SUB, 256), 0)
    lane = lax.broadcasted_iota(jnp.int32, (SUB, 256), 1)
    south_row = jnp.where(y_start == 0, thin[column_of(place, 0, -1), :, 128:], own_rows[0])
    north_row = jnp.where(y_start + SUB == y_cells, thin[column_of(place, 0, 1), :, :128], own_rows[1])
    face_low = thin[column_of(place, -1, 0), 8:, :]
    face_high = thin[column_of(place, 1, 0), :8, :]
    cells = [centre[f * SUB : (f + 1) * SUB, :] for f in range(F)]
    viscosity = viscosity_of(cells, closure)
    changes = []
    for f in range(F):
        value = cells[f]
        west = jnp.where(row == 0, face_low[f : f + 1, :], pltpu.roll(value, 1, 0))
        east = jnp.where(row == SUB - 1, face_high[f : f + 1, :], pltpu.roll(value, SUB - 1, 0))
        edge = pltpu.roll(south_row, (128 - f * SUB) % 128, 1)
        south = jnp.where(lane < SUB, jnp.concatenate([edge, edge], 1), pltpu.roll(value, SUB, 1))
        edge = pltpu.roll(north_row, 112 - f * SUB, 1)
        north = jnp.where(
            lane >= 256 - SUB, jnp.concatenate([edge, edge], 1), pltpu.roll(value, 256 - SUB, 1)
        )
        down = lower[f * SUB : (f + 1) * SUB, :]
        up = upper[f * SUB : (f + 1) * SUB, :]
        laplacian = east + west + north + south + up + down - 6.0 * value
        advection = cells[0] * (east - west) + cells[1] * (north - south) + cells[2] * (up - down)
        change = viscosity * laplacian - 0.5 * advection
        if f == 2:
            change = change + buoyancy * cells[3]
        changes.append(change)
    both = jnp.concatenate(cells + changes, axis=0).astype(jnp.bfloat16)
    payload[...] = dot_rows(both, order[...]).astype(jnp.bfloat16)


def cube_change(sample_block, place, closure, cube, thin, y_cells, z_cells):
    vmem = pl.BlockSpec(memory_space=pltpu.VMEM)
    smem = pl.BlockSpec(memory_space=pltpu.SMEM)
    return pl.pallas_call(
        functools.partial(change_kernel, y_cells, z_cells),
        out_shape=jax.ShapeDtypeStruct((2 * F * SUB, 256), jnp.bfloat16),
        in_specs=[smem] * 3 + [vmem] * 6,
        out_specs=vmem,
        compiler_params=pltpu.CompilerParams(vmem_limit_bytes=16 * 1024 * 1024),
        name="cube_change",
    )(sample_block, place, closure, jnp.asarray(CELL_ORDER, jnp.bfloat16), *cube, thin)


def on_device(
    fields, closure_in, closure_bias, closure_out, master, momentum, sample_block, sample_trainer
):
    group_count = lax.axis_size("grp")
    x_devices = lax.axis_size("gx")
    y_devices = lax.axis_size("gy")
    trainers = x_devices * y_devices
    my_group = lax.axis_index("grp")
    my_column = lax.axis_index("gx") * y_devices + lax.axis_index("gy")
    is_trainer = my_group == group_count - 1
    everyone = ("grp", "gx", "gy")
    sim_groups = group_count - 1
    first_trainer = sim_groups * trainers
    brick = fields[0]
    y_cells, z_cells = brick.shape[2:]
    closure = jnp.concatenate(
        [0.5 * closure_in.T, 0.5 * closure_bias[None], closure_out[None]], axis=0
    )
    place = jnp.stack(
        [
            my_group,
            lax.axis_index("gx"),
            lax.axis_index("gy"),
            jnp.int32(sim_groups),
            jnp.int32(y_devices),
            jnp.int32(x_devices),
        ]
    ).astype(jnp.int32)

    def pairs(x_step, even_step):
        found = []
        for g in range(sim_groups):
            for c in range(trainers):
                gx, gy = c // y_devices, c % y_devices
                gx = (gx + x_step) % x_devices
                gy = (gy + (even_step if gy % 2 == 0 else -even_step)) % y_devices
                found.append((g * trainers + c, (g * x_devices + gx) * y_devices + gy))
        return found

    def x_neighbours(edges):
        if x_devices == 2:
            return lax.ppermute(edges, everyone, pairs(1, 0))
        from_high = lax.ppermute(edges[0], everyone, pairs(-1, 0))
        return jnp.stack([from_high, lax.ppermute(edges[1], everyone, pairs(1, 0))])

    def y_neighbours(for_first, for_second):
        return (
            lax.ppermute(for_first, everyone, pairs(0, 1)),
            lax.ppermute(for_second, everyone, pairs(0, -1)),
        )

    def swap(distance):
        return [(first_trainer + c, first_trainer + (c ^ distance)) for c in range(trainers)]

    def to_trainers(payload):
        return jnp.stack(
            [
                lax.ppermute(
                    payload,
                    everyone,
                    [(g * trainers + c, first_trainer + c) for c in range(trainers)],
                )
                for g in range(sim_groups)
            ]
        )

    def from_line(held):
        return [lax.ppermute(held, everyone, swap(apart)) for apart in range(1, y_devices)]

    def across(apart, held):
        return lax.ppermute(held, everyone, swap(apart * y_devices))

    *cube, thin, x_edges, y_edges = sample_cube(sample_block, place, brick, trainers)
    thin = lax.all_to_all(thin, ("gx", "gy"), split_axis=0, concat_axis=0, tiled=True)
    payload = cube_change(sample_block, place, closure, cube, thin, y_cells, z_cells)
    landed = to_trainers(payload)
    x_edges, y_edges, landed = lax.optimization_barrier((x_edges, y_edges, landed))
    halo = (x_neighbours(x_edges), *y_neighbours(y_edges[0], y_edges[1]))
    near = [landed, *from_line(landed)]
    far = [
        across(apart, pick_cubes(sample_trainer, place, near, y_devices, x_devices, apart))
        for apart in range(1, x_devices)
    ]
    arrived = [*near, *far]

    first_count = CH * TAPS * F
    first = jnp.pad(master[:first_count].reshape(CH, TAPS * F), ((0, 0), (0, 256 - TAPS * F)))
    last = jnp.pad(master[first_count:].reshape(TAPS * F, CH).T, ((0, 0), (0, 256 - TAPS * F)))

    first, last = lax.optimization_barrier((first, last))

    def train_here():
        delta_first, delta_last, new_brick = train_cubes(
            sample_trainer, place, first, last, arrived, brick, y_devices, x_devices
        )
        delta = jnp.concatenate(
            [delta_first[:, : TAPS * F].reshape(-1), delta_last[:, : TAPS * F].T.reshape(-1)]
        )
        return delta, new_brick

    def evolve_here():
        new_brick = evolve(closure, place, brick, *halo)
        return jnp.zeros((NPARAM,), jnp.float32), new_brick

    delta, new_brick = lax.cond(is_trainer, train_here, evolve_here)

    line = sum(from_line(delta), delta)
    total = sum((across(apart, line) for apart in range(1, x_devices)), line)
    final = jnp.where(is_trainer, total, 0.0)
    for g in range(sim_groups):
        pairs = [(first_trainer + c, g * trainers + c) for c in range(trainers)]
        final = final + lax.ppermute(total, everyone, pairs)

    share_size = NPARAM // (group_count * trainers)
    share_start = (my_group * trainers + my_column) * share_size
    momentum_share = lax.dynamic_slice_in_dim(momentum, share_start, share_size)
    master_share = lax.dynamic_slice_in_dim(master, share_start, share_size)
    inverse = 1.0 / jnp.sqrt(jnp.sum(final * final) / NPARAM + norm_epsilon)
    delta_share = lax.dynamic_slice_in_dim(final, share_start, share_size)
    new_momentum = momentum_decay * momentum_share + delta_share * inverse
    new_master = master_share - outer_rate * new_momentum
    return (new_brick[None], new_master, new_momentum)


def solution(mesh):
    in_specs = (P("grp", None, "gx", "gy", None), P(), P(), P(), P(), P(), P(), P())
    out_specs = (P("grp", None, "gx", "gy", None), P(("grp", "gx", "gy")), P(("grp", "gx", "gy")))
    return jax.shard_map(
        on_device, mesh=mesh, in_specs=in_specs, out_specs=out_specs, check_vma=False
    )
```

```python
import functools

import jax
import jax.numpy as jnp
import numpy as np
from jax import lax
from jax.experimental import pallas as pl
from jax.experimental.pallas import tpu as pltpu
from jax.sharding import PartitionSpec as P

F = 5
CH = 64
HID = 64
SUB = 16
TCAP = 6
INNER = 3
CELLS = 4096
NPARAM = 17280
TAPS = 27
PAIRS = TCAP // 2
COLS = (SUB + 2) * 128
PATCH = 16 * F
STACK = 3 * PATCH

time_step = 0.1
base_viscosity = 0.02
viscosity_gain = 0.2
buoyancy = 0.5
inner_rate = 0.02
outer_rate = 0.01
momentum_decay = 0.9
norm_epsilon = 1e-06


def patch_position(row):
    group, py, pz = row // 4, row // 2 % 2, row % 2
    ypos = py + 1 if group in (0, 1) else (3 if py == 0 else 0)
    zpos = pz + 1 if group in (0, 2) else (3 if pz == 0 else 0)
    return ypos - 1, zpos - 1


def selections():
    first = np.zeros((4, 256, STACK), np.float32)
    last = np.zeros((4, 256, STACK), np.float32)
    for cell in range(4):
        py, pz = cell // 2, cell % 2
        for kx in range(3):
            for channel in range(F):
                for row in range(16):
                    ypos, zpos = patch_position(row)
                    column = kx * PATCH + channel * 16 + row
                    dy, dz = ypos - py, zpos - pz
                    if abs(dy) <= 1 and abs(dz) <= 1:
                        tap = 9 * kx + 3 * (dy + 1) + dz + 1
                        first[cell, tap * F + channel, column] = 1.0
                        last[cell, channel * TAPS + 26 - tap, column] = 1.0
    return first, last


SELECT_FIRST, SELECT_LAST = selections()


def column_of(place, x_step, y_step):
    gx = lax.rem(place[1] + x_step + place[5], place[5])
    gy = lax.rem(place[2] + y_step + place[4], place[4])
    return gx * place[4] + gy


def xor_of(left, right, size):
    total = jnp.int32(0)
    for bit in range(size.bit_length() - 1):
        one, other = lax.rem(lax.div(left, 1 << bit), 2), lax.rem(lax.div(right, 1 << bit), 2)
        total = total + jnp.where(one == other, 0, 1 << bit)
    return total


def owner_apart(owner, place, y_devices, x_devices):
    trainers = x_devices * y_devices
    column = lax.rem(owner, trainers)
    y_apart = xor_of(lax.rem(column, y_devices), place[2], y_devices)
    x_apart = xor_of(lax.div(column, y_devices), place[1], x_devices)
    return lax.div(owner, trainers), y_apart, x_apart


def pick_kernel(y_devices, x_devices, apart, trainer_of, place, *refs):
    near, chosen = refs[:y_devices], refs[y_devices]
    wanted = xor_of(place[1], apart, x_devices) * y_devices + place[2]

    def visit(owner, count):
        group, y_apart, x_apart = owner_apart(owner, place, y_devices, x_devices)
        mine = (trainer_of[owner] == wanted) & (x_apart == 0)
        for source in range(y_devices):

            @pl.when(mine & (y_apart == source))
            def _():
                chosen[count] = near[source][group]

        return count + jnp.where(mine, 1, 0)

    lax.fori_loop(0, trainer_of.shape[0], visit, jnp.int32(0))


def pick_cubes(trainer_of, place, near, y_devices, x_devices, apart):
    vmem = pl.BlockSpec(memory_space=pltpu.VMEM)
    smem = pl.BlockSpec(memory_space=pltpu.SMEM)
    return pl.pallas_call(
        functools.partial(pick_kernel, y_devices, x_devices, apart),
        out_shape=jax.ShapeDtypeStruct((TCAP, *near[0].shape[1:]), near[0].dtype),
        in_specs=[smem, smem] + [vmem] * len(near),
        out_specs=vmem,
        compiler_params=pltpu.CompilerParams(vmem_limit_bytes=16 * 1024 * 1024),
        name="pick_cubes",
    )(trainer_of, place, *near)


def dot_rows(left, right):
    return jnp.dot(left, right, preferred_element_type=jnp.float32)


def dot_lanes(left, right):
    return lax.dot_general(left, right, (((1,), (1,)), ((), ())), preferred_element_type=jnp.float32)


def patch_masks():
    row = lax.broadcasted_iota(jnp.int32, (8, 128), 0)
    lane = lax.broadcasted_iota(jnp.int32, (8, 128), 1)
    return {
        "pz0": row % 2 == 0,
        "py0": row // 2 % 2 == 0,
        "centre": row < 4,
        "z_first": lane % 8 == 0,
        "z_last": lane % 8 == 7,
        "y_first": lane // 8 % 8 == 0,
        "y_last": lane // 8 % 8 == 7,
    }


def edge_shift(values, step, parity_zero, first, last, forward):
    before = jnp.where(first, 0.0, pltpu.roll(values, step, 1))
    after = jnp.where(last, 0.0, pltpu.roll(values, 128 - step, 1))
    if forward:
        return jnp.where(parity_zero, after, before)
    return jnp.where(parity_zero, before, after)


def patch_stack(rows, masks):
    both = rows + pltpu.roll(rows, 4, 0)
    z_edge = edge_shift(both, 1, masks["pz0"], masks["z_first"], masks["z_last"], True)
    upper = jnp.where(masks["centre"], both, z_edge)
    lower = edge_shift(upper, 8, masks["py0"], masks["y_first"], masks["y_last"], True)
    return upper, lower


def patch_fold(upper, lower, masks):
    def fold_z(values):
        moved = edge_shift(values, 1, masks["pz0"], masks["z_first"], masks["z_last"], False)
        return values + pltpu.roll(moved, 4, 0)

    shifted = edge_shift(fold_z(lower), 8, masks["py0"], masks["y_first"], masks["y_last"], False)
    return fold_z(upper) + shifted


def store_planes(ref, x, channels):
    stacked = jnp.concatenate([part for both in channels for part in both], axis=0).astype(jnp.bfloat16)
    for kx in range(3):
        start = pl.multiple_of((x + 2 - kx) * 128, 128)
        ref[kx * PATCH : (kx + 1) * PATCH, pl.ds(start, 128)] = stacked


def train_kernel(y_devices, x_devices, *refs):
    sources = y_devices + x_devices - 1
    (trainer_of, place, first_ref, last_ref, far_first, far_last) = refs[:6]
    arrived = refs[6 : 6 + sources]
    fields_ref = refs[6 + sources]
    delta_first, delta_last, new_fields_ref = refs[7 + sources : 10 + sources]
    (
        slots,
        picked,
        cubes,
        table,
        big_first,
        big_last,
        big_last_t,
        grad_first,
        grad_last,
        now_first,
        now_last,
        brick,
        select_first,
        select_last,
        slot_sems,
        field_sem,
        select_sems,
        *pair_refs,
    ) = refs[10 + sources :]
    targets, inputs, errors, hiddens, pre_grads, slopes, partial_out, raw = [
        pair_refs[kind * PAIRS : (kind + 1) * PAIRS] for kind in range(8)
    ]

    field_in = pltpu.make_async_copy(fields_ref, brick, field_sem)
    field_out = pltpu.make_async_copy(brick, new_fields_ref, field_sem)
    select_copies = [
        pltpu.make_async_copy(far_first, select_first, select_sems.at[0]),
        pltpu.make_async_copy(far_last, select_last, select_sems.at[1]),
    ]

    groups = place[3]
    for other in range(x_devices):
        picked[other] = 0

    def visit(owner, count):
        mine = trainer_of[owner] == column_of(place, 0, 0)

        @pl.when(mine)
        def _():
            group, y_apart, x_apart = owner_apart(owner, place, y_devices, x_devices)
            near = x_apart == 0
            slots[0, count] = jnp.where(near, y_apart, y_devices - 1 + x_apart)
            slots[1, count] = jnp.where(near, group, picked[x_apart])
            picked[x_apart] = picked[x_apart] + 1

        return count + jnp.where(mine, 1, 0)

    count = lax.fori_loop(0, trainer_of.shape[0], visit, jnp.int32(0))

    def fetch(slot, wait):
        for source in range(sources):

            @pl.when((slot < count) & (slots[0, slot] == source))
            def _():
                copy = pltpu.make_async_copy(
                    arrived[source].at[slots[1, slot]], cubes.at[slot], slot_sems.at[slot]
                )
                copy.wait() if wait else copy.start()

    for slot in range(TCAP):
        fetch(slot, False)

    for copy in select_copies:
        copy.start()
    field_in.start()
    for slot in range(TCAP):

        @pl.when(slot >= count)
        def _():
            cubes[slot] = jnp.zeros((2 * SUB * F, 256), jnp.bfloat16)

    masks = patch_masks()
    for ref in (*errors, *inputs):
        ref[:PATCH, 128:256] = jnp.zeros((PATCH, 128), jnp.bfloat16)
        ref[2 * PATCH :, COLS - 256 : COLS - 128] = jnp.zeros((PATCH, 128), jnp.bfloat16)
    for ref in partial_out:
        ref[:, :128] = jnp.zeros((STACK, 128), jnp.float32)
        ref[:, COLS - 128 :] = jnp.zeros((STACK, 128), jnp.float32)
    for ref in (table, *targets):
        ref[...] = jnp.zeros(ref.shape, ref.dtype)
    lane = lax.broadcasted_iota(jnp.int32, (8, 128), 1)
    full_weight = 2.0 * (1.0 / (jnp.full((8, 128), count, jnp.int32).astype(jnp.float32) * CELLS))
    weights = [
        jnp.where(lane // 64 + 2 * pair < count, full_weight, 0.0) for pair in range(PAIRS)
    ]
    start_first = first_ref[...].astype(jnp.bfloat16).astype(jnp.float32)
    start_last = last_ref[...].astype(jnp.bfloat16).astype(jnp.float32)
    now_first[...] = start_first
    now_last[...] = start_last

    for slot in range(TCAP):
        fetch(slot, True)

    low_lanes = lax.broadcasted_iota(jnp.int32, (SUB * F, 128), 1) < 64

    def spread_rows(pair, kind, put):
        rows = slice(kind * SUB * F, (kind + 1) * SUB * F)
        even = cubes[2 * pair, rows, :].astype(jnp.float32)
        odd = cubes[2 * pair + 1, rows, :].astype(jnp.float32)
        for half in range(2):
            left = even[:, half * 128 : (half + 1) * 128]
            right = odd[:, half * 128 : (half + 1) * 128]
            put(2 * half, jnp.where(low_lanes, left, pltpu.roll(right, 64, 1)))
            put(2 * half + 1, jnp.where(low_lanes, pltpu.roll(left, 64, 1), right))

    for pair in range(PAIRS):

        def put_input(cell, values):
            table[pl.ds(cell, SUB * F, 8), :] = values

        def put_target(cell, values):
            targets[pair][pl.ds(cell, SUB * F, 8), :] = values

        spread_rows(pair, 0, put_input)
        spread_rows(pair, 1, put_target)

        def stack_plane(x, carry):
            channels = [
                patch_stack(table[pl.ds(pl.multiple_of((c * SUB + x) * 8, 8), 8), :], masks)
                for c in range(F)
            ]
            store_planes(inputs[pair], x, channels)
            return carry

        lax.fori_loop(0, SUB, stack_plane, 0, unroll=8)

    for copy in select_copies:
        copy.wait()
    field_in.wait()
    field_out.start()

    def train_step(step, step_carry):
        first_now = now_first[...].astype(jnp.bfloat16)
        last_now = now_last[...].astype(jnp.bfloat16)
        for cell in range(4):
            rows = slice(cell * CH, (cell + 1) * CH)
            big_first[rows, :] = (0.5 * dot_rows(first_now, select_first[cell])).astype(jnp.bfloat16)
            spread_last = dot_rows(last_now, select_last[cell])
            big_last[rows, :] = (0.5 * spread_last).astype(jnp.bfloat16)
            big_last_t[:, rows] = spread_last.T.astype(jnp.bfloat16)
        grad_first[...] = jnp.zeros(grad_first.shape, jnp.float32)
        grad_last[...] = jnp.zeros(grad_last.shape, jnp.float32)

        def columns_of(quarter):
            return pl.ds(pl.multiple_of(quarter * 512 + 128, 128), 512)

        def first_layer(pair, quarter):
            columns = columns_of(quarter)
            raw[pair][:, columns] = dot_rows(big_first[...], inputs[pair][:, columns])

        def activate(pair, quarter):
            columns = columns_of(quarter)
            for part in range(8):
                rows = slice(part * 32, (part + 1) * 32)
                half = raw[pair][rows, columns]
                curve = jnp.tanh(half)
                above = 1.0 + curve
                value = half * above
                hiddens[pair][rows, columns] = value.astype(jnp.bfloat16)
                slopes[pair][rows, columns] = above + value * (1.0 - curve)

        def last_layer(pair, quarter):
            columns = columns_of(quarter)
            partial_out[pair][:, columns] = dot_rows(big_last_t[...], hiddens[pair][:, columns])

        def find_errors(pair, quarter):
            for plane in range(4):
                x = quarter * 4 + plane
                column = pl.multiple_of((x + 1) * 128, 128)
                total = (
                    partial_out[pair][0:PATCH, pl.ds(pl.multiple_of(column + 128, 128), 128)]
                    + partial_out[pair][PATCH : 2 * PATCH, pl.ds(column, 128)]
                    + partial_out[pair][2 * PATCH :, pl.ds(pl.multiple_of(column - 128, 128), 128)]
                )
                channels = []
                for c in range(F):
                    predicted = patch_fold(
                        total[16 * c : 16 * c + 8], total[16 * c + 8 : 16 * c + 16], masks
                    )
                    row = pl.multiple_of((c * SUB + x) * 8, 8)
                    error = weights[pair] * (predicted - targets[pair][pl.ds(row, 8), :])
                    error = jnp.where(masks["centre"], error, 0.0)
                    error = error.astype(jnp.bfloat16).astype(jnp.float32)
                    channels.append(patch_stack(error, masks))
                store_planes(errors[pair], x, channels)

        def hidden_layer(pair, quarter):
            columns = columns_of(quarter)
            raw[pair][:, columns] = dot_rows(big_last[...], errors[pair][:, columns])

        def scale(pair, quarter):
            columns = columns_of(quarter)
            for part in range(8):
                rows = slice(part * 32, (part + 1) * 32)
                product = raw[pair][rows, columns] * slopes[pair][rows, columns]
                pre_grads[pair][rows, columns] = product.astype(jnp.bfloat16)

        def gradients(pair, quarter):
            columns = columns_of(quarter)
            grad_first[...] += dot_lanes(pre_grads[pair][:, columns], inputs[pair][:, columns])
            grad_last[...] += dot_lanes(hiddens[pair][:, columns], errors[pair][:, columns])

        stages = (first_layer, activate, last_layer, find_errors, hidden_layer, scale, gradients)
        for turn in range(len(stages) + PAIRS - 1):

            def run(quarter, carry):
                for pair in range(PAIRS):
                    if 0 <= turn - pair < len(stages):
                        stages[turn - pair](pair, quarter)
                return carry

            lax.fori_loop(0, 4, run, 0)

        def folded(grad, select_ref):
            total = jnp.zeros((3 * CH, 256), jnp.float32)
            for cell in range(4):
                rest = grad[cell * CH : (cell + 1) * CH, :]
                parts = []
                for _ in range(3):
                    parts.append(rest.astype(jnp.bfloat16))
                    rest = rest - parts[-1].astype(jnp.float32)
                total = total + dot_lanes(jnp.concatenate(parts, axis=0), select_ref[cell])
            return total[:CH] + total[CH : 2 * CH] + total[2 * CH :]

        now_first[...] = now_first[...] - inner_rate * folded(grad_first, select_first)
        now_last[...] = now_last[...] - inner_rate * folded(grad_last, select_last)
        return step_carry

    lax.fori_loop(0, INNER, train_step, 0)
    delta_first[...] = start_first - now_first[...]
    delta_last[...] = start_last - now_last[...]
    field_out.wait()


def train_cubes(trainer_of, place, first, last, arrived, fields, y_devices, x_devices):
    vmem = pl.BlockSpec(memory_space=pltpu.VMEM)
    smem = pl.BlockSpec(memory_space=pltpu.SMEM)
    anywhere = pl.BlockSpec(memory_space=pl.ANY)
    hbm = pl.BlockSpec(memory_space=pltpu.HBM)
    return pl.pallas_call(
        functools.partial(train_kernel, y_devices, x_devices),
        out_shape=(
            jax.ShapeDtypeStruct((CH, 256), jnp.float32),
            jax.ShapeDtypeStruct((CH, 256), jnp.float32),
            jax.ShapeDtypeStruct(fields.shape, fields.dtype),
        ),
        in_specs=[smem] * 2 + [vmem] * 2 + [hbm] * 2 + [anywhere] * len(arrived) + [hbm],
        out_specs=(vmem, vmem, hbm),
        scratch_shapes=[
            pltpu.SMEM((2, TCAP), jnp.int32),
            pltpu.SMEM((x_devices,), jnp.int32),
            pltpu.VMEM((TCAP, 2 * SUB * F, 256), jnp.bfloat16),
            pltpu.VMEM((SUB * F * 8, 128), jnp.float32),
            pltpu.VMEM((4 * CH, STACK), jnp.bfloat16),
            pltpu.VMEM((4 * CH, STACK), jnp.bfloat16),
            pltpu.VMEM((STACK, 4 * CH), jnp.bfloat16),
            pltpu.VMEM((4 * CH, STACK), jnp.float32),
            pltpu.VMEM((4 * CH, STACK), jnp.float32),
            pltpu.VMEM((CH, 256), jnp.float32),
            pltpu.VMEM((CH, 256), jnp.float32),
            pltpu.VMEM(fields.shape, fields.dtype),
            pltpu.VMEM((4, 256, STACK), jnp.bfloat16),
            pltpu.VMEM((4, 256, STACK), jnp.bfloat16),
            pltpu.SemaphoreType.DMA((TCAP,)),
            pltpu.SemaphoreType.DMA,
            pltpu.SemaphoreType.DMA((2,)),
        ]
        + [pltpu.VMEM((SUB * F * 8, 128), jnp.float32)] * PAIRS
        + [pltpu.VMEM((STACK, COLS), jnp.bfloat16)] * (2 * PAIRS)
        + [pltpu.VMEM((4 * CH, COLS), jnp.bfloat16)] * (2 * PAIRS)
        + [pltpu.VMEM((4 * CH, COLS), jnp.float32)] * PAIRS
        + [pltpu.VMEM((STACK, COLS), jnp.float32)] * PAIRS
        + [pltpu.VMEM((4 * CH, COLS), jnp.float32)] * PAIRS,
        compiler_params=pltpu.CompilerParams(vmem_limit_bytes=52 * 1024 * 1024),
        name="train_cubes",
    )(
        trainer_of,
        place,
        first,
        last,
        jnp.asarray(SELECT_FIRST, jnp.bfloat16),
        jnp.asarray(SELECT_LAST, jnp.bfloat16),
        *arrived,
        fields,
    )


def viscosity_of(cells, closure):
    def unit(h, total):
        half = closure[F, h] + closure[0, h] * cells[0]
        for f in range(1, F):
            half = half + closure[f, h] * cells[f]
        return total + closure[F + 1, h] * (half + half * jnp.tanh(half))

    total = lax.fori_loop(0, HID, unit, jnp.zeros(cells[0].shape, jnp.float32), unroll=4)
    soft = jnp.maximum(total, 0.0) + jnp.log1p(jnp.exp(-jnp.abs(total)))
    return base_viscosity + viscosity_gain * soft


def evolve_kernel(closure, place, fields, x_halo, y_first, y_second, new_fields):
    up_first = lax.rem(place[2], 2) == 0
    x_cells, y_cells, z_cells = fields.shape[1:]
    row = lax.broadcasted_iota(jnp.int32, (y_cells, z_cells), 0)
    lane = lax.broadcasted_iota(jnp.int32, (y_cells, z_cells), 1)
    part = y_cells // 2

    def plane(x, carry):
        eddies = []
        for half in range(2):
            rows = pl.ds(half * part, part)
            cells = [fields[f, x, rows, :] for f in range(F)]
            eddies.append(viscosity_of(cells, closure))
        viscosity = jnp.concatenate(eddies, axis=0)
        centre = [fields[f, x] for f in range(F)]
        below = jnp.maximum(x - 1, 0)
        above = jnp.minimum(x + 1, x_cells - 1)
        for f in range(F):
            value = centre[f]
            west = jnp.where(x == 0, x_halo[1, f], fields[f, below])
            east = jnp.where(x == x_cells - 1, x_halo[0, f], fields[f, above])
            first, second = y_first[f, pl.ds(x, 1), :], y_second[f, pl.ds(x, 1), :]
            south = jnp.where(
                row == 0, jnp.where(up_first, second, first), pltpu.roll(value, 1, 0)
            )
            north = jnp.where(
                row == y_cells - 1,
                jnp.where(up_first, first, second),
                pltpu.roll(value, y_cells - 1, 0),
            )
            lower = jnp.where(lane == 0, 0.0, pltpu.roll(value, 1, 1))
            upper = jnp.where(lane == z_cells - 1, 0.0, pltpu.roll(value, z_cells - 1, 1))
            laplacian = east + west + north + south + upper + lower - 6.0 * value
            advection = (
                centre[0] * (east - west) + centre[1] * (north - south) + centre[2] * (upper - lower)
            )
            tendency = viscosity * laplacian - 0.5 * advection
            if f == 2:
                tendency = tendency + buoyancy * centre[3]
            new_fields[f, x] = value + time_step * tendency
        return carry

    lax.fori_loop(0, x_cells, plane, 0)


def evolve(closure, place, fields, x_halo, y_first, y_second):
    vmem = pl.BlockSpec(memory_space=pltpu.VMEM)
    return pl.pallas_call(
        evolve_kernel,
        out_shape=jax.ShapeDtypeStruct(fields.shape, fields.dtype),
        in_specs=[pl.BlockSpec(memory_space=pltpu.SMEM)] * 2 + [vmem] * 4,
        out_specs=vmem,
        compiler_params=pltpu.CompilerParams(vmem_limit_bytes=16 * 1024 * 1024),
        name="evolve_brick",
    )(closure, place, fields, x_halo, y_first, y_second)


def cell_order():
    order = np.zeros((256, 256), np.float32)
    for y in range(SUB):
        for z in range(SUB):
            order[y * SUB + z, (y % 2 * 2 + z % 2) * 64 + y // 2 * 8 + z // 2] = 1.0
    return order


CELL_ORDER = cell_order()


def corner_of(sample_block, place, x_step, y_step, y_cells, z_cells):
    x_devices, y_devices = place[5], place[4]
    gx = lax.rem(place[1] + x_step + x_devices, x_devices)
    gy = lax.rem(place[2] + y_step + y_devices, y_devices)
    group = jnp.minimum(place[0], place[3] - 1)
    block = sample_block[(group * x_devices + gx) * y_devices + gy]
    z_blocks = z_cells // SUB
    return lax.rem(lax.div(block, z_blocks), y_cells // SUB) * SUB, lax.rem(block, z_blocks) * SUB


def sample_kernel(
    y_cells,
    z_cells,
    sample_block,
    place,
    brick,
    centre,
    lower,
    upper,
    own_rows,
    thin,
    x_edges,
    y_edges,
    windows,
    sems,
):
    rows_of_x = y_cells
    rows_of_field = SUB * y_cells
    window_rows = F * rows_of_field
    copies = [
        pltpu.make_async_copy(
            brick.at[:, pl.ds(w * 128, 128)], windows.at[pl.ds(w * window_rows, window_rows)], sems.at[w]
        )
        for w in range(z_cells // 128)
    ]
    for copy in copies:
        copy.start()
    for copy in copies:
        copy.wait()

    def corner(x_step, y_step):
        return corner_of(sample_block, place, x_step, y_step, y_cells, z_cells)

    def piece(row, count, stride, z, lane_start):
        values = windows[pl.ds(lax.div(z, 128) * window_rows + row, count, stride), :]
        return pltpu.roll(values, lax.rem(lane_start - lax.rem(z, 128) + 256, 128), 1)

    lane = lax.broadcasted_iota(jnp.int32, (SUB, 128), 1)
    y_start, z_start = corner(0, 0)
    z_below = jnp.maximum(z_start - 1, 0)
    z_above = jnp.minimum(z_start + SUB, z_cells - 1)
    for field in range(F):
        for half in range(2):
            inside = jnp.zeros((SUB, 128), jnp.float32)
            below = jnp.zeros((SUB, 128), jnp.float32)
            above = jnp.zeros((SUB, 128), jnp.float32)
            for step in range(8):
                row = field * rows_of_field + y_start + half * 8 + step
                first = step * SUB
                inside = jnp.where(lane // SUB == step, piece(row, SUB, rows_of_x, z_start, first), inside)
                below = jnp.where(lane == first, piece(row, SUB, rows_of_x, z_below, first), below)
                last = first + SUB - 1
                above = jnp.where(lane == last, piece(row, SUB, rows_of_x, z_above, last), above)
            below = jnp.where(z_start == 0, 0.0, below)
            above = jnp.where(z_start + SUB == z_cells, 0.0, above)
            at = (slice(field * SUB, (field + 1) * SUB), slice(half * 128, (half + 1) * 128))
            centre[at] = inside
            lower[at] = jnp.where(lane % SUB == 0, below, pltpu.roll(inside, 1, 1))
            upper[at] = jnp.where(lane % SUB == SUB - 1, above, pltpu.roll(inside, 127, 1))

    def y_row(y, z):
        total = jnp.zeros((SUB, 128), jnp.float32)
        for field in range(F):
            part = piece(field * rows_of_field + y, SUB, rows_of_x, z, field * SUB)
            total = jnp.where(lane // SUB == field, part, total)
        return total

    own_rows[0] = y_row(jnp.maximum(y_start - 1, 0), z_start)
    own_rows[1] = y_row(jnp.minimum(y_start + SUB, y_cells - 1), z_start)
    thin[...] = jnp.zeros(thin.shape, thin.dtype)
    thin[column_of(place, 0, -1), :, :128] = y_row(0, corner(0, -1)[1])
    thin[column_of(place, 0, 1), :, 128:] = y_row(y_cells - 1, corner(0, 1)[1])
    lane = lane[:8]
    for face, (x, sign) in enumerate(((0, -1), (SUB - 1, 1))):
        y_there, z_there = corner(sign, 0)
        for half in range(2):
            total = jnp.zeros((8, 128), jnp.float32)
            for step in range(8):
                row = x * rows_of_x + y_there + half * 8 + step
                part = piece(row, 8, rows_of_field, z_there, step * SUB)
                total = jnp.where(lane // SUB == step, part, total)
            at = (column_of(place, sign, 0), slice(face * 8, face * 8 + 8), slice(half * 128, half * 128 + 128))
            thin[at] = total
    up_first = lax.rem(place[2], 2) == 0
    for side in range(2):
        y = jnp.where(up_first == (side == 0), y_cells - 1, 0)
        for field in range(F):
            for w in range(z_cells // 128):
                start = w * window_rows + field * rows_of_field + y
                y_edges[side, field, :, w * 128 : (w + 1) * 128] = windows[
                    pl.ds(start, SUB, rows_of_x), :
                ]
    for side, x in enumerate((0, SUB - 1)):
        for field in range(F):
            for w in range(z_cells // 128):
                start = w * window_rows + field * rows_of_field + x * rows_of_x
                x_edges[side, field, :, w * 128 : (w + 1) * 128] = windows[pl.ds(start, rows_of_x), :]


def sample_cube(sample_block, place, brick, columns):
    fields, x_cells, y_cells, z_cells = brick.shape
    vmem = pl.BlockSpec(memory_space=pltpu.VMEM)
    smem = pl.BlockSpec(memory_space=pltpu.SMEM)
    hbm = pl.BlockSpec(memory_space=pltpu.HBM)
    rows = fields * x_cells * y_cells
    cube = jax.ShapeDtypeStruct((F * SUB, 256), jnp.float32)
    return pl.pallas_call(
        functools.partial(sample_kernel, y_cells, z_cells),
        out_shape=(
            cube,
            cube,
            cube,
            jax.ShapeDtypeStruct((2, SUB, 128), jnp.float32),
            jax.ShapeDtypeStruct((columns, SUB, 256), jnp.float32),
            jax.ShapeDtypeStruct((2, fields, y_cells, z_cells), jnp.float32),
            jax.ShapeDtypeStruct((2, fields, x_cells, z_cells), jnp.float32),
        ),
        in_specs=[smem, smem, hbm],
        out_specs=(vmem,) * 7,
        scratch_shapes=[
            pltpu.VMEM((z_cells // 128 * rows + 4 * x_cells * y_cells, 128), jnp.float32),
            pltpu.SemaphoreType.DMA((z_cells // 128,)),
        ],
        compiler_params=pltpu.CompilerParams(vmem_limit_bytes=16 * 1024 * 1024),
        name="sample_cube",
    )(sample_block, place, brick.reshape(rows, z_cells))


def change_kernel(
    y_cells,
    z_cells,
    sample_block,
    place,
    closure,
    order,
    centre,
    lower,
    upper,
    own_rows,
    thin,
    payload,
):
    y_start = corner_of(sample_block, place, 0, 0, y_cells, z_cells)[0]
    row = lax.broadcasted_iota(jnp.int32, (SUB, 256), 0)
    lane = lax.broadcasted_iota(jnp.int32, (SUB, 256), 1)
    south_row = jnp.where(y_start == 0, thin[column_of(place, 0, -1), :, 128:], own_rows[0])
    north_row = jnp.where(y_start + SUB == y_cells, thin[column_of(place, 0, 1), :, :128], own_rows[1])
    face_low = thin[column_of(place, -1, 0), 8:, :]
    face_high = thin[column_of(place, 1, 0), :8, :]
    cells = [centre[f * SUB : (f + 1) * SUB, :] for f in range(F)]
    viscosity = viscosity_of(cells, closure)
    changes = []
    for f in range(F):
        value = cells[f]
        west = jnp.where(row == 0, face_low[f : f + 1, :], pltpu.roll(value, 1, 0))
        east = jnp.where(row == SUB - 1, face_high[f : f + 1, :], pltpu.roll(value, SUB - 1, 0))
        edge = pltpu.roll(south_row, (128 - f * SUB) % 128, 1)
        south = jnp.where(lane < SUB, jnp.concatenate([edge, edge], 1), pltpu.roll(value, SUB, 1))
        edge = pltpu.roll(north_row, 112 - f * SUB, 1)
        north = jnp.where(
            lane >= 256 - SUB, jnp.concatenate([edge, edge], 1), pltpu.roll(value, 256 - SUB, 1)
        )
        down = lower[f * SUB : (f + 1) * SUB, :]
        up = upper[f * SUB : (f + 1) * SUB, :]
        laplacian = east + west + north + south + up + down - 6.0 * value
        advection = cells[0] * (east - west) + cells[1] * (north - south) + cells[2] * (up - down)
        change = viscosity * laplacian - 0.5 * advection
        if f == 2:
            change = change + buoyancy * cells[3]
        changes.append(change)
    both = jnp.concatenate(cells + changes, axis=0).astype(jnp.bfloat16)
    payload[...] = dot_rows(both, order[...]).astype(jnp.bfloat16)


def cube_change(sample_block, place, closure, cube, thin, y_cells, z_cells):
    vmem = pl.BlockSpec(memory_space=pltpu.VMEM)
    smem = pl.BlockSpec(memory_space=pltpu.SMEM)
    return pl.pallas_call(
        functools.partial(change_kernel, y_cells, z_cells),
        out_shape=jax.ShapeDtypeStruct((2 * F * SUB, 256), jnp.bfloat16),
        in_specs=[smem] * 3 + [vmem] * 6,
        out_specs=vmem,
        compiler_params=pltpu.CompilerParams(vmem_limit_bytes=16 * 1024 * 1024),
        name="cube_change",
    )(sample_block, place, closure, jnp.asarray(CELL_ORDER, jnp.bfloat16), *cube, thin)


def on_device(
    fields, closure_in, closure_bias, closure_out, master, momentum, sample_block, sample_trainer
):
    group_count = lax.axis_size("grp")
    x_devices = lax.axis_size("gx")
    y_devices = lax.axis_size("gy")
    trainers = x_devices * y_devices
    my_group = lax.axis_index("grp")
    my_column = lax.axis_index("gx") * y_devices + lax.axis_index("gy")
    is_trainer = my_group == group_count - 1
    everyone = ("grp", "gx", "gy")
    sim_groups = group_count - 1
    first_trainer = sim_groups * trainers
    brick = fields[0]
    y_cells, z_cells = brick.shape[2:]
    closure = jnp.concatenate(
        [0.5 * closure_in.T, 0.5 * closure_bias[None], closure_out[None]], axis=0
    )
    place = jnp.stack(
        [
            my_group,
            lax.axis_index("gx"),
            lax.axis_index("gy"),
            jnp.int32(sim_groups),
            jnp.int32(y_devices),
            jnp.int32(x_devices),
        ]
    ).astype(jnp.int32)

    def pairs(x_step, even_step):
        found = []
        for g in range(sim_groups):
            for c in range(trainers):
                gx, gy = c // y_devices, c % y_devices
                gx = (gx + x_step) % x_devices
                gy = (gy + (even_step if gy % 2 == 0 else -even_step)) % y_devices
                found.append((g * trainers + c, (g * x_devices + gx) * y_devices + gy))
        return found

    def x_neighbours(edges):
        if x_devices == 2:
            return lax.ppermute(edges, everyone, pairs(1, 0))
        from_high = lax.ppermute(edges[0], everyone, pairs(-1, 0))
        return jnp.stack([from_high, lax.ppermute(edges[1], everyone, pairs(1, 0))])

    def y_neighbours(for_first, for_second):
        return (
            lax.ppermute(for_first, everyone, pairs(0, 1)),
            lax.ppermute(for_second, everyone, pairs(0, -1)),
        )

    def swap(distance):
        return [(first_trainer + c, first_trainer + (c ^ distance)) for c in range(trainers)]

    def to_trainers(payload):
        return jnp.stack(
            [
                lax.ppermute(
                    payload,
                    everyone,
                    [(g * trainers + c, first_trainer + c) for c in range(trainers)],
                )
                for g in range(sim_groups)
            ]
        )

    def from_line(held):
        return [lax.ppermute(held, everyone, swap(apart)) for apart in range(1, y_devices)]

    def across(apart, held):
        return lax.ppermute(held, everyone, swap(apart * y_devices))

    *cube, thin, x_edges, y_edges = sample_cube(sample_block, place, brick, trainers)
    thin = lax.all_to_all(thin, ("gx", "gy"), split_axis=0, concat_axis=0, tiled=True)
    payload = cube_change(sample_block, place, closure, cube, thin, y_cells, z_cells)
    landed = to_trainers(payload)
    x_edges, y_edges, landed = lax.optimization_barrier((x_edges, y_edges, landed))
    halo = (x_neighbours(x_edges), *y_neighbours(y_edges[0], y_edges[1]))
    near = [landed, *from_line(landed)]
    far = [
        across(apart, pick_cubes(sample_trainer, place, near, y_devices, x_devices, apart))
        for apart in range(1, x_devices)
    ]
    arrived = [*near, *far]

    first_count = CH * TAPS * F
    first = jnp.pad(master[:first_count].reshape(CH, TAPS * F), ((0, 0), (0, 256 - TAPS * F)))
    last = jnp.pad(master[first_count:].reshape(TAPS * F, CH).T, ((0, 0), (0, 256 - TAPS * F)))

    first, last = lax.optimization_barrier((first, last))

    def train_here():
        delta_first, delta_last, new_brick = train_cubes(
            sample_trainer, place, first, last, arrived, brick, y_devices, x_devices
        )
        delta = jnp.concatenate(
            [delta_first[:, : TAPS * F].reshape(-1), delta_last[:, : TAPS * F].T.reshape(-1)]
        )
        return delta, new_brick

    def evolve_here():
        new_brick = evolve(closure, place, brick, *halo)
        return jnp.zeros((NPARAM,), jnp.float32), new_brick

    delta, new_brick = lax.cond(is_trainer, train_here, evolve_here)

    line = sum(from_line(delta), delta)
    total = sum((across(apart, line) for apart in range(1, x_devices)), line)
    final = jnp.where(is_trainer, total, 0.0)
    for g in range(sim_groups):
        pairs = [(first_trainer + c, g * trainers + c) for c in range(trainers)]
        final = final + lax.ppermute(total, everyone, pairs)

    share_size = NPARAM // (group_count * trainers)
    share_start = (my_group * trainers + my_column) * share_size
    momentum_share = lax.dynamic_slice_in_dim(momentum, share_start, share_size)
    master_share = lax.dynamic_slice_in_dim(master, share_start, share_size)
    inverse = 1.0 / jnp.sqrt(jnp.sum(final * final) / NPARAM + norm_epsilon)
    delta_share = lax.dynamic_slice_in_dim(final, share_start, share_size)
    new_momentum = momentum_decay * momentum_share + delta_share * inverse
    new_master = master_share - outer_rate * new_momentum
    return (new_brick[None], new_master, new_momentum)


def solution(mesh):
    in_specs = (P("grp", None, "gx", "gy", None), P(), P(), P(), P(), P(), P(), P())
    out_specs = (P("grp", None, "gx", "gy", None), P(("grp", "gx", "gy")), P(("grp", "gx", "gy")))
    return jax.shard_map(
        on_device, mesh=mesh, in_specs=in_specs, out_specs=out_specs, check_vma=False
    )
```

```python
import functools

import jax
import jax.numpy as jnp
import numpy as np
from jax import lax
from jax.experimental import pallas as pl
from jax.experimental.pallas import tpu as pltpu
from jax.sharding import PartitionSpec as P

F = 5
CH = 64
HID = 64
SUB = 16
TCAP = 6
INNER = 3
CELLS = 4096
NPARAM = 17280
TAPS = 27
PAIRS = TCAP // 2
COLS = (SUB + 2) * 128
PATCH = 16 * F
STACK = 3 * PATCH

time_step = 0.1
base_viscosity = 0.02
viscosity_gain = 0.2
buoyancy = 0.5
inner_rate = 0.02
outer_rate = 0.01
momentum_decay = 0.9
norm_epsilon = 1e-06


def patch_position(row):
    group, py, pz = row // 4, row // 2 % 2, row % 2
    ypos = py + 1 if group in (0, 2) else (3 if py == 0 else 0)
    zpos = pz + 1 if group in (0, 1) else (3 if pz == 0 else 0)
    return ypos - 1, zpos - 1


def selections():
    first = np.zeros((4, 256, STACK), np.float32)
    last = np.zeros((4, 256, STACK), np.float32)
    for cell in range(4):
        py, pz = cell // 2, cell % 2
        for kx in range(3):
            for channel in range(F):
                for row in range(16):
                    ypos, zpos = patch_position(row)
                    column = kx * PATCH + channel * 16 + row
                    dy, dz = ypos - py, zpos - pz
                    if abs(dy) <= 1 and abs(dz) <= 1:
                        tap = 9 * kx + 3 * (dy + 1) + dz + 1
                        first[cell, tap * F + channel, column] = 1.0
                        last[cell, channel * TAPS + 26 - tap, column] = 1.0
    return first, last


SELECT_FIRST, SELECT_LAST = selections()


def column_of(place, x_step, y_step):
    gx = lax.rem(place[1] + x_step + place[5], place[5])
    gy = lax.rem(place[2] + y_step + place[4], place[4])
    return gx * place[4] + gy


def xor_of(left, right, size):
    total = jnp.int32(0)
    for bit in range(size.bit_length() - 1):
        one, other = lax.rem(lax.div(left, 1 << bit), 2), lax.rem(lax.div(right, 1 << bit), 2)
        total = total + jnp.where(one == other, 0, 1 << bit)
    return total


def owner_apart(owner, place, y_devices, x_devices):
    trainers = x_devices * y_devices
    column = lax.rem(owner, trainers)
    y_apart = xor_of(lax.rem(column, y_devices), place[2], y_devices)
    x_apart = xor_of(lax.div(column, y_devices), place[1], x_devices)
    return lax.div(owner, trainers), y_apart, x_apart


def pick_kernel(y_devices, x_devices, apart, trainer_of, place, *refs):
    near, chosen = refs[:y_devices], refs[y_devices]
    wanted = xor_of(place[1], apart, x_devices) * y_devices + place[2]

    def visit(owner, count):
        group, y_apart, x_apart = owner_apart(owner, place, y_devices, x_devices)
        mine = (trainer_of[owner] == wanted) & (x_apart == 0)
        for source in range(y_devices):

            @pl.when(mine & (y_apart == source))
            def _():
                chosen[count] = near[source][group]

        return count + jnp.where(mine, 1, 0)

    lax.fori_loop(0, trainer_of.shape[0], visit, jnp.int32(0))


def pick_cubes(trainer_of, place, near, y_devices, x_devices, apart):
    vmem = pl.BlockSpec(memory_space=pltpu.VMEM)
    smem = pl.BlockSpec(memory_space=pltpu.SMEM)
    return pl.pallas_call(
        functools.partial(pick_kernel, y_devices, x_devices, apart),
        out_shape=jax.ShapeDtypeStruct((TCAP, *near[0].shape[1:]), near[0].dtype),
        in_specs=[smem, smem] + [vmem] * len(near),
        out_specs=vmem,
        compiler_params=pltpu.CompilerParams(vmem_limit_bytes=16 * 1024 * 1024),
        name="pick_cubes",
    )(trainer_of, place, *near)


def dot_rows(left, right):
    return jnp.dot(left, right, preferred_element_type=jnp.float32)


def dot_lanes(left, right):
    return lax.dot_general(left, right, (((1,), (1,)), ((), ())), preferred_element_type=jnp.float32)


def patch_masks():
    row = lax.broadcasted_iota(jnp.int32, (8, 128), 0)
    lane = lax.broadcasted_iota(jnp.int32, (8, 128), 1)
    z, y = lane % 8, lane // 8 % 8
    even_z, even_y = row % 2 == 0, row // 2 % 2 == 0
    return {
        "centre": row < 4,
        "even_z": even_z,
        "even_y": even_y,
        "gather_z": jnp.where(even_z, z, 7 - z) < 7,
        "gather_y": jnp.where(even_y, y, 7 - y) < 7,
        "scatter_z": jnp.where(even_z, z, 7 - z) > 0,
        "scatter_y": jnp.where(even_y, y, 7 - y) > 0,
    }


def edge_shift(values, step, even, inside, gather):
    before, after = pltpu.roll(values, step, 1), pltpu.roll(values, 128 - step, 1)
    moved = jnp.where(even, after, before) if gather else jnp.where(even, before, after)
    return jnp.where(inside, moved, 0.0)


def patch_stack(rows, masks):
    both = jnp.where(masks["centre"], rows, pltpu.roll(rows, 4, 0))
    y_edge = edge_shift(both, 8, masks["even_y"], masks["gather_y"], True)
    upper = jnp.where(masks["centre"], both, y_edge)
    return upper, edge_shift(upper, 1, masks["even_z"], masks["gather_z"], True)


def patch_fold(upper, lower, masks):
    line = upper + edge_shift(lower, 1, masks["even_z"], masks["scatter_z"], False)
    return line + pltpu.roll(edge_shift(line, 8, masks["even_y"], masks["scatter_y"], False), 4, 0)


def store_planes(ref, x, channels):
    stacked = jnp.concatenate([part for both in channels for part in both], axis=0).astype(jnp.bfloat16)
    for kx in range(3):
        start = pl.multiple_of((x + 2 - kx) * 128, 128)
        ref[kx * PATCH : (kx + 1) * PATCH, pl.ds(start, 128)] = stacked


def train_kernel(y_devices, x_devices, *refs):
    sources = y_devices + x_devices - 1
    (trainer_of, place, first_ref, last_ref, far_first, far_last) = refs[:6]
    arrived = refs[6 : 6 + sources]
    fields_ref = refs[6 + sources]
    delta_first, delta_last, new_fields_ref = refs[7 + sources : 10 + sources]
    (
        slots,
        picked,
        cubes,
        big_first,
        big_last,
        big_last_t,
        grad_first,
        grad_last,
        now_first,
        now_last,
        brick,
        select_first,
        select_last,
        slot_sems,
        field_sem,
        select_sems,
        *pair_refs,
    ) = refs[10 + sources :]
    targets, tables, inputs, errors, hiddens, pre_grads, slopes, partial_out, raw = [
        pair_refs[kind * PAIRS : (kind + 1) * PAIRS] for kind in range(9)
    ]

    field_in = pltpu.make_async_copy(fields_ref, brick, field_sem)
    field_out = pltpu.make_async_copy(brick, new_fields_ref, field_sem)
    select_copies = [
        pltpu.make_async_copy(far_first, select_first, select_sems.at[0]),
        pltpu.make_async_copy(far_last, select_last, select_sems.at[1]),
    ]

    groups = place[3]
    for other in range(x_devices):
        picked[other] = 0

    def visit(owner, count):
        mine = trainer_of[owner] == column_of(place, 0, 0)

        @pl.when(mine)
        def _():
            group, y_apart, x_apart = owner_apart(owner, place, y_devices, x_devices)
            near = x_apart == 0
            slots[0, count] = jnp.where(near, y_apart, y_devices - 1 + x_apart)
            slots[1, count] = jnp.where(near, group, picked[x_apart])
            picked[x_apart] = picked[x_apart] + 1

        return count + jnp.where(mine, 1, 0)

    count = lax.fori_loop(0, trainer_of.shape[0], visit, jnp.int32(0))

    def fetch(slot, wait):
        for source in range(sources):

            @pl.when((slot < count) & (slots[0, slot] == source))
            def _():
                copy = pltpu.make_async_copy(
                    arrived[source].at[slots[1, slot]], cubes.at[slot], slot_sems.at[slot]
                )
                copy.wait() if wait else copy.start()

    for slot in range(TCAP):
        fetch(slot, False)

    for copy in select_copies:
        copy.start()
    field_in.start()
    for slot in range(TCAP):

        @pl.when(slot >= count)
        def _():
            cubes[slot] = jnp.zeros((2 * SUB * F, 256), jnp.bfloat16)

    masks = patch_masks()
    for ref in (*errors, *inputs):
        ref[:PATCH, 128:256] = jnp.zeros((PATCH, 128), jnp.bfloat16)
        ref[2 * PATCH :, COLS - 256 : COLS - 128] = jnp.zeros((PATCH, 128), jnp.bfloat16)
    for ref in partial_out:
        ref[:, :128] = jnp.zeros((STACK, 128), jnp.float32)
        ref[:, COLS - 128 :] = jnp.zeros((STACK, 128), jnp.float32)
    for ref in (*tables, *targets):
        ref[...] = jnp.zeros(ref.shape, ref.dtype)
    lane = lax.broadcasted_iota(jnp.int32, (8, 128), 1)
    full_weight = 2.0 * (1.0 / (jnp.full((8, 128), count, jnp.int32).astype(jnp.float32) * CELLS))
    weights = [
        jnp.where(lane // 64 + 2 * pair < count, full_weight, 0.0) for pair in range(PAIRS)
    ]
    start_first = first_ref[...].astype(jnp.bfloat16).astype(jnp.float32)
    start_last = last_ref[...].T.astype(jnp.bfloat16).astype(jnp.float32)
    now_first[...] = start_first
    now_last[...] = start_last

    for slot in range(TCAP):
        fetch(slot, True)

    low_lanes = lax.broadcasted_iota(jnp.int32, (SUB * F, 128), 1) < 64

    def spread_rows(pair, kind, put):
        rows = slice(kind * SUB * F, (kind + 1) * SUB * F)
        even = cubes[2 * pair, rows, :].astype(jnp.float32)
        odd = cubes[2 * pair + 1, rows, :].astype(jnp.float32)
        for half in range(2):
            left = even[:, half * 128 : (half + 1) * 128]
            right = odd[:, half * 128 : (half + 1) * 128]
            put(2 * half, jnp.where(low_lanes, left, pltpu.roll(right, 64, 1)))
            put(2 * half + 1, jnp.where(low_lanes, pltpu.roll(left, 64, 1), right))

    for pair in range(PAIRS):

        def put_input(cell, values):
            tables[pair][pl.ds(cell, SUB * F, 8), :] = values

        def put_target(cell, values):
            targets[pair][pl.ds(cell, SUB * F, 8), :] = values

        spread_rows(pair, 0, put_input)
        spread_rows(pair, 1, put_target)

    def stack_planes(quarter, carry):
        for pair in range(PAIRS):
            for plane in range(4):
                x = quarter * 4 + plane
                channels = [
                    patch_stack(tables[pair][pl.ds(pl.multiple_of((c * SUB + x) * 8, 8), 8), :], masks)
                    for c in range(F)
                ]
                store_planes(inputs[pair], x, channels)
        return carry

    lax.fori_loop(0, 4, stack_planes, 0)

    for copy in select_copies:
        copy.wait()
    field_in.wait()
    field_out.start()

    def train_step(step, step_carry):
        first_now = now_first[...].astype(jnp.bfloat16)
        last_now = now_last[...].astype(jnp.bfloat16)
        for cell in range(4):
            rows = slice(cell * CH, (cell + 1) * CH)
            big_first[rows, :] = (0.5 * dot_rows(first_now, select_first[cell])).astype(jnp.bfloat16)
            spread_last = dot_rows(last_now, select_last[cell])
            big_last[rows, :] = (0.5 * spread_last).astype(jnp.bfloat16)
            big_last_t[:, rows] = spread_last.T.astype(jnp.bfloat16)
        grad_first[...] = jnp.zeros(grad_first.shape, jnp.float32)
        grad_last[...] = jnp.zeros(grad_last.shape, jnp.float32)

        def columns_of(quarter):
            return pl.ds(pl.multiple_of(quarter * 512 + 128, 128), 512)

        def first_layer(pair, quarter):
            columns = columns_of(quarter)
            raw[pair][:, columns] = dot_rows(big_first[...], inputs[pair][:, columns])

        def activate(pair, quarter):
            columns = columns_of(quarter)
            for part in range(8):
                rows = slice(part * 32, (part + 1) * 32)
                half = raw[pair][rows, columns]
                curve = jnp.tanh(half)
                above = 1.0 + curve
                value = half * above
                hiddens[pair][rows, columns] = value.astype(jnp.bfloat16)
                slopes[pair][rows, columns] = above + value * (1.0 - curve)

        def last_layer(pair, quarter):
            columns = columns_of(quarter)
            partial_out[pair][:, columns] = dot_rows(big_last_t[...], hiddens[pair][:, columns])

        def find_errors(pair, quarter):
            for plane in range(4):
                x = quarter * 4 + plane
                column = pl.multiple_of((x + 1) * 128, 128)
                total = (
                    partial_out[pair][0:PATCH, pl.ds(pl.multiple_of(column + 128, 128), 128)]
                    + partial_out[pair][PATCH : 2 * PATCH, pl.ds(column, 128)]
                    + partial_out[pair][2 * PATCH :, pl.ds(pl.multiple_of(column - 128, 128), 128)]
                )
                channels = []
                for c in range(F):
                    predicted = patch_fold(
                        total[16 * c : 16 * c + 8], total[16 * c + 8 : 16 * c + 16], masks
                    )
                    row = pl.multiple_of((c * SUB + x) * 8, 8)
                    error = weights[pair] * (predicted - targets[pair][pl.ds(row, 8), :])
                    channels.append(patch_stack(error, masks))
                store_planes(errors[pair], x, channels)

        def hidden_layer(pair, quarter):
            columns = columns_of(quarter)
            raw[pair][:, columns] = dot_rows(big_last[...], errors[pair][:, columns])

        def scale(pair, quarter):
            columns = columns_of(quarter)
            for part in range(8):
                rows = slice(part * 32, (part + 1) * 32)
                product = raw[pair][rows, columns] * slopes[pair][rows, columns]
                pre_grads[pair][rows, columns] = product.astype(jnp.bfloat16)

        def gradients(pair, quarter):
            columns = columns_of(quarter)
            grad_first[...] += dot_lanes(pre_grads[pair][:, columns], inputs[pair][:, columns])
            grad_last[...] += dot_lanes(hiddens[pair][:, columns], errors[pair][:, columns])

        stages = (first_layer, activate, last_layer, find_errors, hidden_layer, scale, gradients)
        for turn in range(len(stages) + PAIRS - 1):

            def run(quarter, carry):
                for pair in range(PAIRS):
                    if 0 <= turn - pair < len(stages):
                        stages[turn - pair](pair, quarter)
                return carry

            lax.fori_loop(0, 4, run, 0)

        def folded(grad, select_ref):
            total = jnp.zeros((3 * CH, 256), jnp.float32)
            for cell in range(4):
                rest = grad[cell * CH : (cell + 1) * CH, :]
                parts = []
                for _ in range(3):
                    parts.append(rest.astype(jnp.bfloat16))
                    rest = rest - parts[-1].astype(jnp.float32)
                total = total + dot_lanes(jnp.concatenate(parts, axis=0), select_ref[cell])
            return total[:CH] + total[CH : 2 * CH] + total[2 * CH :]

        now_first[...] = now_first[...] - inner_rate * folded(grad_first, select_first)
        now_last[...] = now_last[...] - inner_rate * folded(grad_last, select_last)
        return step_carry

    lax.fori_loop(0, INNER, train_step, 0)
    delta_first[...] = start_first - now_first[...]
    delta_last[...] = (start_last - now_last[...]).T
    field_out.wait()


def train_cubes(trainer_of, place, first, last, selects, arrived, fields, y_devices, x_devices):
    vmem = pl.BlockSpec(memory_space=pltpu.VMEM)
    smem = pl.BlockSpec(memory_space=pltpu.SMEM)
    anywhere = pl.BlockSpec(memory_space=pl.ANY)
    hbm = pl.BlockSpec(memory_space=pltpu.HBM)
    return pl.pallas_call(
        functools.partial(train_kernel, y_devices, x_devices),
        out_shape=(
            jax.ShapeDtypeStruct((CH, 256), jnp.float32),
            jax.ShapeDtypeStruct((256, CH), jnp.float32),
            jax.ShapeDtypeStruct(fields.shape, fields.dtype),
        ),
        in_specs=[smem] * 2 + [vmem] * 2 + [hbm] * 2 + [anywhere] * len(arrived) + [hbm],
        out_specs=(vmem, vmem, hbm),
        scratch_shapes=[
            pltpu.SMEM((2, TCAP), jnp.int32),
            pltpu.SMEM((x_devices,), jnp.int32),
            pltpu.VMEM((TCAP, 2 * SUB * F, 256), jnp.bfloat16),
            pltpu.VMEM((4 * CH, STACK), jnp.bfloat16),
            pltpu.VMEM((4 * CH, STACK), jnp.bfloat16),
            pltpu.VMEM((STACK, 4 * CH), jnp.bfloat16),
            pltpu.VMEM((4 * CH, STACK), jnp.float32),
            pltpu.VMEM((4 * CH, STACK), jnp.float32),
            pltpu.VMEM((CH, 256), jnp.float32),
            pltpu.VMEM((CH, 256), jnp.float32),
            pltpu.VMEM(fields.shape, fields.dtype),
            pltpu.VMEM((4, 256, STACK), jnp.bfloat16),
            pltpu.VMEM((4, 256, STACK), jnp.bfloat16),
            pltpu.SemaphoreType.DMA((TCAP,)),
            pltpu.SemaphoreType.DMA,
            pltpu.SemaphoreType.DMA((2,)),
        ]
        + [pltpu.VMEM((SUB * F * 8, 128), jnp.float32)] * (2 * PAIRS)
        + [pltpu.VMEM((STACK, COLS), jnp.bfloat16)] * (2 * PAIRS)
        + [pltpu.VMEM((4 * CH, COLS), jnp.bfloat16)] * (2 * PAIRS)
        + [pltpu.VMEM((4 * CH, COLS), jnp.float32)] * PAIRS
        + [pltpu.VMEM((STACK, COLS), jnp.float32)] * PAIRS
        + [pltpu.VMEM((4 * CH, COLS), jnp.float32)] * PAIRS,
        compiler_params=pltpu.CompilerParams(vmem_limit_bytes=52 * 1024 * 1024),
        name="train_cubes",
    )(
        trainer_of,
        place,
        first,
        last,
        *selects,
        *arrived,
        fields,
    )


def viscosity_of(cells, closure):
    def unit(h, total):
        half = closure[F, h] + closure[0, h] * cells[0]
        for f in range(1, F):
            half = half + closure[f, h] * cells[f]
        return total + closure[F + 1, h] * (half + half * jnp.tanh(half))

    total = lax.fori_loop(0, HID, unit, jnp.zeros(cells[0].shape, jnp.float32), unroll=4)
    soft = jnp.maximum(total, 0.0) + jnp.log1p(jnp.exp(-jnp.abs(total)))
    return base_viscosity + viscosity_gain * soft


def evolve_kernel(closure, place, fields, x_halo, y_first, y_second, new_fields):
    up_first = lax.rem(place[2], 2) == 0
    x_cells, y_cells, z_cells = fields.shape[1:]
    row = lax.broadcasted_iota(jnp.int32, (y_cells, z_cells), 0)
    lane = lax.broadcasted_iota(jnp.int32, (y_cells, z_cells), 1)
    part = y_cells // 2

    def plane(x, carry):
        eddies = []
        for half in range(2):
            rows = pl.ds(half * part, part)
            cells = [fields[f, x, rows, :] for f in range(F)]
            eddies.append(viscosity_of(cells, closure))
        viscosity = jnp.concatenate(eddies, axis=0)
        centre = [fields[f, x] for f in range(F)]
        below = jnp.maximum(x - 1, 0)
        above = jnp.minimum(x + 1, x_cells - 1)
        for f in range(F):
            value = centre[f]
            west = jnp.where(x == 0, x_halo[1, f], fields[f, below])
            east = jnp.where(x == x_cells - 1, x_halo[0, f], fields[f, above])
            first, second = y_first[f, pl.ds(x, 1), :], y_second[f, pl.ds(x, 1), :]
            south = jnp.where(
                row == 0, jnp.where(up_first, second, first), pltpu.roll(value, 1, 0)
            )
            north = jnp.where(
                row == y_cells - 1,
                jnp.where(up_first, first, second),
                pltpu.roll(value, y_cells - 1, 0),
            )
            lower = jnp.where(lane == 0, 0.0, pltpu.roll(value, 1, 1))
            upper = jnp.where(lane == z_cells - 1, 0.0, pltpu.roll(value, z_cells - 1, 1))
            laplacian = east + west + north + south + upper + lower - 6.0 * value
            advection = (
                centre[0] * (east - west) + centre[1] * (north - south) + centre[2] * (upper - lower)
            )
            tendency = viscosity * laplacian - 0.5 * advection
            if f == 2:
                tendency = tendency + buoyancy * centre[3]
            new_fields[f, x] = value + time_step * tendency
        return carry

    lax.fori_loop(0, x_cells, plane, 0)


def evolve(closure, place, fields, x_halo, y_first, y_second):
    vmem = pl.BlockSpec(memory_space=pltpu.VMEM)
    return pl.pallas_call(
        evolve_kernel,
        out_shape=jax.ShapeDtypeStruct(fields.shape, fields.dtype),
        in_specs=[pl.BlockSpec(memory_space=pltpu.SMEM)] * 2 + [vmem] * 4,
        out_specs=vmem,
        compiler_params=pltpu.CompilerParams(vmem_limit_bytes=16 * 1024 * 1024),
        name="evolve_brick",
    )(closure, place, fields, x_halo, y_first, y_second)


def cell_order():
    order = np.zeros((256, 256), np.float32)
    for y in range(SUB):
        for z in range(SUB):
            order[y * SUB + z, (y % 2 * 2 + z % 2) * 64 + y // 2 * 8 + z // 2] = 1.0
    return order


CELL_ORDER = cell_order()


def corner_of(sample_block, place, x_step, y_step, y_cells, z_cells):
    x_devices, y_devices = place[5], place[4]
    gx = lax.rem(place[1] + x_step + x_devices, x_devices)
    gy = lax.rem(place[2] + y_step + y_devices, y_devices)
    group = jnp.minimum(place[0], place[3] - 1)
    block = sample_block[(group * x_devices + gx) * y_devices + gy]
    z_blocks = z_cells // SUB
    return lax.rem(lax.div(block, z_blocks), y_cells // SUB) * SUB, lax.rem(block, z_blocks) * SUB


def thin_kernel(
    y_cells, z_cells, sample_block, place, rows_ref, lines_ref, thin, x_buffer, y_buffer, x_sems, y_sems
):
    def corner(x_step, y_step):
        return corner_of(sample_block, place, x_step, y_step, y_cells, z_cells)

    lane = lax.broadcasted_iota(jnp.int32, (SUB, 128), 1)
    signs = (-1, 1)
    copies = []
    for side, sign in enumerate(signs):
        z_x, z_y = corner(sign, 0)[1], corner(0, sign)[1]
        x, y = side * (SUB - 1), side * (y_cells - 8)
        for field in range(F):
            copies.append(
                pltpu.make_async_copy(
                    rows_ref.at[
                        pl.ds((field * SUB + x) * y_cells, y_cells),
                        pl.ds(pl.multiple_of(lax.div(z_x, 128) * 128, 128), 128),
                    ],
                    x_buffer.at[pl.ds((side * 8 + field) * y_cells, y_cells)],
                    x_sems.at[side, field],
                )
            )
        copies.append(
            pltpu.make_async_copy(
                lines_ref.at[:, pl.ds(y, 8), pl.ds(pl.multiple_of(lax.div(z_y, 128) * 128, 128), 128)],
                y_buffer.at[side],
                y_sems.at[side],
            )
        )
    for copy in copies:
        copy.start()
    thin[...] = jnp.zeros(thin.shape, thin.dtype)
    for copy in copies:
        copy.wait()

    def moved(values, z, lane_start):
        return pltpu.roll(values, lax.rem(lane_start - lax.rem(z, 128) + 256, 128), 1)

    for side, sign in enumerate(signs):
        z = corner(0, sign)[1]
        total = jnp.zeros((SUB, 128), jnp.float32)
        for field in range(F):
            part = y_buffer[side, field * SUB : (field + 1) * SUB, side * 7, :]
            total = jnp.where(lane // SUB == field, moved(part, z, field * SUB), total)
        thin[column_of(place, 0, sign), :, side * 128 : (side + 1) * 128] = total
    for side, sign in enumerate(signs):
        y, z = corner(sign, 0)
        for half in range(2):
            total = jnp.zeros((8, 128), jnp.float32)
            for step in range(8):
                row = side * 8 * y_cells + y + half * 8 + step
                part = moved(x_buffer[pl.ds(row, 8, y_cells), :], z, step * SUB)
                total = jnp.where(lane[:8] // SUB == step, part, total)
            at = (column_of(place, sign, 0), slice(side * 8, side * 8 + 8), slice(half * 128, half * 128 + 128))
            thin[at] = total


def thin_faces(sample_block, place, brick, columns):
    fields, x_cells, y_cells, z_cells = brick.shape
    vmem = pl.BlockSpec(memory_space=pltpu.VMEM)
    smem = pl.BlockSpec(memory_space=pltpu.SMEM)
    hbm = pl.BlockSpec(memory_space=pltpu.HBM)
    return pl.pallas_call(
        functools.partial(thin_kernel, y_cells, z_cells),
        out_shape=jax.ShapeDtypeStruct((columns, SUB, 256), jnp.float32),
        in_specs=[smem, smem, hbm, hbm],
        out_specs=vmem,
        scratch_shapes=[
            pltpu.VMEM((16 * y_cells, 128), jnp.float32),
            pltpu.VMEM((2, fields * x_cells, 8, 128), jnp.float32),
            pltpu.SemaphoreType.DMA((2, fields)),
            pltpu.SemaphoreType.DMA((2,)),
        ],
        compiler_params=pltpu.CompilerParams(vmem_limit_bytes=16 * 1024 * 1024),
        name="thin_faces",
    )(
        sample_block,
        place,
        brick.reshape(fields * x_cells * y_cells, z_cells),
        brick.reshape(fields * x_cells, y_cells, z_cells),
    )


def sample_kernel(
    y_cells,
    z_cells,
    sample_block,
    place,
    brick,
    centre,
    lower,
    upper,
    own_rows,
    x_edges,
    y_edges,
    windows,
    sems,
):
    rows_of_x = y_cells
    rows_of_field = SUB * y_cells
    window_rows = F * rows_of_field
    copies = [
        pltpu.make_async_copy(
            brick.at[:, pl.ds(w * 128, 128)], windows.at[pl.ds(w * window_rows, window_rows)], sems.at[w]
        )
        for w in range(z_cells // 128)
    ]
    for copy in copies:
        copy.start()
    for copy in copies:
        copy.wait()

    def corner(x_step, y_step):
        return corner_of(sample_block, place, x_step, y_step, y_cells, z_cells)

    def piece(row, count, stride, z, lane_start):
        values = windows[pl.ds(lax.div(z, 128) * window_rows + row, count, stride), :]
        return pltpu.roll(values, lax.rem(lane_start - lax.rem(z, 128) + 256, 128), 1)

    lane = lax.broadcasted_iota(jnp.int32, (SUB, 128), 1)
    y_start, z_start = corner(0, 0)
    z_below = jnp.maximum(z_start - 1, 0)
    z_above = jnp.minimum(z_start + SUB, z_cells - 1)
    for field in range(F):
        for half in range(2):
            inside = jnp.zeros((SUB, 128), jnp.float32)
            below = jnp.zeros((SUB, 128), jnp.float32)
            above = jnp.zeros((SUB, 128), jnp.float32)
            for step in range(8):
                row = field * rows_of_field + y_start + half * 8 + step
                first = step * SUB
                inside = jnp.where(lane // SUB == step, piece(row, SUB, rows_of_x, z_start, first), inside)
                below = jnp.where(lane == first, piece(row, SUB, rows_of_x, z_below, first), below)
                last = first + SUB - 1
                above = jnp.where(lane == last, piece(row, SUB, rows_of_x, z_above, last), above)
            below = jnp.where(z_start == 0, 0.0, below)
            above = jnp.where(z_start + SUB == z_cells, 0.0, above)
            at = (slice(field * SUB, (field + 1) * SUB), slice(half * 128, (half + 1) * 128))
            centre[at] = inside
            lower[at] = jnp.where(lane % SUB == 0, below, pltpu.roll(inside, 1, 1))
            upper[at] = jnp.where(lane % SUB == SUB - 1, above, pltpu.roll(inside, 127, 1))

    def y_row(y, z):
        total = jnp.zeros((SUB, 128), jnp.float32)
        for field in range(F):
            part = piece(field * rows_of_field + y, SUB, rows_of_x, z, field * SUB)
            total = jnp.where(lane // SUB == field, part, total)
        return total

    own_rows[0] = y_row(jnp.maximum(y_start - 1, 0), z_start)
    own_rows[1] = y_row(jnp.minimum(y_start + SUB, y_cells - 1), z_start)
    up_first = lax.rem(place[2], 2) == 0
    for side in range(2):
        y = jnp.where(up_first == (side == 0), y_cells - 1, 0)
        for field in range(F):
            for w in range(z_cells // 128):
                start = w * window_rows + field * rows_of_field + y
                y_edges[side, field, :, w * 128 : (w + 1) * 128] = windows[
                    pl.ds(start, SUB, rows_of_x), :
                ]
    for side, x in enumerate((0, SUB - 1)):
        for field in range(F):
            for w in range(z_cells // 128):
                start = w * window_rows + field * rows_of_field + x * rows_of_x
                x_edges[side, field, :, w * 128 : (w + 1) * 128] = windows[pl.ds(start, rows_of_x), :]


def sample_cube(sample_block, place, brick):
    fields, x_cells, y_cells, z_cells = brick.shape
    vmem = pl.BlockSpec(memory_space=pltpu.VMEM)
    smem = pl.BlockSpec(memory_space=pltpu.SMEM)
    hbm = pl.BlockSpec(memory_space=pltpu.HBM)
    rows = fields * x_cells * y_cells
    cube = jax.ShapeDtypeStruct((F * SUB, 256), jnp.float32)
    return pl.pallas_call(
        functools.partial(sample_kernel, y_cells, z_cells),
        out_shape=(
            cube,
            cube,
            cube,
            jax.ShapeDtypeStruct((2, SUB, 128), jnp.float32),
            jax.ShapeDtypeStruct((2, fields, y_cells, z_cells), jnp.float32),
            jax.ShapeDtypeStruct((2, fields, x_cells, z_cells), jnp.float32),
        ),
        in_specs=[smem, smem, hbm],
        out_specs=(vmem,) * 6,
        scratch_shapes=[
            pltpu.VMEM((z_cells // 128 * rows, 128), jnp.float32),
            pltpu.SemaphoreType.DMA((z_cells // 128,)),
        ],
        compiler_params=pltpu.CompilerParams(vmem_limit_bytes=16 * 1024 * 1024),
        cost_estimate=pl.CostEstimate(flops=0, bytes_accessed=16_000_000, transcendentals=0),
        name="sample_cube",
    )(sample_block, place, brick.reshape(rows, z_cells))


def change_kernel(
    y_cells,
    z_cells,
    sample_block,
    place,
    closure,
    order,
    centre,
    lower,
    upper,
    own_rows,
    thin,
    payload,
):
    y_start = corner_of(sample_block, place, 0, 0, y_cells, z_cells)[0]
    row = lax.broadcasted_iota(jnp.int32, (SUB, 256), 0)
    lane = lax.broadcasted_iota(jnp.int32, (SUB, 256), 1)
    south_row = jnp.where(y_start == 0, thin[column_of(place, 0, -1), :, 128:], own_rows[0])
    north_row = jnp.where(y_start + SUB == y_cells, thin[column_of(place, 0, 1), :, :128], own_rows[1])
    face_low = thin[column_of(place, -1, 0), 8:, :]
    face_high = thin[column_of(place, 1, 0), :8, :]
    cells = [centre[f * SUB : (f + 1) * SUB, :] for f in range(F)]
    viscosity = viscosity_of(cells, closure)
    changes = []
    for f in range(F):
        value = cells[f]
        west = jnp.where(row == 0, face_low[f : f + 1, :], pltpu.roll(value, 1, 0))
        east = jnp.where(row == SUB - 1, face_high[f : f + 1, :], pltpu.roll(value, SUB - 1, 0))
        edge = pltpu.roll(south_row, (128 - f * SUB) % 128, 1)
        south = jnp.where(lane < SUB, jnp.concatenate([edge, edge], 1), pltpu.roll(value, SUB, 1))
        edge = pltpu.roll(north_row, 112 - f * SUB, 1)
        north = jnp.where(
            lane >= 256 - SUB, jnp.concatenate([edge, edge], 1), pltpu.roll(value, 256 - SUB, 1)
        )
        down = lower[f * SUB : (f + 1) * SUB, :]
        up = upper[f * SUB : (f + 1) * SUB, :]
        laplacian = east + west + north + south + up + down - 6.0 * value
        advection = cells[0] * (east - west) + cells[1] * (north - south) + cells[2] * (up - down)
        change = viscosity * laplacian - 0.5 * advection
        if f == 2:
            change = change + buoyancy * cells[3]
        changes.append(change)
    both = jnp.concatenate(cells + changes, axis=0).astype(jnp.bfloat16)
    payload[...] = dot_rows(both, order[...]).astype(jnp.bfloat16)


def cube_change(sample_block, place, closure, cube, thin, y_cells, z_cells):
    vmem = pl.BlockSpec(memory_space=pltpu.VMEM)
    smem = pl.BlockSpec(memory_space=pltpu.SMEM)
    return pl.pallas_call(
        functools.partial(change_kernel, y_cells, z_cells),
        out_shape=jax.ShapeDtypeStruct((2 * F * SUB, 256), jnp.bfloat16),
        in_specs=[smem] * 3 + [vmem] * 6,
        out_specs=vmem,
        compiler_params=pltpu.CompilerParams(vmem_limit_bytes=16 * 1024 * 1024),
        name="cube_change",
    )(sample_block, place, closure, jnp.asarray(CELL_ORDER, jnp.bfloat16), *cube, thin)


def on_device(
    fields, closure_in, closure_bias, closure_out, master, momentum, sample_block, sample_trainer
):
    group_count = lax.axis_size("grp")
    x_devices = lax.axis_size("gx")
    y_devices = lax.axis_size("gy")
    trainers = x_devices * y_devices
    my_group = lax.axis_index("grp")
    my_column = lax.axis_index("gx") * y_devices + lax.axis_index("gy")
    is_trainer = my_group == group_count - 1
    everyone = ("grp", "gx", "gy")
    sim_groups = group_count - 1
    first_trainer = sim_groups * trainers
    brick = fields[0]
    y_cells, z_cells = brick.shape[2:]
    closure = jnp.concatenate(
        [0.5 * closure_in.T, 0.5 * closure_bias[None], closure_out[None]], axis=0
    )
    place = jnp.stack(
        [
            my_group,
            lax.axis_index("gx"),
            lax.axis_index("gy"),
            jnp.int32(sim_groups),
            jnp.int32(y_devices),
            jnp.int32(x_devices),
        ]
    ).astype(jnp.int32)

    def pairs(x_step, even_step):
        found = []
        for g in range(sim_groups):
            for c in range(trainers):
                gx, gy = c // y_devices, c % y_devices
                gx = (gx + x_step) % x_devices
                gy = (gy + (even_step if gy % 2 == 0 else -even_step)) % y_devices
                found.append((g * trainers + c, (g * x_devices + gx) * y_devices + gy))
        return found

    def x_neighbours(edges):
        if x_devices == 2:
            return lax.ppermute(edges, everyone, pairs(1, 0))
        from_high = lax.ppermute(edges[0], everyone, pairs(-1, 0))
        return jnp.stack([from_high, lax.ppermute(edges[1], everyone, pairs(1, 0))])

    def y_neighbours(for_first, for_second):
        return (
            lax.ppermute(for_first, everyone, pairs(0, 1)),
            lax.ppermute(for_second, everyone, pairs(0, -1)),
        )

    def swap(distance):
        return [(first_trainer + c, first_trainer + (c ^ distance)) for c in range(trainers)]

    def to_trainers(payload):
        return jnp.stack(
            [
                lax.ppermute(
                    payload,
                    everyone,
                    [(g * trainers + c, first_trainer + c) for c in range(trainers)],
                )
                for g in range(sim_groups)
            ]
        )

    def from_line(held):
        return [lax.ppermute(held, everyone, swap(apart)) for apart in range(1, y_devices)]

    def across(apart, held):
        return lax.ppermute(held, everyone, swap(apart * y_devices))

    thin = thin_faces(sample_block, place, brick, trainers)
    *cube, x_edges, y_edges = sample_cube(sample_block, place, brick)
    thin = lax.all_to_all(thin, ("gx", "gy"), split_axis=0, concat_axis=0, tiled=True)
    payload = cube_change(sample_block, place, closure, cube, thin, y_cells, z_cells)
    landed = to_trainers(payload)
    x_edges, y_edges, landed = lax.optimization_barrier((x_edges, y_edges, landed))
    halo = (x_neighbours(x_edges), *y_neighbours(y_edges[0], y_edges[1]))
    near = [landed, *from_line(landed)]
    far = [
        across(apart, pick_cubes(sample_trainer, place, near, y_devices, x_devices, apart))
        for apart in range(1, x_devices)
    ]
    arrived = [*near, *far]

    first_count = CH * TAPS * F
    first = jnp.pad(master[:first_count].reshape(CH, TAPS * F), ((0, 0), (0, 256 - TAPS * F)))
    last = jnp.pad(master[first_count:].reshape(TAPS * F, CH), ((0, 256 - TAPS * F), (0, 0)))

    first, last, *selects = lax.optimization_barrier(
        (first, last, jnp.asarray(SELECT_FIRST, jnp.bfloat16), jnp.asarray(SELECT_LAST, jnp.bfloat16))
    )

    def train_here():
        delta_first, delta_last, new_brick = train_cubes(
            sample_trainer, place, first, last, selects, arrived, brick, y_devices, x_devices
        )
        delta = jnp.concatenate(
            [delta_first[:, : TAPS * F].reshape(-1), delta_last[: TAPS * F].reshape(-1)]
        )
        return delta, new_brick

    def evolve_here():
        new_brick = evolve(closure, place, brick, *halo)
        return jnp.zeros((NPARAM,), jnp.float32), new_brick

    delta, new_brick = lax.cond(is_trainer, train_here, evolve_here)

    line = sum(from_line(delta), delta)
    total = sum((across(apart, line) for apart in range(1, x_devices)), line)
    final = jnp.where(is_trainer, total, 0.0)
    for g in range(sim_groups):
        pairs = [(first_trainer + c, g * trainers + c) for c in range(trainers)]
        final = final + lax.ppermute(total, everyone, pairs)

    share_size = NPARAM // (group_count * trainers)
    share_start = (my_group * trainers + my_column) * share_size
    momentum_share = lax.dynamic_slice_in_dim(momentum, share_start, share_size)
    master_share = lax.dynamic_slice_in_dim(master, share_start, share_size)
    inverse = 1.0 / jnp.sqrt(jnp.sum(final * final) / NPARAM + norm_epsilon)
    delta_share = lax.dynamic_slice_in_dim(final, share_start, share_size)
    new_momentum = momentum_decay * momentum_share + delta_share * inverse
    new_master = master_share - outer_rate * new_momentum
    return (new_brick[None], new_master, new_momentum)


def solution(mesh):
    in_specs = (P("grp", None, "gx", "gy", None), P(), P(), P(), P(), P(), P(), P())
    out_specs = (P("grp", None, "gx", "gy", None), P(("grp", "gx", "gy")), P(("grp", "gx", "gy")))
    return jax.shard_map(
        on_device, mesh=mesh, in_specs=in_specs, out_specs=out_specs, check_vma=False
    )
```

```python
import functools

import jax
import jax.numpy as jnp
import numpy as np
from jax import lax
from jax.experimental import pallas as pl
from jax.experimental.pallas import tpu as pltpu
from jax.sharding import PartitionSpec as P

F = 5
CH = 64
HID = 64
SUB = 16
TCAP = 6
INNER = 3
CELLS = 4096
NPARAM = 17280
TAPS = 27
PAIRS = TCAP // 2
COLS = (SUB + 2) * 128
PATCH = 16 * F
STACK = 3 * PATCH

time_step = 0.1
base_viscosity = 0.02
viscosity_gain = 0.2
buoyancy = 0.5
inner_rate = 0.02
outer_rate = 0.01
momentum_decay = 0.9
norm_epsilon = 1e-06


def patch_position(row):
    group, py, pz = row // 4, row // 2 % 2, row % 2
    ypos = py + 1 if group in (0, 2) else (3 if py == 0 else 0)
    zpos = pz + 1 if group in (0, 1) else (3 if pz == 0 else 0)
    return ypos - 1, zpos - 1


def selections():
    first = np.zeros((4, 256, STACK), np.float32)
    last = np.zeros((4, 256, STACK), np.float32)
    for cell in range(4):
        py, pz = cell // 2, cell % 2
        for kx in range(3):
            for channel in range(F):
                for row in range(16):
                    ypos, zpos = patch_position(row)
                    column = kx * PATCH + channel * 16 + row
                    dy, dz = ypos - py, zpos - pz
                    if abs(dy) <= 1 and abs(dz) <= 1:
                        tap = 9 * kx + 3 * (dy + 1) + dz + 1
                        first[cell, tap * F + channel, column] = 1.0
                        last[cell, channel * TAPS + 26 - tap, column] = 1.0
    return first, last


SELECT_FIRST, SELECT_LAST = selections()


def column_of(place, x_step, y_step):
    gx = lax.rem(place[1] + x_step + place[5], place[5])
    gy = lax.rem(place[2] + y_step + place[4], place[4])
    return gx * place[4] + gy


def xor_of(left, right, size):
    total = jnp.int32(0)
    for bit in range(size.bit_length() - 1):
        one, other = lax.rem(lax.div(left, 1 << bit), 2), lax.rem(lax.div(right, 1 << bit), 2)
        total = total + jnp.where(one == other, 0, 1 << bit)
    return total


def owner_apart(owner, place, y_devices, x_devices):
    trainers = x_devices * y_devices
    column = lax.rem(owner, trainers)
    y_apart = xor_of(lax.rem(column, y_devices), place[2], y_devices)
    x_apart = xor_of(lax.div(column, y_devices), place[1], x_devices)
    return lax.rem(lax.div(owner, trainers) + 1, 3), y_apart, x_apart


def pick_kernel(y_devices, x_devices, apart, trainer_of, place, *refs):
    near, chosen = refs[:y_devices], refs[y_devices]
    wanted = xor_of(place[1], apart, x_devices) * y_devices + place[2]

    def visit(owner, count):
        group, y_apart, x_apart = owner_apart(owner, place, y_devices, x_devices)
        mine = (trainer_of[owner] == wanted) & (x_apart == 0)
        for source in range(y_devices):

            @pl.when(mine & (y_apart == source))
            def _():
                chosen[count] = near[source][group]

        return count + jnp.where(mine, 1, 0)

    lax.fori_loop(0, trainer_of.shape[0], visit, jnp.int32(0))


def pick_cubes(trainer_of, place, near, y_devices, x_devices, apart):
    vmem = pl.BlockSpec(memory_space=pltpu.VMEM)
    smem = pl.BlockSpec(memory_space=pltpu.SMEM)
    return pl.pallas_call(
        functools.partial(pick_kernel, y_devices, x_devices, apart),
        out_shape=jax.ShapeDtypeStruct((TCAP, *near[0].shape[1:]), near[0].dtype),
        in_specs=[smem, smem] + [vmem] * len(near),
        out_specs=vmem,
        compiler_params=pltpu.CompilerParams(vmem_limit_bytes=16 * 1024 * 1024),
        name="pick_cubes",
    )(trainer_of, place, *near)


def dot_rows(left, right):
    return jnp.dot(left, right, preferred_element_type=jnp.float32)


def dot_lanes(left, right):
    return lax.dot_general(left, right, (((1,), (1,)), ((), ())), preferred_element_type=jnp.float32)


def patch_masks():
    row = lax.broadcasted_iota(jnp.int32, (8, 128), 0)
    lane = lax.broadcasted_iota(jnp.int32, (8, 128), 1)
    z, y = lane % 8, lane // 8 % 8
    even_z, even_y = row % 2 == 0, row // 2 % 2 == 0
    return {
        "centre": row < 4,
        "even_z": even_z,
        "even_y": even_y,
        "gather_z": jnp.where(even_z, z, 7 - z) < 7,
        "gather_y": jnp.where(even_y, y, 7 - y) < 7,
        "scatter_z": jnp.where(even_z, z, 7 - z) > 0,
        "scatter_y": jnp.where(even_y, y, 7 - y) > 0,
    }


def edge_shift(values, step, even, inside, gather):
    before, after = pltpu.roll(values, step, 1), pltpu.roll(values, 128 - step, 1)
    moved = jnp.where(even, after, before) if gather else jnp.where(even, before, after)
    return jnp.where(inside, moved, 0.0)


def patch_stack(rows, masks):
    both = jnp.where(masks["centre"], rows, pltpu.roll(rows, 4, 0))
    y_edge = edge_shift(both, 8, masks["even_y"], masks["gather_y"], True)
    upper = jnp.where(masks["centre"], both, y_edge)
    return upper, edge_shift(upper, 1, masks["even_z"], masks["gather_z"], True)


def patch_fold(upper, lower, masks):
    line = upper + edge_shift(lower, 1, masks["even_z"], masks["scatter_z"], False)
    return line + pltpu.roll(edge_shift(line, 8, masks["even_y"], masks["scatter_y"], False), 4, 0)


def store_planes(ref, x, channels):
    stacked = jnp.concatenate([part for both in channels for part in both], axis=0).astype(jnp.bfloat16)
    for kx in range(3):
        start = pl.multiple_of((x + 2 - kx) * 128, 128)
        ref[kx * PATCH : (kx + 1) * PATCH, pl.ds(start, 128)] = stacked


def train_kernel(y_devices, x_devices, *refs):
    sources = y_devices + x_devices - 1
    (trainer_of, place, first_ref, last_ref, far_first, far_last) = refs[:6]
    arrived = refs[6 : 6 + sources]
    fields_ref = refs[6 + sources]
    delta_first, delta_last, new_fields_ref = refs[7 + sources : 10 + sources]
    (
        slots,
        picked,
        cubes,
        big_first,
        big_last,
        big_last_t,
        grad_first,
        grad_last,
        now_first,
        now_last,
        brick,
        select_first,
        select_last,
        slot_sems,
        field_sem,
        select_sems,
        *pair_refs,
    ) = refs[10 + sources :]
    targets, tables, inputs, errors, hiddens, pre_grads, slopes, partial_out, raw = [
        pair_refs[kind * PAIRS : (kind + 1) * PAIRS] for kind in range(9)
    ]

    field_in = pltpu.make_async_copy(fields_ref, brick, field_sem)
    field_out = pltpu.make_async_copy(brick, new_fields_ref, field_sem)
    select_copies = [
        pltpu.make_async_copy(far_first, select_first, select_sems.at[0]),
        pltpu.make_async_copy(far_last, select_last, select_sems.at[1]),
    ]

    groups = place[3]
    for other in range(x_devices):
        picked[other] = 0

    def visit(owner, count):
        mine = trainer_of[owner] == column_of(place, 0, 0)

        @pl.when(mine)
        def _():
            group, y_apart, x_apart = owner_apart(owner, place, y_devices, x_devices)
            near = x_apart == 0
            slots[0, count] = jnp.where(near, y_apart, y_devices - 1 + x_apart)
            slots[1, count] = jnp.where(near, group, picked[x_apart])
            picked[x_apart] = picked[x_apart] + 1

        return count + jnp.where(mine, 1, 0)

    count = lax.fori_loop(0, trainer_of.shape[0], visit, jnp.int32(0))

    def fetch(slot, wait):
        for source in range(sources):

            @pl.when((slot < count) & (slots[0, slot] == source))
            def _():
                copy = pltpu.make_async_copy(
                    arrived[source].at[slots[1, slot]], cubes.at[slot], slot_sems.at[slot]
                )
                copy.wait() if wait else copy.start()

    for slot in range(TCAP):
        fetch(slot, False)

    for copy in select_copies:
        copy.start()
    field_in.start()
    for slot in range(TCAP):

        @pl.when(slot >= count)
        def _():
            cubes[slot] = jnp.zeros((2 * SUB * F, 256), jnp.bfloat16)

    masks = patch_masks()
    for ref in (*errors, *inputs):
        ref[:PATCH, 128:256] = jnp.zeros((PATCH, 128), jnp.bfloat16)
        ref[2 * PATCH :, COLS - 256 : COLS - 128] = jnp.zeros((PATCH, 128), jnp.bfloat16)
    for ref in partial_out:
        ref[:, :128] = jnp.zeros((STACK, 128), jnp.float32)
        ref[:, COLS - 128 :] = jnp.zeros((STACK, 128), jnp.float32)
    for ref in (*tables, *targets):
        ref[...] = jnp.zeros(ref.shape, ref.dtype)
    lane = lax.broadcasted_iota(jnp.int32, (8, 128), 1)
    full_weight = 2.0 * (1.0 / (jnp.full((8, 128), count, jnp.int32).astype(jnp.float32) * CELLS))
    weights = [
        jnp.where(lane // 64 + 2 * pair < count, full_weight, 0.0) for pair in range(PAIRS)
    ]
    start_first = first_ref[...].astype(jnp.bfloat16).astype(jnp.float32)
    start_last = last_ref[...].T.astype(jnp.bfloat16).astype(jnp.float32)
    now_first[...] = start_first
    now_last[...] = start_last

    for slot in range(TCAP):
        fetch(slot, True)

    low_lanes = lax.broadcasted_iota(jnp.int32, (SUB * F, 128), 1) < 64

    def spread_rows(pair, kind, put):
        rows = slice(kind * SUB * F, (kind + 1) * SUB * F)
        even = cubes[2 * pair, rows, :].astype(jnp.float32)
        odd = cubes[2 * pair + 1, rows, :].astype(jnp.float32)
        for half in range(2):
            left = even[:, half * 128 : (half + 1) * 128]
            right = odd[:, half * 128 : (half + 1) * 128]
            put(2 * half, jnp.where(low_lanes, left, pltpu.roll(right, 64, 1)))
            put(2 * half + 1, jnp.where(low_lanes, pltpu.roll(left, 64, 1), right))

    for pair in range(PAIRS):

        def put_input(cell, values):
            tables[pair][pl.ds(cell, SUB * F, 8), :] = values

        def put_target(cell, values):
            targets[pair][pl.ds(cell, SUB * F, 8), :] = values

        spread_rows(pair, 0, put_input)
        spread_rows(pair, 1, put_target)

    def stack_planes(quarter, carry):
        for pair in range(PAIRS):
            for plane in range(4):
                x = quarter * 4 + plane
                channels = [
                    patch_stack(tables[pair][pl.ds(pl.multiple_of((c * SUB + x) * 8, 8), 8), :], masks)
                    for c in range(F)
                ]
                store_planes(inputs[pair], x, channels)
        return carry

    lax.fori_loop(0, 4, stack_planes, 0)

    for copy in select_copies:
        copy.wait()
    field_in.wait()
    field_out.start()

    def train_step(step, step_carry):
        first_now = now_first[...].astype(jnp.bfloat16)
        last_now = now_last[...].astype(jnp.bfloat16)
        for cell in range(4):
            rows = slice(cell * CH, (cell + 1) * CH)
            big_first[rows, :] = (0.5 * dot_rows(first_now, select_first[cell])).astype(jnp.bfloat16)
            spread_last = dot_rows(last_now, select_last[cell])
            big_last[rows, :] = (0.5 * spread_last).astype(jnp.bfloat16)
            big_last_t[:, rows] = spread_last.T.astype(jnp.bfloat16)
        grad_first[...] = jnp.zeros(grad_first.shape, jnp.float32)
        grad_last[...] = jnp.zeros(grad_last.shape, jnp.float32)

        def columns_of(quarter):
            return pl.ds(pl.multiple_of(quarter * 512 + 128, 128), 512)

        def first_layer(pair, quarter):
            columns = columns_of(quarter)
            raw[pair][:, columns] = dot_rows(big_first[...], inputs[pair][:, columns])

        def activate(pair, quarter):
            columns = columns_of(quarter)
            for part in range(8):
                rows = slice(part * 32, (part + 1) * 32)
                half = raw[pair][rows, columns]
                curve = jnp.tanh(half)
                above = 1.0 + curve
                value = half * above
                hiddens[pair][rows, columns] = value.astype(jnp.bfloat16)
                slopes[pair][rows, columns] = above + value * (1.0 - curve)

        def last_layer(pair, quarter):
            columns = columns_of(quarter)
            partial_out[pair][:, columns] = dot_rows(big_last_t[...], hiddens[pair][:, columns])

        def find_errors(pair, quarter):
            for plane in range(4):
                x = quarter * 4 + plane
                column = pl.multiple_of((x + 1) * 128, 128)
                total = (
                    partial_out[pair][0:PATCH, pl.ds(pl.multiple_of(column + 128, 128), 128)]
                    + partial_out[pair][PATCH : 2 * PATCH, pl.ds(column, 128)]
                    + partial_out[pair][2 * PATCH :, pl.ds(pl.multiple_of(column - 128, 128), 128)]
                )
                channels = []
                for c in range(F):
                    predicted = patch_fold(
                        total[16 * c : 16 * c + 8], total[16 * c + 8 : 16 * c + 16], masks
                    )
                    row = pl.multiple_of((c * SUB + x) * 8, 8)
                    error = weights[pair] * (predicted - targets[pair][pl.ds(row, 8), :])
                    channels.append(patch_stack(error, masks))
                store_planes(errors[pair], x, channels)

        def hidden_layer(pair, quarter):
            columns = columns_of(quarter)
            raw[pair][:, columns] = dot_rows(big_last[...], errors[pair][:, columns])

        def scale(pair, quarter):
            columns = columns_of(quarter)
            for part in range(8):
                rows = slice(part * 32, (part + 1) * 32)
                product = raw[pair][rows, columns] * slopes[pair][rows, columns]
                pre_grads[pair][rows, columns] = product.astype(jnp.bfloat16)

        def gradients(pair, quarter):
            columns = columns_of(quarter)
            grad_first[...] += dot_lanes(pre_grads[pair][:, columns], inputs[pair][:, columns])
            grad_last[...] += dot_lanes(hiddens[pair][:, columns], errors[pair][:, columns])

        stages = (first_layer, activate, last_layer, find_errors, hidden_layer, scale, gradients)
        for turn in range(len(stages) + PAIRS - 1):

            def run(quarter, carry):
                for pair in range(PAIRS):
                    if 0 <= turn - pair < len(stages):
                        stages[turn - pair](pair, quarter)
                return carry

            lax.fori_loop(0, 4, run, 0, unroll=2)

        def folded(grad, select_ref):
            total = jnp.zeros((3 * CH, 256), jnp.float32)
            for cell in range(4):
                rest = grad[cell * CH : (cell + 1) * CH, :]
                parts = []
                for _ in range(3):
                    parts.append(rest.astype(jnp.bfloat16))
                    rest = rest - parts[-1].astype(jnp.float32)
                total = total + dot_lanes(jnp.concatenate(parts, axis=0), select_ref[cell])
            return total[:CH] + total[CH : 2 * CH] + total[2 * CH :]

        now_first[...] = now_first[...] - inner_rate * folded(grad_first, select_first)
        now_last[...] = now_last[...] - inner_rate * folded(grad_last, select_last)
        return step_carry

    lax.fori_loop(0, INNER, train_step, 0)
    delta_first[...] = start_first - now_first[...]
    delta_last[...] = (start_last - now_last[...]).T
    field_out.wait()


def train_cubes(trainer_of, place, first, last, selects, arrived, fields, y_devices, x_devices):
    vmem = pl.BlockSpec(memory_space=pltpu.VMEM)
    smem = pl.BlockSpec(memory_space=pltpu.SMEM)
    anywhere = pl.BlockSpec(memory_space=pl.ANY)
    hbm = pl.BlockSpec(memory_space=pltpu.HBM)
    return pl.pallas_call(
        functools.partial(train_kernel, y_devices, x_devices),
        out_shape=(
            jax.ShapeDtypeStruct((CH, 256), jnp.float32),
            jax.ShapeDtypeStruct((256, CH), jnp.float32),
            jax.ShapeDtypeStruct(fields.shape, fields.dtype),
        ),
        in_specs=[smem] * 2 + [vmem] * 2 + [hbm] * 2 + [anywhere] * len(arrived) + [hbm],
        out_specs=(vmem, vmem, hbm),
        scratch_shapes=[
            pltpu.SMEM((2, TCAP), jnp.int32),
            pltpu.SMEM((x_devices,), jnp.int32),
            pltpu.VMEM((TCAP, 2 * SUB * F, 256), jnp.bfloat16),
            pltpu.VMEM((4 * CH, STACK), jnp.bfloat16),
            pltpu.VMEM((4 * CH, STACK), jnp.bfloat16),
            pltpu.VMEM((STACK, 4 * CH), jnp.bfloat16),
            pltpu.VMEM((4 * CH, STACK), jnp.float32),
            pltpu.VMEM((4 * CH, STACK), jnp.float32),
            pltpu.VMEM((CH, 256), jnp.float32),
            pltpu.VMEM((CH, 256), jnp.float32),
            pltpu.VMEM(fields.shape, fields.dtype),
            pltpu.VMEM((4, 256, STACK), jnp.bfloat16),
            pltpu.VMEM((4, 256, STACK), jnp.bfloat16),
            pltpu.SemaphoreType.DMA((TCAP,)),
            pltpu.SemaphoreType.DMA,
            pltpu.SemaphoreType.DMA((2,)),
        ]
        + [pltpu.VMEM((SUB * F * 8, 128), jnp.float32)] * (2 * PAIRS)
        + [pltpu.VMEM((STACK, COLS), jnp.bfloat16)] * (2 * PAIRS)
        + [pltpu.VMEM((4 * CH, COLS), jnp.bfloat16)] * (2 * PAIRS)
        + [pltpu.VMEM((4 * CH, COLS), jnp.float32)] * PAIRS
        + [pltpu.VMEM((STACK, COLS), jnp.float32)] * PAIRS
        + [pltpu.VMEM((4 * CH, COLS), jnp.float32)] * PAIRS,
        compiler_params=pltpu.CompilerParams(vmem_limit_bytes=52 * 1024 * 1024),
        name="train_cubes",
    )(
        trainer_of,
        place,
        first,
        last,
        *selects,
        *arrived,
        fields,
    )


def viscosity_of(cells, closure):
    def unit(h, total):
        half = closure[F, h] + closure[0, h] * cells[0]
        for f in range(1, F):
            half = half + closure[f, h] * cells[f]
        return total + closure[F + 1, h] * (half + half * jnp.tanh(half))

    total = lax.fori_loop(0, HID, unit, jnp.zeros(cells[0].shape, jnp.float32), unroll=4)
    soft = jnp.maximum(total, 0.0) + jnp.log1p(jnp.exp(-jnp.abs(total)))
    return base_viscosity + viscosity_gain * soft


def viscosity_kernel(closure, fields, viscosity):
    x_cells, y_cells = fields.shape[1:3]
    part = y_cells // 2

    def plane(x, carry):
        for half in range(2):
            rows = pl.ds(half * part, part)
            viscosity[x, rows, :] = viscosity_of([fields[f, x, rows, :] for f in range(F)], closure)
        return carry

    lax.fori_loop(0, x_cells, plane, 0)


def brick_viscosity(closure, fields):
    vmem = pl.BlockSpec(memory_space=pltpu.VMEM)
    return pl.pallas_call(
        viscosity_kernel,
        out_shape=jax.ShapeDtypeStruct(fields.shape[1:], fields.dtype),
        in_specs=[pl.BlockSpec(memory_space=pltpu.SMEM), vmem],
        out_specs=vmem,
        compiler_params=pltpu.CompilerParams(vmem_limit_bytes=16 * 1024 * 1024),
        name="brick_viscosity",
    )(closure, fields)


def evolve_kernel(place, viscosity, fields, x_halo, y_first, y_second, new_fields):
    up_first = lax.rem(place[2], 2) == 0
    x_cells, y_cells, z_cells = fields.shape[1:]
    row = lax.broadcasted_iota(jnp.int32, (y_cells, z_cells), 0)
    lane = lax.broadcasted_iota(jnp.int32, (y_cells, z_cells), 1)

    def plane(x, carry):
        centre = [fields[f, x] for f in range(F)]
        below = jnp.maximum(x - 1, 0)
        above = jnp.minimum(x + 1, x_cells - 1)
        for f in range(F):
            value = centre[f]
            west = jnp.where(x == 0, x_halo[1, f], fields[f, below])
            east = jnp.where(x == x_cells - 1, x_halo[0, f], fields[f, above])
            first, second = y_first[f, pl.ds(x, 1), :], y_second[f, pl.ds(x, 1), :]
            south = jnp.where(
                row == 0, jnp.where(up_first, second, first), pltpu.roll(value, 1, 0)
            )
            north = jnp.where(
                row == y_cells - 1,
                jnp.where(up_first, first, second),
                pltpu.roll(value, y_cells - 1, 0),
            )
            lower = jnp.where(lane == 0, 0.0, pltpu.roll(value, 1, 1))
            upper = jnp.where(lane == z_cells - 1, 0.0, pltpu.roll(value, z_cells - 1, 1))
            laplacian = east + west + north + south + upper + lower - 6.0 * value
            advection = (
                centre[0] * (east - west) + centre[1] * (north - south) + centre[2] * (upper - lower)
            )
            tendency = viscosity[x] * laplacian - 0.5 * advection
            if f == 2:
                tendency = tendency + buoyancy * centre[3]
            new_fields[f, x] = value + time_step * tendency
        return carry

    lax.fori_loop(0, x_cells, plane, 0)


def evolve(place, viscosity, fields, x_halo, y_first, y_second):
    vmem = pl.BlockSpec(memory_space=pltpu.VMEM)
    return pl.pallas_call(
        evolve_kernel,
        out_shape=jax.ShapeDtypeStruct(fields.shape, fields.dtype),
        in_specs=[pl.BlockSpec(memory_space=pltpu.SMEM)] + [vmem] * 5,
        out_specs=vmem,
        compiler_params=pltpu.CompilerParams(vmem_limit_bytes=16 * 1024 * 1024),
        name="evolve_brick",
    )(place, viscosity, fields, x_halo, y_first, y_second)


def cell_order():
    order = np.zeros((256, 256), np.float32)
    for y in range(SUB):
        for z in range(SUB):
            order[y * SUB + z, (y % 2 * 2 + z % 2) * 64 + y // 2 * 8 + z // 2] = 1.0
    return order


CELL_ORDER = cell_order()


def corner_of(sample_block, place, x_step, y_step, y_cells, z_cells):
    x_devices, y_devices = place[5], place[4]
    gx = lax.rem(place[1] + x_step + x_devices, x_devices)
    gy = lax.rem(place[2] + y_step + y_devices, y_devices)
    group = jnp.minimum(place[0], place[3] - 1)
    block = sample_block[(group * x_devices + gx) * y_devices + gy]
    z_blocks = z_cells // SUB
    return lax.rem(lax.div(block, z_blocks), y_cells // SUB) * SUB, lax.rem(block, z_blocks) * SUB


def thin_kernel(
    y_cells, z_cells, sample_block, place, rows_ref, lines_ref, thin, x_buffer, y_buffer, x_sems, y_sems
):
    def corner(x_step, y_step):
        return corner_of(sample_block, place, x_step, y_step, y_cells, z_cells)

    lane = lax.broadcasted_iota(jnp.int32, (SUB, 128), 1)
    signs = (-1, 1)
    copies = []
    for side, sign in enumerate(signs):
        z_x, z_y = corner(sign, 0)[1], corner(0, sign)[1]
        x, y = side * (SUB - 1), side * (y_cells - 8)
        for field in range(F):
            copies.append(
                pltpu.make_async_copy(
                    rows_ref.at[
                        pl.ds((field * SUB + x) * y_cells, y_cells),
                        pl.ds(pl.multiple_of(lax.div(z_x, 128) * 128, 128), 128),
                    ],
                    x_buffer.at[pl.ds((side * 8 + field) * y_cells, y_cells)],
                    x_sems.at[side, field],
                )
            )
        copies.append(
            pltpu.make_async_copy(
                lines_ref.at[:, pl.ds(y, 8), pl.ds(pl.multiple_of(lax.div(z_y, 128) * 128, 128), 128)],
                y_buffer.at[side],
                y_sems.at[side],
            )
        )
    for copy in copies:
        copy.start()
    thin[...] = jnp.zeros(thin.shape, thin.dtype)
    for copy in copies:
        copy.wait()

    def moved(values, z, lane_start):
        return pltpu.roll(values, lax.rem(lane_start - lax.rem(z, 128) + 256, 128), 1)

    for side, sign in enumerate(signs):
        z = corner(0, sign)[1]
        total = jnp.zeros((SUB, 128), jnp.float32)
        for field in range(F):
            part = y_buffer[side, field * SUB : (field + 1) * SUB, side * 7, :]
            total = jnp.where(lane // SUB == field, moved(part, z, field * SUB), total)
        thin[column_of(place, 0, sign), :, side * 128 : (side + 1) * 128] = total
    for side, sign in enumerate(signs):
        y, z = corner(sign, 0)
        for half in range(2):
            total = jnp.zeros((8, 128), jnp.float32)
            for step in range(8):
                row = side * 8 * y_cells + y + half * 8 + step
                part = moved(x_buffer[pl.ds(row, 8, y_cells), :], z, step * SUB)
                total = jnp.where(lane[:8] // SUB == step, part, total)
            at = (column_of(place, sign, 0), slice(side * 8, side * 8 + 8), slice(half * 128, half * 128 + 128))
            thin[at] = total


def thin_faces(sample_block, place, brick, columns):
    fields, x_cells, y_cells, z_cells = brick.shape
    vmem = pl.BlockSpec(memory_space=pltpu.VMEM)
    smem = pl.BlockSpec(memory_space=pltpu.SMEM)
    hbm = pl.BlockSpec(memory_space=pltpu.HBM)
    return pl.pallas_call(
        functools.partial(thin_kernel, y_cells, z_cells),
        out_shape=jax.ShapeDtypeStruct((columns, SUB, 256), jnp.float32),
        in_specs=[smem, smem, hbm, hbm],
        out_specs=vmem,
        scratch_shapes=[
            pltpu.VMEM((16 * y_cells, 128), jnp.float32),
            pltpu.VMEM((2, fields * x_cells, 8, 128), jnp.float32),
            pltpu.SemaphoreType.DMA((2, fields)),
            pltpu.SemaphoreType.DMA((2,)),
        ],
        compiler_params=pltpu.CompilerParams(vmem_limit_bytes=16 * 1024 * 1024),
        name="thin_faces",
    )(
        sample_block,
        place,
        brick.reshape(fields * x_cells * y_cells, z_cells),
        brick.reshape(fields * x_cells, y_cells, z_cells),
    )


def sample_kernel(
    y_cells,
    z_cells,
    sample_block,
    place,
    brick,
    centre,
    lower,
    upper,
    own_rows,
    x_edges,
    y_edges,
    windows,
    sems,
):
    rows_of_x = y_cells
    rows_of_field = SUB * y_cells
    window_rows = F * rows_of_field
    copies = [
        pltpu.make_async_copy(
            brick.at[:, pl.ds(w * 128, 128)], windows.at[pl.ds(w * window_rows, window_rows)], sems.at[w]
        )
        for w in range(z_cells // 128)
    ]
    for copy in copies:
        copy.start()
    for copy in copies:
        copy.wait()

    def corner(x_step, y_step):
        return corner_of(sample_block, place, x_step, y_step, y_cells, z_cells)

    def piece(row, count, stride, z, lane_start):
        values = windows[pl.ds(lax.div(z, 128) * window_rows + row, count, stride), :]
        return pltpu.roll(values, lax.rem(lane_start - lax.rem(z, 128) + 256, 128), 1)

    lane = lax.broadcasted_iota(jnp.int32, (SUB, 128), 1)
    y_start, z_start = corner(0, 0)
    z_below = jnp.maximum(z_start - 1, 0)
    z_above = jnp.minimum(z_start + SUB, z_cells - 1)
    for field in range(F):
        for half in range(2):
            inside = jnp.zeros((SUB, 128), jnp.float32)
            below = jnp.zeros((SUB, 128), jnp.float32)
            above = jnp.zeros((SUB, 128), jnp.float32)
            for step in range(8):
                row = field * rows_of_field + y_start + half * 8 + step
                first = step * SUB
                inside = jnp.where(lane // SUB == step, piece(row, SUB, rows_of_x, z_start, first), inside)
                below = jnp.where(lane == first, piece(row, SUB, rows_of_x, z_below, first), below)
                last = first + SUB - 1
                above = jnp.where(lane == last, piece(row, SUB, rows_of_x, z_above, last), above)
            below = jnp.where(z_start == 0, 0.0, below)
            above = jnp.where(z_start + SUB == z_cells, 0.0, above)
            at = (slice(field * SUB, (field + 1) * SUB), slice(half * 128, (half + 1) * 128))
            centre[at] = inside
            lower[at] = jnp.where(lane % SUB == 0, below, pltpu.roll(inside, 1, 1))
            upper[at] = jnp.where(lane % SUB == SUB - 1, above, pltpu.roll(inside, 127, 1))

    def y_row(y, z):
        total = jnp.zeros((SUB, 128), jnp.float32)
        for field in range(F):
            part = piece(field * rows_of_field + y, SUB, rows_of_x, z, field * SUB)
            total = jnp.where(lane // SUB == field, part, total)
        return total

    own_rows[0] = y_row(jnp.maximum(y_start - 1, 0), z_start)
    own_rows[1] = y_row(jnp.minimum(y_start + SUB, y_cells - 1), z_start)
    up_first = lax.rem(place[2], 2) == 0
    for side in range(2):
        y = jnp.where(up_first == (side == 0), y_cells - 1, 0)
        for field in range(F):
            for w in range(z_cells // 128):
                start = w * window_rows + field * rows_of_field + y
                y_edges[side, field, :, w * 128 : (w + 1) * 128] = windows[
                    pl.ds(start, SUB, rows_of_x), :
                ]
    for side, x in enumerate((0, SUB - 1)):
        for field in range(F):
            for w in range(z_cells // 128):
                start = w * window_rows + field * rows_of_field + x * rows_of_x
                x_edges[side, field, :, w * 128 : (w + 1) * 128] = windows[pl.ds(start, rows_of_x), :]


def sample_cube(sample_block, place, brick):
    fields, x_cells, y_cells, z_cells = brick.shape
    vmem = pl.BlockSpec(memory_space=pltpu.VMEM)
    smem = pl.BlockSpec(memory_space=pltpu.SMEM)
    hbm = pl.BlockSpec(memory_space=pltpu.HBM)
    rows = fields * x_cells * y_cells
    cube = jax.ShapeDtypeStruct((F * SUB, 256), jnp.float32)
    return pl.pallas_call(
        functools.partial(sample_kernel, y_cells, z_cells),
        out_shape=(
            cube,
            cube,
            cube,
            jax.ShapeDtypeStruct((2, SUB, 128), jnp.float32),
            jax.ShapeDtypeStruct((2, fields, y_cells, z_cells), jnp.float32),
            jax.ShapeDtypeStruct((2, fields, x_cells, z_cells), jnp.float32),
        ),
        in_specs=[smem, smem, hbm],
        out_specs=(vmem,) * 6,
        scratch_shapes=[
            pltpu.VMEM((z_cells // 128 * rows, 128), jnp.float32),
            pltpu.SemaphoreType.DMA((z_cells // 128,)),
        ],
        compiler_params=pltpu.CompilerParams(vmem_limit_bytes=16 * 1024 * 1024),
        cost_estimate=pl.CostEstimate(flops=0, bytes_accessed=16_000_000, transcendentals=0),
        name="sample_cube",
    )(sample_block, place, brick.reshape(rows, z_cells))


def change_kernel(
    y_cells,
    z_cells,
    sample_block,
    place,
    closure,
    order,
    centre,
    lower,
    upper,
    own_rows,
    thin,
    payload,
):
    y_start = corner_of(sample_block, place, 0, 0, y_cells, z_cells)[0]
    row = lax.broadcasted_iota(jnp.int32, (SUB, 256), 0)
    lane = lax.broadcasted_iota(jnp.int32, (SUB, 256), 1)
    south_row = jnp.where(y_start == 0, thin[column_of(place, 0, -1), :, 128:], own_rows[0])
    north_row = jnp.where(y_start + SUB == y_cells, thin[column_of(place, 0, 1), :, :128], own_rows[1])
    face_low = thin[column_of(place, -1, 0), 8:, :]
    face_high = thin[column_of(place, 1, 0), :8, :]
    cells = [centre[f * SUB : (f + 1) * SUB, :] for f in range(F)]
    viscosity = viscosity_of(cells, closure)
    changes = []
    for f in range(F):
        value = cells[f]
        west = jnp.where(row == 0, face_low[f : f + 1, :], pltpu.roll(value, 1, 0))
        east = jnp.where(row == SUB - 1, face_high[f : f + 1, :], pltpu.roll(value, SUB - 1, 0))
        edge = pltpu.roll(south_row, (128 - f * SUB) % 128, 1)
        south = jnp.where(lane < SUB, jnp.concatenate([edge, edge], 1), pltpu.roll(value, SUB, 1))
        edge = pltpu.roll(north_row, 112 - f * SUB, 1)
        north = jnp.where(
            lane >= 256 - SUB, jnp.concatenate([edge, edge], 1), pltpu.roll(value, 256 - SUB, 1)
        )
        down = lower[f * SUB : (f + 1) * SUB, :]
        up = upper[f * SUB : (f + 1) * SUB, :]
        laplacian = east + west + north + south + up + down - 6.0 * value
        advection = cells[0] * (east - west) + cells[1] * (north - south) + cells[2] * (up - down)
        change = viscosity * laplacian - 0.5 * advection
        if f == 2:
            change = change + buoyancy * cells[3]
        changes.append(change)
    both = jnp.concatenate(cells + changes, axis=0).astype(jnp.bfloat16)
    payload[...] = dot_rows(both, order[...]).astype(jnp.bfloat16)


def cube_change(sample_block, place, closure, cube, thin, y_cells, z_cells):
    vmem = pl.BlockSpec(memory_space=pltpu.VMEM)
    smem = pl.BlockSpec(memory_space=pltpu.SMEM)
    return pl.pallas_call(
        functools.partial(change_kernel, y_cells, z_cells),
        out_shape=jax.ShapeDtypeStruct((2 * F * SUB, 256), jnp.bfloat16),
        in_specs=[smem] * 3 + [vmem] * 6,
        out_specs=vmem,
        compiler_params=pltpu.CompilerParams(vmem_limit_bytes=16 * 1024 * 1024),
        name="cube_change",
    )(sample_block, place, closure, jnp.asarray(CELL_ORDER, jnp.bfloat16), *cube, thin)


def on_device(
    fields, closure_in, closure_bias, closure_out, master, momentum, sample_block, sample_trainer
):
    group_count = lax.axis_size("grp")
    x_devices = lax.axis_size("gx")
    y_devices = lax.axis_size("gy")
    trainers = x_devices * y_devices
    my_group = lax.axis_index("grp")
    my_column = lax.axis_index("gx") * y_devices + lax.axis_index("gy")
    is_trainer = my_group == group_count - 1
    everyone = ("grp", "gx", "gy")
    sim_groups = group_count - 1
    first_trainer = sim_groups * trainers
    brick = fields[0]
    y_cells, z_cells = brick.shape[2:]
    closure = jnp.concatenate(
        [0.5 * closure_in.T, 0.5 * closure_bias[None], closure_out[None]], axis=0
    )
    place = jnp.stack(
        [
            my_group,
            lax.axis_index("gx"),
            lax.axis_index("gy"),
            jnp.int32(sim_groups),
            jnp.int32(y_devices),
            jnp.int32(x_devices),
        ]
    ).astype(jnp.int32)

    def pairs(x_step, even_step):
        found = []
        for g in range(sim_groups):
            for c in range(trainers):
                gx, gy = c // y_devices, c % y_devices
                gx = (gx + x_step) % x_devices
                gy = (gy + (even_step if gy % 2 == 0 else -even_step)) % y_devices
                found.append((g * trainers + c, (g * x_devices + gx) * y_devices + gy))
        return found

    def x_neighbours(edges):
        if x_devices == 2:
            return lax.ppermute(edges, everyone, pairs(1, 0))
        from_high = lax.ppermute(edges[0], everyone, pairs(-1, 0))
        return jnp.stack([from_high, lax.ppermute(edges[1], everyone, pairs(1, 0))])

    def y_neighbours(for_first, for_second):
        return (
            lax.ppermute(for_first, everyone, pairs(0, 1)),
            lax.ppermute(for_second, everyone, pairs(0, -1)),
        )

    def swap(distance):
        return [(first_trainer + c, first_trainer + (c ^ distance)) for c in range(trainers)]

    def to_trainers(payload):
        hop = lax.ppermute(
            payload,
            everyone,
            [(g * trainers + c, (g + 2) * trainers + c) for g in range(2) for c in range(trainers)],
        )
        both = lax.ppermute(
            jnp.stack([payload, hop]),
            everyone,
            [(2 * trainers + c, first_trainer + c) for c in range(trainers)],
        )
        return jnp.concatenate([both, hop[None]], axis=0)

    def from_line(held):
        return [lax.ppermute(held, everyone, swap(apart)) for apart in range(1, y_devices)]

    def across(apart, held):
        return lax.ppermute(held, everyone, swap(apart * y_devices))

    thin = thin_faces(sample_block, place, brick, trainers)
    *cube, x_edges, y_edges = sample_cube(sample_block, place, brick)
    thin = lax.all_to_all(thin, ("gx", "gy"), split_axis=0, concat_axis=0, tiled=True)
    payload = cube_change(sample_block, place, closure, cube, thin, y_cells, z_cells)
    landed = to_trainers(payload)
    closure, landed = lax.optimization_barrier((closure, landed))
    viscosity = lax.cond(
        is_trainer,
        lambda: jnp.zeros(brick.shape[1:], jnp.float32),
        lambda: brick_viscosity(closure, brick),
    )
    x_edges, y_edges, viscosity = lax.optimization_barrier((x_edges, y_edges, viscosity))
    halo = (x_neighbours(x_edges), *y_neighbours(y_edges[0], y_edges[1]))
    near = [landed, *from_line(landed)]
    far = [
        across(apart, pick_cubes(sample_trainer, place, near, y_devices, x_devices, apart))
        for apart in range(1, x_devices)
    ]
    arrived = [*near, *far]

    first_count = CH * TAPS * F
    first = jnp.pad(master[:first_count].reshape(CH, TAPS * F), ((0, 0), (0, 256 - TAPS * F)))
    last = jnp.pad(master[first_count:].reshape(TAPS * F, CH), ((0, 256 - TAPS * F), (0, 0)))

    first, last, *selects = lax.optimization_barrier(
        (first, last, jnp.asarray(SELECT_FIRST, jnp.bfloat16), jnp.asarray(SELECT_LAST, jnp.bfloat16))
    )

    def train_here():
        delta_first, delta_last, new_brick = train_cubes(
            sample_trainer, place, first, last, selects, arrived, brick, y_devices, x_devices
        )
        delta = jnp.concatenate(
            [delta_first[:, : TAPS * F].reshape(-1), delta_last[: TAPS * F].reshape(-1)]
        )
        return delta, new_brick

    def evolve_here():
        new_brick = evolve(place, viscosity, brick, *halo)
        return jnp.zeros((NPARAM,), jnp.float32), new_brick

    delta, new_brick = lax.cond(is_trainer, train_here, evolve_here)

    held = delta
    for g in range(sim_groups):
        held = held + lax.ppermute(
            delta, everyone, [(first_trainer + c, g * trainers + c) for c in range(trainers)]
        )
    final = delta
    for first_apart in range(1, trainers, group_count):
        meets = [
            (g * trainers + c, g * trainers + (c ^ (first_apart + g)))
            for g in range(group_count)
            for c in range(trainers)
            if first_apart + g < trainers
        ]
        final = final + lax.ppermute(held, everyone, meets)
    for apart in (1, 2):
        final = final + lax.ppermute(
            final,
            everyone,
            [(g * trainers + c, (g ^ apart) * trainers + c) for g in range(group_count) for c in range(trainers)],
        )

    share_size = NPARAM // (group_count * trainers)
    share_start = (my_group * trainers + my_column) * share_size
    momentum_share = lax.dynamic_slice_in_dim(momentum, share_start, share_size)
    master_share = lax.dynamic_slice_in_dim(master, share_start, share_size)
    inverse = 1.0 / jnp.sqrt(jnp.sum(final * final) / NPARAM + norm_epsilon)
    delta_share = lax.dynamic_slice_in_dim(final, share_start, share_size)
    new_momentum = momentum_decay * momentum_share + delta_share * inverse
    new_master = master_share - outer_rate * new_momentum
    return (new_brick[None], new_master, new_momentum)


def solution(mesh):
    in_specs = (P("grp", None, "gx", "gy", None), P(), P(), P(), P(), P(), P(), P())
    out_specs = (P("grp", None, "gx", "gy", None), P(("grp", "gx", "gy")), P(("grp", "gx", "gy")))
    return jax.shard_map(
        on_device, mesh=mesh, in_specs=in_specs, out_specs=out_specs, check_vma=False
    )
```

```python
import functools

import jax
import jax.numpy as jnp
import numpy as np
from jax import lax
from jax.experimental import pallas as pl
from jax.experimental.pallas import tpu as pltpu
from jax.sharding import PartitionSpec as P

F = 5
CH = 64
HID = 64
SUB = 16
TCAP = 6
INNER = 3
CELLS = 4096
NPARAM = 17280
TAPS = 27
PAIRS = TCAP // 2
COLS = (SUB + 2) * 128
PATCH = 16 * F
STACK = 3 * PATCH

time_step = 0.1
base_viscosity = 0.02
viscosity_gain = 0.2
buoyancy = 0.5
inner_rate = 0.02
outer_rate = 0.01
momentum_decay = 0.9
norm_epsilon = 1e-06


def patch_position(row):
    group, py, pz = row // 4, row // 2 % 2, row % 2
    ypos = py + 1 if group in (0, 2) else (3 if py == 0 else 0)
    zpos = pz + 1 if group in (0, 1) else (3 if pz == 0 else 0)
    return ypos - 1, zpos - 1


def selections():
    first = np.zeros((4, 256, STACK), np.float32)
    last = np.zeros((4, 256, STACK), np.float32)
    for cell in range(4):
        py, pz = cell // 2, cell % 2
        for kx in range(3):
            for channel in range(F):
                for row in range(16):
                    ypos, zpos = patch_position(row)
                    column = kx * PATCH + channel * 16 + row
                    dy, dz = ypos - py, zpos - pz
                    if abs(dy) <= 1 and abs(dz) <= 1:
                        tap = 9 * kx + 3 * (dy + 1) + dz + 1
                        first[cell, tap * F + channel, column] = 1.0
                        last[cell, channel * TAPS + 26 - tap, column] = 1.0
    return first, last


SELECT_FIRST, SELECT_LAST = selections()


def column_of(place, x_step, y_step):
    gx = lax.rem(place[1] + x_step + place[5], place[5])
    gy = lax.rem(place[2] + y_step + place[4], place[4])
    return gx * place[4] + gy


def owner_apart(owner, place, y_devices, x_devices):
    group, column = divmod(owner, x_devices * y_devices)
    y_apart = jnp.bitwise_xor(place[2], jnp.int32(column % y_devices))
    return group, y_apart, jnp.bitwise_xor(place[1], jnp.int32(column // y_devices))


def pick_kernel(y_devices, x_devices, apart, trainer_of, place, *refs):
    near, chosen, owners = refs[:y_devices], refs[y_devices], refs[y_devices + 1]
    wanted = jnp.bitwise_xor(place[1], jnp.int32(apart)) * y_devices + place[2]
    count = jnp.int32(0)
    for owner in range(trainer_of.shape[0]):
        group, y_apart, x_apart = owner_apart(owner, place, y_devices, x_devices)
        mine = (trainer_of[owner] == wanted) & (x_apart == 0)

        @pl.when(mine)
        def _():
            owners[0, count] = y_apart
            owners[1, count] = group

        count = count + jnp.where(mine, 1, 0)

    def copy_slot(slot, carry):
        for source in range(y_devices):

            @pl.when(owners[0, slot] == source)
            def _():
                chosen[slot] = near[source][owners[1, slot]]

        return carry

    lax.fori_loop(0, count, copy_slot, 0)


def pick_cubes(trainer_of, place, near, y_devices, x_devices, apart):
    vmem = pl.BlockSpec(memory_space=pltpu.VMEM)
    smem = pl.BlockSpec(memory_space=pltpu.SMEM)
    return pl.pallas_call(
        functools.partial(pick_kernel, y_devices, x_devices, apart),
        out_shape=jax.ShapeDtypeStruct((TCAP, *near[0].shape[1:]), near[0].dtype),
        in_specs=[smem, smem] + [vmem] * len(near),
        out_specs=vmem,
        scratch_shapes=[pltpu.SMEM((2, TCAP), jnp.int32)],
        compiler_params=pltpu.CompilerParams(vmem_limit_bytes=16 * 1024 * 1024),
        name="pick_cubes",
    )(trainer_of, place, *near)


def dot_rows(left, right):
    return jnp.dot(left, right, preferred_element_type=jnp.float32)


def dot_lanes(left, right):
    return lax.dot_general(left, right, (((1,), (1,)), ((), ())), preferred_element_type=jnp.float32)


def patch_masks():
    row = lax.broadcasted_iota(jnp.int32, (8, 128), 0)
    lane = lax.broadcasted_iota(jnp.int32, (8, 128), 1)
    z, y = lane % 8, lane // 8 % 8
    even_z, even_y = row % 2 == 0, row // 2 % 2 == 0
    return {
        "centre": row < 4,
        "even_z": even_z,
        "even_y": even_y,
        "gather_z": jnp.where(even_z, z, 7 - z) < 7,
        "gather_y": jnp.where(even_y, y, 7 - y) < 7,
        "scatter_z": jnp.where(even_z, z, 7 - z) > 0,
        "scatter_y": jnp.where(even_y, y, 7 - y) > 0,
    }


def edge_shift(values, step, even, inside, gather):
    before, after = pltpu.roll(values, step, 1), pltpu.roll(values, 128 - step, 1)
    moved = jnp.where(even, after, before) if gather else jnp.where(even, before, after)
    return jnp.where(inside, moved, 0.0)


def patch_stack(rows, masks):
    both = jnp.where(masks["centre"], rows, pltpu.roll(rows, 4, 0))
    y_edge = edge_shift(both, 8, masks["even_y"], masks["gather_y"], True)
    upper = jnp.where(masks["centre"], both, y_edge)
    return upper, edge_shift(upper, 1, masks["even_z"], masks["gather_z"], True)


def patch_fold(upper, lower, masks):
    line = upper + edge_shift(lower, 1, masks["even_z"], masks["scatter_z"], False)
    return line + pltpu.roll(edge_shift(line, 8, masks["even_y"], masks["scatter_y"], False), 4, 0)


def store_planes(ref, x, channels):
    stacked = jnp.concatenate([part for both in channels for part in both], axis=0).astype(jnp.bfloat16)
    for kx in range(3):
        start = pl.multiple_of((x + 2 - kx) * 128, 128)
        ref[kx * PATCH : (kx + 1) * PATCH, pl.ds(start, 128)] = stacked


def train_kernel(y_devices, x_devices, *refs):
    sources = y_devices + x_devices - 1
    (trainer_of, place, first_ref, last_ref, far_first, far_last) = refs[:6]
    arrived = refs[6 : 6 + sources]
    fields_ref = refs[6 + sources]
    delta_first, delta_last, new_fields_ref = refs[7 + sources : 10 + sources]
    (
        slots,
        picked,
        cubes,
        big_first,
        big_last,
        big_last_t,
        grad_first,
        grad_last,
        now_first,
        now_last,
        brick,
        select_first,
        select_last,
        slot_sems,
        field_sem,
        select_sems,
        *pair_refs,
    ) = refs[10 + sources :]
    targets, tables, inputs, errors, hiddens, pre_grads, slopes, partial_out, raw = [
        pair_refs[kind * PAIRS : (kind + 1) * PAIRS] for kind in range(9)
    ]

    field_in = pltpu.make_async_copy(fields_ref, brick, field_sem)
    field_out = pltpu.make_async_copy(brick, new_fields_ref, field_sem)
    select_copies = [
        pltpu.make_async_copy(far_first, select_first, select_sems.at[0]),
        pltpu.make_async_copy(far_last, select_last, select_sems.at[1]),
    ]

    column = place[1] * y_devices + place[2]
    for other in range(x_devices):
        picked[other] = 0
    count = jnp.int32(0)
    for owner in range(trainer_of.shape[0]):
        group, y_apart, x_apart = owner_apart(owner, place, y_devices, x_devices)
        mine = trainer_of[owner] == column

        @pl.when(mine)
        def _():
            near = x_apart == 0
            slots[0, count] = jnp.where(near, y_apart, y_devices - 1 + x_apart)
            slots[1, count] = jnp.where(near, group, picked[x_apart])
            picked[x_apart] = picked[x_apart] + 1

        count = count + jnp.where(mine, 1, 0)

    def fetch(slot, wait):
        for source in range(sources):

            @pl.when((slot < count) & (slots[0, slot] == source))
            def _():
                copy = pltpu.make_async_copy(
                    arrived[source].at[slots[1, slot]], cubes.at[slot], slot_sems.at[slot]
                )
                copy.wait() if wait else copy.start()

    for slot in range(TCAP):
        fetch(slot, False)

    for copy in select_copies:
        copy.start()
    field_in.start()
    for slot in range(TCAP):

        @pl.when(slot >= count)
        def _():
            cubes[slot] = jnp.zeros(cubes.shape[1:], jnp.bfloat16)

    masks = patch_masks()
    for ref in (*errors, *inputs):
        ref[:PATCH, 128:256] = jnp.zeros((PATCH, 128), jnp.bfloat16)
        ref[2 * PATCH :, COLS - 256 : COLS - 128] = jnp.zeros((PATCH, 128), jnp.bfloat16)
    for ref in partial_out:
        ref[:, :128] = jnp.zeros((STACK, 128), jnp.float32)
        ref[:, COLS - 128 :] = jnp.zeros((STACK, 128), jnp.float32)
    lane = lax.broadcasted_iota(jnp.int32, (8, 128), 1)
    full_weight = 2.0 * (1.0 / (jnp.full((8, 128), count, jnp.int32).astype(jnp.float32) * CELLS))
    weights = [
        jnp.where(lane // 64 + 2 * pair < count, full_weight, 0.0) for pair in range(PAIRS)
    ]
    start_first = first_ref[...].astype(jnp.bfloat16).astype(jnp.float32)
    start_last = last_ref[...].T.astype(jnp.bfloat16).astype(jnp.float32)
    now_first[...] = start_first
    now_last[...] = start_last

    for slot in range(TCAP):
        fetch(slot, True)

    low_lanes = lax.broadcasted_iota(jnp.int32, (SUB * F * 2, 128), 1) < 64
    for pair in range(PAIRS):
        for kind, ref in enumerate((tables[pair], targets[pair])):
            rows = slice(kind * SUB * F * 2, (kind + 1) * SUB * F * 2)
            even = cubes[2 * pair, rows, :].astype(jnp.float32)
            odd = cubes[2 * pair + 1, rows, :].astype(jnp.float32)
            ref[0] = jnp.where(low_lanes, even, pltpu.roll(odd, 64, 1))
            ref[1] = jnp.where(low_lanes, pltpu.roll(even, 64, 1), odd)

    def patch_cells(ref, quarter, plane, channel):
        start = pl.multiple_of(channel * 32 + quarter % 2 * 16 + plane // 2 * 8, 8)
        rows = ref[quarter // 2, pl.ds(start, 8), :]
        return rows if plane % 2 == 0 else pltpu.roll(rows, 4, 0)

    def stack_planes(quarter, carry):
        for pair in range(PAIRS):
            for plane in range(4):
                x = quarter * 4 + plane
                channels = [
                    patch_stack(patch_cells(tables[pair], quarter, plane, c), masks) for c in range(F)
                ]
                store_planes(inputs[pair], x, channels)
        return carry

    lax.fori_loop(0, 4, stack_planes, 0, unroll=2)

    for copy in select_copies:
        copy.wait()
    field_in.wait()
    field_out.start()

    def train_step(step, step_carry):
        first_now = now_first[...].astype(jnp.bfloat16)
        last_now = now_last[...].astype(jnp.bfloat16)
        for cell in range(4):
            rows = slice(cell * CH, (cell + 1) * CH)
            big_first[rows, :] = (0.5 * dot_rows(first_now, select_first[cell])).astype(jnp.bfloat16)
            spread_last = dot_rows(last_now, select_last[cell])
            big_last[rows, :] = (0.5 * spread_last).astype(jnp.bfloat16)
            big_last_t[:, rows] = spread_last.T.astype(jnp.bfloat16)
        grad_first[...] = jnp.zeros(grad_first.shape, jnp.float32)
        grad_last[...] = jnp.zeros(grad_last.shape, jnp.float32)

        def columns_of(quarter):
            return pl.ds(pl.multiple_of(quarter * 512 + 128, 128), 512)

        def first_layer(pair, quarter):
            columns = columns_of(quarter)
            raw[pair][:, columns] = dot_rows(big_first[...], inputs[pair][:, columns])

        def activate(pair, quarter):
            columns = columns_of(quarter)
            for part in range(8):
                rows = slice(part * 32, (part + 1) * 32)
                half = raw[pair][rows, columns]
                curve = jnp.tanh(half)
                above = 1.0 + curve
                value = half * above
                hiddens[pair][rows, columns] = value.astype(jnp.bfloat16)
                slopes[pair][rows, columns] = above + value * (1.0 - curve)

        def last_layer(pair, quarter):
            columns = columns_of(quarter)
            partial_out[pair][:, columns] = dot_rows(big_last_t[...], hiddens[pair][:, columns])

        def find_errors(pair, quarter):
            for plane in range(4):
                x = quarter * 4 + plane
                column = pl.multiple_of((x + 1) * 128, 128)
                total = (
                    partial_out[pair][0:PATCH, pl.ds(pl.multiple_of(column + 128, 128), 128)]
                    + partial_out[pair][PATCH : 2 * PATCH, pl.ds(column, 128)]
                    + partial_out[pair][2 * PATCH :, pl.ds(pl.multiple_of(column - 128, 128), 128)]
                )
                channels = []
                for c in range(F):
                    predicted = patch_fold(
                        total[16 * c : 16 * c + 8], total[16 * c + 8 : 16 * c + 16], masks
                    )
                    wanted = patch_cells(targets[pair], quarter, plane, c)
                    error = weights[pair] * (predicted - wanted)
                    channels.append(patch_stack(error, masks))
                store_planes(errors[pair], x, channels)

        def hidden_layer(pair, quarter):
            columns = columns_of(quarter)
            raw[pair][:, columns] = dot_rows(big_last[...], errors[pair][:, columns])

        def scale(pair, quarter):
            columns = columns_of(quarter)
            for part in range(8):
                rows = slice(part * 32, (part + 1) * 32)
                product = raw[pair][rows, columns] * slopes[pair][rows, columns]
                pre_grads[pair][rows, columns] = product.astype(jnp.bfloat16)

        def gradients(pair, quarter):
            columns = columns_of(quarter)
            grad_first[...] += dot_lanes(pre_grads[pair][:, columns], inputs[pair][:, columns])
            grad_last[...] += dot_lanes(hiddens[pair][:, columns], errors[pair][:, columns])

        stages = (first_layer, activate, last_layer, find_errors, hidden_layer, scale, gradients)
        for turn in range(len(stages) + PAIRS - 1):

            def run(quarter, carry):
                for pair in range(PAIRS):
                    if 0 <= turn - pair < len(stages):
                        stages[turn - pair](pair, quarter)
                return carry

            lax.fori_loop(0, 4, run, 0, unroll=4)

        def folded(grad, select_ref):
            total = jnp.zeros((3 * CH, 256), jnp.float32)
            for cell in range(4):
                rest = grad[cell * CH : (cell + 1) * CH, :]
                parts = []
                for _ in range(3):
                    parts.append(rest.astype(jnp.bfloat16))
                    rest = rest - parts[-1].astype(jnp.float32)
                total = total + dot_lanes(jnp.concatenate(parts, axis=0), select_ref[cell])
            return total[:CH] + total[CH : 2 * CH] + total[2 * CH :]

        now_first[...] = now_first[...] - inner_rate * folded(grad_first, select_first)
        now_last[...] = now_last[...] - inner_rate * folded(grad_last, select_last)
        return step_carry

    lax.fori_loop(0, INNER, train_step, 0)
    delta_first[...] = start_first - now_first[...]
    delta_last[...] = (start_last - now_last[...]).T
    field_out.wait()


def train_cubes(trainer_of, place, first, last, selects, arrived, fields, y_devices, x_devices):
    vmem = pl.BlockSpec(memory_space=pltpu.VMEM)
    smem = pl.BlockSpec(memory_space=pltpu.SMEM)
    anywhere = pl.BlockSpec(memory_space=pl.ANY)
    hbm = pl.BlockSpec(memory_space=pltpu.HBM)
    return pl.pallas_call(
        functools.partial(train_kernel, y_devices, x_devices),
        out_shape=(
            jax.ShapeDtypeStruct((CH, 256), jnp.float32),
            jax.ShapeDtypeStruct((256, CH), jnp.float32),
            jax.ShapeDtypeStruct(fields.shape, fields.dtype),
        ),
        in_specs=[smem] * 2 + [vmem] * 2 + [hbm] * 2 + [anywhere] * len(arrived) + [hbm],
        out_specs=(vmem, vmem, hbm),
        scratch_shapes=[
            pltpu.SMEM((2, TCAP), jnp.int32),
            pltpu.SMEM((x_devices,), jnp.int32),
            pltpu.VMEM((TCAP, 4 * SUB * F, 128), jnp.bfloat16),
            pltpu.VMEM((4 * CH, STACK), jnp.bfloat16),
            pltpu.VMEM((4 * CH, STACK), jnp.bfloat16),
            pltpu.VMEM((STACK, 4 * CH), jnp.bfloat16),
            pltpu.VMEM((4 * CH, STACK), jnp.float32),
            pltpu.VMEM((4 * CH, STACK), jnp.float32),
            pltpu.VMEM((CH, 256), jnp.float32),
            pltpu.VMEM((CH, 256), jnp.float32),
            pltpu.VMEM(fields.shape, fields.dtype),
            pltpu.VMEM((4, 256, STACK), jnp.bfloat16),
            pltpu.VMEM((4, 256, STACK), jnp.bfloat16),
            pltpu.SemaphoreType.DMA((TCAP,)),
            pltpu.SemaphoreType.DMA,
            pltpu.SemaphoreType.DMA((2,)),
        ]
        + [pltpu.VMEM((2, SUB * F * 2, 128), jnp.float32)] * (2 * PAIRS)
        + [pltpu.VMEM((STACK, COLS), jnp.bfloat16)] * (2 * PAIRS)
        + [pltpu.VMEM((4 * CH, COLS), jnp.bfloat16)] * (2 * PAIRS)
        + [pltpu.VMEM((4 * CH, COLS), jnp.float32)] * PAIRS
        + [pltpu.VMEM((STACK, COLS), jnp.float32)] * PAIRS
        + [pltpu.VMEM((4 * CH, COLS), jnp.float32)] * PAIRS,
        compiler_params=pltpu.CompilerParams(vmem_limit_bytes=52 * 1024 * 1024),
        name="train_cubes",
    )(
        trainer_of,
        place,
        first,
        last,
        *selects,
        *arrived,
        fields,
    )


def viscosity_of(cells, closure):
    def unit(h, total):
        half = closure[F, h] + closure[0, h] * cells[0]
        for f in range(1, F):
            half = half + closure[f, h] * cells[f]
        return total + closure[F + 1, h] * (half + half * jnp.tanh(half))

    total = lax.fori_loop(0, HID, unit, jnp.zeros(cells[0].shape, jnp.float32), unroll=4)
    soft = jnp.maximum(total, 0.0) + jnp.log1p(jnp.exp(-jnp.abs(total)))
    return base_viscosity + viscosity_gain * soft


def viscosity_kernel(closure, fields, viscosity):
    x_cells, y_cells = fields.shape[1:3]
    part = y_cells // 2

    def plane(x, carry):
        for half in range(2):
            rows = pl.ds(half * part, part)
            viscosity[x, rows, :] = viscosity_of([fields[f, x, rows, :] for f in range(F)], closure)
        return carry

    lax.fori_loop(0, x_cells, plane, 0)


def brick_viscosity(closure, fields):
    vmem = pl.BlockSpec(memory_space=pltpu.VMEM)
    return pl.pallas_call(
        viscosity_kernel,
        out_shape=jax.ShapeDtypeStruct(fields.shape[1:], fields.dtype),
        in_specs=[pl.BlockSpec(memory_space=pltpu.SMEM), vmem],
        out_specs=vmem,
        compiler_params=pltpu.CompilerParams(vmem_limit_bytes=16 * 1024 * 1024),
        name="brick_viscosity",
    )(closure, fields)


def evolve_kernel(place, viscosity, fields, x_halo, y_first, y_second, new_fields):
    up_first = lax.rem(place[2], 2) == 0
    x_cells, y_cells, z_cells = fields.shape[1:]
    row = lax.broadcasted_iota(jnp.int32, (y_cells, z_cells), 0)
    lane = lax.broadcasted_iota(jnp.int32, (y_cells, z_cells), 1)

    def plane(x, carry):
        centre = [fields[f, x] for f in range(F)]
        below = jnp.maximum(x - 1, 0)
        above = jnp.minimum(x + 1, x_cells - 1)
        for f in range(F):
            value = centre[f]
            west = jnp.where(x == 0, x_halo[1, f], fields[f, below])
            east = jnp.where(x == x_cells - 1, x_halo[0, f], fields[f, above])
            first, second = y_first[f, pl.ds(x, 1), :], y_second[f, pl.ds(x, 1), :]
            south = jnp.where(
                row == 0, jnp.where(up_first, second, first), pltpu.roll(value, 1, 0)
            )
            north = jnp.where(
                row == y_cells - 1,
                jnp.where(up_first, first, second),
                pltpu.roll(value, y_cells - 1, 0),
            )
            lower = jnp.where(lane == 0, 0.0, pltpu.roll(value, 1, 1))
            upper = jnp.where(lane == z_cells - 1, 0.0, pltpu.roll(value, z_cells - 1, 1))
            laplacian = east + west + north + south + upper + lower - 6.0 * value
            advection = (
                centre[0] * (east - west) + centre[1] * (north - south) + centre[2] * (upper - lower)
            )
            tendency = viscosity[x] * laplacian - 0.5 * advection
            if f == 2:
                tendency = tendency + buoyancy * centre[3]
            new_fields[f, x] = value + time_step * tendency
        return carry

    lax.fori_loop(0, x_cells, plane, 0)


def evolve(place, viscosity, fields, x_halo, y_first, y_second):
    vmem = pl.BlockSpec(memory_space=pltpu.VMEM)
    return pl.pallas_call(
        evolve_kernel,
        out_shape=jax.ShapeDtypeStruct(fields.shape, fields.dtype),
        in_specs=[pl.BlockSpec(memory_space=pltpu.SMEM)] + [vmem] * 5,
        out_specs=vmem,
        compiler_params=pltpu.CompilerParams(vmem_limit_bytes=16 * 1024 * 1024),
        name="evolve_brick",
    )(place, viscosity, fields, x_halo, y_first, y_second)


def cell_order():
    order = np.zeros((256, 256), np.float32)
    for y in range(SUB):
        for z in range(SUB):
            order[y * SUB + z, (y % 2 * 2 + z % 2) * 64 + y // 2 * 8 + z // 2] = 1.0
    return order


CELL_ORDER = cell_order()


def corner_of(sample_block, place, x_step, y_step, y_cells, z_cells):
    x_devices, y_devices = place[5], place[4]
    gx = lax.rem(place[1] + x_step + x_devices, x_devices)
    gy = lax.rem(place[2] + y_step + y_devices, y_devices)
    group = jnp.minimum(place[0], place[3] - 1)
    block = sample_block[(group * x_devices + gx) * y_devices + gy]
    z_blocks = z_cells // SUB
    return lax.rem(lax.div(block, z_blocks), y_cells // SUB) * SUB, lax.rem(block, z_blocks) * SUB


def thin_kernel(
    y_cells, z_cells, sample_block, place, rows_ref, lines_ref, thin, x_buffer, y_buffer, x_sems, y_sems
):
    def corner(x_step, y_step):
        return corner_of(sample_block, place, x_step, y_step, y_cells, z_cells)

    lane = lax.broadcasted_iota(jnp.int32, (SUB, 128), 1)
    signs = (-1, 1)
    copies = []
    for side, sign in enumerate(signs):
        z_x, z_y = corner(sign, 0)[1], corner(0, sign)[1]
        x, y = side * (SUB - 1), side * (y_cells - 8)
        for field in range(F):
            copies.append(
                pltpu.make_async_copy(
                    rows_ref.at[
                        pl.ds((field * SUB + x) * y_cells, y_cells),
                        pl.ds(pl.multiple_of(lax.div(z_x, 128) * 128, 128), 128),
                    ],
                    x_buffer.at[pl.ds((side * 8 + field) * y_cells, y_cells)],
                    x_sems.at[side, field],
                )
            )
        copies.append(
            pltpu.make_async_copy(
                lines_ref.at[:, pl.ds(y, 8), pl.ds(pl.multiple_of(lax.div(z_y, 128) * 128, 128), 128)],
                y_buffer.at[side],
                y_sems.at[side],
            )
        )
    for copy in copies:
        copy.start()
    thin[...] = jnp.zeros(thin.shape, thin.dtype)
    for copy in copies:
        copy.wait()

    def moved(values, z, lane_start):
        return pltpu.roll(values, lax.rem(lane_start - lax.rem(z, 128) + 256, 128), 1)

    for side, sign in enumerate(signs):
        z = corner(0, sign)[1]
        total = jnp.zeros((SUB, 128), jnp.float32)
        for field in range(F):
            part = y_buffer[side, field * SUB : (field + 1) * SUB, side * 7, :]
            total = jnp.where(lane // SUB == field, moved(part, z, field * SUB), total)
        thin[column_of(place, 0, sign), :, side * 128 : (side + 1) * 128] = total
    for side, sign in enumerate(signs):
        y, z = corner(sign, 0)
        for half in range(2):
            total = jnp.zeros((8, 128), jnp.float32)
            for step in range(8):
                row = side * 8 * y_cells + y + half * 8 + step
                part = moved(x_buffer[pl.ds(row, 8, y_cells), :], z, step * SUB)
                total = jnp.where(lane[:8] // SUB == step, part, total)
            at = (column_of(place, sign, 0), slice(side * 8, side * 8 + 8), slice(half * 128, half * 128 + 128))
            thin[at] = total


def thin_faces(sample_block, place, brick, columns):
    fields, x_cells, y_cells, z_cells = brick.shape
    vmem = pl.BlockSpec(memory_space=pltpu.VMEM)
    smem = pl.BlockSpec(memory_space=pltpu.SMEM)
    hbm = pl.BlockSpec(memory_space=pltpu.HBM)
    return pl.pallas_call(
        functools.partial(thin_kernel, y_cells, z_cells),
        out_shape=jax.ShapeDtypeStruct((columns, SUB, 256), jnp.float32),
        in_specs=[smem, smem, hbm, hbm],
        out_specs=vmem,
        scratch_shapes=[
            pltpu.VMEM((16 * y_cells, 128), jnp.float32),
            pltpu.VMEM((2, fields * x_cells, 8, 128), jnp.float32),
            pltpu.SemaphoreType.DMA((2, fields)),
            pltpu.SemaphoreType.DMA((2,)),
        ],
        compiler_params=pltpu.CompilerParams(vmem_limit_bytes=16 * 1024 * 1024),
        name="thin_faces",
    )(
        sample_block,
        place,
        brick.reshape(fields * x_cells * y_cells, z_cells),
        brick.reshape(fields * x_cells, y_cells, z_cells),
    )


def sample_kernel(
    y_cells,
    z_cells,
    sample_block,
    place,
    brick,
    centre,
    lower,
    upper,
    own_rows,
    x_edges,
    y_edges,
    windows,
    sems,
):
    rows_of_x = y_cells
    rows_of_field = SUB * y_cells
    window_rows = F * rows_of_field
    copies = [
        pltpu.make_async_copy(
            brick.at[:, pl.ds(w * 128, 128)], windows.at[pl.ds(w * window_rows, window_rows)], sems.at[w]
        )
        for w in range(z_cells // 128)
    ]
    for copy in copies:
        copy.start()
    for copy in copies:
        copy.wait()

    def corner(x_step, y_step):
        return corner_of(sample_block, place, x_step, y_step, y_cells, z_cells)

    def piece(row, count, stride, z, lane_start):
        values = windows[pl.ds(lax.div(z, 128) * window_rows + row, count, stride), :]
        return pltpu.roll(values, lax.rem(lane_start - lax.rem(z, 128) + 256, 128), 1)

    lane = lax.broadcasted_iota(jnp.int32, (SUB, 128), 1)
    y_start, z_start = corner(0, 0)
    z_below = jnp.maximum(z_start - 1, 0)
    z_above = jnp.minimum(z_start + SUB, z_cells - 1)
    for field in range(F):
        for half in range(2):
            inside = jnp.zeros((SUB, 128), jnp.float32)
            below = jnp.zeros((SUB, 128), jnp.float32)
            above = jnp.zeros((SUB, 128), jnp.float32)
            for step in range(8):
                row = field * rows_of_field + y_start + half * 8 + step
                first = step * SUB
                inside = jnp.where(lane // SUB == step, piece(row, SUB, rows_of_x, z_start, first), inside)
                below = jnp.where(lane == first, piece(row, SUB, rows_of_x, z_below, first), below)
                last = first + SUB - 1
                above = jnp.where(lane == last, piece(row, SUB, rows_of_x, z_above, last), above)
            below = jnp.where(z_start == 0, 0.0, below)
            above = jnp.where(z_start + SUB == z_cells, 0.0, above)
            at = (slice(field * SUB, (field + 1) * SUB), slice(half * 128, (half + 1) * 128))
            centre[at] = inside
            lower[at] = jnp.where(lane % SUB == 0, below, pltpu.roll(inside, 1, 1))
            upper[at] = jnp.where(lane % SUB == SUB - 1, above, pltpu.roll(inside, 127, 1))

    def y_row(y, z):
        total = jnp.zeros((SUB, 128), jnp.float32)
        for field in range(F):
            part = piece(field * rows_of_field + y, SUB, rows_of_x, z, field * SUB)
            total = jnp.where(lane // SUB == field, part, total)
        return total

    own_rows[0] = y_row(jnp.maximum(y_start - 1, 0), z_start)
    own_rows[1] = y_row(jnp.minimum(y_start + SUB, y_cells - 1), z_start)
    up_first = lax.rem(place[2], 2) == 0
    for side in range(2):
        y = jnp.where(up_first == (side == 0), y_cells - 1, 0)
        for field in range(F):
            for w in range(z_cells // 128):
                start = w * window_rows + field * rows_of_field + y
                y_edges[side, field, :, w * 128 : (w + 1) * 128] = windows[
                    pl.ds(start, SUB, rows_of_x), :
                ]
    for side, x in enumerate((0, SUB - 1)):
        for field in range(F):
            for w in range(z_cells // 128):
                start = w * window_rows + field * rows_of_field + x * rows_of_x
                x_edges[side, field, :, w * 128 : (w + 1) * 128] = windows[pl.ds(start, rows_of_x), :]


def sample_cube(sample_block, place, brick):
    fields, x_cells, y_cells, z_cells = brick.shape
    vmem = pl.BlockSpec(memory_space=pltpu.VMEM)
    smem = pl.BlockSpec(memory_space=pltpu.SMEM)
    hbm = pl.BlockSpec(memory_space=pltpu.HBM)
    rows = fields * x_cells * y_cells
    cube = jax.ShapeDtypeStruct((F * SUB, 256), jnp.float32)
    return pl.pallas_call(
        functools.partial(sample_kernel, y_cells, z_cells),
        out_shape=(
            cube,
            cube,
            cube,
            jax.ShapeDtypeStruct((2, SUB, 128), jnp.float32),
            jax.ShapeDtypeStruct((2, fields, y_cells, z_cells), jnp.float32),
            jax.ShapeDtypeStruct((2, fields, x_cells, z_cells), jnp.float32),
        ),
        in_specs=[smem, smem, hbm],
        out_specs=(vmem,) * 6,
        scratch_shapes=[
            pltpu.VMEM((z_cells // 128 * rows, 128), jnp.float32),
            pltpu.SemaphoreType.DMA((z_cells // 128,)),
        ],
        compiler_params=pltpu.CompilerParams(vmem_limit_bytes=16 * 1024 * 1024),
        cost_estimate=pl.CostEstimate(flops=0, bytes_accessed=16_000_000, transcendentals=0),
        name="sample_cube",
    )(sample_block, place, brick.reshape(rows, z_cells))


def change_kernel(
    y_cells,
    z_cells,
    sample_block,
    place,
    closure,
    order,
    centre,
    lower,
    upper,
    own_rows,
    thin,
    payload,
    table,
):
    y_start = corner_of(sample_block, place, 0, 0, y_cells, z_cells)[0]
    row = lax.broadcasted_iota(jnp.int32, (SUB, 256), 0)
    lane = lax.broadcasted_iota(jnp.int32, (SUB, 256), 1)
    south_row = jnp.where(y_start == 0, thin[column_of(place, 0, -1), :, 128:], own_rows[0])
    north_row = jnp.where(y_start + SUB == y_cells, thin[column_of(place, 0, 1), :, :128], own_rows[1])
    face_low = thin[column_of(place, -1, 0), 8:, :]
    face_high = thin[column_of(place, 1, 0), :8, :]
    cells = [centre[f * SUB : (f + 1) * SUB, :] for f in range(F)]
    viscosity = viscosity_of(cells, closure)
    changes = []
    for f in range(F):
        value = cells[f]
        west = jnp.where(row == 0, face_low[f : f + 1, :], pltpu.roll(value, 1, 0))
        east = jnp.where(row == SUB - 1, face_high[f : f + 1, :], pltpu.roll(value, SUB - 1, 0))
        edge = pltpu.roll(south_row, (128 - f * SUB) % 128, 1)
        south = jnp.where(lane < SUB, jnp.concatenate([edge, edge], 1), pltpu.roll(value, SUB, 1))
        edge = pltpu.roll(north_row, 112 - f * SUB, 1)
        north = jnp.where(
            lane >= 256 - SUB, jnp.concatenate([edge, edge], 1), pltpu.roll(value, 256 - SUB, 1)
        )
        down = lower[f * SUB : (f + 1) * SUB, :]
        up = upper[f * SUB : (f + 1) * SUB, :]
        laplacian = east + west + north + south + up + down - 6.0 * value
        advection = cells[0] * (east - west) + cells[1] * (north - south) + cells[2] * (up - down)
        change = viscosity * laplacian - 0.5 * advection
        if f == 2:
            change = change + buoyancy * cells[3]
        changes.append(change)
    ordered = dot_rows(jnp.concatenate(cells + changes, axis=0).astype(jnp.bfloat16), order[...])
    low_lanes = lane[:8, :128] < 64
    for part in range(2 * F):
        for cell in range(4):
            columns = slice(cell // 2 * 128, cell // 2 * 128 + 128)
            low = ordered[part * SUB : part * SUB + 8, columns]
            high = ordered[part * SUB + 8 : part * SUB + SUB, columns]
            if cell % 2 == 0:
                high = pltpu.roll(high, 64, 1)
            else:
                low = pltpu.roll(low, 64, 1)
            table[pl.ds(part * 32 + cell, 8, 4), :] = jnp.where(low_lanes, low, high)
    payload[...] = table[...].astype(jnp.bfloat16)


def cube_change(sample_block, place, closure, cube, thin, y_cells, z_cells):
    vmem = pl.BlockSpec(memory_space=pltpu.VMEM)
    smem = pl.BlockSpec(memory_space=pltpu.SMEM)
    return pl.pallas_call(
        functools.partial(change_kernel, y_cells, z_cells),
        out_shape=jax.ShapeDtypeStruct((4 * F * SUB, 128), jnp.bfloat16),
        in_specs=[smem] * 3 + [vmem] * 6,
        out_specs=vmem,
        scratch_shapes=[pltpu.VMEM((4 * F * SUB, 128), jnp.float32)],
        compiler_params=pltpu.CompilerParams(vmem_limit_bytes=16 * 1024 * 1024),
        name="cube_change",
    )(sample_block, place, closure, jnp.asarray(CELL_ORDER, jnp.bfloat16), *cube, thin)


def on_device(
    fields, closure_in, closure_bias, closure_out, master, momentum, sample_block, sample_trainer
):
    group_count = lax.axis_size("grp")
    x_devices = lax.axis_size("gx")
    y_devices = lax.axis_size("gy")
    trainers = x_devices * y_devices
    my_group = lax.axis_index("grp")
    my_column = lax.axis_index("gx") * y_devices + lax.axis_index("gy")
    is_trainer = my_group == group_count - 1
    everyone = ("grp", "gx", "gy")
    sim_groups = group_count - 1
    first_trainer = sim_groups * trainers
    brick = fields[0]
    y_cells, z_cells = brick.shape[2:]
    closure = jnp.concatenate(
        [0.5 * closure_in.T, 0.5 * closure_bias[None], closure_out[None]], axis=0
    )
    place = jnp.stack(
        [
            my_group,
            lax.axis_index("gx"),
            lax.axis_index("gy"),
            jnp.int32(sim_groups),
            jnp.int32(y_devices),
            jnp.int32(x_devices),
        ]
    ).astype(jnp.int32)

    def pairs(x_step, even_step):
        found = []
        for g in range(sim_groups):
            for c in range(trainers):
                gx, gy = c // y_devices, c % y_devices
                gx = (gx + x_step) % x_devices
                gy = (gy + (even_step if gy % 2 == 0 else -even_step)) % y_devices
                found.append((g * trainers + c, (g * x_devices + gx) * y_devices + gy))
        return found

    def x_neighbours(edges):
        if x_devices == 2:
            return lax.ppermute(edges, everyone, pairs(1, 0))
        from_high = lax.ppermute(edges[0], everyone, pairs(-1, 0))
        return jnp.stack([from_high, lax.ppermute(edges[1], everyone, pairs(1, 0))])

    def y_neighbours(for_first, for_second):
        return (
            lax.ppermute(for_first, everyone, pairs(0, 1)),
            lax.ppermute(for_second, everyone, pairs(0, -1)),
        )

    def swap(distance):
        return [(first_trainer + c, first_trainer + (c ^ distance)) for c in range(trainers)]

    def to_trainers(payload):
        return jnp.stack(
            [
                lax.ppermute(
                    payload, everyone, [(g * trainers + c, first_trainer + c) for c in range(trainers)]
                )
                for g in range(sim_groups)
            ]
        )

    def from_line(held):
        return [lax.ppermute(held, everyone, swap(apart)) for apart in range(1, y_devices)]

    def across(apart, held):
        return lax.ppermute(held, everyone, swap(apart * y_devices))

    thin = thin_faces(sample_block, place, brick, trainers)
    *cube, x_edges, y_edges = sample_cube(sample_block, place, brick)
    thin = lax.all_to_all(thin, ("gx", "gy"), split_axis=0, concat_axis=0, tiled=True)
    payload = cube_change(sample_block, place, closure, cube, thin, y_cells, z_cells)
    landed = to_trainers(payload)
    closure, landed = lax.optimization_barrier((closure, landed))
    viscosity = lax.cond(
        is_trainer,
        lambda: jnp.zeros(brick.shape[1:], jnp.float32),
        lambda: brick_viscosity(closure, brick),
    )
    x_edges, y_edges, viscosity = lax.optimization_barrier((x_edges, y_edges, viscosity))
    halo = (x_neighbours(x_edges), *y_neighbours(y_edges[0], y_edges[1]))
    near = [landed, *from_line(landed)]
    far = [
        across(apart, pick_cubes(sample_trainer, place, near, y_devices, x_devices, apart))
        for apart in range(1, x_devices)
    ]
    arrived = [*near, *far]

    first_count = CH * TAPS * F
    first = jnp.pad(master[:first_count].reshape(CH, TAPS * F), ((0, 0), (0, 256 - TAPS * F)))
    last = jnp.pad(master[first_count:].reshape(TAPS * F, CH), ((0, 256 - TAPS * F), (0, 0)))

    first, last, *selects = lax.optimization_barrier(
        (first, last, jnp.asarray(SELECT_FIRST, jnp.bfloat16), jnp.asarray(SELECT_LAST, jnp.bfloat16))
    )

    def train_here():
        delta_first, delta_last, new_brick = train_cubes(
            sample_trainer, place, first, last, selects, arrived, brick, y_devices, x_devices
        )
        delta = jnp.concatenate(
            [delta_first[:, : TAPS * F].reshape(-1), delta_last[: TAPS * F].reshape(-1)]
        )
        return delta, new_brick

    def evolve_here():
        new_brick = evolve(place, viscosity, brick, *halo)
        return jnp.zeros((NPARAM,), jnp.float32), new_brick

    delta, new_brick = lax.cond(is_trainer, train_here, evolve_here)

    held = delta
    for g in range(sim_groups):
        held = held + lax.ppermute(
            delta, everyone, [(first_trainer + c, g * trainers + c) for c in range(trainers)]
        )
    final = delta
    for first_apart in range(1, trainers, group_count):
        meets = [
            (g * trainers + c, g * trainers + (c ^ (first_apart + g)))
            for g in range(group_count)
            for c in range(trainers)
            if first_apart + g < trainers
        ]
        final = final + lax.ppermute(held, everyone, meets)
    for apart in (1, 2):
        final = final + lax.ppermute(
            final,
            everyone,
            [(g * trainers + c, (g ^ apart) * trainers + c) for g in range(group_count) for c in range(trainers)],
        )

    share_size = NPARAM // (group_count * trainers)
    share_start = (my_group * trainers + my_column) * share_size
    momentum_share = lax.dynamic_slice_in_dim(momentum, share_start, share_size)
    master_share = lax.dynamic_slice_in_dim(master, share_start, share_size)
    inverse = 1.0 / jnp.sqrt(jnp.sum(final * final) / NPARAM + norm_epsilon)
    delta_share = lax.dynamic_slice_in_dim(final, share_start, share_size)
    new_momentum = momentum_decay * momentum_share + delta_share * inverse
    new_master = master_share - outer_rate * new_momentum
    return (new_brick[None], new_master, new_momentum)


def solution(mesh):
    in_specs = (P("grp", None, "gx", "gy", None), P(), P(), P(), P(), P(), P(), P())
    out_specs = (P("grp", None, "gx", "gy", None), P(("grp", "gx", "gy")), P(("grp", "gx", "gy")))
    return jax.shard_map(
        on_device, mesh=mesh, in_specs=in_specs, out_specs=out_specs, check_vma=False
    )
```

```python
import functools

import jax
import jax.numpy as jnp
import numpy as np
from jax import lax
from jax.experimental import pallas as pl
from jax.experimental.pallas import tpu as pltpu
from jax.sharding import PartitionSpec as P

F = 5
CH = 64
HID = 64
SUB = 16
TCAP = 6
INNER = 3
CELLS = 4096
NPARAM = 17280
TAPS = 27
PAIRS = TCAP // 2
COLS = (SUB + 2) * 128
PATCH = 16 * F
STACK = 3 * PATCH

time_step = 0.1
base_viscosity = 0.02
viscosity_gain = 0.2
buoyancy = 0.5
inner_rate = 0.02
outer_rate = 0.01
momentum_decay = 0.9
norm_epsilon = 1e-06


def patch_position(row):
    group, py, pz = row // 4, row // 2 % 2, row % 2
    ypos = py + 1 if group in (0, 2) else (3 if py == 0 else 0)
    zpos = pz + 1 if group in (0, 1) else (3 if pz == 0 else 0)
    return ypos - 1, zpos - 1


def selections():
    first = np.zeros((4, 256, STACK), np.float32)
    last = np.zeros((4, 256, STACK), np.float32)
    for cell in range(4):
        py, pz = cell // 2, cell % 2
        for kx in range(3):
            for channel in range(F):
                for row in range(16):
                    ypos, zpos = patch_position(row)
                    column = kx * PATCH + channel * 16 + row
                    dy, dz = ypos - py, zpos - pz
                    if abs(dy) <= 1 and abs(dz) <= 1:
                        tap = 9 * kx + 3 * (dy + 1) + dz + 1
                        first[cell, tap * F + channel, column] = 1.0
                        last[cell, channel * TAPS + 26 - tap, column] = 1.0
    return first, last


SELECT_FIRST, SELECT_LAST = selections()


def column_of(place, x_step, y_step):
    gx = lax.rem(place[1] + x_step + place[5], place[5])
    gy = lax.rem(place[2] + y_step + place[4], place[4])
    return gx * place[4] + gy


def owner_apart(owner, place, y_devices, x_devices):
    group, column = divmod(owner, x_devices * y_devices)
    y_apart = jnp.bitwise_xor(place[2], jnp.int32(column % y_devices))
    return group, y_apart, jnp.bitwise_xor(place[1], jnp.int32(column // y_devices))


def pick_kernel(y_devices, x_devices, apart, trainer_of, place, *refs):
    near, chosen, owners = refs[:y_devices], refs[y_devices], refs[y_devices + 1]
    wanted = jnp.bitwise_xor(place[1], jnp.int32(apart)) * y_devices + place[2]
    count = jnp.int32(0)
    for owner in range(trainer_of.shape[0]):
        group, y_apart, x_apart = owner_apart(owner, place, y_devices, x_devices)
        mine = (trainer_of[owner] == wanted) & (x_apart == 0)

        @pl.when(mine)
        def _():
            owners[0, count] = y_apart
            owners[1, count] = group

        count = count + jnp.where(mine, 1, 0)

    def copy_slot(slot, carry):
        for source in range(y_devices):

            @pl.when(owners[0, slot] == source)
            def _():
                chosen[slot] = near[source][owners[1, slot]]

        return carry

    lax.fori_loop(0, count, copy_slot, 0)


def pick_cubes(trainer_of, place, near, y_devices, x_devices, apart):
    vmem = pl.BlockSpec(memory_space=pltpu.VMEM)
    smem = pl.BlockSpec(memory_space=pltpu.SMEM)
    return pl.pallas_call(
        functools.partial(pick_kernel, y_devices, x_devices, apart),
        out_shape=jax.ShapeDtypeStruct((TCAP, *near[0].shape[1:]), near[0].dtype),
        in_specs=[smem, smem] + [vmem] * len(near),
        out_specs=vmem,
        scratch_shapes=[pltpu.SMEM((2, TCAP), jnp.int32)],
        compiler_params=pltpu.CompilerParams(vmem_limit_bytes=16 * 1024 * 1024),
        name="pick_cubes",
    )(trainer_of, place, *near)


def dot_rows(left, right):
    return jnp.dot(left, right, preferred_element_type=jnp.float32)


def dot_lanes(left, right):
    return lax.dot_general(left, right, (((1,), (1,)), ((), ())), preferred_element_type=jnp.float32)


def patch_masks():
    row = lax.broadcasted_iota(jnp.int32, (8, 128), 0)
    lane = lax.broadcasted_iota(jnp.int32, (8, 128), 1)
    z, y = lane % 8, lane // 8 % 8
    even_z, even_y = row % 2 == 0, row // 2 % 2 == 0
    return {
        "centre": row < 4,
        "even_z": even_z,
        "even_y": even_y,
        "gather_z": jnp.where(even_z, z, 7 - z) < 7,
        "gather_y": jnp.where(even_y, y, 7 - y) < 7,
        "scatter_z": jnp.where(even_z, z, 7 - z) > 0,
        "scatter_y": jnp.where(even_y, y, 7 - y) > 0,
    }


def edge_shift(values, step, even, inside, gather):
    before, after = pltpu.roll(values, step, 1), pltpu.roll(values, 128 - step, 1)
    moved = jnp.where(even, after, before) if gather else jnp.where(even, before, after)
    return jnp.where(inside, moved, 0.0)


def patch_stack(rows, masks):
    both = jnp.where(masks["centre"], rows, pltpu.roll(rows, 4, 0))
    y_edge = edge_shift(both, 8, masks["even_y"], masks["gather_y"], True)
    upper = jnp.where(masks["centre"], both, y_edge)
    return upper, edge_shift(upper, 1, masks["even_z"], masks["gather_z"], True)


def patch_fold(upper, lower, masks):
    line = upper + edge_shift(lower, 1, masks["even_z"], masks["scatter_z"], False)
    return line + pltpu.roll(edge_shift(line, 8, masks["even_y"], masks["scatter_y"], False), 4, 0)


def store_planes(ref, x, channels):
    stacked = jnp.concatenate([part for both in channels for part in both], axis=0).astype(jnp.bfloat16)
    for kx in range(3):
        start = pl.multiple_of((x + 2 - kx) * 128, 128)
        ref[kx * PATCH : (kx + 1) * PATCH, pl.ds(start, 128)] = stacked


def train_kernel(y_devices, x_devices, *refs):
    sources = y_devices + x_devices - 1
    (trainer_of, place, first_ref, last_ref, far_first, far_last) = refs[:6]
    arrived = refs[6 : 6 + sources]
    fields_ref = refs[6 + sources]
    delta_first, delta_last, new_fields_ref = refs[7 + sources : 10 + sources]
    (
        slots,
        picked,
        cubes,
        big_first,
        big_last,
        big_last_t,
        grad_first,
        grad_last,
        now_first,
        now_last,
        brick,
        select_first,
        select_last,
        slot_sems,
        field_sem,
        select_sems,
        *pair_refs,
    ) = refs[10 + sources :]
    targets, tables, inputs, errors, hiddens, pre_grads, slopes, partial_out, raw = [
        pair_refs[kind * PAIRS : (kind + 1) * PAIRS] for kind in range(9)
    ]

    field_in = pltpu.make_async_copy(fields_ref, brick, field_sem)
    field_out = pltpu.make_async_copy(brick, new_fields_ref, field_sem)
    select_copies = [
        pltpu.make_async_copy(far_first, select_first, select_sems.at[0]),
        pltpu.make_async_copy(far_last, select_last, select_sems.at[1]),
    ]

    column = place[1] * y_devices + place[2]
    for other in range(x_devices):
        picked[other] = 0
    count = jnp.int32(0)
    for owner in range(trainer_of.shape[0]):
        group, y_apart, x_apart = owner_apart(owner, place, y_devices, x_devices)
        mine = trainer_of[owner] == column

        @pl.when(mine)
        def _():
            near = x_apart == 0
            slots[0, count] = jnp.where(near, y_apart, y_devices - 1 + x_apart)
            slots[1, count] = jnp.where(near, group, picked[x_apart])
            picked[x_apart] = picked[x_apart] + 1

        count = count + jnp.where(mine, 1, 0)

    def fetch(slot, wait):
        for source in range(sources):

            @pl.when((slot < count) & (slots[0, slot] == source))
            def _():
                copy = pltpu.make_async_copy(
                    arrived[source].at[slots[1, slot]], cubes.at[slot], slot_sems.at[slot]
                )
                copy.wait() if wait else copy.start()

    for slot in range(TCAP):
        fetch(slot, False)

    for copy in select_copies:
        copy.start()
    field_in.start()
    for slot in range(TCAP):

        @pl.when(slot >= count)
        def _():
            cubes[slot] = jnp.zeros(cubes.shape[1:], jnp.bfloat16)

    masks = patch_masks()
    for ref in (*errors, *inputs):
        ref[:PATCH, 128:256] = jnp.zeros((PATCH, 128), jnp.bfloat16)
        ref[2 * PATCH :, COLS - 256 : COLS - 128] = jnp.zeros((PATCH, 128), jnp.bfloat16)
    for ref in partial_out:
        ref[:, :128] = jnp.zeros((STACK, 128), jnp.float32)
        ref[:, COLS - 128 :] = jnp.zeros((STACK, 128), jnp.float32)
    lane = lax.broadcasted_iota(jnp.int32, (8, 128), 1)
    full_weight = 2.0 * (1.0 / (jnp.full((8, 128), count, jnp.int32).astype(jnp.float32) * CELLS))
    weights = [
        jnp.where(lane // 64 + 2 * pair < count, full_weight, 0.0) for pair in range(PAIRS)
    ]
    start_first = first_ref[...].astype(jnp.bfloat16).astype(jnp.float32)
    start_last = last_ref[...].T.astype(jnp.bfloat16).astype(jnp.float32)
    now_first[...] = start_first
    now_last[...] = start_last

    for slot in range(TCAP):
        fetch(slot, True)

    low_lanes = lax.broadcasted_iota(jnp.int32, (SUB * F * 2, 128), 1) < 64
    for pair in range(PAIRS):
        for kind, ref in enumerate((tables[pair], targets[pair])):
            rows = slice(kind * SUB * F * 2, (kind + 1) * SUB * F * 2)
            even = cubes[2 * pair, rows, :].astype(jnp.float32)
            odd = cubes[2 * pair + 1, rows, :].astype(jnp.float32)
            ref[0] = jnp.where(low_lanes, even, pltpu.roll(odd, 64, 1))
            ref[1] = jnp.where(low_lanes, pltpu.roll(even, 64, 1), odd)

    def patch_cells(ref, quarter, plane, channel):
        start = pl.multiple_of(channel * 32 + quarter % 2 * 16 + plane // 2 * 8, 8)
        rows = ref[quarter // 2, pl.ds(start, 8), :]
        return rows if plane % 2 == 0 else pltpu.roll(rows, 4, 0)

    def stack_planes(quarter, carry):
        for pair in range(PAIRS):
            for plane in range(4):
                x = quarter * 4 + plane
                channels = [
                    patch_stack(patch_cells(tables[pair], quarter, plane, c), masks) for c in range(F)
                ]
                store_planes(inputs[pair], x, channels)
        return carry

    lax.fori_loop(0, 4, stack_planes, 0, unroll=4)

    for copy in select_copies:
        copy.wait()
    field_in.wait()
    field_out.start()

    def train_step(step, step_carry):
        first_now = now_first[...].astype(jnp.bfloat16)
        last_now = now_last[...].astype(jnp.bfloat16)
        for cell in range(4):
            rows = slice(cell * CH, (cell + 1) * CH)
            big_first[rows, :] = (0.5 * dot_rows(first_now, select_first[cell])).astype(jnp.bfloat16)
            spread_last = dot_rows(last_now, select_last[cell])
            big_last[rows, :] = (0.5 * spread_last).astype(jnp.bfloat16)
            big_last_t[:, rows] = spread_last.T.astype(jnp.bfloat16)
        grad_first[...] = jnp.zeros(grad_first.shape, jnp.float32)
        grad_last[...] = jnp.zeros(grad_last.shape, jnp.float32)

        def columns_of(quarter):
            return pl.ds(pl.multiple_of(quarter * 512 + 128, 128), 512)

        def first_layer(pair, quarter):
            columns = columns_of(quarter)
            raw[pair][:, columns] = dot_rows(big_first[...], inputs[pair][:, columns])

        def activate(pair, quarter):
            columns = columns_of(quarter)
            for part in range(8):
                rows = slice(part * 32, (part + 1) * 32)
                half = raw[pair][rows, columns]
                curve = jnp.tanh(half)
                above = 1.0 + curve
                value = half * above
                hiddens[pair][rows, columns] = value.astype(jnp.bfloat16)
                slopes[pair][rows, columns] = above + value * (1.0 - curve)

        def last_layer(pair, quarter):
            columns = columns_of(quarter)
            partial_out[pair][:, columns] = dot_rows(big_last_t[...], hiddens[pair][:, columns])

        def find_errors(pair, quarter):
            for plane in range(4):
                x = quarter * 4 + plane
                column = pl.multiple_of((x + 1) * 128, 128)
                total = (
                    partial_out[pair][0:PATCH, pl.ds(pl.multiple_of(column + 128, 128), 128)]
                    + partial_out[pair][PATCH : 2 * PATCH, pl.ds(column, 128)]
                    + partial_out[pair][2 * PATCH :, pl.ds(pl.multiple_of(column - 128, 128), 128)]
                )
                channels = []
                for c in range(F):
                    predicted = patch_fold(
                        total[16 * c : 16 * c + 8], total[16 * c + 8 : 16 * c + 16], masks
                    )
                    wanted = patch_cells(targets[pair], quarter, plane, c)
                    error = weights[pair] * (predicted - wanted)
                    channels.append(patch_stack(error, masks))
                store_planes(errors[pair], x, channels)

        def hidden_layer(pair, quarter):
            columns = columns_of(quarter)
            raw[pair][:, columns] = dot_rows(big_last[...], errors[pair][:, columns])

        def scale(pair, quarter):
            columns = columns_of(quarter)
            for part in range(8):
                rows = slice(part * 32, (part + 1) * 32)
                product = raw[pair][rows, columns] * slopes[pair][rows, columns]
                pre_grads[pair][rows, columns] = product.astype(jnp.bfloat16)

        def gradients(pair, quarter):
            columns = columns_of(quarter)
            grad_first[...] += dot_lanes(pre_grads[pair][:, columns], inputs[pair][:, columns])
            grad_last[...] += dot_lanes(hiddens[pair][:, columns], errors[pair][:, columns])

        stages = (first_layer, activate, last_layer, find_errors, hidden_layer, scale, gradients)
        for turn in range(len(stages) + PAIRS - 1):

            def run(quarter, carry):
                for pair in range(PAIRS):
                    if 0 <= turn - pair < len(stages):
                        stages[turn - pair](pair, quarter)
                return carry

            lax.fori_loop(0, 4, run, 0, unroll=4)

        def folded(grad, select_ref):
            total = jnp.zeros((3 * CH, 256), jnp.float32)
            for cell in range(4):
                rest = grad[cell * CH : (cell + 1) * CH, :]
                parts = []
                for _ in range(3):
                    parts.append(rest.astype(jnp.bfloat16))
                    rest = rest - parts[-1].astype(jnp.float32)
                total = total + dot_lanes(jnp.concatenate(parts, axis=0), select_ref[cell])
            return total[:CH] + total[CH : 2 * CH] + total[2 * CH :]

        now_first[...] = now_first[...] - inner_rate * folded(grad_first, select_first)
        now_last[...] = now_last[...] - inner_rate * folded(grad_last, select_last)
        return step_carry

    lax.fori_loop(0, INNER, train_step, 0)
    delta_first[...] = start_first - now_first[...]
    delta_last[...] = (start_last - now_last[...]).T
    field_out.wait()


def train_cubes(trainer_of, place, first, last, selects, arrived, fields, y_devices, x_devices):
    vmem = pl.BlockSpec(memory_space=pltpu.VMEM)
    smem = pl.BlockSpec(memory_space=pltpu.SMEM)
    anywhere = pl.BlockSpec(memory_space=pl.ANY)
    hbm = pl.BlockSpec(memory_space=pltpu.HBM)
    return pl.pallas_call(
        functools.partial(train_kernel, y_devices, x_devices),
        out_shape=(
            jax.ShapeDtypeStruct((CH, 256), jnp.float32),
            jax.ShapeDtypeStruct((256, CH), jnp.float32),
            jax.ShapeDtypeStruct(fields.shape, fields.dtype),
        ),
        in_specs=[smem] * 2 + [vmem] * 2 + [hbm] * 2 + [anywhere] * len(arrived) + [hbm],
        out_specs=(vmem, vmem, hbm),
        scratch_shapes=[
            pltpu.SMEM((2, TCAP), jnp.int32),
            pltpu.SMEM((x_devices,), jnp.int32),
            pltpu.VMEM((TCAP, 4 * SUB * F, 128), jnp.bfloat16),
            pltpu.VMEM((4 * CH, STACK), jnp.bfloat16),
            pltpu.VMEM((4 * CH, STACK), jnp.bfloat16),
            pltpu.VMEM((STACK, 4 * CH), jnp.bfloat16),
            pltpu.VMEM((4 * CH, STACK), jnp.float32),
            pltpu.VMEM((4 * CH, STACK), jnp.float32),
            pltpu.VMEM((CH, 256), jnp.float32),
            pltpu.VMEM((CH, 256), jnp.float32),
            pltpu.VMEM(fields.shape, fields.dtype),
            pltpu.VMEM((4, 256, STACK), jnp.bfloat16),
            pltpu.VMEM((4, 256, STACK), jnp.bfloat16),
            pltpu.SemaphoreType.DMA((TCAP,)),
            pltpu.SemaphoreType.DMA,
            pltpu.SemaphoreType.DMA((2,)),
        ]
        + [pltpu.VMEM((2, SUB * F * 2, 128), jnp.float32)] * (2 * PAIRS)
        + [pltpu.VMEM((STACK, COLS), jnp.bfloat16)] * (2 * PAIRS)
        + [pltpu.VMEM((4 * CH, COLS), jnp.bfloat16)] * (2 * PAIRS)
        + [pltpu.VMEM((4 * CH, COLS), jnp.float32)] * PAIRS
        + [pltpu.VMEM((STACK, COLS), jnp.float32)] * PAIRS
        + [pltpu.VMEM((4 * CH, COLS), jnp.float32)] * PAIRS,
        compiler_params=pltpu.CompilerParams(vmem_limit_bytes=52 * 1024 * 1024),
        name="train_cubes",
    )(
        trainer_of,
        place,
        first,
        last,
        *selects,
        *arrived,
        fields,
    )


def viscosity_of(cells, closure):
    def unit(h, total):
        half = closure[F, h] + closure[0, h] * cells[0]
        for f in range(1, F):
            half = half + closure[f, h] * cells[f]
        return total + closure[F + 1, h] * (half * jnp.tanh(half))

    total = closure[F, HID] + closure[0, HID] * cells[0]
    for f in range(1, F):
        total = total + closure[f, HID] * cells[f]
    total = lax.fori_loop(0, HID, unit, total, unroll=8)
    soft = jnp.maximum(total, 0.0) + jnp.log1p(jnp.exp(-jnp.abs(total)))
    return base_viscosity + viscosity_gain * soft


def viscosity_kernel(closure, fields, viscosity):
    x_cells, y_cells = fields.shape[1:3]
    part = y_cells // 2

    def plane(x, carry):
        for half in range(2):
            rows = pl.ds(half * part, part)
            viscosity[x, rows, :] = viscosity_of([fields[f, x, rows, :] for f in range(F)], closure)
        return carry

    lax.fori_loop(0, x_cells, plane, 0)


def half_viscosity(closure, fields, side):
    count, x_cells, y_cells, z_cells = fields.shape
    return pl.pallas_call(
        viscosity_kernel,
        grid=(1,),
        out_shape=jax.ShapeDtypeStruct((x_cells // 2, y_cells, z_cells), fields.dtype),
        in_specs=[
            pl.BlockSpec(memory_space=pltpu.SMEM),
            pl.BlockSpec((count, x_cells // 2, y_cells, z_cells), lambda i: (0, side, 0, 0)),
        ],
        out_specs=pl.BlockSpec((x_cells // 2, y_cells, z_cells), lambda i: (0, 0, 0)),
        compiler_params=pltpu.CompilerParams(vmem_limit_bytes=16 * 1024 * 1024),
        name="half_viscosity",
    )(closure, fields)


def evolve_kernel(place, low_viscosity, high_viscosity, fields, x_halo, y_first, y_second, new_fields):
    up_first = lax.rem(place[2], 2) == 0
    x_cells, y_cells, z_cells = fields.shape[1:]
    row = lax.broadcasted_iota(jnp.int32, (y_cells, z_cells), 0)
    lane = lax.broadcasted_iota(jnp.int32, (y_cells, z_cells), 1)

    def plane(x, carry):
        centre = [fields[f, x] for f in range(F)]
        low_x = jnp.minimum(x, x_cells // 2 - 1)
        high_x = jnp.maximum(x - x_cells // 2, 0)
        viscosity = jnp.where(x < x_cells // 2, low_viscosity[low_x], high_viscosity[high_x])
        below = jnp.maximum(x - 1, 0)
        above = jnp.minimum(x + 1, x_cells - 1)
        for f in range(F):
            value = centre[f]
            west = jnp.where(x == 0, x_halo[1, f], fields[f, below])
            east = jnp.where(x == x_cells - 1, x_halo[0, f], fields[f, above])
            first, second = y_first[f, pl.ds(x, 1), :], y_second[f, pl.ds(x, 1), :]
            south = jnp.where(
                row == 0, jnp.where(up_first, second, first), pltpu.roll(value, 1, 0)
            )
            north = jnp.where(
                row == y_cells - 1,
                jnp.where(up_first, first, second),
                pltpu.roll(value, y_cells - 1, 0),
            )
            lower = jnp.where(lane == 0, 0.0, pltpu.roll(value, 1, 1))
            upper = jnp.where(lane == z_cells - 1, 0.0, pltpu.roll(value, z_cells - 1, 1))
            laplacian = east + west + north + south + upper + lower - 6.0 * value
            advection = (
                centre[0] * (east - west) + centre[1] * (north - south) + centre[2] * (upper - lower)
            )
            tendency = viscosity * laplacian - 0.5 * advection
            if f == 2:
                tendency = tendency + buoyancy * centre[3]
            new_fields[f, x] = value + time_step * tendency
        return carry

    lax.fori_loop(0, x_cells, plane, 0)


def evolve(place, viscosities, fields, x_halo, y_first, y_second):
    vmem = pl.BlockSpec(memory_space=pltpu.VMEM)
    return pl.pallas_call(
        evolve_kernel,
        out_shape=jax.ShapeDtypeStruct(fields.shape, fields.dtype),
        in_specs=[pl.BlockSpec(memory_space=pltpu.SMEM)] + [vmem] * 6,
        out_specs=vmem,
        compiler_params=pltpu.CompilerParams(vmem_limit_bytes=16 * 1024 * 1024),
        name="evolve_brick",
    )(place, *viscosities, fields, x_halo, y_first, y_second)


def cell_order():
    order = np.zeros((256, 256), np.float32)
    for y in range(SUB):
        for z in range(SUB):
            order[y * SUB + z, (y % 2 * 2 + z % 2) * 64 + y // 2 * 8 + z // 2] = 1.0
    return order


CELL_ORDER = cell_order()


def corner_of(sample_block, place, x_step, y_step, y_cells, z_cells):
    x_devices, y_devices = place[5], place[4]
    gx = lax.rem(place[1] + x_step + x_devices, x_devices)
    gy = lax.rem(place[2] + y_step + y_devices, y_devices)
    group = jnp.minimum(place[0], place[3] - 1)
    block = sample_block[(group * x_devices + gx) * y_devices + gy]
    z_blocks = z_cells // SUB
    return lax.rem(lax.div(block, z_blocks), y_cells // SUB) * SUB, lax.rem(block, z_blocks) * SUB


def thin_kernel(
    y_cells, z_cells, sample_block, place, rows_ref, lines_ref, thin, x_buffer, y_buffer, x_sems, y_sems
):
    def corner(x_step, y_step):
        return corner_of(sample_block, place, x_step, y_step, y_cells, z_cells)

    lane = lax.broadcasted_iota(jnp.int32, (SUB, 128), 1)
    signs = (-1, 1)
    copies = []
    for side, sign in enumerate(signs):
        z_x, z_y = corner(sign, 0)[1], corner(0, sign)[1]
        x, y = side * (SUB - 1), side * (y_cells - 8)
        for field in range(F):
            copies.append(
                pltpu.make_async_copy(
                    rows_ref.at[
                        pl.ds((field * SUB + x) * y_cells, y_cells),
                        pl.ds(pl.multiple_of(lax.div(z_x, 128) * 128, 128), 128),
                    ],
                    x_buffer.at[pl.ds((side * 8 + field) * y_cells, y_cells)],
                    x_sems.at[side, field],
                )
            )
        copies.append(
            pltpu.make_async_copy(
                lines_ref.at[:, pl.ds(y, 8), pl.ds(pl.multiple_of(lax.div(z_y, 128) * 128, 128), 128)],
                y_buffer.at[side],
                y_sems.at[side],
            )
        )
    for copy in copies:
        copy.start()
    thin[...] = jnp.zeros(thin.shape, thin.dtype)
    for copy in copies:
        copy.wait()

    def moved(values, z, lane_start):
        return pltpu.roll(values, lax.rem(lane_start - lax.rem(z, 128) + 256, 128), 1)

    for side, sign in enumerate(signs):
        z = corner(0, sign)[1]
        total = jnp.zeros((SUB, 128), jnp.float32)
        for field in range(F):
            part = y_buffer[side, field * SUB : (field + 1) * SUB, side * 7, :]
            total = jnp.where(lane // SUB == field, moved(part, z, field * SUB), total)
        thin[column_of(place, 0, sign), :, side * 128 : (side + 1) * 128] = total
    for side, sign in enumerate(signs):
        y, z = corner(sign, 0)
        for half in range(2):
            total = jnp.zeros((8, 128), jnp.float32)
            for step in range(8):
                row = side * 8 * y_cells + y + half * 8 + step
                part = moved(x_buffer[pl.ds(row, 8, y_cells), :], z, step * SUB)
                total = jnp.where(lane[:8] // SUB == step, part, total)
            at = (column_of(place, sign, 0), slice(side * 8, side * 8 + 8), slice(half * 128, half * 128 + 128))
            thin[at] = total


def thin_faces(sample_block, place, brick, columns):
    fields, x_cells, y_cells, z_cells = brick.shape
    vmem = pl.BlockSpec(memory_space=pltpu.VMEM)
    smem = pl.BlockSpec(memory_space=pltpu.SMEM)
    hbm = pl.BlockSpec(memory_space=pltpu.HBM)
    return pl.pallas_call(
        functools.partial(thin_kernel, y_cells, z_cells),
        out_shape=jax.ShapeDtypeStruct((columns, SUB, 256), jnp.float32),
        in_specs=[smem, smem, hbm, hbm],
        out_specs=vmem,
        scratch_shapes=[
            pltpu.VMEM((16 * y_cells, 128), jnp.float32),
            pltpu.VMEM((2, fields * x_cells, 8, 128), jnp.float32),
            pltpu.SemaphoreType.DMA((2, fields)),
            pltpu.SemaphoreType.DMA((2,)),
        ],
        compiler_params=pltpu.CompilerParams(vmem_limit_bytes=16 * 1024 * 1024),
        name="thin_faces",
    )(
        sample_block,
        place,
        brick.reshape(fields * x_cells * y_cells, z_cells),
        brick.reshape(fields * x_cells, y_cells, z_cells),
    )


def sample_kernel(
    y_cells,
    z_cells,
    sample_block,
    place,
    brick,
    centre,
    lower,
    upper,
    own_rows,
    x_edges,
    y_edges,
    windows,
    sems,
):
    rows_of_x = y_cells
    rows_of_field = SUB * y_cells
    window_rows = F * rows_of_field
    copies = [
        pltpu.make_async_copy(
            brick.at[:, pl.ds(w * 128, 128)], windows.at[pl.ds(w * window_rows, window_rows)], sems.at[w]
        )
        for w in range(z_cells // 128)
    ]
    for copy in copies:
        copy.start()
    for copy in copies:
        copy.wait()

    def corner(x_step, y_step):
        return corner_of(sample_block, place, x_step, y_step, y_cells, z_cells)

    def window(row, z):
        return windows[pl.ds(lax.div(z, 128) * window_rows + row, SUB, rows_of_x), :]

    lane = lax.broadcasted_iota(jnp.int32, (SUB, 128), 1)
    y_start, z_start = corner(0, 0)
    z_below = jnp.maximum(z_start - 1, 0)
    z_above = jnp.minimum(z_start + SUB, z_cells - 1)
    for field in range(F):
        for half in range(2):
            inside = jnp.zeros((SUB, 128), jnp.float32)
            below = jnp.zeros((SUB, 128), jnp.float32)
            above = jnp.zeros((SUB, 128), jnp.float32)
            for step in range(8):
                row = field * rows_of_field + y_start + half * 8 + step
                first = step * SUB
                values = jnp.where(lane == 127, window(row, z_below), window(row, z_start))
                values = jnp.where(lane == 0, window(row, z_above), values)
                values = pltpu.roll(values, lax.rem(first - lax.rem(z_start, 128) + 256, 128), 1)
                inside = jnp.where(lane // SUB == step, values, inside)
                below = jnp.where(lane == (first - 1) % 128, values, below)
                above = jnp.where(lane == (first + SUB) % 128, values, above)
            below = jnp.where(z_start == 0, 0.0, pltpu.roll(below, 1, 1))
            above = jnp.where(z_start + SUB == z_cells, 0.0, pltpu.roll(above, 127, 1))
            at = (slice(field * SUB, (field + 1) * SUB), slice(half * 128, (half + 1) * 128))
            centre[at] = inside
            lower[at] = jnp.where(lane % SUB == 0, below, pltpu.roll(inside, 1, 1))
            upper[at] = jnp.where(lane % SUB == SUB - 1, above, pltpu.roll(inside, 127, 1))

    def y_row(y, z):
        total = jnp.zeros((SUB, 128), jnp.float32)
        for field in range(F):
            part = window(field * rows_of_field + y, z)
            part = pltpu.roll(part, lax.rem(field * SUB - lax.rem(z, 128) + 256, 128), 1)
            total = jnp.where(lane // SUB == field, part, total)
        return total

    own_rows[0] = y_row(jnp.maximum(y_start - 1, 0), z_start)
    own_rows[1] = y_row(jnp.minimum(y_start + SUB, y_cells - 1), z_start)
    up_first = lax.rem(place[2], 2) == 0
    for side in range(2):
        y = jnp.where(up_first == (side == 0), y_cells - 1, 0)
        for field in range(F):
            for w in range(z_cells // 128):
                start = w * window_rows + field * rows_of_field + y
                y_edges[side, field, :, w * 128 : (w + 1) * 128] = windows[
                    pl.ds(start, SUB, rows_of_x), :
                ]
    for side, x in enumerate((0, SUB - 1)):
        for field in range(F):
            for w in range(z_cells // 128):
                start = w * window_rows + field * rows_of_field + x * rows_of_x
                x_edges[side, field, :, w * 128 : (w + 1) * 128] = windows[pl.ds(start, rows_of_x), :]


def sample_cube(sample_block, place, brick):
    fields, x_cells, y_cells, z_cells = brick.shape
    vmem = pl.BlockSpec(memory_space=pltpu.VMEM)
    smem = pl.BlockSpec(memory_space=pltpu.SMEM)
    hbm = pl.BlockSpec(memory_space=pltpu.HBM)
    rows = fields * x_cells * y_cells
    cube = jax.ShapeDtypeStruct((F * SUB, 256), jnp.float32)
    return pl.pallas_call(
        functools.partial(sample_kernel, y_cells, z_cells),
        out_shape=(
            cube,
            cube,
            cube,
            jax.ShapeDtypeStruct((2, SUB, 128), jnp.float32),
            jax.ShapeDtypeStruct((2, fields, y_cells, z_cells), jnp.float32),
            jax.ShapeDtypeStruct((2, fields, x_cells, z_cells), jnp.float32),
        ),
        in_specs=[smem, smem, hbm],
        out_specs=(vmem,) * 6,
        scratch_shapes=[
            pltpu.VMEM((z_cells // 128 * rows, 128), jnp.float32),
            pltpu.SemaphoreType.DMA((z_cells // 128,)),
        ],
        compiler_params=pltpu.CompilerParams(vmem_limit_bytes=16 * 1024 * 1024),
        cost_estimate=pl.CostEstimate(flops=0, bytes_accessed=16_000_000, transcendentals=0),
        name="sample_cube",
    )(sample_block, place, brick.reshape(rows, z_cells))


def change_kernel(
    y_cells,
    z_cells,
    sample_block,
    place,
    closure,
    order,
    centre,
    lower,
    upper,
    own_rows,
    thin,
    payload,
    table,
):
    y_start = corner_of(sample_block, place, 0, 0, y_cells, z_cells)[0]
    row = lax.broadcasted_iota(jnp.int32, (SUB, 256), 0)
    lane = lax.broadcasted_iota(jnp.int32, (SUB, 256), 1)
    south_row = jnp.where(y_start == 0, thin[column_of(place, 0, -1), :, 128:], own_rows[0])
    north_row = jnp.where(y_start + SUB == y_cells, thin[column_of(place, 0, 1), :, :128], own_rows[1])
    face_low = thin[column_of(place, -1, 0), 8:, :]
    face_high = thin[column_of(place, 1, 0), :8, :]
    cells = [centre[f * SUB : (f + 1) * SUB, :] for f in range(F)]
    viscosity = viscosity_of(cells, closure)
    changes = []
    for f in range(F):
        value = cells[f]
        west = jnp.where(row == 0, face_low[f : f + 1, :], pltpu.roll(value, 1, 0))
        east = jnp.where(row == SUB - 1, face_high[f : f + 1, :], pltpu.roll(value, SUB - 1, 0))
        edge = pltpu.roll(south_row, (128 - f * SUB) % 128, 1)
        south = jnp.where(lane < SUB, jnp.concatenate([edge, edge], 1), pltpu.roll(value, SUB, 1))
        edge = pltpu.roll(north_row, 112 - f * SUB, 1)
        north = jnp.where(
            lane >= 256 - SUB, jnp.concatenate([edge, edge], 1), pltpu.roll(value, 256 - SUB, 1)
        )
        down = lower[f * SUB : (f + 1) * SUB, :]
        up = upper[f * SUB : (f + 1) * SUB, :]
        laplacian = east + west + north + south + up + down - 6.0 * value
        advection = cells[0] * (east - west) + cells[1] * (north - south) + cells[2] * (up - down)
        change = viscosity * laplacian - 0.5 * advection
        if f == 2:
            change = change + buoyancy * cells[3]
        changes.append(change)
    ordered = dot_rows(jnp.concatenate(cells + changes, axis=0).astype(jnp.bfloat16), order[...])
    low_lanes = lane[:8, :128] < 64
    for part in range(2 * F):
        for cell in range(4):
            columns = slice(cell // 2 * 128, cell // 2 * 128 + 128)
            low = ordered[part * SUB : part * SUB + 8, columns]
            high = ordered[part * SUB + 8 : part * SUB + SUB, columns]
            if cell % 2 == 0:
                high = pltpu.roll(high, 64, 1)
            else:
                low = pltpu.roll(low, 64, 1)
            table[pl.ds(part * 32 + cell, 8, 4), :] = jnp.where(low_lanes, low, high)
    payload[...] = table[...].astype(jnp.bfloat16)


def cube_change(sample_block, place, closure, cube, thin, y_cells, z_cells):
    vmem = pl.BlockSpec(memory_space=pltpu.VMEM)
    smem = pl.BlockSpec(memory_space=pltpu.SMEM)
    return pl.pallas_call(
        functools.partial(change_kernel, y_cells, z_cells),
        out_shape=jax.ShapeDtypeStruct((4 * F * SUB, 128), jnp.bfloat16),
        in_specs=[smem] * 3 + [vmem] * 6,
        out_specs=vmem,
        scratch_shapes=[pltpu.VMEM((4 * F * SUB, 128), jnp.float32)],
        compiler_params=pltpu.CompilerParams(vmem_limit_bytes=16 * 1024 * 1024),
        name="cube_change",
    )(sample_block, place, closure, jnp.asarray(CELL_ORDER, jnp.bfloat16), *cube, thin)


def on_device(
    fields, closure_in, closure_bias, closure_out, master, momentum, sample_block, sample_trainer
):
    group_count = lax.axis_size("grp")
    x_devices = lax.axis_size("gx")
    y_devices = lax.axis_size("gy")
    trainers = x_devices * y_devices
    my_group = lax.axis_index("grp")
    my_column = lax.axis_index("gx") * y_devices + lax.axis_index("gy")
    is_trainer = my_group == group_count - 1
    everyone = ("grp", "gx", "gy")
    sim_groups = group_count - 1
    first_trainer = sim_groups * trainers
    brick = fields[0]
    y_cells, z_cells = brick.shape[2:]
    closure = jnp.concatenate(
        [0.5 * closure_in.T, 0.5 * closure_bias[None], closure_out[None]], axis=0
    )
    linear = jnp.sum(closure * closure_out[None], axis=1, keepdims=True)
    closure = jnp.concatenate([closure, linear], axis=1)
    place = jnp.stack(
        [
            my_group,
            lax.axis_index("gx"),
            lax.axis_index("gy"),
            jnp.int32(sim_groups),
            jnp.int32(y_devices),
            jnp.int32(x_devices),
        ]
    ).astype(jnp.int32)

    def pairs(x_step, even_step):
        found = []
        for g in range(sim_groups):
            for c in range(trainers):
                gx, gy = c // y_devices, c % y_devices
                gx = (gx + x_step) % x_devices
                gy = (gy + (even_step if gy % 2 == 0 else -even_step)) % y_devices
                found.append((g * trainers + c, (g * x_devices + gx) * y_devices + gy))
        return found

    def x_neighbours(edges):
        if x_devices == 2:
            return lax.ppermute(edges, everyone, pairs(1, 0))
        from_high = lax.ppermute(edges[0], everyone, pairs(-1, 0))
        return jnp.stack([from_high, lax.ppermute(edges[1], everyone, pairs(1, 0))])

    def y_neighbours(for_first, for_second):
        return (
            lax.ppermute(for_first, everyone, pairs(0, 1)),
            lax.ppermute(for_second, everyone, pairs(0, -1)),
        )

    def swap(distance):
        return [(first_trainer + c, first_trainer + (c ^ distance)) for c in range(trainers)]

    def to_trainers(payload):
        landed = [
            lax.ppermute(
                payload, everyone, [(g * trainers + c, first_trainer + c) for c in range(trainers)]
            )
            for g in reversed(range(sim_groups))
        ]
        return jnp.stack(landed[::-1])

    def from_line(held):
        return [lax.ppermute(held, everyone, swap(apart)) for apart in range(1, y_devices)]

    def across(apart, held):
        return lax.ppermute(held, everyone, swap(apart * y_devices))

    thin = thin_faces(sample_block, place, brick, trainers)
    *cube, x_edges, y_edges = sample_cube(sample_block, place, brick)
    first_count = CH * TAPS * F
    first = jnp.pad(master[:first_count].reshape(CH, TAPS * F), ((0, 0), (0, 256 - TAPS * F)))
    last = jnp.pad(master[first_count:].reshape(TAPS * F, CH), ((0, 256 - TAPS * F), (0, 0)))

    *cube, first, last = lax.optimization_barrier((*cube, first, last))
    selects = lax.optimization_barrier(
        (jnp.asarray(SELECT_FIRST, jnp.bfloat16), jnp.asarray(SELECT_LAST, jnp.bfloat16))
    )

    thin = lax.all_to_all(thin, ("gx", "gy"), split_axis=0, concat_axis=0, tiled=True)
    payload = cube_change(sample_block, place, closure, cube, thin, y_cells, z_cells)
    landed = to_trainers(payload)
    closure, landed = lax.optimization_barrier((closure, landed))

    def viscosity_part(closure, side):
        return lax.cond(
            is_trainer,
            lambda: jnp.zeros((brick.shape[1] // 2, y_cells, z_cells), jnp.float32),
            lambda: half_viscosity(closure, brick, side),
        )

    low_part = viscosity_part(closure, 0)
    x_edges, y_edges, low_part = lax.optimization_barrier((x_edges, y_edges, low_part))
    x_halo = x_neighbours(x_edges)
    y_halo = y_neighbours(y_edges[0], y_edges[1])
    closure, *y_halo = lax.optimization_barrier((closure, *y_halo))
    viscosity = (low_part, viscosity_part(closure, 1))
    halo = (x_halo, *y_halo)
    near = [landed, *from_line(landed)]
    far = [
        across(apart, pick_cubes(sample_trainer, place, near, y_devices, x_devices, apart))
        for apart in range(1, x_devices)
    ]
    arrived = [*near, *far]

    def train_here():
        delta_first, delta_last, new_brick = train_cubes(
            sample_trainer, place, first, last, selects, arrived, brick, y_devices, x_devices
        )
        delta = jnp.concatenate(
            [delta_first[:, : TAPS * F].reshape(-1), delta_last[: TAPS * F].reshape(-1)]
        )
        return delta, new_brick

    def evolve_here():
        new_brick = evolve(place, viscosity, brick, *halo)
        return jnp.zeros((NPARAM,), jnp.float32), new_brick

    delta, new_brick = lax.cond(is_trainer, train_here, evolve_here)

    held = delta
    for g in range(sim_groups):
        held = held + lax.ppermute(
            delta, everyone, [(first_trainer + c, g * trainers + c) for c in range(trainers)]
        )
    final = delta
    for first_apart in range(1, trainers, group_count):
        meets = [
            (g * trainers + c, g * trainers + (c ^ (first_apart + g)))
            for g in range(group_count)
            for c in range(trainers)
            if first_apart + g < trainers
        ]
        final = final + lax.ppermute(held, everyone, meets)
    for apart in (1, 2):
        final = final + lax.ppermute(
            final,
            everyone,
            [(g * trainers + c, (g ^ apart) * trainers + c) for g in range(group_count) for c in range(trainers)],
        )

    share_size = NPARAM // (group_count * trainers)
    share_start = (my_group * trainers + my_column) * share_size
    momentum_share = lax.dynamic_slice_in_dim(momentum, share_start, share_size)
    master_share = lax.dynamic_slice_in_dim(master, share_start, share_size)
    inverse = 1.0 / jnp.sqrt(jnp.sum(final * final) / NPARAM + norm_epsilon)
    delta_share = lax.dynamic_slice_in_dim(final, share_start, share_size)
    new_momentum = momentum_decay * momentum_share + delta_share * inverse
    new_master = master_share - outer_rate * new_momentum
    return (new_brick[None], new_master, new_momentum)


def solution(mesh):
    in_specs = (P("grp", None, "gx", "gy", None), P(), P(), P(), P(), P(), P(), P())
    out_specs = (P("grp", None, "gx", "gy", None), P(("grp", "gx", "gy")), P(("grp", "gx", "gy")))
    return jax.shard_map(
        on_device, mesh=mesh, in_specs=in_specs, out_specs=out_specs, check_vma=False
    )
```

```python
import functools

import jax
import jax.numpy as jnp
import numpy as np
from jax import lax
from jax.experimental import pallas as pl
from jax.experimental.pallas import tpu as pltpu
from jax.sharding import PartitionSpec as P

F = 5
CH = 64
HID = 64
SUB = 16
TCAP = 6
INNER = 3
CELLS = 4096
NPARAM = 17280
TAPS = 27
PAIRS = TCAP // 2
COLS = (SUB + 2) * 128
PATCH = 16 * F
STACK = 3 * PATCH

time_step = 0.1
base_viscosity = 0.02
viscosity_gain = 0.2
buoyancy = 0.5
inner_rate = 0.02
outer_rate = 0.01
momentum_decay = 0.9
norm_epsilon = 1e-06


def patch_position(row):
    group, py, pz = row // 4, row // 2 % 2, row % 2
    ypos = py + 1 if group in (0, 2) else (3 if py == 0 else 0)
    zpos = pz + 1 if group in (0, 1) else (3 if pz == 0 else 0)
    return ypos - 1, zpos - 1


def selections():
    first = np.zeros((4, 256, STACK), np.float32)
    last = np.zeros((4, 256, STACK), np.float32)
    for cell in range(4):
        py, pz = cell // 2, cell % 2
        for kx in range(3):
            for channel in range(F):
                for row in range(16):
                    ypos, zpos = patch_position(row)
                    column = kx * PATCH + channel * 16 + row
                    dy, dz = ypos - py, zpos - pz
                    if abs(dy) <= 1 and abs(dz) <= 1:
                        tap = 9 * kx + 3 * (dy + 1) + dz + 1
                        first[cell, tap * F + channel, column] = 1.0
                        last[cell, channel * TAPS + 26 - tap, column] = 1.0
    return first, last


SELECT_FIRST, SELECT_LAST = selections()


def column_of(place, x_step, y_step):
    gx = lax.rem(place[1] + x_step + place[5], place[5])
    gy = lax.rem(place[2] + y_step + place[4], place[4])
    return gx * place[4] + gy


def owner_apart(owner, place, y_devices, x_devices):
    group, column = divmod(owner, x_devices * y_devices)
    y_apart = jnp.bitwise_xor(place[2], jnp.int32(column % y_devices))
    return group, y_apart, jnp.bitwise_xor(place[1], jnp.int32(column // y_devices))


def pick_kernel(y_devices, x_devices, apart, trainer_of, place, *refs):
    near, chosen, owners = refs[:y_devices], refs[y_devices], refs[y_devices + 1]
    wanted = jnp.bitwise_xor(place[1], jnp.int32(apart)) * y_devices + place[2]
    count = jnp.int32(0)
    for owner in range(trainer_of.shape[0]):
        group, y_apart, x_apart = owner_apart(owner, place, y_devices, x_devices)
        mine = (trainer_of[owner] == wanted) & (x_apart == 0)

        @pl.when(mine)
        def _():
            owners[0, count] = y_apart
            owners[1, count] = group

        count = count + jnp.where(mine, 1, 0)

    def copy_slot(slot, carry):
        for source in range(y_devices):

            @pl.when(owners[0, slot] == source)
            def _():
                chosen[slot] = near[source][owners[1, slot]]

        return carry

    lax.fori_loop(0, count, copy_slot, 0)


def pick_cubes(trainer_of, place, near, y_devices, x_devices, apart):
    vmem = pl.BlockSpec(memory_space=pltpu.VMEM)
    smem = pl.BlockSpec(memory_space=pltpu.SMEM)
    return pl.pallas_call(
        functools.partial(pick_kernel, y_devices, x_devices, apart),
        out_shape=jax.ShapeDtypeStruct((TCAP, *near[0].shape[1:]), near[0].dtype),
        in_specs=[smem, smem] + [vmem] * len(near),
        out_specs=vmem,
        scratch_shapes=[pltpu.SMEM((2, TCAP), jnp.int32)],
        compiler_params=pltpu.CompilerParams(vmem_limit_bytes=16 * 1024 * 1024),
        name="pick_cubes",
    )(trainer_of, place, *near)


def dot_rows(left, right):
    return jnp.dot(left, right, preferred_element_type=jnp.float32)


def dot_lanes(left, right):
    return lax.dot_general(left, right, (((1,), (1,)), ((), ())), preferred_element_type=jnp.float32)


def patch_masks():
    row = lax.broadcasted_iota(jnp.int32, (8, 128), 0)
    lane = lax.broadcasted_iota(jnp.int32, (8, 128), 1)
    z, y = lane % 8, lane // 8 % 8
    even_z, even_y = row % 2 == 0, row // 2 % 2 == 0
    return {
        "centre": row < 4,
        "even_z": even_z,
        "even_y": even_y,
        "gather_z": jnp.where(even_z, z, 7 - z) < 7,
        "gather_y": jnp.where(even_y, y, 7 - y) < 7,
        "scatter_z": jnp.where(even_z, z, 7 - z) > 0,
        "scatter_y": jnp.where(even_y, y, 7 - y) > 0,
    }


def edge_shift(values, step, even, inside, gather):
    before, after = pltpu.roll(values, step, 1), pltpu.roll(values, 128 - step, 1)
    moved = jnp.where(even, after, before) if gather else jnp.where(even, before, after)
    return jnp.where(inside, moved, 0.0)


def patch_stack(rows, masks):
    both = jnp.where(masks["centre"], rows, pltpu.roll(rows, 4, 0))
    y_edge = edge_shift(both, 8, masks["even_y"], masks["gather_y"], True)
    upper = jnp.where(masks["centre"], both, y_edge)
    return upper, edge_shift(upper, 1, masks["even_z"], masks["gather_z"], True)


def patch_fold(upper, lower, masks):
    line = upper + edge_shift(lower, 1, masks["even_z"], masks["scatter_z"], False)
    return line + pltpu.roll(edge_shift(line, 8, masks["even_y"], masks["scatter_y"], False), 4, 0)


def store_planes(ref, x, channels):
    stacked = jnp.concatenate([part for both in channels for part in both], axis=0).astype(jnp.bfloat16)
    for kx in range(3):
        start = pl.multiple_of((x + 2 - kx) * 128, 128)
        ref[kx * PATCH : (kx + 1) * PATCH, pl.ds(start, 128)] = stacked


def train_kernel(y_devices, x_devices, *refs):
    sources = y_devices + x_devices - 1
    (trainer_of, place, first_ref, last_ref, far_first, far_last) = refs[:6]
    arrived = refs[6 : 6 + sources]
    fields_ref = refs[6 + sources]
    delta_first, delta_last, new_fields_ref = refs[7 + sources : 10 + sources]
    (
        slots,
        picked,
        cubes,
        big_first,
        big_last,
        big_last_t,
        grad_first,
        grad_last,
        now_first,
        now_last,
        brick,
        select_first,
        select_last,
        slot_sems,
        field_sem,
        select_sems,
        *pair_refs,
    ) = refs[10 + sources :]
    targets, tables, inputs, errors, hiddens, pre_grads, slopes, partial_out, raw = [
        pair_refs[kind * PAIRS : (kind + 1) * PAIRS] for kind in range(9)
    ]

    field_in = pltpu.make_async_copy(fields_ref, brick, field_sem)
    field_out = pltpu.make_async_copy(brick, new_fields_ref, field_sem)
    select_copies = [
        pltpu.make_async_copy(far_first, select_first, select_sems.at[0]),
        pltpu.make_async_copy(far_last, select_last, select_sems.at[1]),
    ]

    column = place[1] * y_devices + place[2]
    for other in range(x_devices):
        picked[other] = 0
    count = jnp.int32(0)
    for owner in range(trainer_of.shape[0]):
        group, y_apart, x_apart = owner_apart(owner, place, y_devices, x_devices)
        mine = trainer_of[owner] == column

        @pl.when(mine)
        def _():
            near = x_apart == 0
            slots[0, count] = jnp.where(near, y_apart, y_devices - 1 + x_apart)
            slots[1, count] = jnp.where(near, group, picked[x_apart])
            picked[x_apart] = picked[x_apart] + 1

        count = count + jnp.where(mine, 1, 0)

    def fetch(slot, wait):
        for source in range(sources):

            @pl.when((slot < count) & (slots[0, slot] == source))
            def _():
                copy = pltpu.make_async_copy(
                    arrived[source].at[slots[1, slot]], cubes.at[slot], slot_sems.at[slot]
                )
                copy.wait() if wait else copy.start()

    for slot in range(TCAP):
        fetch(slot, False)

    for copy in select_copies:
        copy.start()
    field_in.start()
    for slot in range(TCAP):

        @pl.when(slot >= count)
        def _():
            cubes[slot] = jnp.zeros(cubes.shape[1:], jnp.bfloat16)

    masks = patch_masks()
    for ref in (*errors, *inputs):
        ref[:PATCH, 128:256] = jnp.zeros((PATCH, 128), jnp.bfloat16)
        ref[2 * PATCH :, COLS - 256 : COLS - 128] = jnp.zeros((PATCH, 128), jnp.bfloat16)
    for ref in partial_out:
        ref[:, :128] = jnp.zeros((STACK, 128), jnp.float32)
        ref[:, COLS - 128 :] = jnp.zeros((STACK, 128), jnp.float32)
    lane = lax.broadcasted_iota(jnp.int32, (8, 128), 1)
    full_weight = 2.0 * (1.0 / (jnp.full((8, 128), count, jnp.int32).astype(jnp.float32) * CELLS))
    weights = [
        jnp.where(lane // 64 + 2 * pair < count, full_weight, 0.0) for pair in range(PAIRS)
    ]
    start_first = first_ref[...].astype(jnp.bfloat16).astype(jnp.float32)
    start_last = last_ref[...].T.astype(jnp.bfloat16).astype(jnp.float32)
    now_first[...] = start_first
    now_last[...] = start_last

    for slot in range(TCAP):
        fetch(slot, True)

    low_lanes = lax.broadcasted_iota(jnp.int32, (SUB * F * 2, 128), 1) < 64
    for pair in range(PAIRS):
        for kind, ref in enumerate((tables[pair], targets[pair])):
            rows = slice(kind * SUB * F * 2, (kind + 1) * SUB * F * 2)
            even = cubes[2 * pair, rows, :].astype(jnp.float32)
            odd = cubes[2 * pair + 1, rows, :].astype(jnp.float32)
            ref[0] = jnp.where(low_lanes, even, pltpu.roll(odd, 64, 1))
            ref[1] = jnp.where(low_lanes, pltpu.roll(even, 64, 1), odd)

    def patch_cells(ref, quarter, plane, channel):
        start = pl.multiple_of(channel * 32 + quarter % 2 * 16 + plane // 2 * 8, 8)
        rows = ref[quarter // 2, pl.ds(start, 8), :]
        return rows if plane % 2 == 0 else pltpu.roll(rows, 4, 0)

    def stack_planes(quarter, carry):
        for pair in range(PAIRS):
            for plane in range(4):
                x = quarter * 4 + plane
                channels = [
                    patch_stack(patch_cells(tables[pair], quarter, plane, c), masks) for c in range(F)
                ]
                store_planes(inputs[pair], x, channels)
        return carry

    lax.fori_loop(0, 4, stack_planes, 0, unroll=2)

    for copy in select_copies:
        copy.wait()
    field_in.wait()
    field_out.start()

    def train_step(step, step_carry):
        first_now = now_first[...].astype(jnp.bfloat16)
        last_now = now_last[...].astype(jnp.bfloat16)
        for cell in range(4):
            rows = slice(cell * CH, (cell + 1) * CH)
            big_first[rows, :] = (0.5 * dot_rows(first_now, select_first[cell])).astype(jnp.bfloat16)
            spread_last = dot_rows(last_now, select_last[cell])
            big_last[rows, :] = (0.5 * spread_last).astype(jnp.bfloat16)
            big_last_t[:, rows] = spread_last.T.astype(jnp.bfloat16)
        grad_first[...] = jnp.zeros(grad_first.shape, jnp.float32)
        grad_last[...] = jnp.zeros(grad_last.shape, jnp.float32)

        def columns_of(quarter):
            return pl.ds(pl.multiple_of(quarter * 512 + 128, 128), 512)

        def first_layer(pair, quarter):
            columns = columns_of(quarter)
            raw[pair][:, columns] = dot_rows(big_first[...], inputs[pair][:, columns])

        def activate(pair, quarter):
            columns = columns_of(quarter)
            for part in range(8):
                rows = slice(part * 32, (part + 1) * 32)
                half = raw[pair][rows, columns]
                curve = jnp.tanh(half)
                above = 1.0 + curve
                value = half * above
                hiddens[pair][rows, columns] = value.astype(jnp.bfloat16)
                slopes[pair][rows, columns] = above + value * (1.0 - curve)

        def last_layer(pair, quarter):
            columns = columns_of(quarter)
            partial_out[pair][:, columns] = dot_rows(big_last_t[...], hiddens[pair][:, columns])

        def find_errors(pair, quarter):
            for plane in range(4):
                x = quarter * 4 + plane
                column = pl.multiple_of((x + 1) * 128, 128)
                total = (
                    partial_out[pair][0:PATCH, pl.ds(pl.multiple_of(column + 128, 128), 128)]
                    + partial_out[pair][PATCH : 2 * PATCH, pl.ds(column, 128)]
                    + partial_out[pair][2 * PATCH :, pl.ds(pl.multiple_of(column - 128, 128), 128)]
                )
                channels = []
                for c in range(F):
                    predicted = patch_fold(
                        total[16 * c : 16 * c + 8], total[16 * c + 8 : 16 * c + 16], masks
                    )
                    wanted = patch_cells(targets[pair], quarter, plane, c)
                    error = weights[pair] * (predicted - wanted)
                    channels.append(patch_stack(error, masks))
                store_planes(errors[pair], x, channels)

        def hidden_layer(pair, quarter):
            columns = columns_of(quarter)
            raw[pair][:, columns] = dot_rows(big_last[...], errors[pair][:, columns])

        def scale(pair, quarter):
            columns = columns_of(quarter)
            for part in range(8):
                rows = slice(part * 32, (part + 1) * 32)
                product = raw[pair][rows, columns] * slopes[pair][rows, columns]
                pre_grads[pair][rows, columns] = product.astype(jnp.bfloat16)

        def gradients(pair, quarter):
            columns = columns_of(quarter)
            grad_first[...] += dot_lanes(pre_grads[pair][:, columns], inputs[pair][:, columns])
            grad_last[...] += dot_lanes(hiddens[pair][:, columns], errors[pair][:, columns])

        stages = (first_layer, activate, last_layer, find_errors, hidden_layer, scale, gradients)
        for turn in range(len(stages) + PAIRS - 1):

            def run(quarter, carry):
                for pair in range(PAIRS):
                    if 0 <= turn - pair < len(stages):
                        stages[turn - pair](pair, quarter)
                return carry

            lax.fori_loop(0, 4, run, 0, unroll=4)

        def folded(grad, select_ref):
            total = jnp.zeros((3 * CH, 256), jnp.float32)
            for cell in range(4):
                rest = grad[cell * CH : (cell + 1) * CH, :]
                parts = []
                for _ in range(3):
                    parts.append(rest.astype(jnp.bfloat16))
                    rest = rest - parts[-1].astype(jnp.float32)
                total = total + dot_lanes(jnp.concatenate(parts, axis=0), select_ref[cell])
            return total[:CH] + total[CH : 2 * CH] + total[2 * CH :]

        now_first[...] = now_first[...] - inner_rate * folded(grad_first, select_first)
        now_last[...] = now_last[...] - inner_rate * folded(grad_last, select_last)
        return step_carry

    lax.fori_loop(0, INNER, train_step, 0)
    delta_first[...] = start_first - now_first[...]
    delta_last[...] = (start_last - now_last[...]).T
    field_out.wait()


def train_cubes(trainer_of, place, first, last, selects, arrived, fields, y_devices, x_devices):
    vmem = pl.BlockSpec(memory_space=pltpu.VMEM)
    smem = pl.BlockSpec(memory_space=pltpu.SMEM)
    anywhere = pl.BlockSpec(memory_space=pl.ANY)
    hbm = pl.BlockSpec(memory_space=pltpu.HBM)
    return pl.pallas_call(
        functools.partial(train_kernel, y_devices, x_devices),
        out_shape=(
            jax.ShapeDtypeStruct((CH, 256), jnp.float32),
            jax.ShapeDtypeStruct((256, CH), jnp.float32),
            jax.ShapeDtypeStruct(fields.shape, fields.dtype),
        ),
        in_specs=[smem] * 2 + [vmem] * 2 + [hbm] * 2 + [anywhere] * len(arrived) + [hbm],
        out_specs=(vmem, vmem, hbm),
        scratch_shapes=[
            pltpu.SMEM((2, TCAP), jnp.int32),
            pltpu.SMEM((x_devices,), jnp.int32),
            pltpu.VMEM((TCAP, 4 * SUB * F, 128), jnp.bfloat16),
            pltpu.VMEM((4 * CH, STACK), jnp.bfloat16),
            pltpu.VMEM((4 * CH, STACK), jnp.bfloat16),
            pltpu.VMEM((STACK, 4 * CH), jnp.bfloat16),
            pltpu.VMEM((4 * CH, STACK), jnp.float32),
            pltpu.VMEM((4 * CH, STACK), jnp.float32),
            pltpu.VMEM((CH, 256), jnp.float32),
            pltpu.VMEM((CH, 256), jnp.float32),
            pltpu.VMEM(fields.shape, fields.dtype),
            pltpu.VMEM((4, 256, STACK), jnp.bfloat16),
            pltpu.VMEM((4, 256, STACK), jnp.bfloat16),
            pltpu.SemaphoreType.DMA((TCAP,)),
            pltpu.SemaphoreType.DMA,
            pltpu.SemaphoreType.DMA((2,)),
        ]
        + [pltpu.VMEM((2, SUB * F * 2, 128), jnp.float32)] * (2 * PAIRS)
        + [pltpu.VMEM((STACK, COLS), jnp.bfloat16)] * (2 * PAIRS)
        + [pltpu.VMEM((4 * CH, COLS), jnp.bfloat16)] * (2 * PAIRS)
        + [pltpu.VMEM((4 * CH, COLS), jnp.float32)] * PAIRS
        + [pltpu.VMEM((STACK, COLS), jnp.float32)] * PAIRS
        + [pltpu.VMEM((4 * CH, COLS), jnp.float32)] * PAIRS,
        compiler_params=pltpu.CompilerParams(vmem_limit_bytes=52 * 1024 * 1024),
        name="train_cubes",
    )(
        trainer_of,
        place,
        first,
        last,
        *selects,
        *arrived,
        fields,
    )


def viscosity_of(cells, closure):
    def unit(h, total):
        half = closure[F, h] + closure[0, h] * cells[0]
        for f in range(1, F):
            half = half + closure[f, h] * cells[f]
        return total + closure[F + 1, h] * (half * jnp.tanh(half))

    total = closure[F, HID] + closure[0, HID] * cells[0]
    for f in range(1, F):
        total = total + closure[f, HID] * cells[f]
    total = lax.fori_loop(0, HID, unit, total, unroll=8)
    soft = jnp.maximum(total, 0.0) + jnp.log1p(jnp.exp(-jnp.abs(total)))
    return base_viscosity + viscosity_gain * soft


def viscosity_kernel(closure, fields, viscosity, weights, out_column):
    x_cells, y_cells, z_cells = fields.shape[1:]
    plain = closure[...]
    high = plain.astype(jnp.bfloat16).astype(jnp.float32)
    low = plain - high
    blank = jnp.zeros((8, 128), jnp.float32)
    for j in range(8):
        turned = [pltpu.roll(part, j, 0) if j else part for part in (high, high, low)]
        stacked = jnp.concatenate([*turned, blank], axis=0)
        weights[j] = stacked.T[: HID + 8].astype(jnp.bfloat16)
    out_column[...] = jnp.broadcast_to(plain.T[:HID, F + 1 : F + 2], (HID, 128))
    sublane = lax.broadcasted_iota(jnp.int32, (8, z_cells), 0)
    wide = z_cells // 128
    tiles = y_cells // 8

    def tile(index, carry):
        x, rows = index // tiles, pl.ds(pl.multiple_of(index % tiles * 8, 8), 8)
        turned = [fields[f, x, rows, :] for f in range(F)]
        turned = [pltpu.roll(turned[f], f, 0) if f else turned[f] for f in range(F)]
        sums = jnp.zeros((8, z_cells), jnp.float32)
        for j in range(8):
            cells = jnp.where(sublane == (j + F) % 8, 1.0, 0.0)
            for f in range(F):
                cells = jnp.where(sublane == (j + f) % 8, turned[f], cells)
            top = cells.astype(jnp.bfloat16).astype(jnp.float32)
            stacked = jnp.concatenate([top, cells - top, top, jnp.zeros_like(top)], axis=0)
            half = dot_rows(weights[j], stacked.astype(jnp.bfloat16))
            total = half[HID:]
            for group in range(HID // 8):
                part = half[group * 8 : group * 8 + 8]
                column = jnp.concatenate([out_column[group * 8 : group * 8 + 8, :]] * wide, axis=1)
                total = total + column * (part * jnp.tanh(part))
            for step in (4, 2, 1):
                total = total + pltpu.roll(total, step, 0)
            sums = jnp.where(sublane == j, total, sums)
        soft = jnp.maximum(sums, 0.0) + jnp.log1p(jnp.exp(-jnp.abs(sums)))
        viscosity[x, rows, :] = base_viscosity + viscosity_gain * soft
        return carry

    lax.fori_loop(0, x_cells * tiles, tile, 0)


def brick_viscosity(closure, fields):
    vmem = pl.BlockSpec(memory_space=pltpu.VMEM)
    return pl.pallas_call(
        viscosity_kernel,
        out_shape=jax.ShapeDtypeStruct(fields.shape[1:], fields.dtype),
        in_specs=[vmem, vmem],
        out_specs=vmem,
        scratch_shapes=[
            pltpu.VMEM((8, HID + 8, 32), jnp.bfloat16),
            pltpu.VMEM((HID, 128), jnp.float32),
        ],
        compiler_params=pltpu.CompilerParams(vmem_limit_bytes=16 * 1024 * 1024),
        name="brick_viscosity",
    )(closure, fields)


def evolve_kernel(place, viscosity, fields, x_halo, y_first, y_second, new_fields):
    up_first = lax.rem(place[2], 2) == 0
    x_cells, y_cells, z_cells = fields.shape[1:]
    row = lax.broadcasted_iota(jnp.int32, (y_cells, z_cells), 0)
    lane = lax.broadcasted_iota(jnp.int32, (y_cells, z_cells), 1)

    def plane(x, carry):
        centre = [fields[f, x] for f in range(F)]
        below = jnp.maximum(x - 1, 0)
        above = jnp.minimum(x + 1, x_cells - 1)
        for f in range(F):
            value = centre[f]
            west = jnp.where(x == 0, x_halo[1, f], fields[f, below])
            east = jnp.where(x == x_cells - 1, x_halo[0, f], fields[f, above])
            first, second = y_first[f, pl.ds(x, 1), :], y_second[f, pl.ds(x, 1), :]
            south = jnp.where(
                row == 0, jnp.where(up_first, second, first), pltpu.roll(value, 1, 0)
            )
            north = jnp.where(
                row == y_cells - 1,
                jnp.where(up_first, first, second),
                pltpu.roll(value, y_cells - 1, 0),
            )
            lower = jnp.where(lane == 0, 0.0, pltpu.roll(value, 1, 1))
            upper = jnp.where(lane == z_cells - 1, 0.0, pltpu.roll(value, z_cells - 1, 1))
            laplacian = east + west + north + south + upper + lower - 6.0 * value
            advection = (
                centre[0] * (east - west) + centre[1] * (north - south) + centre[2] * (upper - lower)
            )
            tendency = viscosity[x] * laplacian - 0.5 * advection
            if f == 2:
                tendency = tendency + buoyancy * centre[3]
            new_fields[f, x] = value + time_step * tendency
        return carry

    lax.fori_loop(0, x_cells, plane, 0)


def evolve(place, viscosity, fields, x_halo, y_first, y_second):
    vmem = pl.BlockSpec(memory_space=pltpu.VMEM)
    return pl.pallas_call(
        evolve_kernel,
        out_shape=jax.ShapeDtypeStruct(fields.shape, fields.dtype),
        in_specs=[pl.BlockSpec(memory_space=pltpu.SMEM)] + [vmem] * 5,
        out_specs=vmem,
        compiler_params=pltpu.CompilerParams(vmem_limit_bytes=16 * 1024 * 1024),
        name="evolve_brick",
    )(place, viscosity, fields, x_halo, y_first, y_second)


def cell_order():
    order = np.zeros((256, 256), np.float32)
    for y in range(SUB):
        for z in range(SUB):
            order[y * SUB + z, (y % 2 * 2 + z % 2) * 64 + y // 2 * 8 + z // 2] = 1.0
    return order


CELL_ORDER = cell_order()


def corner_of(sample_block, place, x_step, y_step, y_cells, z_cells):
    x_devices, y_devices = place[5], place[4]
    gx = lax.rem(place[1] + x_step + x_devices, x_devices)
    gy = lax.rem(place[2] + y_step + y_devices, y_devices)
    group = jnp.minimum(place[0], place[3] - 1)
    block = sample_block[(group * x_devices + gx) * y_devices + gy]
    z_blocks = z_cells // SUB
    return lax.rem(lax.div(block, z_blocks), y_cells // SUB) * SUB, lax.rem(block, z_blocks) * SUB


def thin_kernel(
    y_cells, z_cells, sample_block, place, rows_ref, lines_ref, thin, x_buffer, y_buffer, x_sems, y_sems
):
    def corner(x_step, y_step):
        return corner_of(sample_block, place, x_step, y_step, y_cells, z_cells)

    lane = lax.broadcasted_iota(jnp.int32, (SUB, 128), 1)
    signs = (-1, 1)
    copies = []
    for side, sign in enumerate(signs):
        z_x, z_y = corner(sign, 0)[1], corner(0, sign)[1]
        x, y = side * (SUB - 1), side * (y_cells - 8)
        for field in range(F):
            copies.append(
                pltpu.make_async_copy(
                    rows_ref.at[
                        pl.ds((field * SUB + x) * y_cells, y_cells),
                        pl.ds(pl.multiple_of(lax.div(z_x, 128) * 128, 128), 128),
                    ],
                    x_buffer.at[pl.ds((side * 8 + field) * y_cells, y_cells)],
                    x_sems.at[side, field],
                )
            )
        copies.append(
            pltpu.make_async_copy(
                lines_ref.at[:, pl.ds(y, 8), pl.ds(pl.multiple_of(lax.div(z_y, 128) * 128, 128), 128)],
                y_buffer.at[side],
                y_sems.at[side],
            )
        )
    for copy in copies:
        copy.start()
    thin[...] = jnp.zeros(thin.shape, thin.dtype)
    for copy in copies:
        copy.wait()

    def moved(values, z, lane_start):
        return pltpu.roll(values, lax.rem(lane_start - lax.rem(z, 128) + 256, 128), 1)

    for side, sign in enumerate(signs):
        z = corner(0, sign)[1]
        total = jnp.zeros((SUB, 128), jnp.float32)
        for field in range(F):
            part = y_buffer[side, field * SUB : (field + 1) * SUB, side * 7, :]
            total = jnp.where(lane // SUB == field, moved(part, z, field * SUB), total)
        thin[column_of(place, 0, sign), :, side * 128 : (side + 1) * 128] = total
    for side, sign in enumerate(signs):
        y, z = corner(sign, 0)
        for half in range(2):
            total = jnp.zeros((8, 128), jnp.float32)
            for step in range(8):
                row = side * 8 * y_cells + y + half * 8 + step
                part = moved(x_buffer[pl.ds(row, 8, y_cells), :], z, step * SUB)
                total = jnp.where(lane[:8] // SUB == step, part, total)
            at = (column_of(place, sign, 0), slice(side * 8, side * 8 + 8), slice(half * 128, half * 128 + 128))
            thin[at] = total


def thin_faces(sample_block, place, brick, columns):
    fields, x_cells, y_cells, z_cells = brick.shape
    vmem = pl.BlockSpec(memory_space=pltpu.VMEM)
    smem = pl.BlockSpec(memory_space=pltpu.SMEM)
    hbm = pl.BlockSpec(memory_space=pltpu.HBM)
    return pl.pallas_call(
        functools.partial(thin_kernel, y_cells, z_cells),
        out_shape=jax.ShapeDtypeStruct((columns, SUB, 256), jnp.float32),
        in_specs=[smem, smem, hbm, hbm],
        out_specs=vmem,
        scratch_shapes=[
            pltpu.VMEM((16 * y_cells, 128), jnp.float32),
            pltpu.VMEM((2, fields * x_cells, 8, 128), jnp.float32),
            pltpu.SemaphoreType.DMA((2, fields)),
            pltpu.SemaphoreType.DMA((2,)),
        ],
        compiler_params=pltpu.CompilerParams(vmem_limit_bytes=16 * 1024 * 1024),
        name="thin_faces",
    )(
        sample_block,
        place,
        brick.reshape(fields * x_cells * y_cells, z_cells),
        brick.reshape(fields * x_cells, y_cells, z_cells),
    )


def sample_kernel(
    y_cells,
    z_cells,
    sample_block,
    place,
    brick,
    centre,
    lower,
    upper,
    own_rows,
    x_edges,
    y_edges,
    windows,
    sems,
):
    rows_of_x = y_cells
    rows_of_field = SUB * y_cells
    window_rows = F * rows_of_field
    copies = [
        pltpu.make_async_copy(
            brick.at[:, pl.ds(w * 128, 128)], windows.at[pl.ds(w * window_rows, window_rows)], sems.at[w]
        )
        for w in range(z_cells // 128)
    ]
    for copy in copies:
        copy.start()
    for copy in copies:
        copy.wait()

    def corner(x_step, y_step):
        return corner_of(sample_block, place, x_step, y_step, y_cells, z_cells)

    def window(row, z):
        return windows[pl.ds(lax.div(z, 128) * window_rows + row, SUB, rows_of_x), :]

    lane = lax.broadcasted_iota(jnp.int32, (SUB, 128), 1)
    y_start, z_start = corner(0, 0)
    z_below = jnp.maximum(z_start - 1, 0)
    z_above = jnp.minimum(z_start + SUB, z_cells - 1)
    for field in range(F):
        for half in range(2):
            inside = jnp.zeros((SUB, 128), jnp.float32)
            below = jnp.zeros((SUB, 128), jnp.float32)
            above = jnp.zeros((SUB, 128), jnp.float32)
            for step in range(8):
                row = field * rows_of_field + y_start + half * 8 + step
                first = step * SUB
                values = jnp.where(lane == 127, window(row, z_below), window(row, z_start))
                values = jnp.where(lane == 0, window(row, z_above), values)
                values = pltpu.roll(values, lax.rem(first - lax.rem(z_start, 128) + 256, 128), 1)
                inside = jnp.where(lane // SUB == step, values, inside)
                below = jnp.where(lane == (first - 1) % 128, values, below)
                above = jnp.where(lane == (first + SUB) % 128, values, above)
            below = jnp.where(z_start == 0, 0.0, pltpu.roll(below, 1, 1))
            above = jnp.where(z_start + SUB == z_cells, 0.0, pltpu.roll(above, 127, 1))
            at = (slice(field * SUB, (field + 1) * SUB), slice(half * 128, (half + 1) * 128))
            centre[at] = inside
            lower[at] = jnp.where(lane % SUB == 0, below, pltpu.roll(inside, 1, 1))
            upper[at] = jnp.where(lane % SUB == SUB - 1, above, pltpu.roll(inside, 127, 1))

    def y_row(y, z):
        total = jnp.zeros((SUB, 128), jnp.float32)
        for field in range(F):
            part = window(field * rows_of_field + y, z)
            part = pltpu.roll(part, lax.rem(field * SUB - lax.rem(z, 128) + 256, 128), 1)
            total = jnp.where(lane // SUB == field, part, total)
        return total

    own_rows[0] = y_row(jnp.maximum(y_start - 1, 0), z_start)
    own_rows[1] = y_row(jnp.minimum(y_start + SUB, y_cells - 1), z_start)
    up_first = lax.rem(place[2], 2) == 0
    for side in range(2):
        y = jnp.where(up_first == (side == 0), y_cells - 1, 0)
        for field in range(F):
            for w in range(z_cells // 128):
                start = w * window_rows + field * rows_of_field + y
                y_edges[side, field, :, w * 128 : (w + 1) * 128] = windows[
                    pl.ds(start, SUB, rows_of_x), :
                ]
    for side, x in enumerate((0, SUB - 1)):
        for field in range(F):
            for w in range(z_cells // 128):
                start = w * window_rows + field * rows_of_field + x * rows_of_x
                x_edges[side, field, :, w * 128 : (w + 1) * 128] = windows[pl.ds(start, rows_of_x), :]


def sample_cube(sample_block, place, brick):
    fields, x_cells, y_cells, z_cells = brick.shape
    vmem = pl.BlockSpec(memory_space=pltpu.VMEM)
    smem = pl.BlockSpec(memory_space=pltpu.SMEM)
    hbm = pl.BlockSpec(memory_space=pltpu.HBM)
    rows = fields * x_cells * y_cells
    cube = jax.ShapeDtypeStruct((F * SUB, 256), jnp.float32)
    return pl.pallas_call(
        functools.partial(sample_kernel, y_cells, z_cells),
        out_shape=(
            cube,
            cube,
            cube,
            jax.ShapeDtypeStruct((2, SUB, 128), jnp.float32),
            jax.ShapeDtypeStruct((2, fields, y_cells, z_cells), jnp.float32),
            jax.ShapeDtypeStruct((2, fields, x_cells, z_cells), jnp.float32),
        ),
        in_specs=[smem, smem, hbm],
        out_specs=(vmem,) * 6,
        scratch_shapes=[
            pltpu.VMEM((z_cells // 128 * rows, 128), jnp.float32),
            pltpu.SemaphoreType.DMA((z_cells // 128,)),
        ],
        compiler_params=pltpu.CompilerParams(vmem_limit_bytes=16 * 1024 * 1024),
        cost_estimate=pl.CostEstimate(flops=0, bytes_accessed=16_000_000, transcendentals=0),
        name="sample_cube",
    )(sample_block, place, brick.reshape(rows, z_cells))


def change_kernel(
    y_cells,
    z_cells,
    sample_block,
    place,
    closure,
    order,
    centre,
    lower,
    upper,
    own_rows,
    thin,
    payload,
    table,
):
    y_start = corner_of(sample_block, place, 0, 0, y_cells, z_cells)[0]
    row = lax.broadcasted_iota(jnp.int32, (SUB, 256), 0)
    lane = lax.broadcasted_iota(jnp.int32, (SUB, 256), 1)
    south_row = jnp.where(y_start == 0, thin[column_of(place, 0, -1), :, 128:], own_rows[0])
    north_row = jnp.where(y_start + SUB == y_cells, thin[column_of(place, 0, 1), :, :128], own_rows[1])
    face_low = thin[column_of(place, -1, 0), 8:, :]
    face_high = thin[column_of(place, 1, 0), :8, :]
    cells = [centre[f * SUB : (f + 1) * SUB, :] for f in range(F)]
    viscosity = viscosity_of(cells, closure)
    changes = []
    for f in range(F):
        value = cells[f]
        west = jnp.where(row == 0, face_low[f : f + 1, :], pltpu.roll(value, 1, 0))
        east = jnp.where(row == SUB - 1, face_high[f : f + 1, :], pltpu.roll(value, SUB - 1, 0))
        edge = pltpu.roll(south_row, (128 - f * SUB) % 128, 1)
        south = jnp.where(lane < SUB, jnp.concatenate([edge, edge], 1), pltpu.roll(value, SUB, 1))
        edge = pltpu.roll(north_row, 112 - f * SUB, 1)
        north = jnp.where(
            lane >= 256 - SUB, jnp.concatenate([edge, edge], 1), pltpu.roll(value, 256 - SUB, 1)
        )
        down = lower[f * SUB : (f + 1) * SUB, :]
        up = upper[f * SUB : (f + 1) * SUB, :]
        laplacian = east + west + north + south + up + down - 6.0 * value
        advection = cells[0] * (east - west) + cells[1] * (north - south) + cells[2] * (up - down)
        change = viscosity * laplacian - 0.5 * advection
        if f == 2:
            change = change + buoyancy * cells[3]
        changes.append(change)
    ordered = dot_rows(jnp.concatenate(cells + changes, axis=0).astype(jnp.bfloat16), order[...])
    low_lanes = lane[:8, :128] < 64
    for part in range(2 * F):
        for cell in range(4):
            columns = slice(cell // 2 * 128, cell // 2 * 128 + 128)
            low = ordered[part * SUB : part * SUB + 8, columns]
            high = ordered[part * SUB + 8 : part * SUB + SUB, columns]
            if cell % 2 == 0:
                high = pltpu.roll(high, 64, 1)
            else:
                low = pltpu.roll(low, 64, 1)
            table[pl.ds(part * 32 + cell, 8, 4), :] = jnp.where(low_lanes, low, high)
    payload[...] = table[...].astype(jnp.bfloat16)


def cube_change(sample_block, place, closure, cube, thin, y_cells, z_cells):
    vmem = pl.BlockSpec(memory_space=pltpu.VMEM)
    smem = pl.BlockSpec(memory_space=pltpu.SMEM)
    return pl.pallas_call(
        functools.partial(change_kernel, y_cells, z_cells),
        out_shape=jax.ShapeDtypeStruct((4 * F * SUB, 128), jnp.bfloat16),
        in_specs=[smem] * 3 + [vmem] * 6,
        out_specs=vmem,
        scratch_shapes=[pltpu.VMEM((4 * F * SUB, 128), jnp.float32)],
        compiler_params=pltpu.CompilerParams(vmem_limit_bytes=16 * 1024 * 1024),
        name="cube_change",
    )(sample_block, place, closure, jnp.asarray(CELL_ORDER, jnp.bfloat16), *cube, thin)


def on_device(
    fields, closure_in, closure_bias, closure_out, master, momentum, sample_block, sample_trainer
):
    group_count = lax.axis_size("grp")
    x_devices = lax.axis_size("gx")
    y_devices = lax.axis_size("gy")
    trainers = x_devices * y_devices
    my_group = lax.axis_index("grp")
    my_column = lax.axis_index("gx") * y_devices + lax.axis_index("gy")
    is_trainer = my_group == group_count - 1
    everyone = ("grp", "gx", "gy")
    sim_groups = group_count - 1
    first_trainer = sim_groups * trainers
    brick = fields[0]
    y_cells, z_cells = brick.shape[2:]
    closure = jnp.concatenate(
        [0.5 * closure_in.T, 0.5 * closure_bias[None], closure_out[None]], axis=0
    )
    linear = jnp.sum(closure * closure_out[None], axis=1, keepdims=True)
    closure = jnp.pad(jnp.concatenate([closure, linear], axis=1), ((0, 1), (0, 127 - HID)))
    place = jnp.stack(
        [
            my_group,
            lax.axis_index("gx"),
            lax.axis_index("gy"),
            jnp.int32(sim_groups),
            jnp.int32(y_devices),
            jnp.int32(x_devices),
        ]
    ).astype(jnp.int32)

    def pairs(x_step, even_step):
        found = []
        for g in range(sim_groups):
            for c in range(trainers):
                gx, gy = c // y_devices, c % y_devices
                gx = (gx + x_step) % x_devices
                gy = (gy + (even_step if gy % 2 == 0 else -even_step)) % y_devices
                found.append((g * trainers + c, (g * x_devices + gx) * y_devices + gy))
        return found

    def x_neighbours(edges):
        if x_devices == 2:
            return lax.ppermute(edges, everyone, pairs(1, 0))
        from_high = lax.ppermute(edges[0], everyone, pairs(-1, 0))
        return jnp.stack([from_high, lax.ppermute(edges[1], everyone, pairs(1, 0))])

    def y_neighbours(for_first, for_second):
        return (
            lax.ppermute(for_first, everyone, pairs(0, 1)),
            lax.ppermute(for_second, everyone, pairs(0, -1)),
        )

    def swap(distance):
        return [(first_trainer + c, first_trainer + (c ^ distance)) for c in range(trainers)]

    def to_trainers(payload):
        landed = [
            lax.ppermute(
                payload, everyone, [(g * trainers + c, first_trainer + c) for c in range(trainers)]
            )
            for g in reversed(range(sim_groups))
        ]
        return jnp.stack(landed[::-1])

    def from_line(held):
        return [lax.ppermute(held, everyone, swap(apart)) for apart in range(1, y_devices)]

    def across(apart, held):
        return lax.ppermute(held, everyone, swap(apart * y_devices))

    thin = thin_faces(sample_block, place, brick, trainers)
    *cube, x_edges, y_edges = sample_cube(sample_block, place, brick)
    first_count = CH * TAPS * F
    first = jnp.pad(master[:first_count].reshape(CH, TAPS * F), ((0, 0), (0, 256 - TAPS * F)))
    last = jnp.pad(master[first_count:].reshape(TAPS * F, CH), ((0, 256 - TAPS * F), (0, 0)))

    *cube, first, last = lax.optimization_barrier((*cube, first, last))
    selects = lax.optimization_barrier(
        (jnp.asarray(SELECT_FIRST, jnp.bfloat16), jnp.asarray(SELECT_LAST, jnp.bfloat16))
    )

    thin = lax.all_to_all(thin, ("gx", "gy"), split_axis=0, concat_axis=0, tiled=True)
    payload = cube_change(sample_block, place, closure, cube, thin, y_cells, z_cells)
    landed = to_trainers(payload)
    closure, landed = lax.optimization_barrier((closure, landed))

    viscosity = lax.cond(
        is_trainer,
        lambda: jnp.zeros(brick.shape[1:], jnp.float32),
        lambda: brick_viscosity(closure, brick),
    )
    y_edges, viscosity = lax.optimization_barrier((y_edges, viscosity))
    y_halo = y_neighbours(y_edges[0], y_edges[1])
    x_edges, *y_halo = lax.optimization_barrier((x_edges, *y_halo))
    halo = (x_neighbours(x_edges), *y_halo)
    near = [landed, *from_line(landed)]
    far = [
        across(apart, pick_cubes(sample_trainer, place, near, y_devices, x_devices, apart))
        for apart in range(1, x_devices)
    ]
    arrived = [*near, *far]

    def train_here():
        delta_first, delta_last, new_brick = train_cubes(
            sample_trainer, place, first, last, selects, arrived, brick, y_devices, x_devices
        )
        delta = jnp.concatenate(
            [delta_first[:, : TAPS * F].reshape(-1), delta_last[: TAPS * F].reshape(-1)]
        )
        return delta, new_brick

    def evolve_here():
        new_brick = evolve(place, viscosity, brick, *halo)
        return jnp.zeros((NPARAM,), jnp.float32), new_brick

    delta, new_brick = lax.cond(is_trainer, train_here, evolve_here)

    held = delta
    for g in range(sim_groups):
        held = held + lax.ppermute(
            delta, everyone, [(first_trainer + c, g * trainers + c) for c in range(trainers)]
        )
    final = delta
    for first_apart in range(1, trainers, group_count):
        meets = [
            (g * trainers + c, g * trainers + (c ^ (first_apart + g)))
            for g in range(group_count)
            for c in range(trainers)
            if first_apart + g < trainers
        ]
        final = final + lax.ppermute(held, everyone, meets)
    for apart in (1, 2):
        final = final + lax.ppermute(
            final,
            everyone,
            [(g * trainers + c, (g ^ apart) * trainers + c) for g in range(group_count) for c in range(trainers)],
        )

    share_size = NPARAM // (group_count * trainers)
    share_start = (my_group * trainers + my_column) * share_size
    momentum_share = lax.dynamic_slice_in_dim(momentum, share_start, share_size)
    master_share = lax.dynamic_slice_in_dim(master, share_start, share_size)
    inverse = 1.0 / jnp.sqrt(jnp.sum(final * final) / NPARAM + norm_epsilon)
    delta_share = lax.dynamic_slice_in_dim(final, share_start, share_size)
    new_momentum = momentum_decay * momentum_share + delta_share * inverse
    new_master = master_share - outer_rate * new_momentum
    return (new_brick[None], new_master, new_momentum)


def solution(mesh):
    in_specs = (P("grp", None, "gx", "gy", None), P(), P(), P(), P(), P(), P(), P())
    out_specs = (P("grp", None, "gx", "gy", None), P(("grp", "gx", "gy")), P(("grp", "gx", "gy")))
    return jax.shard_map(
        on_device, mesh=mesh, in_specs=in_specs, out_specs=out_specs, check_vma=False
    )
```

```python
import functools

import jax
import jax.numpy as jnp
import numpy as np
from jax import lax
from jax.experimental import pallas as pl
from jax.experimental.pallas import tpu as pltpu
from jax.sharding import PartitionSpec as P

F = 5
CH = 64
HID = 64
SUB = 16
TCAP = 6
INNER = 3
CELLS = 4096
NPARAM = 17280
TAPS = 27
PAIRS = TCAP // 2
COLS = (SUB + 2) * 128
PATCH = 16 * F
STACK = 3 * PATCH

time_step = 0.1
base_viscosity = 0.02
viscosity_gain = 0.2
buoyancy = 0.5
inner_rate = 0.02
outer_rate = 0.01
momentum_decay = 0.9
norm_epsilon = 1e-06


def patch_position(row):
    group, py, pz = row // 4, row // 2 % 2, row % 2
    ypos = py + 1 if group in (0, 2) else (3 if py == 0 else 0)
    zpos = pz + 1 if group in (0, 1) else (3 if pz == 0 else 0)
    return ypos - 1, zpos - 1


def selections():
    first = np.zeros((4, 256, STACK), np.float32)
    last = np.zeros((4, 256, STACK), np.float32)
    for cell in range(4):
        py, pz = cell // 2, cell % 2
        for kx in range(3):
            for channel in range(F):
                for row in range(16):
                    ypos, zpos = patch_position(row)
                    column = kx * PATCH + channel * 16 + row
                    dy, dz = ypos - py, zpos - pz
                    if abs(dy) <= 1 and abs(dz) <= 1:
                        tap = 9 * kx + 3 * (dy + 1) + dz + 1
                        first[cell, tap * F + channel, column] = 1.0
                        last[cell, channel * TAPS + 26 - tap, column] = 1.0
    return first, last


SELECT_FIRST, SELECT_LAST = selections()


def column_of(place, x_step, y_step):
    gx = lax.rem(place[1] + x_step + place[5], place[5])
    gy = lax.rem(place[2] + y_step + place[4], place[4])
    return gx * place[4] + gy


def owner_apart(owner, place, y_devices, x_devices):
    group, column = divmod(owner, x_devices * y_devices)
    y_apart = jnp.bitwise_xor(place[2], jnp.int32(column % y_devices))
    return group, y_apart, jnp.bitwise_xor(place[1], jnp.int32(column // y_devices))


def pick_kernel(y_devices, x_devices, apart, trainer_of, place, *refs):
    near, chosen, owners = refs[:y_devices], refs[y_devices], refs[y_devices + 1]
    wanted = jnp.bitwise_xor(place[1], jnp.int32(apart)) * y_devices + place[2]
    count = jnp.int32(0)
    for owner in range(trainer_of.shape[0]):
        group, y_apart, x_apart = owner_apart(owner, place, y_devices, x_devices)
        mine = (trainer_of[owner] == wanted) & (x_apart == 0)

        @pl.when(mine)
        def _():
            owners[0, count] = y_apart
            owners[1, count] = group

        count = count + jnp.where(mine, 1, 0)

    def copy_slot(slot, carry):
        for source in range(y_devices):

            @pl.when(owners[0, slot] == source)
            def _():
                chosen[slot] = near[source][owners[1, slot]]

        return carry

    lax.fori_loop(0, count, copy_slot, 0)


def pick_cubes(trainer_of, place, near, y_devices, x_devices, apart):
    vmem = pl.BlockSpec(memory_space=pltpu.VMEM)
    smem = pl.BlockSpec(memory_space=pltpu.SMEM)
    return pl.pallas_call(
        functools.partial(pick_kernel, y_devices, x_devices, apart),
        out_shape=jax.ShapeDtypeStruct((TCAP, *near[0].shape[1:]), near[0].dtype),
        in_specs=[smem, smem] + [vmem] * len(near),
        out_specs=vmem,
        scratch_shapes=[pltpu.SMEM((2, TCAP), jnp.int32)],
        compiler_params=pltpu.CompilerParams(vmem_limit_bytes=16 * 1024 * 1024),
        name="pick_cubes",
    )(trainer_of, place, *near)


def dot_rows(left, right):
    return jnp.dot(left, right, preferred_element_type=jnp.float32)


def dot_lanes(left, right):
    return lax.dot_general(left, right, (((1,), (1,)), ((), ())), preferred_element_type=jnp.float32)


def patch_masks():
    row = lax.broadcasted_iota(jnp.int32, (8, 128), 0)
    lane = lax.broadcasted_iota(jnp.int32, (8, 128), 1)
    z, y = lane % 8, lane // 8 % 8
    even_z, even_y = row % 2 == 0, row // 2 % 2 == 0
    return {
        "centre": row < 4,
        "even_z": even_z,
        "even_y": even_y,
        "gather_z": jnp.where(even_z, z, 7 - z) < 7,
        "gather_y": jnp.where(even_y, y, 7 - y) < 7,
        "scatter_z": jnp.where(even_z, z, 7 - z) > 0,
        "scatter_y": jnp.where(even_y, y, 7 - y) > 0,
    }


def edge_shift(values, step, even, inside, gather):
    before, after = pltpu.roll(values, step, 1), pltpu.roll(values, 128 - step, 1)
    moved = jnp.where(even, after, before) if gather else jnp.where(even, before, after)
    return jnp.where(inside, moved, 0.0)


def patch_stack(rows, masks):
    both = jnp.where(masks["centre"], rows, pltpu.roll(rows, 4, 0))
    y_edge = edge_shift(both, 8, masks["even_y"], masks["gather_y"], True)
    upper = jnp.where(masks["centre"], both, y_edge)
    return upper, edge_shift(upper, 1, masks["even_z"], masks["gather_z"], True)


def patch_fold(upper, lower, masks):
    line = upper + edge_shift(lower, 1, masks["even_z"], masks["scatter_z"], False)
    return line + pltpu.roll(edge_shift(line, 8, masks["even_y"], masks["scatter_y"], False), 4, 0)


def store_planes(ref, x, channels):
    stacked = jnp.concatenate([part for both in channels for part in both], axis=0).astype(jnp.bfloat16)
    for kx in range(3):
        start = pl.multiple_of((x + 2 - kx) * 128, 128)
        ref[kx * PATCH : (kx + 1) * PATCH, pl.ds(start, 128)] = stacked


def train_kernel(y_devices, x_devices, *refs):
    sources = y_devices + x_devices - 1
    (trainer_of, place, first_ref, last_ref, far_first, far_last) = refs[:6]
    arrived = refs[6 : 6 + sources]
    fields_ref = refs[6 + sources]
    delta_first, delta_last, new_fields_ref = refs[7 + sources : 10 + sources]
    (
        slots,
        picked,
        cubes,
        big_first,
        big_last,
        big_last_t,
        grad_first,
        grad_last,
        now_first,
        now_last,
        brick,
        select_first,
        select_last,
        slot_sems,
        field_sem,
        select_sems,
        *pair_refs,
    ) = refs[10 + sources :]
    targets, tables, inputs, errors, hiddens, pre_grads, slopes, partial_out, raw = [
        pair_refs[kind * PAIRS : (kind + 1) * PAIRS] for kind in range(9)
    ]

    field_in = pltpu.make_async_copy(fields_ref, brick, field_sem)
    field_out = pltpu.make_async_copy(brick, new_fields_ref, field_sem)
    select_copies = [
        pltpu.make_async_copy(far_first, select_first, select_sems.at[0]),
        pltpu.make_async_copy(far_last, select_last, select_sems.at[1]),
    ]

    column = place[1] * y_devices + place[2]
    for other in range(x_devices):
        picked[other] = 0
    count = jnp.int32(0)
    for owner in range(trainer_of.shape[0]):
        group, y_apart, x_apart = owner_apart(owner, place, y_devices, x_devices)
        mine = trainer_of[owner] == column

        @pl.when(mine)
        def _():
            near = x_apart == 0
            slots[0, count] = jnp.where(near, y_apart, y_devices - 1 + x_apart)
            slots[1, count] = jnp.where(near, group, picked[x_apart])
            picked[x_apart] = picked[x_apart] + 1

        count = count + jnp.where(mine, 1, 0)

    def fetch(slot, wait):
        for source in range(sources):

            @pl.when((slot < count) & (slots[0, slot] == source))
            def _():
                copy = pltpu.make_async_copy(
                    arrived[source].at[slots[1, slot]], cubes.at[slot], slot_sems.at[slot]
                )
                copy.wait() if wait else copy.start()

    for slot in range(TCAP):
        fetch(slot, False)

    for copy in select_copies:
        copy.start()
    field_in.start()
    for slot in range(TCAP):

        @pl.when(slot >= count)
        def _():
            cubes[slot] = jnp.zeros(cubes.shape[1:], jnp.bfloat16)

    masks = patch_masks()
    for ref in (*errors, *inputs):
        ref[:PATCH, 128:256] = jnp.zeros((PATCH, 128), jnp.bfloat16)
        ref[2 * PATCH :, COLS - 256 : COLS - 128] = jnp.zeros((PATCH, 128), jnp.bfloat16)
    for ref in partial_out:
        ref[:, :128] = jnp.zeros((STACK, 128), jnp.float32)
        ref[:, COLS - 128 :] = jnp.zeros((STACK, 128), jnp.float32)
    lane = lax.broadcasted_iota(jnp.int32, (8, 128), 1)
    full_weight = 2.0 * (1.0 / (jnp.full((8, 128), count, jnp.int32).astype(jnp.float32) * CELLS))
    weights = [
        jnp.where(lane // 64 + 2 * pair < count, full_weight, 0.0) for pair in range(PAIRS)
    ]
    start_first = first_ref[...].astype(jnp.bfloat16).astype(jnp.float32)
    start_last = last_ref[...].T.astype(jnp.bfloat16).astype(jnp.float32)
    now_first[...] = start_first
    now_last[...] = start_last

    for slot in range(TCAP):
        fetch(slot, True)

    low_lanes = lax.broadcasted_iota(jnp.int32, (SUB * F * 2, 128), 1) < 64
    for pair in range(PAIRS):
        for kind, ref in enumerate((tables[pair], targets[pair])):
            rows = slice(kind * SUB * F * 2, (kind + 1) * SUB * F * 2)
            even = cubes[2 * pair, rows, :].astype(jnp.float32)
            odd = cubes[2 * pair + 1, rows, :].astype(jnp.float32)
            ref[0] = jnp.where(low_lanes, even, pltpu.roll(odd, 64, 1))
            ref[1] = jnp.where(low_lanes, pltpu.roll(even, 64, 1), odd)

    def patch_cells(ref, quarter, plane, channel):
        start = pl.multiple_of(channel * 32 + quarter % 2 * 16 + plane // 2 * 8, 8)
        rows = ref[quarter // 2, pl.ds(start, 8), :]
        return rows if plane % 2 == 0 else pltpu.roll(rows, 4, 0)

    def stack_planes(quarter, carry):
        for pair in range(PAIRS):
            for plane in range(4):
                x = quarter * 4 + plane
                channels = [
                    patch_stack(patch_cells(tables[pair], quarter, plane, c), masks) for c in range(F)
                ]
                store_planes(inputs[pair], x, channels)
        return carry

    lax.fori_loop(0, 4, stack_planes, 0, unroll=2)

    for copy in select_copies:
        copy.wait()
    field_in.wait()
    field_out.start()

    def train_step(step, step_carry):
        first_now = now_first[...].astype(jnp.bfloat16)
        last_now = now_last[...].astype(jnp.bfloat16)
        for cell in range(4):
            rows = slice(cell * CH, (cell + 1) * CH)
            big_first[rows, :] = (0.5 * dot_rows(first_now, select_first[cell])).astype(jnp.bfloat16)
            spread_last = dot_rows(last_now, select_last[cell])
            big_last[rows, :] = (0.5 * spread_last).astype(jnp.bfloat16)
            big_last_t[:, rows] = spread_last.T.astype(jnp.bfloat16)
        grad_first[...] = jnp.zeros(grad_first.shape, jnp.float32)
        grad_last[...] = jnp.zeros(grad_last.shape, jnp.float32)

        def columns_of(quarter):
            return pl.ds(pl.multiple_of(quarter * 512 + 128, 128), 512)

        def first_layer(pair, quarter):
            columns = columns_of(quarter)
            raw[pair][:, columns] = dot_rows(big_first[...], inputs[pair][:, columns])

        def activate(pair, quarter):
            columns = columns_of(quarter)
            for part in range(8):
                rows = slice(part * 32, (part + 1) * 32)
                half = raw[pair][rows, columns]
                curve = jnp.tanh(half)
                above = 1.0 + curve
                value = half * above
                hiddens[pair][rows, columns] = value.astype(jnp.bfloat16)
                slopes[pair][rows, columns] = above + value * (1.0 - curve)

        def last_layer(pair, quarter):
            columns = columns_of(quarter)
            partial_out[pair][:, columns] = dot_rows(big_last_t[...], hiddens[pair][:, columns])

        def find_errors(pair, quarter):
            for plane in range(4):
                x = quarter * 4 + plane
                column = pl.multiple_of((x + 1) * 128, 128)
                total = (
                    partial_out[pair][0:PATCH, pl.ds(pl.multiple_of(column + 128, 128), 128)]
                    + partial_out[pair][PATCH : 2 * PATCH, pl.ds(column, 128)]
                    + partial_out[pair][2 * PATCH :, pl.ds(pl.multiple_of(column - 128, 128), 128)]
                )
                channels = []
                for c in range(F):
                    predicted = patch_fold(
                        total[16 * c : 16 * c + 8], total[16 * c + 8 : 16 * c + 16], masks
                    )
                    wanted = patch_cells(targets[pair], quarter, plane, c)
                    error = weights[pair] * (predicted - wanted)
                    channels.append(patch_stack(error, masks))
                store_planes(errors[pair], x, channels)

        def hidden_layer(pair, quarter):
            columns = columns_of(quarter)
            raw[pair][:, columns] = dot_rows(big_last[...], errors[pair][:, columns])

        def scale(pair, quarter):
            columns = columns_of(quarter)
            for part in range(8):
                rows = slice(part * 32, (part + 1) * 32)
                product = raw[pair][rows, columns] * slopes[pair][rows, columns]
                pre_grads[pair][rows, columns] = product.astype(jnp.bfloat16)

        def gradients(pair, quarter):
            columns = columns_of(quarter)
            grad_first[...] += dot_lanes(pre_grads[pair][:, columns], inputs[pair][:, columns])
            grad_last[...] += dot_lanes(hiddens[pair][:, columns], errors[pair][:, columns])

        stages = (first_layer, activate, last_layer, find_errors, hidden_layer, scale, gradients)
        for turn in range(len(stages) + PAIRS - 1):

            def run(quarter, carry):
                for pair in range(PAIRS):
                    if 0 <= turn - pair < len(stages):
                        stages[turn - pair](pair, quarter)
                return carry

            lax.fori_loop(0, 4, run, 0, unroll=4)

        def folded(grad, select_ref):
            total = jnp.zeros((3 * CH, 256), jnp.float32)
            for cell in range(4):
                rest = grad[cell * CH : (cell + 1) * CH, :]
                parts = []
                for _ in range(3):
                    parts.append(rest.astype(jnp.bfloat16))
                    rest = rest - parts[-1].astype(jnp.float32)
                total = total + dot_lanes(jnp.concatenate(parts, axis=0), select_ref[cell])
            return total[:CH] + total[CH : 2 * CH] + total[2 * CH :]

        now_first[...] = now_first[...] - inner_rate * folded(grad_first, select_first)
        now_last[...] = now_last[...] - inner_rate * folded(grad_last, select_last)
        return step_carry

    lax.fori_loop(0, INNER, train_step, 0)
    delta_first[...] = start_first - now_first[...]
    delta_last[...] = (start_last - now_last[...]).T
    field_out.wait()


def train_cubes(trainer_of, place, first, last, selects, arrived, fields, y_devices, x_devices):
    vmem = pl.BlockSpec(memory_space=pltpu.VMEM)
    smem = pl.BlockSpec(memory_space=pltpu.SMEM)
    anywhere = pl.BlockSpec(memory_space=pl.ANY)
    hbm = pl.BlockSpec(memory_space=pltpu.HBM)
    return pl.pallas_call(
        functools.partial(train_kernel, y_devices, x_devices),
        out_shape=(
            jax.ShapeDtypeStruct((CH, 256), jnp.float32),
            jax.ShapeDtypeStruct((256, CH), jnp.float32),
            jax.ShapeDtypeStruct(fields.shape, fields.dtype),
        ),
        in_specs=[smem] * 2 + [vmem] * 2 + [hbm] * 2 + [anywhere] * len(arrived) + [hbm],
        out_specs=(vmem, vmem, hbm),
        scratch_shapes=[
            pltpu.SMEM((2, TCAP), jnp.int32),
            pltpu.SMEM((x_devices,), jnp.int32),
            pltpu.VMEM((TCAP, 4 * SUB * F, 128), jnp.bfloat16),
            pltpu.VMEM((4 * CH, STACK), jnp.bfloat16),
            pltpu.VMEM((4 * CH, STACK), jnp.bfloat16),
            pltpu.VMEM((STACK, 4 * CH), jnp.bfloat16),
            pltpu.VMEM((4 * CH, STACK), jnp.float32),
            pltpu.VMEM((4 * CH, STACK), jnp.float32),
            pltpu.VMEM((CH, 256), jnp.float32),
            pltpu.VMEM((CH, 256), jnp.float32),
            pltpu.VMEM(fields.shape, fields.dtype),
            pltpu.VMEM((4, 256, STACK), jnp.bfloat16),
            pltpu.VMEM((4, 256, STACK), jnp.bfloat16),
            pltpu.SemaphoreType.DMA((TCAP,)),
            pltpu.SemaphoreType.DMA,
            pltpu.SemaphoreType.DMA((2,)),
        ]
        + [pltpu.VMEM((2, SUB * F * 2, 128), jnp.float32)] * (2 * PAIRS)
        + [pltpu.VMEM((STACK, COLS), jnp.bfloat16)] * (2 * PAIRS)
        + [pltpu.VMEM((4 * CH, COLS), jnp.bfloat16)] * (2 * PAIRS)
        + [pltpu.VMEM((4 * CH, COLS), jnp.float32)] * PAIRS
        + [pltpu.VMEM((STACK, COLS), jnp.float32)] * PAIRS
        + [pltpu.VMEM((4 * CH, COLS), jnp.float32)] * PAIRS,
        compiler_params=pltpu.CompilerParams(vmem_limit_bytes=52 * 1024 * 1024),
        name="train_cubes",
    )(
        trainer_of,
        place,
        first,
        last,
        *selects,
        *arrived,
        fields,
    )


def viscosity_of(cells, closure):
    def unit(h, total):
        half = closure[F, h] + closure[0, h] * cells[0]
        for f in range(1, F):
            half = half + closure[f, h] * cells[f]
        return total + closure[F + 1, h] * (half * jnp.tanh(half))

    total = closure[F, HID] + closure[0, HID] * cells[0]
    for f in range(1, F):
        total = total + closure[f, HID] * cells[f]
    total = lax.fori_loop(0, HID, unit, total, unroll=8)
    soft = jnp.maximum(total, 0.0) + jnp.log1p(jnp.exp(-jnp.abs(total)))
    return base_viscosity + viscosity_gain * soft


def viscosity_kernel(closure, place, fields, viscosity, x_edges, y_edges, weights, out_column):
    x_cells, y_cells, z_cells = fields.shape[1:]
    up_first = lax.rem(place[2], 2) == 0
    for f in range(F):
        x_edges[0, f] = fields[f, 0]
        x_edges[1, f] = fields[f, x_cells - 1]
        low, high = fields[f, :, 0, :], fields[f, :, y_cells - 1, :]
        y_edges[0, f] = jnp.where(up_first, high, low)
        y_edges[1, f] = jnp.where(up_first, low, high)
    plain = closure[...]
    high = plain.astype(jnp.bfloat16).astype(jnp.float32)
    low = plain - high
    blank = jnp.zeros((8, 128), jnp.float32)
    for j in range(8):
        turned = [pltpu.roll(part, j, 0) if j else part for part in (high, high, low)]
        stacked = jnp.concatenate([*turned, blank], axis=0)
        weights[j] = stacked.T[: HID + 8].astype(jnp.bfloat16)
    out_column[...] = jnp.broadcast_to(plain.T[:HID, F + 1 : F + 2], (HID, 128))
    sublane = lax.broadcasted_iota(jnp.int32, (8, z_cells), 0)
    wide = z_cells // 128
    tiles = y_cells // 8

    def tile(index, carry):
        x, rows = index // tiles, pl.ds(pl.multiple_of(index % tiles * 8, 8), 8)
        turned = [fields[f, x, rows, :] for f in range(F)]
        turned = [pltpu.roll(turned[f], f, 0) if f else turned[f] for f in range(F)]
        sums = jnp.zeros((8, z_cells), jnp.float32)
        for j in range(8):
            cells = jnp.where(sublane == (j + F) % 8, 1.0, 0.0)
            for f in range(F):
                cells = jnp.where(sublane == (j + f) % 8, turned[f], cells)
            top = cells.astype(jnp.bfloat16).astype(jnp.float32)
            stacked = jnp.concatenate([top, cells - top, top, jnp.zeros_like(top)], axis=0)
            half = dot_rows(weights[j], stacked.astype(jnp.bfloat16))
            total = half[HID:]
            for group in range(HID // 8):
                part = half[group * 8 : group * 8 + 8]
                column = jnp.concatenate([out_column[group * 8 : group * 8 + 8, :]] * wide, axis=1)
                total = total + column * (part * jnp.tanh(part))
            for step in (4, 2, 1):
                total = total + pltpu.roll(total, step, 0)
            sums = jnp.where(sublane == j, total, sums)
        soft = jnp.maximum(sums, 0.0) + jnp.log1p(jnp.exp(-jnp.abs(sums)))
        viscosity[x, rows, :] = base_viscosity + viscosity_gain * soft
        return carry

    lax.fori_loop(0, x_cells * tiles, tile, 0)


def brick_viscosity(closure, place, fields):
    count, x_cells, y_cells, z_cells = fields.shape
    vmem = pl.BlockSpec(memory_space=pltpu.VMEM)
    return pl.pallas_call(
        viscosity_kernel,
        out_shape=(
            jax.ShapeDtypeStruct(fields.shape[1:], fields.dtype),
            jax.ShapeDtypeStruct((2, count, y_cells, z_cells), fields.dtype),
            jax.ShapeDtypeStruct((2, count, x_cells, z_cells), fields.dtype),
        ),
        in_specs=[vmem, pl.BlockSpec(memory_space=pltpu.SMEM), vmem],
        out_specs=(vmem,) * 3,
        scratch_shapes=[
            pltpu.VMEM((8, HID + 8, 32), jnp.bfloat16),
            pltpu.VMEM((HID, 128), jnp.float32),
        ],
        compiler_params=pltpu.CompilerParams(vmem_limit_bytes=16 * 1024 * 1024),
        name="brick_viscosity",
    )(closure, place, fields)


def evolve_kernel(place, viscosity, fields, x_halo, y_first, y_second, new_fields):
    up_first = lax.rem(place[2], 2) == 0
    x_cells, y_cells, z_cells = fields.shape[1:]
    row = lax.broadcasted_iota(jnp.int32, (y_cells, z_cells), 0)
    lane = lax.broadcasted_iota(jnp.int32, (y_cells, z_cells), 1)

    def plane(x, carry):
        centre = [fields[f, x] for f in range(F)]
        below = jnp.maximum(x - 1, 0)
        above = jnp.minimum(x + 1, x_cells - 1)
        for f in range(F):
            value = centre[f]
            west = jnp.where(x == 0, x_halo[1, f], fields[f, below])
            east = jnp.where(x == x_cells - 1, x_halo[0, f], fields[f, above])
            first, second = y_first[f, pl.ds(x, 1), :], y_second[f, pl.ds(x, 1), :]
            south = jnp.where(
                row == 0, jnp.where(up_first, second, first), pltpu.roll(value, 1, 0)
            )
            north = jnp.where(
                row == y_cells - 1,
                jnp.where(up_first, first, second),
                pltpu.roll(value, y_cells - 1, 0),
            )
            lower = jnp.where(lane == 0, 0.0, pltpu.roll(value, 1, 1))
            upper = jnp.where(lane == z_cells - 1, 0.0, pltpu.roll(value, z_cells - 1, 1))
            laplacian = east + west + north + south + upper + lower - 6.0 * value
            advection = (
                centre[0] * (east - west) + centre[1] * (north - south) + centre[2] * (upper - lower)
            )
            tendency = viscosity[x] * laplacian - 0.5 * advection
            if f == 2:
                tendency = tendency + buoyancy * centre[3]
            new_fields[f, x] = value + time_step * tendency
        return carry

    lax.fori_loop(0, x_cells, plane, 0)


def evolve(place, viscosity, fields, x_halo, y_first, y_second):
    vmem = pl.BlockSpec(memory_space=pltpu.VMEM)
    return pl.pallas_call(
        evolve_kernel,
        out_shape=jax.ShapeDtypeStruct(fields.shape, fields.dtype),
        in_specs=[pl.BlockSpec(memory_space=pltpu.SMEM)] + [vmem] * 5,
        out_specs=vmem,
        compiler_params=pltpu.CompilerParams(vmem_limit_bytes=16 * 1024 * 1024),
        name="evolve_brick",
    )(place, viscosity, fields, x_halo, y_first, y_second)


def cell_order():
    order = np.zeros((256, 256), np.float32)
    for y in range(SUB):
        for z in range(SUB):
            order[y * SUB + z, (y % 2 * 2 + z % 2) * 64 + y // 2 * 8 + z // 2] = 1.0
    return order


CELL_ORDER = cell_order()


def corner_of(sample_block, place, x_step, y_step, y_cells, z_cells):
    x_devices, y_devices = place[5], place[4]
    gx = lax.rem(place[1] + x_step + x_devices, x_devices)
    gy = lax.rem(place[2] + y_step + y_devices, y_devices)
    group = jnp.minimum(place[0], place[3] - 1)
    block = sample_block[(group * x_devices + gx) * y_devices + gy]
    z_blocks = z_cells // SUB
    return lax.rem(lax.div(block, z_blocks), y_cells // SUB) * SUB, lax.rem(block, z_blocks) * SUB


def thin_kernel(
    y_cells, z_cells, sample_block, place, rows_ref, lines_ref, thin, x_buffer, y_buffer, x_sems, y_sems
):
    def corner(x_step, y_step):
        return corner_of(sample_block, place, x_step, y_step, y_cells, z_cells)

    lane = lax.broadcasted_iota(jnp.int32, (SUB, 128), 1)
    signs = (-1, 1)
    copies = []
    for side, sign in enumerate(signs):
        z_x, z_y = corner(sign, 0)[1], corner(0, sign)[1]
        x, y = side * (SUB - 1), side * (y_cells - 8)
        for field in range(F):
            copies.append(
                pltpu.make_async_copy(
                    rows_ref.at[
                        pl.ds((field * SUB + x) * y_cells, y_cells),
                        pl.ds(pl.multiple_of(lax.div(z_x, 128) * 128, 128), 128),
                    ],
                    x_buffer.at[pl.ds((side * 8 + field) * y_cells, y_cells)],
                    x_sems.at[side, field],
                )
            )
        copies.append(
            pltpu.make_async_copy(
                lines_ref.at[:, pl.ds(y, 8), pl.ds(pl.multiple_of(lax.div(z_y, 128) * 128, 128), 128)],
                y_buffer.at[side],
                y_sems.at[side],
            )
        )
    for copy in copies:
        copy.start()
    thin[...] = jnp.zeros(thin.shape, thin.dtype)
    for copy in copies:
        copy.wait()

    def moved(values, z, lane_start):
        return pltpu.roll(values, lax.rem(lane_start - lax.rem(z, 128) + 256, 128), 1)

    for side, sign in enumerate(signs):
        z = corner(0, sign)[1]
        total = jnp.zeros((SUB, 128), jnp.float32)
        for field in range(F):
            part = y_buffer[side, field * SUB : (field + 1) * SUB, side * 7, :]
            total = jnp.where(lane // SUB == field, moved(part, z, field * SUB), total)
        thin[column_of(place, 0, sign), :, side * 128 : (side + 1) * 128] = total
    for side, sign in enumerate(signs):
        y, z = corner(sign, 0)
        for half in range(2):
            total = jnp.zeros((8, 128), jnp.float32)
            for step in range(8):
                row = side * 8 * y_cells + y + half * 8 + step
                part = moved(x_buffer[pl.ds(row, 8, y_cells), :], z, step * SUB)
                total = jnp.where(lane[:8] // SUB == step, part, total)
            at = (column_of(place, sign, 0), slice(side * 8, side * 8 + 8), slice(half * 128, half * 128 + 128))
            thin[at] = total


def thin_faces(sample_block, place, brick, columns):
    fields, x_cells, y_cells, z_cells = brick.shape
    vmem = pl.BlockSpec(memory_space=pltpu.VMEM)
    smem = pl.BlockSpec(memory_space=pltpu.SMEM)
    hbm = pl.BlockSpec(memory_space=pltpu.HBM)
    return pl.pallas_call(
        functools.partial(thin_kernel, y_cells, z_cells),
        out_shape=jax.ShapeDtypeStruct((columns, SUB, 256), jnp.float32),
        in_specs=[smem, smem, hbm, hbm],
        out_specs=vmem,
        scratch_shapes=[
            pltpu.VMEM((16 * y_cells, 128), jnp.float32),
            pltpu.VMEM((2, fields * x_cells, 8, 128), jnp.float32),
            pltpu.SemaphoreType.DMA((2, fields)),
            pltpu.SemaphoreType.DMA((2,)),
        ],
        compiler_params=pltpu.CompilerParams(vmem_limit_bytes=16 * 1024 * 1024),
        name="thin_faces",
    )(
        sample_block,
        place,
        brick.reshape(fields * x_cells * y_cells, z_cells),
        brick.reshape(fields * x_cells, y_cells, z_cells),
    )


def sample_kernel(
    y_cells,
    z_cells,
    sample_block,
    place,
    brick,
    centre,
    lower,
    upper,
    own_rows,
    windows,
    sems,
):
    rows_of_x = y_cells
    rows_of_field = SUB * y_cells
    window_rows = F * rows_of_field

    def corner(x_step, y_step):
        return corner_of(sample_block, place, x_step, y_step, y_cells, z_cells)

    y_start, z_start = corner(0, 0)
    z_below = jnp.maximum(z_start - 1, 0)
    z_above = jnp.minimum(z_start + SUB, z_cells - 1)
    first_window = lax.div(z_below, 128)
    second_window = jnp.minimum(first_window + 1, z_cells // 128 - 1)
    copies = [
        pltpu.make_async_copy(
            brick.at[:, pl.ds(pl.multiple_of(at * 128, 128), 128)],
            windows.at[pl.ds(slot * window_rows, window_rows)],
            sems.at[slot],
        )
        for slot, at in enumerate((first_window, second_window))
    ]
    for copy in copies:
        copy.start()
    for copy in copies:
        copy.wait()

    def window(row, z):
        slot = lax.div(z, 128) - first_window
        return windows[pl.ds(slot * window_rows + row, SUB, rows_of_x), :]

    lane = lax.broadcasted_iota(jnp.int32, (SUB, 128), 1)
    for field in range(F):
        for half in range(2):
            inside = jnp.zeros((SUB, 128), jnp.float32)
            below = jnp.zeros((SUB, 128), jnp.float32)
            above = jnp.zeros((SUB, 128), jnp.float32)
            for step in range(8):
                row = field * rows_of_field + y_start + half * 8 + step
                first = step * SUB
                values = jnp.where(lane == 127, window(row, z_below), window(row, z_start))
                values = jnp.where(lane == 0, window(row, z_above), values)
                values = pltpu.roll(values, lax.rem(first - lax.rem(z_start, 128) + 256, 128), 1)
                inside = jnp.where(lane // SUB == step, values, inside)
                below = jnp.where(lane == (first - 1) % 128, values, below)
                above = jnp.where(lane == (first + SUB) % 128, values, above)
            below = jnp.where(z_start == 0, 0.0, pltpu.roll(below, 1, 1))
            above = jnp.where(z_start + SUB == z_cells, 0.0, pltpu.roll(above, 127, 1))
            at = (slice(field * SUB, (field + 1) * SUB), slice(half * 128, (half + 1) * 128))
            centre[at] = inside
            lower[at] = jnp.where(lane % SUB == 0, below, pltpu.roll(inside, 1, 1))
            upper[at] = jnp.where(lane % SUB == SUB - 1, above, pltpu.roll(inside, 127, 1))

    def y_row(y, z):
        total = jnp.zeros((SUB, 128), jnp.float32)
        for field in range(F):
            part = window(field * rows_of_field + y, z)
            part = pltpu.roll(part, lax.rem(field * SUB - lax.rem(z, 128) + 256, 128), 1)
            total = jnp.where(lane // SUB == field, part, total)
        return total

    own_rows[0] = y_row(jnp.maximum(y_start - 1, 0), z_start)
    own_rows[1] = y_row(jnp.minimum(y_start + SUB, y_cells - 1), z_start)

def sample_cube(sample_block, place, brick):
    fields, x_cells, y_cells, z_cells = brick.shape
    vmem = pl.BlockSpec(memory_space=pltpu.VMEM)
    smem = pl.BlockSpec(memory_space=pltpu.SMEM)
    hbm = pl.BlockSpec(memory_space=pltpu.HBM)
    rows = fields * x_cells * y_cells
    cube = jax.ShapeDtypeStruct((F * SUB, 256), jnp.float32)
    return pl.pallas_call(
        functools.partial(sample_kernel, y_cells, z_cells),
        out_shape=(
            cube,
            cube,
            cube,
            jax.ShapeDtypeStruct((2, SUB, 128), jnp.float32),
        ),
        in_specs=[smem, smem, hbm],
        out_specs=(vmem,) * 4,
        scratch_shapes=[
            pltpu.VMEM((2 * rows, 128), jnp.float32),
            pltpu.SemaphoreType.DMA((2,)),
        ],
        compiler_params=pltpu.CompilerParams(vmem_limit_bytes=16 * 1024 * 1024),
        cost_estimate=pl.CostEstimate(flops=0, bytes_accessed=16_000_000, transcendentals=0),
        name="sample_cube",
    )(sample_block, place, brick.reshape(rows, z_cells))


def change_kernel(
    y_cells,
    z_cells,
    sample_block,
    place,
    closure,
    order,
    centre,
    lower,
    upper,
    own_rows,
    thin,
    payload,
    table,
):
    y_start = corner_of(sample_block, place, 0, 0, y_cells, z_cells)[0]
    row = lax.broadcasted_iota(jnp.int32, (SUB, 256), 0)
    lane = lax.broadcasted_iota(jnp.int32, (SUB, 256), 1)
    south_row = jnp.where(y_start == 0, thin[column_of(place, 0, -1), :, 128:], own_rows[0])
    north_row = jnp.where(y_start + SUB == y_cells, thin[column_of(place, 0, 1), :, :128], own_rows[1])
    face_low = thin[column_of(place, -1, 0), 8:, :]
    face_high = thin[column_of(place, 1, 0), :8, :]
    cells = [centre[f * SUB : (f + 1) * SUB, :] for f in range(F)]
    viscosity = viscosity_of(cells, closure)
    changes = []
    for f in range(F):
        value = cells[f]
        west = jnp.where(row == 0, face_low[f : f + 1, :], pltpu.roll(value, 1, 0))
        east = jnp.where(row == SUB - 1, face_high[f : f + 1, :], pltpu.roll(value, SUB - 1, 0))
        edge = pltpu.roll(south_row, (128 - f * SUB) % 128, 1)
        south = jnp.where(lane < SUB, jnp.concatenate([edge, edge], 1), pltpu.roll(value, SUB, 1))
        edge = pltpu.roll(north_row, 112 - f * SUB, 1)
        north = jnp.where(
            lane >= 256 - SUB, jnp.concatenate([edge, edge], 1), pltpu.roll(value, 256 - SUB, 1)
        )
        down = lower[f * SUB : (f + 1) * SUB, :]
        up = upper[f * SUB : (f + 1) * SUB, :]
        laplacian = east + west + north + south + up + down - 6.0 * value
        advection = cells[0] * (east - west) + cells[1] * (north - south) + cells[2] * (up - down)
        change = viscosity * laplacian - 0.5 * advection
        if f == 2:
            change = change + buoyancy * cells[3]
        changes.append(change)
    ordered = dot_rows(jnp.concatenate(cells + changes, axis=0).astype(jnp.bfloat16), order[...])
    low_lanes = lane[:8, :128] < 64
    for part in range(2 * F):
        for cell in range(4):
            columns = slice(cell // 2 * 128, cell // 2 * 128 + 128)
            low = ordered[part * SUB : part * SUB + 8, columns]
            high = ordered[part * SUB + 8 : part * SUB + SUB, columns]
            if cell % 2 == 0:
                high = pltpu.roll(high, 64, 1)
            else:
                low = pltpu.roll(low, 64, 1)
            table[pl.ds(part * 32 + cell, 8, 4), :] = jnp.where(low_lanes, low, high)
    payload[...] = table[...].astype(jnp.bfloat16)


def cube_change(sample_block, place, closure, cube, thin, y_cells, z_cells):
    vmem = pl.BlockSpec(memory_space=pltpu.VMEM)
    smem = pl.BlockSpec(memory_space=pltpu.SMEM)
    return pl.pallas_call(
        functools.partial(change_kernel, y_cells, z_cells),
        out_shape=jax.ShapeDtypeStruct((4 * F * SUB, 128), jnp.bfloat16),
        in_specs=[smem] * 3 + [vmem] * 6,
        out_specs=vmem,
        scratch_shapes=[pltpu.VMEM((4 * F * SUB, 128), jnp.float32)],
        compiler_params=pltpu.CompilerParams(vmem_limit_bytes=16 * 1024 * 1024),
        name="cube_change",
    )(sample_block, place, closure, jnp.asarray(CELL_ORDER, jnp.bfloat16), *cube, thin)


def on_device(
    fields, closure_in, closure_bias, closure_out, master, momentum, sample_block, sample_trainer
):
    group_count = lax.axis_size("grp")
    x_devices = lax.axis_size("gx")
    y_devices = lax.axis_size("gy")
    trainers = x_devices * y_devices
    my_group = lax.axis_index("grp")
    my_column = lax.axis_index("gx") * y_devices + lax.axis_index("gy")
    is_trainer = my_group == group_count - 1
    everyone = ("grp", "gx", "gy")
    sim_groups = group_count - 1
    first_trainer = sim_groups * trainers
    brick = fields[0]
    y_cells, z_cells = brick.shape[2:]
    closure = jnp.concatenate(
        [0.5 * closure_in.T, 0.5 * closure_bias[None], closure_out[None]], axis=0
    )
    linear = jnp.sum(closure * closure_out[None], axis=1, keepdims=True)
    closure = jnp.pad(jnp.concatenate([closure, linear], axis=1), ((0, 1), (0, 127 - HID)))
    place = jnp.stack(
        [
            my_group,
            lax.axis_index("gx"),
            lax.axis_index("gy"),
            jnp.int32(sim_groups),
            jnp.int32(y_devices),
            jnp.int32(x_devices),
        ]
    ).astype(jnp.int32)

    def pairs(x_step, even_step):
        found = []
        for g in range(sim_groups):
            for c in range(trainers):
                gx, gy = c // y_devices, c % y_devices
                gx = (gx + x_step) % x_devices
                gy = (gy + (even_step if gy % 2 == 0 else -even_step)) % y_devices
                found.append((g * trainers + c, (g * x_devices + gx) * y_devices + gy))
        return found

    def x_neighbours(edges):
        if x_devices == 2:
            return lax.ppermute(edges, everyone, pairs(1, 0))
        from_high = lax.ppermute(edges[0], everyone, pairs(-1, 0))
        return jnp.stack([from_high, lax.ppermute(edges[1], everyone, pairs(1, 0))])

    def y_neighbours(for_first, for_second):
        return (
            lax.ppermute(for_first, everyone, pairs(0, 1)),
            lax.ppermute(for_second, everyone, pairs(0, -1)),
        )

    def swap(distance):
        return [(first_trainer + c, first_trainer + (c ^ distance)) for c in range(trainers)]

    def to_trainers(payload):
        landed = [
            lax.ppermute(
                payload, everyone, [(g * trainers + c, first_trainer + c) for c in range(trainers)]
            )
            for g in reversed(range(sim_groups))
        ]
        return jnp.stack(landed[::-1])

    def from_line(held):
        return [lax.ppermute(held, everyone, swap(apart)) for apart in range(1, y_devices)]

    def across(apart, held):
        return lax.ppermute(held, everyone, swap(apart * y_devices))

    thin = thin_faces(sample_block, place, brick, trainers)
    cube = sample_cube(sample_block, place, brick)
    first_count = CH * TAPS * F
    first = jnp.pad(master[:first_count].reshape(CH, TAPS * F), ((0, 0), (0, 256 - TAPS * F)))
    last = jnp.pad(master[first_count:].reshape(TAPS * F, CH), ((0, 256 - TAPS * F), (0, 0)))

    *cube, first, last = lax.optimization_barrier((*cube, first, last))
    selects = lax.optimization_barrier(
        (jnp.asarray(SELECT_FIRST, jnp.bfloat16), jnp.asarray(SELECT_LAST, jnp.bfloat16))
    )

    thin = lax.all_to_all(thin, ("gx", "gy"), split_axis=0, concat_axis=0, tiled=True)
    payload = cube_change(sample_block, place, closure, cube, thin, y_cells, z_cells)
    landed = to_trainers(payload)
    closure, landed = lax.optimization_barrier((closure, landed))

    fields_count, x_cells = brick.shape[:2]
    viscosity, x_edges, y_edges = lax.cond(
        is_trainer,
        lambda: (
            jnp.zeros((x_cells, y_cells, z_cells), jnp.float32),
            jnp.zeros((2, fields_count, y_cells, z_cells), jnp.float32),
            jnp.zeros((2, fields_count, x_cells, z_cells), jnp.float32),
        ),
        lambda: brick_viscosity(closure, place, brick),
    )
    halo = (x_neighbours(x_edges), *y_neighbours(y_edges[0], y_edges[1]))
    near = [landed, *from_line(landed)]
    far = [
        across(apart, pick_cubes(sample_trainer, place, near, y_devices, x_devices, apart))
        for apart in range(1, x_devices)
    ]
    arrived = [*near, *far]

    def train_here():
        delta_first, delta_last, new_brick = train_cubes(
            sample_trainer, place, first, last, selects, arrived, brick, y_devices, x_devices
        )
        delta = jnp.concatenate(
            [delta_first[:, : TAPS * F].reshape(-1), delta_last[: TAPS * F].reshape(-1)]
        )
        return delta, new_brick

    def evolve_here():
        new_brick = evolve(place, viscosity, brick, *halo)
        return jnp.zeros((NPARAM,), jnp.float32), new_brick

    delta, new_brick = lax.cond(is_trainer, train_here, evolve_here)

    held = delta
    for g in range(sim_groups):
        held = held + lax.ppermute(
            delta, everyone, [(first_trainer + c, g * trainers + c) for c in range(trainers)]
        )
    final = delta
    for first_apart in range(1, trainers, group_count):
        meets = [
            (g * trainers + c, g * trainers + (c ^ (first_apart + g)))
            for g in range(group_count)
            for c in range(trainers)
            if first_apart + g < trainers
        ]
        final = final + lax.ppermute(held, everyone, meets)
    for apart in (1, 2):
        final = final + lax.ppermute(
            final,
            everyone,
            [(g * trainers + c, (g ^ apart) * trainers + c) for g in range(group_count) for c in range(trainers)],
        )

    share_size = NPARAM // (group_count * trainers)
    share_start = (my_group * trainers + my_column) * share_size
    momentum_share = lax.dynamic_slice_in_dim(momentum, share_start, share_size)
    master_share = lax.dynamic_slice_in_dim(master, share_start, share_size)
    inverse = 1.0 / jnp.sqrt(jnp.sum(final * final) / NPARAM + norm_epsilon)
    delta_share = lax.dynamic_slice_in_dim(final, share_start, share_size)
    new_momentum = momentum_decay * momentum_share + delta_share * inverse
    new_master = master_share - outer_rate * new_momentum
    return (new_brick[None], new_master, new_momentum)


def solution(mesh):
    in_specs = (P("grp", None, "gx", "gy", None), P(), P(), P(), P(), P(), P(), P())
    out_specs = (P("grp", None, "gx", "gy", None), P(("grp", "gx", "gy")), P(("grp", "gx", "gy")))
    return jax.shard_map(
        on_device, mesh=mesh, in_specs=in_specs, out_specs=out_specs, check_vma=False
    )
```

```python
import functools

import jax
import jax.numpy as jnp
import numpy as np
from jax import lax
from jax.experimental import pallas as pl
from jax.experimental.pallas import tpu as pltpu
from jax.sharding import PartitionSpec as P

F = 5
CH = 64
HID = 64
SUB = 16
TCAP = 6
INNER = 3
CELLS = 4096
NPARAM = 17280
TAPS = 27
PAIRS = TCAP // 2
COLS = (SUB + 2) * 128
PATCH = 16 * F
STACK = 3 * PATCH

time_step = 0.1
base_viscosity = 0.02
viscosity_gain = 0.2
buoyancy = 0.5
inner_rate = 0.02
outer_rate = 0.01
momentum_decay = 0.9
norm_epsilon = 1e-06


def patch_position(row):
    group, py, pz = row // 4, row // 2 % 2, row % 2
    ypos = py + 1 if group in (0, 2) else (3 if py == 0 else 0)
    zpos = pz + 1 if group in (0, 1) else (3 if pz == 0 else 0)
    return ypos - 1, zpos - 1


def selections():
    first = np.zeros((4, 256, STACK), np.float32)
    last = np.zeros((4, 256, STACK), np.float32)
    for cell in range(4):
        py, pz = cell // 2, cell % 2
        for kx in range(3):
            for channel in range(F):
                for row in range(16):
                    ypos, zpos = patch_position(row)
                    column = kx * PATCH + channel * 16 + row
                    dy, dz = ypos - py, zpos - pz
                    if abs(dy) <= 1 and abs(dz) <= 1:
                        tap = 9 * kx + 3 * (dy + 1) + dz + 1
                        first[cell, tap * F + channel, column] = 1.0
                        last[cell, channel * TAPS + 26 - tap, column] = 1.0
    return first, last


SELECT_FIRST, SELECT_LAST = selections()


def column_of(place, x_step, y_step):
    gx = lax.rem(place[1] + x_step + place[5], place[5])
    gy = lax.rem(place[2] + y_step + place[4], place[4])
    return gx * place[4] + gy


def owner_apart(owner, groups, place, y_devices, x_devices):
    group, column = divmod(owner, x_devices * y_devices)
    entry = groups - 1 - group
    y_apart = jnp.bitwise_xor(place[2], jnp.int32(column % y_devices))
    return entry, y_apart, jnp.bitwise_xor(place[1], jnp.int32(column // y_devices))


def pick_kernel(y_devices, x_devices, apart, trainer_of, place, *refs):
    near, chosen, owners = refs[:y_devices], refs[y_devices], refs[y_devices + 1]
    wanted = jnp.bitwise_xor(place[1], jnp.int32(apart)) * y_devices + place[2]
    count = jnp.int32(0)
    groups = trainer_of.shape[0] // (x_devices * y_devices)
    for owner in range(trainer_of.shape[0]):
        group, y_apart, x_apart = owner_apart(owner, groups, place, y_devices, x_devices)
        mine = (trainer_of[owner] == wanted) & (x_apart == 0)

        @pl.when(mine)
        def _():
            owners[0, count] = y_apart
            owners[1, count] = group

        count = count + jnp.where(mine, 1, 0)

    def copy_slot(slot, carry):
        for source in range(y_devices):

            @pl.when(owners[0, slot] == source)
            def _():
                chosen[slot] = near[source][owners[1, slot]]

        return carry

    lax.fori_loop(0, count, copy_slot, 0)


def pick_cubes(trainer_of, place, near, y_devices, x_devices, apart):
    vmem = pl.BlockSpec(memory_space=pltpu.VMEM)
    smem = pl.BlockSpec(memory_space=pltpu.SMEM)
    return pl.pallas_call(
        functools.partial(pick_kernel, y_devices, x_devices, apart),
        out_shape=jax.ShapeDtypeStruct((TCAP, *near[0].shape[1:]), near[0].dtype),
        in_specs=[smem, smem] + [vmem] * len(near),
        out_specs=vmem,
        scratch_shapes=[pltpu.SMEM((2, TCAP), jnp.int32)],
        compiler_params=pltpu.CompilerParams(vmem_limit_bytes=16 * 1024 * 1024),
        name="pick_cubes",
    )(trainer_of, place, *near)


def dot_rows(left, right):
    return jnp.dot(left, right, preferred_element_type=jnp.float32)


def dot_lanes(left, right):
    return lax.dot_general(left, right, (((1,), (1,)), ((), ())), preferred_element_type=jnp.float32)


def patch_masks():
    row = lax.broadcasted_iota(jnp.int32, (8, 128), 0)
    lane = lax.broadcasted_iota(jnp.int32, (8, 128), 1)
    z, y = lane % 8, lane // 8 % 8
    even_z, even_y = row % 2 == 0, row // 2 % 2 == 0
    return {
        "centre": row < 4,
        "even_z": even_z,
        "even_y": even_y,
        "gather_z": jnp.where(even_z, z, 7 - z) < 7,
        "gather_y": jnp.where(even_y, y, 7 - y) < 7,
        "scatter_z": jnp.where(even_z, z, 7 - z) > 0,
        "scatter_y": jnp.where(even_y, y, 7 - y) > 0,
    }


def edge_shift(values, step, even, inside, gather):
    before, after = pltpu.roll(values, step, 1), pltpu.roll(values, 128 - step, 1)
    moved = jnp.where(even, after, before) if gather else jnp.where(even, before, after)
    return jnp.where(inside, moved, 0.0)


def patch_stack(rows, masks):
    both = jnp.where(masks["centre"], rows, pltpu.roll(rows, 4, 0))
    y_edge = edge_shift(both, 8, masks["even_y"], masks["gather_y"], True)
    upper = jnp.where(masks["centre"], both, y_edge)
    return upper, edge_shift(upper, 1, masks["even_z"], masks["gather_z"], True)


def patch_fold(upper, lower, masks):
    line = upper + edge_shift(lower, 1, masks["even_z"], masks["scatter_z"], False)
    return line + pltpu.roll(edge_shift(line, 8, masks["even_y"], masks["scatter_y"], False), 4, 0)


def store_planes(ref, x, channels):
    stacked = jnp.concatenate([part for both in channels for part in both], axis=0).astype(jnp.bfloat16)
    for kx in range(3):
        start = pl.multiple_of((x + 2 - kx) * 128, 128)
        ref[kx * PATCH : (kx + 1) * PATCH, pl.ds(start, 128)] = stacked


def train_kernel(y_devices, x_devices, *refs):
    sources = y_devices + x_devices - 1
    (trainer_of, place, first_ref, last_ref, far_first, far_last) = refs[:6]
    arrived = refs[6 : 6 + sources]
    fields_ref = refs[6 + sources]
    delta_first, delta_last, new_fields_ref = refs[7 + sources : 10 + sources]
    (
        slots,
        picked,
        cubes,
        big_first,
        big_last,
        big_last_t,
        grad_first,
        grad_last,
        now_first,
        now_last,
        brick,
        select_first,
        select_last,
        slot_sems,
        field_sem,
        select_sems,
        *pair_refs,
    ) = refs[10 + sources :]
    targets, tables, inputs, errors, hiddens, pre_grads, slopes, partial_out, raw = [
        pair_refs[kind * PAIRS : (kind + 1) * PAIRS] for kind in range(9)
    ]

    field_in = pltpu.make_async_copy(fields_ref, brick, field_sem)
    field_out = pltpu.make_async_copy(brick, new_fields_ref, field_sem)
    select_copies = [
        pltpu.make_async_copy(far_first, select_first, select_sems.at[0]),
        pltpu.make_async_copy(far_last, select_last, select_sems.at[1]),
    ]

    column = place[1] * y_devices + place[2]
    for other in range(x_devices):
        picked[other] = 0
    count = jnp.int32(0)
    groups = trainer_of.shape[0] // (x_devices * y_devices)
    for owner in range(trainer_of.shape[0]):
        group, y_apart, x_apart = owner_apart(owner, groups, place, y_devices, x_devices)
        mine = trainer_of[owner] == column

        @pl.when(mine)
        def _():
            near = x_apart == 0
            slots[0, count] = jnp.where(near, y_apart, y_devices - 1 + x_apart)
            slots[1, count] = jnp.where(near, group, picked[x_apart])
            picked[x_apart] = picked[x_apart] + 1

        count = count + jnp.where(mine, 1, 0)

    def fetch(slot, wait):
        for source in range(sources):

            @pl.when((slot < count) & (slots[0, slot] == source))
            def _():
                copy = pltpu.make_async_copy(
                    arrived[source].at[slots[1, slot]], cubes.at[slot], slot_sems.at[slot]
                )
                copy.wait() if wait else copy.start()

    for slot in range(TCAP):
        fetch(slot, False)

    for copy in select_copies:
        copy.start()
    field_in.start()
    for slot in range(TCAP):

        @pl.when(slot >= count)
        def _():
            cubes[slot] = jnp.zeros(cubes.shape[1:], jnp.bfloat16)

    masks = patch_masks()
    for ref in (*errors, *inputs):
        ref[:PATCH, 128:256] = jnp.zeros((PATCH, 128), jnp.bfloat16)
        ref[2 * PATCH :, COLS - 256 : COLS - 128] = jnp.zeros((PATCH, 128), jnp.bfloat16)
    for ref in partial_out:
        ref[:, :128] = jnp.zeros((STACK, 128), jnp.float32)
        ref[:, COLS - 128 :] = jnp.zeros((STACK, 128), jnp.float32)
    lane = lax.broadcasted_iota(jnp.int32, (8, 128), 1)
    full_weight = 2.0 * (1.0 / (jnp.full((8, 128), count, jnp.int32).astype(jnp.float32) * CELLS))
    weights = [
        jnp.where(lane // 64 + 2 * pair < count, full_weight, 0.0) for pair in range(PAIRS)
    ]
    start_first = first_ref[...].astype(jnp.bfloat16).astype(jnp.float32)
    start_last = last_ref[...].T.astype(jnp.bfloat16).astype(jnp.float32)
    now_first[...] = start_first
    now_last[...] = start_last

    for slot in range(TCAP):
        fetch(slot, True)

    low_lanes = lax.broadcasted_iota(jnp.int32, (SUB * F * 2, 128), 1) < 64
    for pair in range(PAIRS):
        for kind, ref in enumerate((tables[pair], targets[pair])):
            rows = slice(kind * SUB * F * 2, (kind + 1) * SUB * F * 2)
            even = cubes[2 * pair, rows, :].astype(jnp.float32)
            odd = cubes[2 * pair + 1, rows, :].astype(jnp.float32)
            ref[0] = jnp.where(low_lanes, even, pltpu.roll(odd, 64, 1))
            ref[1] = jnp.where(low_lanes, pltpu.roll(even, 64, 1), odd)

    def patch_cells(ref, quarter, plane, channel):
        start = pl.multiple_of(channel * 32 + quarter % 2 * 16 + plane // 2 * 8, 8)
        rows = ref[quarter // 2, pl.ds(start, 8), :]
        return rows if plane % 2 == 0 else pltpu.roll(rows, 4, 0)

    def stack_planes(quarter, carry):
        for pair in range(PAIRS):
            for plane in range(4):
                x = quarter * 4 + plane
                channels = [
                    patch_stack(patch_cells(tables[pair], quarter, plane, c), masks) for c in range(F)
                ]
                store_planes(inputs[pair], x, channels)
        return carry

    lax.fori_loop(0, 4, stack_planes, 0, unroll=2)

    for copy in select_copies:
        copy.wait()
    field_in.wait()
    field_out.start()

    def train_step(step, step_carry):
        first_now = now_first[...].astype(jnp.bfloat16)
        last_now = now_last[...].astype(jnp.bfloat16)
        for cell in range(4):
            rows = slice(cell * CH, (cell + 1) * CH)
            big_first[rows, :] = (0.5 * dot_rows(first_now, select_first[cell])).astype(jnp.bfloat16)
            spread_last = dot_rows(last_now, select_last[cell])
            big_last[rows, :] = (0.5 * spread_last).astype(jnp.bfloat16)
            big_last_t[:, rows] = spread_last.T.astype(jnp.bfloat16)
        grad_first[...] = jnp.zeros(grad_first.shape, jnp.float32)
        grad_last[...] = jnp.zeros(grad_last.shape, jnp.float32)

        def columns_of(quarter):
            return pl.ds(pl.multiple_of(quarter * 512 + 128, 128), 512)

        def first_layer(pair, quarter):
            columns = columns_of(quarter)
            raw[pair][:, columns] = dot_rows(big_first[...], inputs[pair][:, columns])

        def activate(pair, quarter):
            columns = columns_of(quarter)
            for part in range(8):
                rows = slice(part * 32, (part + 1) * 32)
                half = raw[pair][rows, columns]
                curve = jnp.tanh(half)
                above = 1.0 + curve
                value = half * above
                hiddens[pair][rows, columns] = value.astype(jnp.bfloat16)
                slopes[pair][rows, columns] = above + value * (1.0 - curve)

        def last_layer(pair, quarter):
            columns = columns_of(quarter)
            partial_out[pair][:, columns] = dot_rows(big_last_t[...], hiddens[pair][:, columns])

        def find_errors(pair, quarter):
            for plane in range(4):
                x = quarter * 4 + plane
                column = pl.multiple_of((x + 1) * 128, 128)
                total = (
                    partial_out[pair][0:PATCH, pl.ds(pl.multiple_of(column + 128, 128), 128)]
                    + partial_out[pair][PATCH : 2 * PATCH, pl.ds(column, 128)]
                    + partial_out[pair][2 * PATCH :, pl.ds(pl.multiple_of(column - 128, 128), 128)]
                )
                channels = []
                for c in range(F):
                    predicted = patch_fold(
                        total[16 * c : 16 * c + 8], total[16 * c + 8 : 16 * c + 16], masks
                    )
                    wanted = patch_cells(targets[pair], quarter, plane, c)
                    error = weights[pair] * (predicted - wanted)
                    channels.append(patch_stack(error, masks))
                store_planes(errors[pair], x, channels)

        def hidden_layer(pair, quarter):
            columns = columns_of(quarter)
            raw[pair][:, columns] = dot_rows(big_last[...], errors[pair][:, columns])

        def scale(pair, quarter):
            columns = columns_of(quarter)
            for part in range(8):
                rows = slice(part * 32, (part + 1) * 32)
                product = raw[pair][rows, columns] * slopes[pair][rows, columns]
                pre_grads[pair][rows, columns] = product.astype(jnp.bfloat16)

        def gradients(pair, quarter):
            columns = columns_of(quarter)
            grad_first[...] += dot_lanes(pre_grads[pair][:, columns], inputs[pair][:, columns])
            grad_last[...] += dot_lanes(hiddens[pair][:, columns], errors[pair][:, columns])

        stages = (first_layer, activate, last_layer, find_errors, hidden_layer, scale, gradients)
        for turn in range(len(stages) + PAIRS - 1):

            def run(quarter, carry):
                for pair in range(PAIRS):
                    if 0 <= turn - pair < len(stages):
                        stages[turn - pair](pair, quarter)
                return carry

            lax.fori_loop(0, 4, run, 0, unroll=4)

        def folded(grad, select_ref):
            total = jnp.zeros((3 * CH, 256), jnp.float32)
            for cell in range(4):
                rest = grad[cell * CH : (cell + 1) * CH, :]
                parts = []
                for _ in range(3):
                    parts.append(rest.astype(jnp.bfloat16))
                    rest = rest - parts[-1].astype(jnp.float32)
                total = total + dot_lanes(jnp.concatenate(parts, axis=0), select_ref[cell])
            return total[:CH] + total[CH : 2 * CH] + total[2 * CH :]

        now_first[...] = now_first[...] - inner_rate * folded(grad_first, select_first)
        now_last[...] = now_last[...] - inner_rate * folded(grad_last, select_last)
        return step_carry

    lax.fori_loop(0, INNER, train_step, 0)
    delta_first[...] = start_first - now_first[...]
    delta_last[...] = (start_last - now_last[...]).T
    field_out.wait()


def train_cubes(trainer_of, place, first, last, selects, arrived, fields, y_devices, x_devices):
    vmem = pl.BlockSpec(memory_space=pltpu.VMEM)
    smem = pl.BlockSpec(memory_space=pltpu.SMEM)
    anywhere = pl.BlockSpec(memory_space=pl.ANY)
    hbm = pl.BlockSpec(memory_space=pltpu.HBM)
    return pl.pallas_call(
        functools.partial(train_kernel, y_devices, x_devices),
        out_shape=(
            jax.ShapeDtypeStruct((CH, 256), jnp.float32),
            jax.ShapeDtypeStruct((256, CH), jnp.float32),
            jax.ShapeDtypeStruct(fields.shape, fields.dtype),
        ),
        in_specs=[smem] * 2 + [vmem] * 2 + [hbm] * 2 + [anywhere] * len(arrived) + [hbm],
        out_specs=(vmem, vmem, hbm),
        scratch_shapes=[
            pltpu.SMEM((2, TCAP), jnp.int32),
            pltpu.SMEM((x_devices,), jnp.int32),
            pltpu.VMEM((TCAP, 4 * SUB * F, 128), jnp.bfloat16),
            pltpu.VMEM((4 * CH, STACK), jnp.bfloat16),
            pltpu.VMEM((4 * CH, STACK), jnp.bfloat16),
            pltpu.VMEM((STACK, 4 * CH), jnp.bfloat16),
            pltpu.VMEM((4 * CH, STACK), jnp.float32),
            pltpu.VMEM((4 * CH, STACK), jnp.float32),
            pltpu.VMEM((CH, 256), jnp.float32),
            pltpu.VMEM((CH, 256), jnp.float32),
            pltpu.VMEM(fields.shape, fields.dtype),
            pltpu.VMEM((4, 256, STACK), jnp.bfloat16),
            pltpu.VMEM((4, 256, STACK), jnp.bfloat16),
            pltpu.SemaphoreType.DMA((TCAP,)),
            pltpu.SemaphoreType.DMA,
            pltpu.SemaphoreType.DMA((2,)),
        ]
        + [pltpu.VMEM((2, SUB * F * 2, 128), jnp.float32)] * (2 * PAIRS)
        + [pltpu.VMEM((STACK, COLS), jnp.bfloat16)] * (2 * PAIRS)
        + [pltpu.VMEM((4 * CH, COLS), jnp.bfloat16)] * (2 * PAIRS)
        + [pltpu.VMEM((4 * CH, COLS), jnp.float32)] * PAIRS
        + [pltpu.VMEM((STACK, COLS), jnp.float32)] * PAIRS
        + [pltpu.VMEM((4 * CH, COLS), jnp.float32)] * PAIRS,
        compiler_params=pltpu.CompilerParams(vmem_limit_bytes=52 * 1024 * 1024),
        name="train_cubes",
    )(
        trainer_of,
        place,
        first,
        last,
        *selects,
        *arrived,
        fields,
    )


def viscosity_of(cells, closure):
    def unit(h, total):
        half = closure[F, h] + closure[0, h] * cells[0]
        for f in range(1, F):
            half = half + closure[f, h] * cells[f]
        return total + closure[F + 1, h] * (half * jnp.tanh(half))

    total = closure[F, HID] + closure[0, HID] * cells[0]
    for f in range(1, F):
        total = total + closure[f, HID] * cells[f]
    total = lax.fori_loop(0, HID, unit, total, unroll=8)
    soft = jnp.maximum(total, 0.0) + jnp.log1p(jnp.exp(-jnp.abs(total)))
    return base_viscosity + viscosity_gain * soft


def logistic(half):
    below = 1.0 + jnp.exp2((-2.0 / np.log(2.0)) * half)
    inverse = pl.reciprocal(below, approx=True)
    return inverse * (2.0 - below * inverse)


def viscosity_kernel(closure, place, fields, viscosity, x_edges, y_edges, weights, out_column):
    x_cells, y_cells, z_cells = fields.shape[1:]
    up_first = lax.rem(place[2], 2) == 0
    for f in range(F):
        x_edges[0, f] = fields[f, 0]
        x_edges[1, f] = fields[f, x_cells - 1]
        low, high = fields[f, :, 0, :], fields[f, :, y_cells - 1, :]
        y_edges[0, f] = jnp.where(up_first, high, low)
        y_edges[1, f] = jnp.where(up_first, low, high)
    plain = closure[...]
    high = plain.astype(jnp.bfloat16).astype(jnp.float32)
    low = plain - high
    blank = jnp.zeros((8, 128), jnp.float32)
    for j in range(8):
        turned = [pltpu.roll(part, j, 0) if j else part for part in (high, high, low)]
        stacked = jnp.concatenate([*turned, blank], axis=0)
        weights[j] = stacked.T[:HID].astype(jnp.bfloat16)
    out_column[...] = jnp.broadcast_to(2.0 * plain.T[:HID, F + 1 : F + 2], (HID, 128))
    sublane = lax.broadcasted_iota(jnp.int32, (8, z_cells), 0)
    wide = z_cells // 128
    tiles = y_cells // 8

    def tile(index, carry):
        x, rows = index // tiles, pl.ds(pl.multiple_of(index % tiles * 8, 8), 8)
        turned = [fields[f, x, rows, :] for f in range(F)]
        turned = [pltpu.roll(turned[f], f, 0) if f else turned[f] for f in range(F)]
        sums = jnp.zeros((8, z_cells), jnp.float32)
        for j in range(8):
            cells = jnp.where(sublane == (j + F) % 8, 1.0, 0.0)
            for f in range(F):
                cells = jnp.where(sublane == (j + f) % 8, turned[f], cells)
            top = cells.astype(jnp.bfloat16).astype(jnp.float32)
            stacked = jnp.concatenate([top, cells - top, top, jnp.zeros_like(top)], axis=0)
            half = dot_rows(weights[j], stacked.astype(jnp.bfloat16))
            total = jnp.zeros((8, z_cells), jnp.float32)
            for group in range(HID // 8):
                part = half[group * 8 : group * 8 + 8]
                column = jnp.concatenate([out_column[group * 8 : group * 8 + 8, :]] * wide, axis=1)
                total = total + column * (part * logistic(part))
            for step in (4, 2, 1):
                total = total + pltpu.roll(total, step, 0)
            sums = jnp.where(sublane == j, total, sums)
        soft = jnp.maximum(sums, 0.0) + jnp.log1p(jnp.exp(-jnp.abs(sums)))
        viscosity[x, rows, :] = base_viscosity + viscosity_gain * soft
        return carry

    lax.fori_loop(0, x_cells * tiles, tile, 0)


def brick_viscosity(closure, place, fields):
    count, x_cells, y_cells, z_cells = fields.shape
    vmem = pl.BlockSpec(memory_space=pltpu.VMEM)
    return pl.pallas_call(
        viscosity_kernel,
        out_shape=(
            jax.ShapeDtypeStruct(fields.shape[1:], fields.dtype),
            jax.ShapeDtypeStruct((2, count, y_cells, z_cells), fields.dtype),
            jax.ShapeDtypeStruct((2, count, x_cells, z_cells), fields.dtype),
        ),
        in_specs=[vmem, pl.BlockSpec(memory_space=pltpu.SMEM), vmem],
        out_specs=(vmem,) * 3,
        scratch_shapes=[
            pltpu.VMEM((8, HID, 32), jnp.bfloat16),
            pltpu.VMEM((HID, 128), jnp.float32),
        ],
        compiler_params=pltpu.CompilerParams(vmem_limit_bytes=16 * 1024 * 1024),
        name="brick_viscosity",
    )(closure, place, fields)


def evolve_kernel(place, viscosity, fields, x_halo, y_first, y_second, new_fields):
    up_first = lax.rem(place[2], 2) == 0
    x_cells, y_cells, z_cells = fields.shape[1:]
    row = lax.broadcasted_iota(jnp.int32, (y_cells, z_cells), 0)
    lane = lax.broadcasted_iota(jnp.int32, (y_cells, z_cells), 1)

    def plane(x, carry):
        centre = [fields[f, x] for f in range(F)]
        below = jnp.maximum(x - 1, 0)
        above = jnp.minimum(x + 1, x_cells - 1)
        for f in range(F):
            value = centre[f]
            west = jnp.where(x == 0, x_halo[1, f], fields[f, below])
            east = jnp.where(x == x_cells - 1, x_halo[0, f], fields[f, above])
            first, second = y_first[f, pl.ds(x, 1), :], y_second[f, pl.ds(x, 1), :]
            south = jnp.where(
                row == 0, jnp.where(up_first, second, first), pltpu.roll(value, 1, 0)
            )
            north = jnp.where(
                row == y_cells - 1,
                jnp.where(up_first, first, second),
                pltpu.roll(value, y_cells - 1, 0),
            )
            lower = jnp.where(lane == 0, 0.0, pltpu.roll(value, 1, 1))
            upper = jnp.where(lane == z_cells - 1, 0.0, pltpu.roll(value, z_cells - 1, 1))
            laplacian = east + west + north + south + upper + lower - 6.0 * value
            advection = (
                centre[0] * (east - west) + centre[1] * (north - south) + centre[2] * (upper - lower)
            )
            tendency = viscosity[x] * laplacian - 0.5 * advection
            if f == 2:
                tendency = tendency + buoyancy * centre[3]
            new_fields[f, x] = value + time_step * tendency
        return carry

    lax.fori_loop(0, x_cells, plane, 0, unroll=2)


def evolve(place, viscosity, fields, x_halo, y_first, y_second):
    vmem = pl.BlockSpec(memory_space=pltpu.VMEM)
    return pl.pallas_call(
        evolve_kernel,
        out_shape=jax.ShapeDtypeStruct(fields.shape, fields.dtype),
        in_specs=[pl.BlockSpec(memory_space=pltpu.SMEM)] + [vmem] * 5,
        out_specs=vmem,
        compiler_params=pltpu.CompilerParams(vmem_limit_bytes=16 * 1024 * 1024),
        name="evolve_brick",
    )(place, viscosity, fields, x_halo, y_first, y_second)


def cell_order():
    order = np.zeros((256, 256), np.float32)
    for y in range(SUB):
        for z in range(SUB):
            order[y * SUB + z, (y % 2 * 2 + z % 2) * 64 + y // 2 * 8 + z // 2] = 1.0
    return order


CELL_ORDER = cell_order()


def corner_of(sample_block, place, x_step, y_step, y_cells, z_cells):
    x_devices, y_devices = place[5], place[4]
    gx = lax.rem(place[1] + x_step + x_devices, x_devices)
    gy = lax.rem(place[2] + y_step + y_devices, y_devices)
    group = jnp.minimum(place[0], place[3] - 1)
    block = sample_block[(group * x_devices + gx) * y_devices + gy]
    z_blocks = z_cells // SUB
    return lax.rem(lax.div(block, z_blocks), y_cells // SUB) * SUB, lax.rem(block, z_blocks) * SUB


def thin_kernel(
    y_cells, z_cells, sample_block, place, rows_ref, lines_ref, thin, x_buffer, y_buffer, x_sems, y_sems
):
    def corner(x_step, y_step):
        return corner_of(sample_block, place, x_step, y_step, y_cells, z_cells)

    lane = lax.broadcasted_iota(jnp.int32, (SUB, 128), 1)
    signs = (-1, 1)
    copies = []
    for side, sign in enumerate(signs):
        z_x, z_y = corner(sign, 0)[1], corner(0, sign)[1]
        x, y = side * (SUB - 1), side * (y_cells - 8)
        for field in range(F):
            copies.append(
                pltpu.make_async_copy(
                    rows_ref.at[
                        pl.ds((field * SUB + x) * y_cells, y_cells),
                        pl.ds(pl.multiple_of(lax.div(z_x, 128) * 128, 128), 128),
                    ],
                    x_buffer.at[pl.ds((side * 8 + field) * y_cells, y_cells)],
                    x_sems.at[side, field],
                )
            )
        copies.append(
            pltpu.make_async_copy(
                lines_ref.at[:, pl.ds(y, 8), pl.ds(pl.multiple_of(lax.div(z_y, 128) * 128, 128), 128)],
                y_buffer.at[side],
                y_sems.at[side],
            )
        )
    for copy in copies:
        copy.start()
    thin[...] = jnp.zeros(thin.shape, thin.dtype)
    for copy in copies:
        copy.wait()

    def moved(values, z, lane_start):
        return pltpu.roll(values, lax.rem(lane_start - lax.rem(z, 128) + 256, 128), 1)

    for side, sign in enumerate(signs):
        z = corner(0, sign)[1]
        total = jnp.zeros((SUB, 128), jnp.float32)
        for field in range(F):
            part = y_buffer[side, field * SUB : (field + 1) * SUB, side * 7, :]
            total = jnp.where(lane // SUB == field, moved(part, z, field * SUB), total)
        thin[column_of(place, 0, sign), :, side * 128 : (side + 1) * 128] = total
    for side, sign in enumerate(signs):
        y, z = corner(sign, 0)
        for half in range(2):
            total = jnp.zeros((8, 128), jnp.float32)
            for step in range(8):
                row = side * 8 * y_cells + y + half * 8 + step
                part = moved(x_buffer[pl.ds(row, 8, y_cells), :], z, step * SUB)
                total = jnp.where(lane[:8] // SUB == step, part, total)
            at = (column_of(place, sign, 0), slice(side * 8, side * 8 + 8), slice(half * 128, half * 128 + 128))
            thin[at] = total


def thin_faces(sample_block, place, brick, columns):
    fields, x_cells, y_cells, z_cells = brick.shape
    vmem = pl.BlockSpec(memory_space=pltpu.VMEM)
    smem = pl.BlockSpec(memory_space=pltpu.SMEM)
    hbm = pl.BlockSpec(memory_space=pltpu.HBM)
    return pl.pallas_call(
        functools.partial(thin_kernel, y_cells, z_cells),
        out_shape=jax.ShapeDtypeStruct((columns, SUB, 256), jnp.float32),
        in_specs=[smem, smem, hbm, hbm],
        out_specs=vmem,
        scratch_shapes=[
            pltpu.VMEM((16 * y_cells, 128), jnp.float32),
            pltpu.VMEM((2, fields * x_cells, 8, 128), jnp.float32),
            pltpu.SemaphoreType.DMA((2, fields)),
            pltpu.SemaphoreType.DMA((2,)),
        ],
        compiler_params=pltpu.CompilerParams(vmem_limit_bytes=16 * 1024 * 1024),
        name="thin_faces",
    )(
        sample_block,
        place,
        brick.reshape(fields * x_cells * y_cells, z_cells),
        brick.reshape(fields * x_cells, y_cells, z_cells),
    )


def sample_kernel(
    y_cells,
    z_cells,
    sample_block,
    place,
    brick,
    centre,
    lower,
    upper,
    own_rows,
    windows,
    sems,
):
    rows_of_x = y_cells
    rows_of_field = SUB * y_cells
    window_rows = F * rows_of_field

    def corner(x_step, y_step):
        return corner_of(sample_block, place, x_step, y_step, y_cells, z_cells)

    y_start, z_start = corner(0, 0)
    z_below = jnp.maximum(z_start - 1, 0)
    z_above = jnp.minimum(z_start + SUB, z_cells - 1)
    first_window = lax.div(z_below, 128)
    second_window = jnp.minimum(first_window + 1, z_cells // 128 - 1)
    copies = [
        pltpu.make_async_copy(
            brick.at[:, pl.ds(pl.multiple_of(at * 128, 128), 128)],
            windows.at[pl.ds(slot * window_rows, window_rows)],
            sems.at[slot],
        )
        for slot, at in enumerate((first_window, second_window))
    ]
    for copy in copies:
        copy.start()
    for copy in copies:
        copy.wait()

    def window(row, z):
        slot = lax.div(z, 128) - first_window
        return windows[pl.ds(slot * window_rows + row, SUB, rows_of_x), :]

    lane = lax.broadcasted_iota(jnp.int32, (SUB, 128), 1)
    for field in range(F):
        for half in range(2):
            inside = jnp.zeros((SUB, 128), jnp.float32)
            below = jnp.zeros((SUB, 128), jnp.float32)
            above = jnp.zeros((SUB, 128), jnp.float32)
            for step in range(8):
                row = field * rows_of_field + y_start + half * 8 + step
                first = step * SUB
                values = jnp.where(lane == 127, window(row, z_below), window(row, z_start))
                values = jnp.where(lane == 0, window(row, z_above), values)
                values = pltpu.roll(values, lax.rem(first - lax.rem(z_start, 128) + 256, 128), 1)
                inside = jnp.where(lane // SUB == step, values, inside)
                below = jnp.where(lane == (first - 1) % 128, values, below)
                above = jnp.where(lane == (first + SUB) % 128, values, above)
            below = jnp.where(z_start == 0, 0.0, pltpu.roll(below, 1, 1))
            above = jnp.where(z_start + SUB == z_cells, 0.0, pltpu.roll(above, 127, 1))
            at = (slice(field * SUB, (field + 1) * SUB), slice(half * 128, (half + 1) * 128))
            centre[at] = inside
            lower[at] = jnp.where(lane % SUB == 0, below, pltpu.roll(inside, 1, 1))
            upper[at] = jnp.where(lane % SUB == SUB - 1, above, pltpu.roll(inside, 127, 1))

    def y_row(y, z):
        total = jnp.zeros((SUB, 128), jnp.float32)
        for field in range(F):
            part = window(field * rows_of_field + y, z)
            part = pltpu.roll(part, lax.rem(field * SUB - lax.rem(z, 128) + 256, 128), 1)
            total = jnp.where(lane // SUB == field, part, total)
        return total

    own_rows[0] = y_row(jnp.maximum(y_start - 1, 0), z_start)
    own_rows[1] = y_row(jnp.minimum(y_start + SUB, y_cells - 1), z_start)

def sample_cube(sample_block, place, brick):
    fields, x_cells, y_cells, z_cells = brick.shape
    vmem = pl.BlockSpec(memory_space=pltpu.VMEM)
    smem = pl.BlockSpec(memory_space=pltpu.SMEM)
    hbm = pl.BlockSpec(memory_space=pltpu.HBM)
    rows = fields * x_cells * y_cells
    cube = jax.ShapeDtypeStruct((F * SUB, 256), jnp.float32)
    return pl.pallas_call(
        functools.partial(sample_kernel, y_cells, z_cells),
        out_shape=(
            cube,
            cube,
            cube,
            jax.ShapeDtypeStruct((2, SUB, 128), jnp.float32),
        ),
        in_specs=[smem, smem, hbm],
        out_specs=(vmem,) * 4,
        scratch_shapes=[
            pltpu.VMEM((2 * rows, 128), jnp.float32),
            pltpu.SemaphoreType.DMA((2,)),
        ],
        compiler_params=pltpu.CompilerParams(vmem_limit_bytes=16 * 1024 * 1024),
        cost_estimate=pl.CostEstimate(flops=0, bytes_accessed=16_000_000, transcendentals=0),
        name="sample_cube",
    )(sample_block, place, brick.reshape(rows, z_cells))


def change_kernel(
    y_cells,
    z_cells,
    sample_block,
    place,
    closure,
    order,
    centre,
    lower,
    upper,
    own_rows,
    thin,
    payload,
    table,
):
    y_start = corner_of(sample_block, place, 0, 0, y_cells, z_cells)[0]
    row = lax.broadcasted_iota(jnp.int32, (SUB, 256), 0)
    lane = lax.broadcasted_iota(jnp.int32, (SUB, 256), 1)
    south_row = jnp.where(y_start == 0, thin[column_of(place, 0, -1), :, 128:], own_rows[0])
    north_row = jnp.where(y_start + SUB == y_cells, thin[column_of(place, 0, 1), :, :128], own_rows[1])
    face_low = thin[column_of(place, -1, 0), 8:, :]
    face_high = thin[column_of(place, 1, 0), :8, :]
    cells = [centre[f * SUB : (f + 1) * SUB, :] for f in range(F)]
    viscosity = viscosity_of(cells, closure)
    changes = []
    for f in range(F):
        value = cells[f]
        west = jnp.where(row == 0, face_low[f : f + 1, :], pltpu.roll(value, 1, 0))
        east = jnp.where(row == SUB - 1, face_high[f : f + 1, :], pltpu.roll(value, SUB - 1, 0))
        edge = pltpu.roll(south_row, (128 - f * SUB) % 128, 1)
        south = jnp.where(lane < SUB, jnp.concatenate([edge, edge], 1), pltpu.roll(value, SUB, 1))
        edge = pltpu.roll(north_row, 112 - f * SUB, 1)
        north = jnp.where(
            lane >= 256 - SUB, jnp.concatenate([edge, edge], 1), pltpu.roll(value, 256 - SUB, 1)
        )
        down = lower[f * SUB : (f + 1) * SUB, :]
        up = upper[f * SUB : (f + 1) * SUB, :]
        laplacian = east + west + north + south + up + down - 6.0 * value
        advection = cells[0] * (east - west) + cells[1] * (north - south) + cells[2] * (up - down)
        change = viscosity * laplacian - 0.5 * advection
        if f == 2:
            change = change + buoyancy * cells[3]
        changes.append(change)
    ordered = dot_rows(jnp.concatenate(cells + changes, axis=0).astype(jnp.bfloat16), order[...])
    low_lanes = lane[:8, :128] < 64
    for part in range(2 * F):
        for cell in range(4):
            columns = slice(cell // 2 * 128, cell // 2 * 128 + 128)
            low = ordered[part * SUB : part * SUB + 8, columns]
            high = ordered[part * SUB + 8 : part * SUB + SUB, columns]
            if cell % 2 == 0:
                high = pltpu.roll(high, 64, 1)
            else:
                low = pltpu.roll(low, 64, 1)
            table[pl.ds(part * 32 + cell, 8, 4), :] = jnp.where(low_lanes, low, high)
    payload[...] = table[...].astype(jnp.bfloat16)


def cube_change(sample_block, place, closure, cube, thin, y_cells, z_cells):
    vmem = pl.BlockSpec(memory_space=pltpu.VMEM)
    smem = pl.BlockSpec(memory_space=pltpu.SMEM)
    return pl.pallas_call(
        functools.partial(change_kernel, y_cells, z_cells),
        out_shape=jax.ShapeDtypeStruct((4 * F * SUB, 128), jnp.bfloat16),
        in_specs=[smem] * 3 + [vmem] * 6,
        out_specs=vmem,
        scratch_shapes=[pltpu.VMEM((4 * F * SUB, 128), jnp.float32)],
        compiler_params=pltpu.CompilerParams(vmem_limit_bytes=16 * 1024 * 1024),
        name="cube_change",
    )(sample_block, place, closure, jnp.asarray(CELL_ORDER, jnp.bfloat16), *cube, thin)


def on_device(
    fields, closure_in, closure_bias, closure_out, master, momentum, sample_block, sample_trainer
):
    group_count = lax.axis_size("grp")
    x_devices = lax.axis_size("gx")
    y_devices = lax.axis_size("gy")
    trainers = x_devices * y_devices
    my_group = lax.axis_index("grp")
    my_column = lax.axis_index("gx") * y_devices + lax.axis_index("gy")
    is_trainer = my_group == group_count - 1
    everyone = ("grp", "gx", "gy")
    sim_groups = group_count - 1
    first_trainer = sim_groups * trainers
    brick = fields[0]
    y_cells, z_cells = brick.shape[2:]
    closure = jnp.concatenate(
        [0.5 * closure_in.T, 0.5 * closure_bias[None], closure_out[None]], axis=0
    )
    linear = jnp.sum(closure * closure_out[None], axis=1, keepdims=True)
    closure = jnp.pad(jnp.concatenate([closure, linear], axis=1), ((0, 1), (0, 127 - HID)))
    place = jnp.stack(
        [
            my_group,
            lax.axis_index("gx"),
            lax.axis_index("gy"),
            jnp.int32(sim_groups),
            jnp.int32(y_devices),
            jnp.int32(x_devices),
        ]
    ).astype(jnp.int32)

    def pairs(x_step, even_step):
        found = []
        for g in range(sim_groups):
            for c in range(trainers):
                gx, gy = c // y_devices, c % y_devices
                gx = (gx + x_step) % x_devices
                gy = (gy + (even_step if gy % 2 == 0 else -even_step)) % y_devices
                found.append((g * trainers + c, (g * x_devices + gx) * y_devices + gy))
        return found

    def x_neighbours(edges):
        if x_devices == 2:
            return lax.ppermute(edges, everyone, pairs(1, 0))
        from_high = lax.ppermute(edges[0], everyone, pairs(-1, 0))
        return jnp.stack([from_high, lax.ppermute(edges[1], everyone, pairs(1, 0))])

    def y_neighbours(for_first, for_second):
        return (
            lax.ppermute(for_first, everyone, pairs(0, 1)),
            lax.ppermute(for_second, everyone, pairs(0, -1)),
        )

    def swap(distance):
        return [(first_trainer + c, first_trainer + (c ^ distance)) for c in range(trainers)]

    def to_trainers(payload):
        landed = [
            lax.ppermute(
                payload, everyone, [(g * trainers + c, first_trainer + c) for c in range(trainers)]
            )
            for g in reversed(range(sim_groups))
        ]
        return jnp.stack(landed)

    def from_line(held):
        return [lax.ppermute(held, everyone, swap(apart)) for apart in range(1, y_devices)]

    def across(apart, held):
        return lax.ppermute(held, everyone, swap(apart * y_devices))

    thin = thin_faces(sample_block, place, brick, trainers)
    cube = sample_cube(sample_block, place, brick)
    first_count = CH * TAPS * F
    first = jnp.pad(master[:first_count].reshape(CH, TAPS * F), ((0, 0), (0, 256 - TAPS * F)))
    last = jnp.pad(master[first_count:].reshape(TAPS * F, CH), ((0, 256 - TAPS * F), (0, 0)))

    *cube, first, last = lax.optimization_barrier((*cube, first, last))
    selects = lax.optimization_barrier(
        (jnp.asarray(SELECT_FIRST, jnp.bfloat16), jnp.asarray(SELECT_LAST, jnp.bfloat16))
    )

    thin = lax.all_to_all(thin, ("gx", "gy"), split_axis=0, concat_axis=0, tiled=True)
    payload = cube_change(sample_block, place, closure, cube, thin, y_cells, z_cells)
    landed = to_trainers(payload)
    closure, landed = lax.optimization_barrier((closure, landed))

    fields_count, x_cells = brick.shape[:2]
    viscosity, x_edges, y_edges = lax.cond(
        is_trainer,
        lambda: (
            jnp.zeros((x_cells, y_cells, z_cells), jnp.float32),
            jnp.zeros((2, fields_count, y_cells, z_cells), jnp.float32),
            jnp.zeros((2, fields_count, x_cells, z_cells), jnp.float32),
        ),
        lambda: brick_viscosity(closure, place, brick),
    )
    halo = (x_neighbours(x_edges), *y_neighbours(y_edges[0], y_edges[1]))
    near = [landed, *from_line(landed)]
    far = [
        across(apart, pick_cubes(sample_trainer, place, near, y_devices, x_devices, apart))
        for apart in range(1, x_devices)
    ]
    arrived = [*near, *far]

    def train_here():
        delta_first, delta_last, new_brick = train_cubes(
            sample_trainer, place, first, last, selects, arrived, brick, y_devices, x_devices
        )
        delta = jnp.concatenate(
            [delta_first[:, : TAPS * F].reshape(-1), delta_last[: TAPS * F].reshape(-1)]
        )
        return delta, new_brick

    def evolve_here():
        new_brick = evolve(place, viscosity, brick, *halo)
        return jnp.zeros((NPARAM,), jnp.float32), new_brick

    delta, new_brick = lax.cond(is_trainer, train_here, evolve_here)

    held = delta
    for g in reversed(range(sim_groups)):
        held = held + lax.ppermute(
            delta, everyone, [(first_trainer + c, g * trainers + c) for c in range(trainers)]
        )
    final = delta
    for first_apart in range(1, trainers, group_count):
        meets = [
            (g * trainers + c, g * trainers + (c ^ (first_apart + g)))
            for g in range(group_count)
            for c in range(trainers)
            if first_apart + g < trainers
        ]
        final = final + lax.ppermute(held, everyone, meets)
    for apart in (1, 2):
        final = final + lax.ppermute(
            final,
            everyone,
            [(g * trainers + c, (g ^ apart) * trainers + c) for g in range(group_count) for c in range(trainers)],
        )

    share_size = NPARAM // (group_count * trainers)
    share_start = (my_group * trainers + my_column) * share_size
    momentum_share = lax.dynamic_slice_in_dim(momentum, share_start, share_size)
    master_share = lax.dynamic_slice_in_dim(master, share_start, share_size)
    inverse = 1.0 / jnp.sqrt(jnp.sum(final * final) / NPARAM + norm_epsilon)
    delta_share = lax.dynamic_slice_in_dim(final, share_start, share_size)
    new_momentum = momentum_decay * momentum_share + delta_share * inverse
    new_master = master_share - outer_rate * new_momentum
    return (new_brick[None], new_master, new_momentum)


def solution(mesh):
    in_specs = (P("grp", None, "gx", "gy", None), P(), P(), P(), P(), P(), P(), P())
    out_specs = (P("grp", None, "gx", "gy", None), P(("grp", "gx", "gy")), P(("grp", "gx", "gy")))
    return jax.shard_map(
        on_device, mesh=mesh, in_specs=in_specs, out_specs=out_specs, check_vma=False
    )
```

```python
import functools

import jax
import jax.numpy as jnp
import numpy as np
from jax import lax
from jax.experimental import pallas as pl
from jax.experimental.pallas import tpu as pltpu
from jax.sharding import PartitionSpec as P

F = 5
CH = 64
HID = 64
SUB = 16
TCAP = 6
INNER = 3
CELLS = 4096
NPARAM = 17280
TAPS = 27
PAIRS = TCAP // 2
COLS = (SUB + 2) * 128
PATCH = 16 * F
STACK = 3 * PATCH

time_step = 0.1
base_viscosity = 0.02
viscosity_gain = 0.2
buoyancy = 0.5
inner_rate = 0.02
outer_rate = 0.01
momentum_decay = 0.9
norm_epsilon = 1e-06


def patch_position(row):
    group, py, pz = row // 4, row // 2 % 2, row % 2
    ypos = py + 1 if group in (0, 2) else (3 if py == 0 else 0)
    zpos = pz + 1 if group in (0, 1) else (3 if pz == 0 else 0)
    return ypos - 1, zpos - 1


def selections():
    first = np.zeros((4, 256, STACK), np.float32)
    last = np.zeros((4, 256, STACK), np.float32)
    for cell in range(4):
        py, pz = cell // 2, cell % 2
        for kx in range(3):
            for channel in range(F):
                for row in range(16):
                    ypos, zpos = patch_position(row)
                    column = kx * PATCH + channel * 16 + row
                    dy, dz = ypos - py, zpos - pz
                    if abs(dy) <= 1 and abs(dz) <= 1:
                        tap = 9 * kx + 3 * (dy + 1) + dz + 1
                        first[cell, tap * F + channel, column] = 1.0
                        last[cell, channel * TAPS + 26 - tap, column] = 1.0
    return first, last


SELECT_FIRST, SELECT_LAST = selections()


def column_of(place, x_step, y_step):
    gx = lax.rem(place[1] + x_step + place[5], place[5])
    gy = lax.rem(place[2] + y_step + place[4], place[4])
    return gx * place[4] + gy


def owner_apart(owner, groups, place, y_devices, x_devices):
    group, column = divmod(owner, x_devices * y_devices)
    entry = groups - 1 - group
    y_apart = jnp.bitwise_xor(place[2], jnp.int32(column % y_devices))
    return entry, y_apart, jnp.bitwise_xor(place[1], jnp.int32(column // y_devices))


def pick_kernel(y_devices, x_devices, apart, trainer_of, place, *refs):
    near, chosen, owners = refs[:y_devices], refs[y_devices], refs[y_devices + 1]
    wanted = jnp.bitwise_xor(place[1], jnp.int32(apart)) * y_devices + place[2]
    count = jnp.int32(0)
    groups = trainer_of.shape[0] // (x_devices * y_devices)
    for owner in range(trainer_of.shape[0]):
        group, y_apart, x_apart = owner_apart(owner, groups, place, y_devices, x_devices)
        mine = (trainer_of[owner] == wanted) & (x_apart == 0)

        @pl.when(mine)
        def _():
            owners[0, count] = y_apart
            owners[1, count] = group

        count = count + jnp.where(mine, 1, 0)

    def copy_slot(slot, carry):
        for source in range(y_devices):

            @pl.when(owners[0, slot] == source)
            def _():
                chosen[slot] = near[source][owners[1, slot]]

        return carry

    lax.fori_loop(0, count, copy_slot, 0)


def pick_cubes(trainer_of, place, near, y_devices, x_devices, apart):
    vmem = pl.BlockSpec(memory_space=pltpu.VMEM)
    smem = pl.BlockSpec(memory_space=pltpu.SMEM)
    return pl.pallas_call(
        functools.partial(pick_kernel, y_devices, x_devices, apart),
        out_shape=jax.ShapeDtypeStruct((TCAP, *near[0].shape[1:]), near[0].dtype),
        in_specs=[smem, smem] + [vmem] * len(near),
        out_specs=vmem,
        scratch_shapes=[pltpu.SMEM((2, TCAP), jnp.int32)],
        compiler_params=pltpu.CompilerParams(vmem_limit_bytes=16 * 1024 * 1024),
        name="pick_cubes",
    )(trainer_of, place, *near)


def dot_rows(left, right):
    return jnp.dot(left, right, preferred_element_type=jnp.float32)


def dot_lanes(left, right):
    return lax.dot_general(left, right, (((1,), (1,)), ((), ())), preferred_element_type=jnp.float32)


def patch_masks():
    row = lax.broadcasted_iota(jnp.int32, (8, 128), 0)
    lane = lax.broadcasted_iota(jnp.int32, (8, 128), 1)
    z, y = lane % 8, lane // 8 % 8
    even_z, even_y = row % 2 == 0, row // 2 % 2 == 0
    return {
        "centre": row < 4,
        "even_z": even_z,
        "even_y": even_y,
        "gather_z": jnp.where(even_z, z, 7 - z) < 7,
        "gather_y": jnp.where(even_y, y, 7 - y) < 7,
        "scatter_z": jnp.where(even_z, z, 7 - z) > 0,
        "scatter_y": jnp.where(even_y, y, 7 - y) > 0,
    }


def edge_shift(values, step, even, inside, gather):
    before, after = pltpu.roll(values, step, 1), pltpu.roll(values, 128 - step, 1)
    moved = jnp.where(even, after, before) if gather else jnp.where(even, before, after)
    return jnp.where(inside, moved, 0.0)


def patch_stack(rows, masks):
    both = jnp.where(masks["centre"], rows, pltpu.roll(rows, 4, 0))
    y_edge = edge_shift(both, 8, masks["even_y"], masks["gather_y"], True)
    upper = jnp.where(masks["centre"], both, y_edge)
    return upper, edge_shift(upper, 1, masks["even_z"], masks["gather_z"], True)


def patch_fold(upper, lower, masks):
    line = upper + edge_shift(lower, 1, masks["even_z"], masks["scatter_z"], False)
    return line + pltpu.roll(edge_shift(line, 8, masks["even_y"], masks["scatter_y"], False), 4, 0)


def store_planes(ref, x, channels):
    stacked = jnp.concatenate([part for both in channels for part in both], axis=0).astype(jnp.bfloat16)
    for kx in range(3):
        start = pl.multiple_of((x + 2 - kx) * 128, 128)
        ref[kx * PATCH : (kx + 1) * PATCH, pl.ds(start, 128)] = stacked


def train_kernel(y_devices, x_devices, *refs):
    sources = y_devices + x_devices - 1
    (trainer_of, place, first_ref, last_ref, far_first, far_last) = refs[:6]
    arrived = refs[6 : 6 + sources]
    fields_ref = refs[6 + sources]
    delta_first, delta_last, new_fields_ref = refs[7 + sources : 10 + sources]
    (
        slots,
        picked,
        cubes,
        big_first,
        big_last,
        big_last_t,
        grad_first,
        grad_last,
        now_first,
        now_last,
        brick,
        select_first,
        select_last,
        slot_sems,
        field_sem,
        select_sems,
        *pair_refs,
    ) = refs[10 + sources :]
    targets, tables, inputs, errors, hiddens, pre_grads, slopes, partial_out, raw = [
        pair_refs[kind * PAIRS : (kind + 1) * PAIRS] for kind in range(9)
    ]

    field_in = pltpu.make_async_copy(fields_ref, brick, field_sem)
    field_out = pltpu.make_async_copy(brick, new_fields_ref, field_sem)
    select_copies = [
        pltpu.make_async_copy(far_first, select_first, select_sems.at[0]),
        pltpu.make_async_copy(far_last, select_last, select_sems.at[1]),
    ]

    column = place[1] * y_devices + place[2]
    for other in range(x_devices):
        picked[other] = 0
    count = jnp.int32(0)
    groups = trainer_of.shape[0] // (x_devices * y_devices)
    for owner in range(trainer_of.shape[0]):
        group, y_apart, x_apart = owner_apart(owner, groups, place, y_devices, x_devices)
        mine = trainer_of[owner] == column

        @pl.when(mine)
        def _():
            near = x_apart == 0
            slots[0, count] = jnp.where(near, y_apart, y_devices - 1 + x_apart)
            slots[1, count] = jnp.where(near, group, picked[x_apart])
            picked[x_apart] = picked[x_apart] + 1

        count = count + jnp.where(mine, 1, 0)

    def fetch(slot, wait):
        for source in range(sources):

            @pl.when((slot < count) & (slots[0, slot] == source))
            def _():
                copy = pltpu.make_async_copy(
                    arrived[source].at[slots[1, slot]], cubes.at[slot], slot_sems.at[slot]
                )
                copy.wait() if wait else copy.start()

    for slot in range(TCAP):
        fetch(slot, False)

    for copy in select_copies:
        copy.start()
    field_in.start()
    for slot in range(TCAP):

        @pl.when(slot >= count)
        def _():
            cubes[slot] = jnp.zeros(cubes.shape[1:], jnp.bfloat16)

    masks = patch_masks()
    for ref in (*errors, *inputs):
        ref[:PATCH, 128:256] = jnp.zeros((PATCH, 128), jnp.bfloat16)
        ref[2 * PATCH :, COLS - 256 : COLS - 128] = jnp.zeros((PATCH, 128), jnp.bfloat16)
    for ref in partial_out:
        ref[:, :128] = jnp.zeros((STACK, 128), jnp.float32)
        ref[:, COLS - 128 :] = jnp.zeros((STACK, 128), jnp.float32)
    lane = lax.broadcasted_iota(jnp.int32, (8, 128), 1)
    full_weight = 2.0 * (1.0 / (jnp.full((8, 128), count, jnp.int32).astype(jnp.float32) * CELLS))
    weights = [
        jnp.where(lane // 64 + 2 * pair < count, full_weight, 0.0) for pair in range(PAIRS)
    ]
    start_first = first_ref[...].astype(jnp.bfloat16).astype(jnp.float32)
    start_last = last_ref[...].T.astype(jnp.bfloat16).astype(jnp.float32)
    now_first[...] = start_first
    now_last[...] = start_last

    for slot in range(TCAP):
        fetch(slot, True)

    low_lanes = lax.broadcasted_iota(jnp.int32, (SUB * F * 2, 128), 1) < 64
    for pair in range(PAIRS):
        for kind, ref in enumerate((tables[pair], targets[pair])):
            rows = slice(kind * SUB * F * 2, (kind + 1) * SUB * F * 2)
            even = cubes[2 * pair, rows, :].astype(jnp.float32)
            odd = cubes[2 * pair + 1, rows, :].astype(jnp.float32)
            ref[0] = jnp.where(low_lanes, even, pltpu.roll(odd, 64, 1))
            ref[1] = jnp.where(low_lanes, pltpu.roll(even, 64, 1), odd)

    def patch_cells(ref, quarter, plane, channel):
        start = pl.multiple_of(channel * 32 + quarter % 2 * 16 + plane // 2 * 8, 8)
        rows = ref[quarter // 2, pl.ds(start, 8), :]
        return rows if plane % 2 == 0 else pltpu.roll(rows, 4, 0)

    def stack_planes(quarter, carry):
        for pair in range(PAIRS):
            for plane in range(4):
                x = quarter * 4 + plane
                channels = [
                    patch_stack(patch_cells(tables[pair], quarter, plane, c), masks) for c in range(F)
                ]
                store_planes(inputs[pair], x, channels)
        return carry

    lax.fori_loop(0, 4, stack_planes, 0, unroll=2)

    for copy in select_copies:
        copy.wait()
    field_in.wait()
    field_out.start()

    def train_step(step, step_carry):
        first_now = now_first[...].astype(jnp.bfloat16)
        last_now = now_last[...].astype(jnp.bfloat16)
        for cell in range(4):
            rows = slice(cell * CH, (cell + 1) * CH)
            big_first[rows, :] = (0.5 * dot_rows(first_now, select_first[cell])).astype(jnp.bfloat16)
            spread_last = dot_rows(last_now, select_last[cell])
            big_last[rows, :] = (0.5 * spread_last).astype(jnp.bfloat16)
            big_last_t[:, rows] = spread_last.T.astype(jnp.bfloat16)
        grad_first[...] = jnp.zeros(grad_first.shape, jnp.float32)
        grad_last[...] = jnp.zeros(grad_last.shape, jnp.float32)

        def columns_of(quarter):
            return pl.ds(pl.multiple_of(quarter * 512 + 128, 128), 512)

        def first_layer(pair, quarter):
            columns = columns_of(quarter)
            raw[pair][:, columns] = dot_rows(big_first[...], inputs[pair][:, columns])

        def activate(pair, quarter):
            columns = columns_of(quarter)
            for part in range(8):
                rows = slice(part * 32, (part + 1) * 32)
                half = raw[pair][rows, columns]
                curve = jnp.tanh(half)
                above = 1.0 + curve
                value = half * above
                hiddens[pair][rows, columns] = value.astype(jnp.bfloat16)
                slopes[pair][rows, columns] = above + value * (1.0 - curve)

        def last_layer(pair, quarter):
            columns = columns_of(quarter)
            partial_out[pair][:, columns] = dot_rows(big_last_t[...], hiddens[pair][:, columns])

        def find_errors(pair, quarter):
            for plane in range(4):
                x = quarter * 4 + plane
                column = pl.multiple_of((x + 1) * 128, 128)
                total = (
                    partial_out[pair][0:PATCH, pl.ds(pl.multiple_of(column + 128, 128), 128)]
                    + partial_out[pair][PATCH : 2 * PATCH, pl.ds(column, 128)]
                    + partial_out[pair][2 * PATCH :, pl.ds(pl.multiple_of(column - 128, 128), 128)]
                )
                channels = []
                for c in range(F):
                    predicted = patch_fold(
                        total[16 * c : 16 * c + 8], total[16 * c + 8 : 16 * c + 16], masks
                    )
                    wanted = patch_cells(targets[pair], quarter, plane, c)
                    error = weights[pair] * (predicted - wanted)
                    channels.append(patch_stack(error, masks))
                store_planes(errors[pair], x, channels)

        def hidden_layer(pair, quarter):
            columns = columns_of(quarter)
            raw[pair][:, columns] = dot_rows(big_last[...], errors[pair][:, columns])

        def scale(pair, quarter):
            columns = columns_of(quarter)
            for part in range(8):
                rows = slice(part * 32, (part + 1) * 32)
                product = raw[pair][rows, columns] * slopes[pair][rows, columns]
                pre_grads[pair][rows, columns] = product.astype(jnp.bfloat16)

        def gradients(pair, quarter):
            columns = columns_of(quarter)
            grad_first[...] += dot_lanes(pre_grads[pair][:, columns], inputs[pair][:, columns])
            grad_last[...] += dot_lanes(hiddens[pair][:, columns], errors[pair][:, columns])

        stages = (first_layer, activate, last_layer, find_errors, hidden_layer, scale, gradients)
        for turn in range(len(stages) + PAIRS - 1):

            def run(quarter, carry):
                for pair in range(PAIRS):
                    if 0 <= turn - pair < len(stages):
                        stages[turn - pair](pair, quarter)
                return carry

            lax.fori_loop(0, 4, run, 0, unroll=4)

        def folded(grad, select_ref):
            total = jnp.zeros((3 * CH, 256), jnp.float32)
            for cell in range(4):
                rest = grad[cell * CH : (cell + 1) * CH, :]
                parts = []
                for _ in range(3):
                    parts.append(rest.astype(jnp.bfloat16))
                    rest = rest - parts[-1].astype(jnp.float32)
                total = total + dot_lanes(jnp.concatenate(parts, axis=0), select_ref[cell])
            return total[:CH] + total[CH : 2 * CH] + total[2 * CH :]

        now_first[...] = now_first[...] - inner_rate * folded(grad_first, select_first)
        now_last[...] = now_last[...] - inner_rate * folded(grad_last, select_last)
        return step_carry

    lax.fori_loop(0, INNER, train_step, 0)
    delta_first[...] = start_first - now_first[...]
    delta_last[...] = (start_last - now_last[...]).T
    field_out.wait()


def train_cubes(trainer_of, place, first, last, selects, arrived, fields, y_devices, x_devices):
    vmem = pl.BlockSpec(memory_space=pltpu.VMEM)
    smem = pl.BlockSpec(memory_space=pltpu.SMEM)
    anywhere = pl.BlockSpec(memory_space=pl.ANY)
    hbm = pl.BlockSpec(memory_space=pltpu.HBM)
    return pl.pallas_call(
        functools.partial(train_kernel, y_devices, x_devices),
        out_shape=(
            jax.ShapeDtypeStruct((CH, 256), jnp.float32),
            jax.ShapeDtypeStruct((256, CH), jnp.float32),
            jax.ShapeDtypeStruct(fields.shape, fields.dtype),
        ),
        in_specs=[smem] * 2 + [vmem] * 2 + [hbm] * 2 + [anywhere] * len(arrived) + [hbm],
        out_specs=(vmem, vmem, hbm),
        scratch_shapes=[
            pltpu.SMEM((2, TCAP), jnp.int32),
            pltpu.SMEM((x_devices,), jnp.int32),
            pltpu.VMEM((TCAP, 4 * SUB * F, 128), jnp.bfloat16),
            pltpu.VMEM((4 * CH, STACK), jnp.bfloat16),
            pltpu.VMEM((4 * CH, STACK), jnp.bfloat16),
            pltpu.VMEM((STACK, 4 * CH), jnp.bfloat16),
            pltpu.VMEM((4 * CH, STACK), jnp.float32),
            pltpu.VMEM((4 * CH, STACK), jnp.float32),
            pltpu.VMEM((CH, 256), jnp.float32),
            pltpu.VMEM((CH, 256), jnp.float32),
            pltpu.VMEM(fields.shape, fields.dtype),
            pltpu.VMEM((4, 256, STACK), jnp.bfloat16),
            pltpu.VMEM((4, 256, STACK), jnp.bfloat16),
            pltpu.SemaphoreType.DMA((TCAP,)),
            pltpu.SemaphoreType.DMA,
            pltpu.SemaphoreType.DMA((2,)),
        ]
        + [pltpu.VMEM((2, SUB * F * 2, 128), jnp.float32)] * (2 * PAIRS)
        + [pltpu.VMEM((STACK, COLS), jnp.bfloat16)] * (2 * PAIRS)
        + [pltpu.VMEM((4 * CH, COLS), jnp.bfloat16)] * (2 * PAIRS)
        + [pltpu.VMEM((4 * CH, COLS), jnp.float32)] * PAIRS
        + [pltpu.VMEM((STACK, COLS), jnp.float32)] * PAIRS
        + [pltpu.VMEM((4 * CH, COLS), jnp.float32)] * PAIRS,
        compiler_params=pltpu.CompilerParams(vmem_limit_bytes=52 * 1024 * 1024),
        name="train_cubes",
    )(
        trainer_of,
        place,
        first,
        last,
        *selects,
        *arrived,
        fields,
    )


def viscosity_of(cells, closure):
    def unit(h, total):
        half = closure[F, h] + closure[0, h] * cells[0]
        for f in range(1, F):
            half = half + closure[f, h] * cells[f]
        return total + closure[F + 1, h] * (half * jnp.tanh(half))

    total = closure[F, HID] + closure[0, HID] * cells[0]
    for f in range(1, F):
        total = total + closure[f, HID] * cells[f]
    total = lax.fori_loop(0, HID, unit, total, unroll=8)
    soft = jnp.maximum(total, 0.0) + jnp.log1p(jnp.exp(-jnp.abs(total)))
    return base_viscosity + viscosity_gain * soft


def viscosity_kernel(closure, place, fields, viscosity, x_edges, y_edges, weights, out_column):
    y_cells, z_cells = fields.shape[2:]
    x, x_cells = pl.program_id(0), pl.num_programs(0)
    up_first = lax.rem(place[2], 2) == 0
    for f in range(F):
        low, high = fields[f, 0, 0:1, :], fields[f, 0, y_cells - 1 : y_cells, :]
        y_edges[0, f, pl.ds(x, 1), :] = jnp.where(up_first, high, low)
        y_edges[1, f, pl.ds(x, 1), :] = jnp.where(up_first, low, high)

    @pl.when(x == x_cells - 1)
    def _():
        x_edges[1] = fields[:, 0]

    @pl.when(x == 0)
    def _():
        x_edges[0] = fields[:, 0]
        plain = closure[...]
        high = plain.astype(jnp.bfloat16).astype(jnp.float32)
        low = plain - high
        blank = jnp.zeros((8, 128), jnp.float32)
        for j in range(8):
            turned = [pltpu.roll(part, j, 0) if j else part for part in (high, high, low)]
            stacked = jnp.concatenate([*turned, blank], axis=0)
            weights[j] = stacked.T[: HID + 8].astype(jnp.bfloat16)
        out_column[...] = jnp.broadcast_to(plain.T[:HID, F + 1 : F + 2], (HID, 128))

    sublane = lax.broadcasted_iota(jnp.int32, (8, z_cells), 0)
    wide = z_cells // 128
    tiles = y_cells // 8

    def tile(index, carry):
        rows = pl.ds(pl.multiple_of(index * 8, 8), 8)
        turned = [fields[f, 0, rows, :] for f in range(F)]
        turned = [pltpu.roll(turned[f], f, 0) if f else turned[f] for f in range(F)]
        sums = jnp.zeros((8, z_cells), jnp.float32)
        for j in range(8):
            cells = jnp.where(sublane == (j + F) % 8, 1.0, 0.0)
            for f in range(F):
                cells = jnp.where(sublane == (j + f) % 8, turned[f], cells)
            top = cells.astype(jnp.bfloat16).astype(jnp.float32)
            stacked = jnp.concatenate([top, cells - top, top, jnp.zeros_like(top)], axis=0)
            half = dot_rows(weights[j], stacked.astype(jnp.bfloat16))
            total = half[HID:]
            for group in range(HID // 8):
                part = half[group * 8 : group * 8 + 8]
                column = jnp.concatenate([out_column[group * 8 : group * 8 + 8, :]] * wide, axis=1)
                total = total + column * (part * jnp.tanh(part))
            for step in (4, 2, 1):
                total = total + pltpu.roll(total, step, 0)
            sums = jnp.where(sublane == j, total, sums)
        soft = jnp.maximum(sums, 0.0) + jnp.log1p(jnp.exp(-jnp.abs(sums)))
        viscosity[0, rows, :] = base_viscosity + viscosity_gain * soft
        return carry

    lax.fori_loop(0, tiles, tile, 0)


def brick_viscosity(closure, place, fields):
    count, x_cells, y_cells, z_cells = fields.shape
    return pl.pallas_call(
        viscosity_kernel,
        out_shape=(
            jax.ShapeDtypeStruct(fields.shape[1:], fields.dtype),
            jax.ShapeDtypeStruct((2, count, y_cells, z_cells), fields.dtype),
            jax.ShapeDtypeStruct((2, count, x_cells, z_cells), fields.dtype),
        ),
        grid=(x_cells,),
        in_specs=[
            pl.BlockSpec((8, 128), lambda x: (0, 0)),
            pl.BlockSpec(memory_space=pltpu.SMEM),
            pl.BlockSpec((count, 1, y_cells, z_cells), lambda x: (0, x, 0, 0)),
        ],
        out_specs=(
            pl.BlockSpec((1, y_cells, z_cells), lambda x: (x, 0, 0)),
            pl.BlockSpec((2, count, y_cells, z_cells), lambda x: (0, 0, 0, 0)),
            pl.BlockSpec((2, count, x_cells, z_cells), lambda x: (0, 0, 0, 0)),
        ),
        scratch_shapes=[
            pltpu.VMEM((8, HID + 8, 32), jnp.bfloat16),
            pltpu.VMEM((HID, 128), jnp.float32),
        ],
        compiler_params=pltpu.CompilerParams(vmem_limit_bytes=16 * 1024 * 1024),
        name="brick_viscosity",
    )(closure, place, fields)


def evolve_kernel(place, viscosity, fields, x_halo, y_first, y_second, new_fields):
    up_first = lax.rem(place[2], 2) == 0
    x_cells, y_cells, z_cells = fields.shape[1:]
    row = lax.broadcasted_iota(jnp.int32, (y_cells, z_cells), 0)
    lane = lax.broadcasted_iota(jnp.int32, (y_cells, z_cells), 1)

    x = pl.program_id(0)
    centre = [fields[f, x] for f in range(F)]
    below = jnp.maximum(x - 1, 0)
    above = jnp.minimum(x + 1, x_cells - 1)
    for f in range(F):
        value = centre[f]
        west = jnp.where(x == 0, x_halo[1, f], fields[f, below])
        east = jnp.where(x == x_cells - 1, x_halo[0, f], fields[f, above])
        first, second = y_first[f, pl.ds(x, 1), :], y_second[f, pl.ds(x, 1), :]
        south = jnp.where(
            row == 0, jnp.where(up_first, second, first), pltpu.roll(value, 1, 0)
        )
        north = jnp.where(
            row == y_cells - 1,
            jnp.where(up_first, first, second),
            pltpu.roll(value, y_cells - 1, 0),
        )
        lower = jnp.where(lane == 0, 0.0, pltpu.roll(value, 1, 1))
        upper = jnp.where(lane == z_cells - 1, 0.0, pltpu.roll(value, z_cells - 1, 1))
        laplacian = east + west + north + south + upper + lower - 6.0 * value
        advection = (
            centre[0] * (east - west) + centre[1] * (north - south) + centre[2] * (upper - lower)
        )
        tendency = viscosity[0] * laplacian - 0.5 * advection
        if f == 2:
            tendency = tendency + buoyancy * centre[3]
        new_fields[f, 0] = value + time_step * tendency


def evolve(place, viscosity, fields, x_halo, y_first, y_second):
    count, x_cells, y_cells, z_cells = fields.shape

    def whole(shape):
        return pl.BlockSpec(shape, lambda x: (0,) * len(shape), pipeline_mode=pl.Buffered(1))

    return pl.pallas_call(
        evolve_kernel,
        out_shape=jax.ShapeDtypeStruct(fields.shape, fields.dtype),
        grid=(x_cells,),
        in_specs=[
            pl.BlockSpec(memory_space=pltpu.SMEM),
            pl.BlockSpec((1, y_cells, z_cells), lambda x: (x, 0, 0)),
            *[whole(array.shape) for array in (fields, x_halo, y_first, y_second)],
        ],
        out_specs=pl.BlockSpec((count, 1, y_cells, z_cells), lambda x: (0, x, 0, 0)),
        compiler_params=pltpu.CompilerParams(vmem_limit_bytes=16 * 1024 * 1024),
        name="evolve_brick",
    )(place, viscosity, fields, x_halo, y_first, y_second)


def cell_order():
    order = np.zeros((256, 256), np.float32)
    for y in range(SUB):
        for z in range(SUB):
            order[y * SUB + z, (y % 2 * 2 + z % 2) * 64 + y // 2 * 8 + z // 2] = 1.0
    return order


CELL_ORDER = cell_order()


def corner_of(sample_block, place, x_step, y_step, y_cells, z_cells):
    x_devices, y_devices = place[5], place[4]
    gx = lax.rem(place[1] + x_step + x_devices, x_devices)
    gy = lax.rem(place[2] + y_step + y_devices, y_devices)
    group = jnp.minimum(place[0], place[3] - 1)
    block = sample_block[(group * x_devices + gx) * y_devices + gy]
    z_blocks = z_cells // SUB
    return lax.rem(lax.div(block, z_blocks), y_cells // SUB) * SUB, lax.rem(block, z_blocks) * SUB


def thin_kernel(
    y_cells, z_cells, sample_block, place, rows_ref, lines_ref, thin, x_buffer, y_buffer, x_sems, y_sems
):
    def corner(x_step, y_step):
        return corner_of(sample_block, place, x_step, y_step, y_cells, z_cells)

    lane = lax.broadcasted_iota(jnp.int32, (SUB, 128), 1)
    signs = (-1, 1)
    copies = []
    for side, sign in enumerate(signs):
        z_x, z_y = corner(sign, 0)[1], corner(0, sign)[1]
        x, y = side * (SUB - 1), side * (y_cells - 8)
        for field in range(F):
            copies.append(
                pltpu.make_async_copy(
                    rows_ref.at[
                        pl.ds((field * SUB + x) * y_cells, y_cells),
                        pl.ds(pl.multiple_of(lax.div(z_x, 128) * 128, 128), 128),
                    ],
                    x_buffer.at[pl.ds((side * 8 + field) * y_cells, y_cells)],
                    x_sems.at[side, field],
                )
            )
        copies.append(
            pltpu.make_async_copy(
                lines_ref.at[:, pl.ds(y, 8), pl.ds(pl.multiple_of(lax.div(z_y, 128) * 128, 128), 128)],
                y_buffer.at[side],
                y_sems.at[side],
            )
        )
    for copy in copies:
        copy.start()
    thin[...] = jnp.zeros(thin.shape, thin.dtype)
    for copy in copies:
        copy.wait()

    def moved(values, z, lane_start):
        return pltpu.roll(values, lax.rem(lane_start - lax.rem(z, 128) + 256, 128), 1)

    for side, sign in enumerate(signs):
        z = corner(0, sign)[1]
        total = jnp.zeros((SUB, 128), jnp.float32)
        for field in range(F):
            part = y_buffer[side, field * SUB : (field + 1) * SUB, side * 7, :]
            total = jnp.where(lane // SUB == field, moved(part, z, field * SUB), total)
        thin[column_of(place, 0, sign), :, side * 128 : (side + 1) * 128] = total
    for side, sign in enumerate(signs):
        y, z = corner(sign, 0)
        for half in range(2):
            total = jnp.zeros((8, 128), jnp.float32)
            for step in range(8):
                row = side * 8 * y_cells + y + half * 8 + step
                part = moved(x_buffer[pl.ds(row, 8, y_cells), :], z, step * SUB)
                total = jnp.where(lane[:8] // SUB == step, part, total)
            at = (column_of(place, sign, 0), slice(side * 8, side * 8 + 8), slice(half * 128, half * 128 + 128))
            thin[at] = total


def thin_faces(sample_block, place, brick, columns):
    fields, x_cells, y_cells, z_cells = brick.shape
    vmem = pl.BlockSpec(memory_space=pltpu.VMEM)
    smem = pl.BlockSpec(memory_space=pltpu.SMEM)
    hbm = pl.BlockSpec(memory_space=pltpu.HBM)
    return pl.pallas_call(
        functools.partial(thin_kernel, y_cells, z_cells),
        out_shape=jax.ShapeDtypeStruct((columns, SUB, 256), jnp.float32),
        in_specs=[smem, smem, hbm, hbm],
        out_specs=vmem,
        scratch_shapes=[
            pltpu.VMEM((16 * y_cells, 128), jnp.float32),
            pltpu.VMEM((2, fields * x_cells, 8, 128), jnp.float32),
            pltpu.SemaphoreType.DMA((2, fields)),
            pltpu.SemaphoreType.DMA((2,)),
        ],
        compiler_params=pltpu.CompilerParams(vmem_limit_bytes=16 * 1024 * 1024),
        name="thin_faces",
    )(
        sample_block,
        place,
        brick.reshape(fields * x_cells * y_cells, z_cells),
        brick.reshape(fields * x_cells, y_cells, z_cells),
    )


def sample_kernel(
    y_cells,
    z_cells,
    sample_block,
    place,
    brick,
    centre,
    lower,
    upper,
    own_rows,
    windows,
    sems,
):
    rows_of_x = y_cells
    rows_of_field = SUB * y_cells
    window_rows = F * rows_of_field

    def corner(x_step, y_step):
        return corner_of(sample_block, place, x_step, y_step, y_cells, z_cells)

    y_start, z_start = corner(0, 0)
    z_below = jnp.maximum(z_start - 1, 0)
    z_above = jnp.minimum(z_start + SUB, z_cells - 1)
    first_window = lax.div(z_below, 128)
    second_window = jnp.minimum(first_window + 1, z_cells // 128 - 1)
    copies = [
        pltpu.make_async_copy(
            brick.at[:, pl.ds(pl.multiple_of(at * 128, 128), 128)],
            windows.at[pl.ds(slot * window_rows, window_rows)],
            sems.at[slot],
        )
        for slot, at in enumerate((first_window, second_window))
    ]
    for copy in copies:
        copy.start()
    for copy in copies:
        copy.wait()

    def window(row, z):
        slot = lax.div(z, 128) - first_window
        return windows[pl.ds(slot * window_rows + row, SUB, rows_of_x), :]

    lane = lax.broadcasted_iota(jnp.int32, (SUB, 128), 1)
    for field in range(F):
        for half in range(2):
            inside = jnp.zeros((SUB, 128), jnp.float32)
            below = jnp.zeros((SUB, 128), jnp.float32)
            above = jnp.zeros((SUB, 128), jnp.float32)
            for step in range(8):
                row = field * rows_of_field + y_start + half * 8 + step
                first = step * SUB
                values = jnp.where(lane == 127, window(row, z_below), window(row, z_start))
                values = jnp.where(lane == 0, window(row, z_above), values)
                values = pltpu.roll(values, lax.rem(first - lax.rem(z_start, 128) + 256, 128), 1)
                inside = jnp.where(lane // SUB == step, values, inside)
                below = jnp.where(lane == (first - 1) % 128, values, below)
                above = jnp.where(lane == (first + SUB) % 128, values, above)
            below = jnp.where(z_start == 0, 0.0, pltpu.roll(below, 1, 1))
            above = jnp.where(z_start + SUB == z_cells, 0.0, pltpu.roll(above, 127, 1))
            at = (slice(field * SUB, (field + 1) * SUB), slice(half * 128, (half + 1) * 128))
            centre[at] = inside
            lower[at] = jnp.where(lane % SUB == 0, below, pltpu.roll(inside, 1, 1))
            upper[at] = jnp.where(lane % SUB == SUB - 1, above, pltpu.roll(inside, 127, 1))

    def y_row(y, z):
        total = jnp.zeros((SUB, 128), jnp.float32)
        for field in range(F):
            part = window(field * rows_of_field + y, z)
            part = pltpu.roll(part, lax.rem(field * SUB - lax.rem(z, 128) + 256, 128), 1)
            total = jnp.where(lane // SUB == field, part, total)
        return total

    own_rows[0] = y_row(jnp.maximum(y_start - 1, 0), z_start)
    own_rows[1] = y_row(jnp.minimum(y_start + SUB, y_cells - 1), z_start)

def sample_cube(sample_block, place, brick):
    fields, x_cells, y_cells, z_cells = brick.shape
    vmem = pl.BlockSpec(memory_space=pltpu.VMEM)
    smem = pl.BlockSpec(memory_space=pltpu.SMEM)
    hbm = pl.BlockSpec(memory_space=pltpu.HBM)
    rows = fields * x_cells * y_cells
    cube = jax.ShapeDtypeStruct((F * SUB, 256), jnp.float32)
    return pl.pallas_call(
        functools.partial(sample_kernel, y_cells, z_cells),
        out_shape=(
            cube,
            cube,
            cube,
            jax.ShapeDtypeStruct((2, SUB, 128), jnp.float32),
        ),
        in_specs=[smem, smem, hbm],
        out_specs=(vmem,) * 4,
        scratch_shapes=[
            pltpu.VMEM((2 * rows, 128), jnp.float32),
            pltpu.SemaphoreType.DMA((2,)),
        ],
        compiler_params=pltpu.CompilerParams(vmem_limit_bytes=16 * 1024 * 1024),
        cost_estimate=pl.CostEstimate(flops=0, bytes_accessed=16_000_000, transcendentals=0),
        name="sample_cube",
    )(sample_block, place, brick.reshape(rows, z_cells))


def change_kernel(
    y_cells,
    z_cells,
    sample_block,
    place,
    closure,
    order,
    centre,
    lower,
    upper,
    own_rows,
    thin,
    payload,
    table,
):
    y_start = corner_of(sample_block, place, 0, 0, y_cells, z_cells)[0]
    row = lax.broadcasted_iota(jnp.int32, (SUB, 256), 0)
    lane = lax.broadcasted_iota(jnp.int32, (SUB, 256), 1)
    south_row = jnp.where(y_start == 0, thin[column_of(place, 0, -1), :, 128:], own_rows[0])
    north_row = jnp.where(y_start + SUB == y_cells, thin[column_of(place, 0, 1), :, :128], own_rows[1])
    face_low = thin[column_of(place, -1, 0), 8:, :]
    face_high = thin[column_of(place, 1, 0), :8, :]
    cells = [centre[f * SUB : (f + 1) * SUB, :] for f in range(F)]
    viscosity = viscosity_of(cells, closure)
    changes = []
    for f in range(F):
        value = cells[f]
        west = jnp.where(row == 0, face_low[f : f + 1, :], pltpu.roll(value, 1, 0))
        east = jnp.where(row == SUB - 1, face_high[f : f + 1, :], pltpu.roll(value, SUB - 1, 0))
        edge = pltpu.roll(south_row, (128 - f * SUB) % 128, 1)
        south = jnp.where(lane < SUB, jnp.concatenate([edge, edge], 1), pltpu.roll(value, SUB, 1))
        edge = pltpu.roll(north_row, 112 - f * SUB, 1)
        north = jnp.where(
            lane >= 256 - SUB, jnp.concatenate([edge, edge], 1), pltpu.roll(value, 256 - SUB, 1)
        )
        down = lower[f * SUB : (f + 1) * SUB, :]
        up = upper[f * SUB : (f + 1) * SUB, :]
        laplacian = east + west + north + south + up + down - 6.0 * value
        advection = cells[0] * (east - west) + cells[1] * (north - south) + cells[2] * (up - down)
        change = viscosity * laplacian - 0.5 * advection
        if f == 2:
            change = change + buoyancy * cells[3]
        changes.append(change)
    ordered = dot_rows(jnp.concatenate(cells + changes, axis=0).astype(jnp.bfloat16), order[...])
    low_lanes = lane[:8, :128] < 64
    for part in range(2 * F):
        for cell in range(4):
            columns = slice(cell // 2 * 128, cell // 2 * 128 + 128)
            low = ordered[part * SUB : part * SUB + 8, columns]
            high = ordered[part * SUB + 8 : part * SUB + SUB, columns]
            if cell % 2 == 0:
                high = pltpu.roll(high, 64, 1)
            else:
                low = pltpu.roll(low, 64, 1)
            table[pl.ds(part * 32 + cell, 8, 4), :] = jnp.where(low_lanes, low, high)
    payload[...] = table[...].astype(jnp.bfloat16)


def cube_change(sample_block, place, closure, cube, thin, y_cells, z_cells):
    vmem = pl.BlockSpec(memory_space=pltpu.VMEM)
    smem = pl.BlockSpec(memory_space=pltpu.SMEM)
    return pl.pallas_call(
        functools.partial(change_kernel, y_cells, z_cells),
        out_shape=jax.ShapeDtypeStruct((4 * F * SUB, 128), jnp.bfloat16),
        in_specs=[smem] * 3 + [vmem] * 6,
        out_specs=vmem,
        scratch_shapes=[pltpu.VMEM((4 * F * SUB, 128), jnp.float32)],
        compiler_params=pltpu.CompilerParams(vmem_limit_bytes=16 * 1024 * 1024),
        name="cube_change",
    )(sample_block, place, closure, jnp.asarray(CELL_ORDER, jnp.bfloat16), *cube, thin)


def on_device(
    fields, closure_in, closure_bias, closure_out, master, momentum, sample_block, sample_trainer
):
    group_count = lax.axis_size("grp")
    x_devices = lax.axis_size("gx")
    y_devices = lax.axis_size("gy")
    trainers = x_devices * y_devices
    my_group = lax.axis_index("grp")
    my_column = lax.axis_index("gx") * y_devices + lax.axis_index("gy")
    is_trainer = my_group == group_count - 1
    everyone = ("grp", "gx", "gy")
    sim_groups = group_count - 1
    first_trainer = sim_groups * trainers
    brick = fields[0]
    y_cells, z_cells = brick.shape[2:]
    closure = jnp.concatenate(
        [0.5 * closure_in.T, 0.5 * closure_bias[None], closure_out[None]], axis=0
    )
    linear = jnp.sum(closure * closure_out[None], axis=1, keepdims=True)
    closure = jnp.pad(jnp.concatenate([closure, linear], axis=1), ((0, 1), (0, 127 - HID)))
    place = jnp.stack(
        [
            my_group,
            lax.axis_index("gx"),
            lax.axis_index("gy"),
            jnp.int32(sim_groups),
            jnp.int32(y_devices),
            jnp.int32(x_devices),
        ]
    ).astype(jnp.int32)

    def pairs(x_step, even_step):
        found = []
        for g in range(sim_groups):
            for c in range(trainers):
                gx, gy = c // y_devices, c % y_devices
                gx = (gx + x_step) % x_devices
                gy = (gy + (even_step if gy % 2 == 0 else -even_step)) % y_devices
                found.append((g * trainers + c, (g * x_devices + gx) * y_devices + gy))
        return found

    def x_neighbours(edges):
        if x_devices == 2:
            return lax.ppermute(edges, everyone, pairs(1, 0))
        from_high = lax.ppermute(edges[0], everyone, pairs(-1, 0))
        return jnp.stack([from_high, lax.ppermute(edges[1], everyone, pairs(1, 0))])

    def y_neighbours(for_first, for_second):
        return (
            lax.ppermute(for_first, everyone, pairs(0, 1)),
            lax.ppermute(for_second, everyone, pairs(0, -1)),
        )

    def swap(distance):
        return [(first_trainer + c, first_trainer + (c ^ distance)) for c in range(trainers)]

    def to_trainers(payload):
        landed = [
            lax.ppermute(
                payload, everyone, [(g * trainers + c, first_trainer + c) for c in range(trainers)]
            )
            for g in reversed(range(sim_groups))
        ]
        return jnp.stack(landed)

    def from_line(held):
        return [lax.ppermute(held, everyone, swap(apart)) for apart in range(1, y_devices)]

    def across(apart, held):
        return lax.ppermute(held, everyone, swap(apart * y_devices))

    thin = thin_faces(sample_block, place, brick, trainers)
    cube = sample_cube(sample_block, place, brick)
    first_count = CH * TAPS * F
    first = jnp.pad(master[:first_count].reshape(CH, TAPS * F), ((0, 0), (0, 256 - TAPS * F)))
    last = jnp.pad(master[first_count:].reshape(TAPS * F, CH), ((0, 256 - TAPS * F), (0, 0)))

    *cube, first, last = lax.optimization_barrier((*cube, first, last))
    selects = lax.optimization_barrier(
        (jnp.asarray(SELECT_FIRST, jnp.bfloat16), jnp.asarray(SELECT_LAST, jnp.bfloat16))
    )

    thin = lax.all_to_all(thin, ("gx", "gy"), split_axis=0, concat_axis=0, tiled=True)
    payload = cube_change(sample_block, place, closure, cube, thin, y_cells, z_cells)
    landed = to_trainers(payload)
    closure, landed = lax.optimization_barrier((closure, landed))

    fields_count, x_cells = brick.shape[:2]
    viscosity, x_edges, y_edges = lax.cond(
        is_trainer,
        lambda: (
            jnp.zeros((x_cells, y_cells, z_cells), jnp.float32),
            jnp.zeros((2, fields_count, y_cells, z_cells), jnp.float32),
            jnp.zeros((2, fields_count, x_cells, z_cells), jnp.float32),
        ),
        lambda: brick_viscosity(closure, place, brick),
    )
    halo = (x_neighbours(x_edges), *y_neighbours(y_edges[0], y_edges[1]))
    near = [landed, *from_line(landed)]
    far = [
        across(apart, pick_cubes(sample_trainer, place, near, y_devices, x_devices, apart))
        for apart in range(1, x_devices)
    ]
    arrived = [*near, *far]

    def train_here():
        delta_first, delta_last, new_brick = train_cubes(
            sample_trainer, place, first, last, selects, arrived, brick, y_devices, x_devices
        )
        delta = jnp.concatenate(
            [delta_first[:, : TAPS * F].reshape(-1), delta_last[: TAPS * F].reshape(-1)]
        )
        return delta, new_brick

    def evolve_here():
        new_brick = evolve(place, viscosity, brick, *halo)
        return jnp.zeros((NPARAM,), jnp.float32), new_brick

    delta, new_brick = lax.cond(is_trainer, train_here, evolve_here)

    held = delta
    for g in reversed(range(sim_groups)):
        held = held + lax.ppermute(
            delta, everyone, [(first_trainer + c, g * trainers + c) for c in range(trainers)]
        )
    final = delta
    for first_apart in range(1, trainers, group_count):
        meets = [
            (g * trainers + c, g * trainers + (c ^ (first_apart + g)))
            for g in range(group_count)
            for c in range(trainers)
            if first_apart + g < trainers
        ]
        final = final + lax.ppermute(held, everyone, meets)
    for apart in (1, 2):
        final = final + lax.ppermute(
            final,
            everyone,
            [(g * trainers + c, (g ^ apart) * trainers + c) for g in range(group_count) for c in range(trainers)],
        )

    share_size = NPARAM // (group_count * trainers)
    share_start = (my_group * trainers + my_column) * share_size
    momentum_share = lax.dynamic_slice_in_dim(momentum, share_start, share_size)
    master_share = lax.dynamic_slice_in_dim(master, share_start, share_size)
    inverse = 1.0 / jnp.sqrt(jnp.sum(final * final) / NPARAM + norm_epsilon)
    delta_share = lax.dynamic_slice_in_dim(final, share_start, share_size)
    new_momentum = momentum_decay * momentum_share + delta_share * inverse
    new_master = master_share - outer_rate * new_momentum
    return (new_brick[None], new_master, new_momentum)


def solution(mesh):
    in_specs = (P("grp", None, "gx", "gy", None), P(), P(), P(), P(), P(), P(), P())
    out_specs = (P("grp", None, "gx", "gy", None), P(("grp", "gx", "gy")), P(("grp", "gx", "gy")))
    return jax.shard_map(
        on_device, mesh=mesh, in_specs=in_specs, out_specs=out_specs, check_vma=False
    )
```

```python
import functools

import jax
import jax.numpy as jnp
import numpy as np
from jax import lax
from jax.experimental import pallas as pl
from jax.experimental.pallas import tpu as pltpu
from jax.sharding import PartitionSpec as P

F = 5
CH = 64
HID = 64
SUB = 16
TCAP = 6
INNER = 3
CELLS = 4096
NPARAM = 17280
TAPS = 27
PAIRS = TCAP // 2
COLS = (SUB + 2) * 128
PATCH = 16 * F
STACK = 3 * PATCH

time_step = 0.1
base_viscosity = 0.02
viscosity_gain = 0.2
buoyancy = 0.5
inner_rate = 0.02
outer_rate = 0.01
momentum_decay = 0.9
norm_epsilon = 1e-06


def patch_position(row):
    group, py, pz = row // 4, row // 2 % 2, row % 2
    ypos = py + 1 if group in (0, 2) else (3 if py == 0 else 0)
    zpos = pz + 1 if group in (0, 1) else (3 if pz == 0 else 0)
    return ypos - 1, zpos - 1


def selections():
    found = np.zeros((4, 256, STACK), np.float32)
    for cell in range(4):
        py, pz = cell // 2, cell % 2
        for kx in range(3):
            for channel in range(F):
                for row in range(16):
                    ypos, zpos = patch_position(row)
                    dy, dz = ypos - py, zpos - pz
                    if abs(dy) <= 1 and abs(dz) <= 1:
                        tap = 9 * kx + 3 * (dy + 1) + dz + 1
                        found[cell, tap * F + channel, kx * PATCH + channel * 16 + row] = 1.0
    return found


def last_order():
    order = np.zeros((256, 256), np.float32)
    for channel in range(F):
        for tap in range(TAPS):
            order[channel * TAPS + tap, (TAPS - 1 - tap) * F + channel] = 1.0
    return order


SELECT, LAST_ORDER = selections(), last_order()


def column_of(place, x_step, y_step):
    gx = lax.rem(place[1] + x_step + place[5], place[5])
    gy = lax.rem(place[2] + y_step + place[4], place[4])
    return gx * place[4] + gy


def owner_apart(owner, groups, place, y_devices, x_devices):
    group, column = divmod(owner, x_devices * y_devices)
    entry = groups - 1 - group
    y_apart = jnp.bitwise_xor(place[2], jnp.int32(column % y_devices))
    return entry, y_apart, jnp.bitwise_xor(place[1], jnp.int32(column // y_devices))


def pick_kernel(y_devices, x_devices, apart, trainer_of, place, *refs):
    near, chosen, owners = refs[:y_devices], refs[y_devices], refs[y_devices + 1]
    wanted = jnp.bitwise_xor(place[1], jnp.int32(apart)) * y_devices + place[2]
    count = jnp.int32(0)
    groups = trainer_of.shape[0] // (x_devices * y_devices)
    for owner in range(trainer_of.shape[0]):
        group, y_apart, x_apart = owner_apart(owner, groups, place, y_devices, x_devices)
        mine = (trainer_of[owner] == wanted) & (x_apart == 0)

        @pl.when(mine)
        def _():
            owners[0, count] = y_apart
            owners[1, count] = group

        count = count + jnp.where(mine, 1, 0)

    def copy_slot(slot, carry):
        for source in range(y_devices):

            @pl.when(owners[0, slot] == source)
            def _():
                chosen[slot] = near[source][owners[1, slot]]

        return carry

    lax.fori_loop(0, count, copy_slot, 0)


def pick_cubes(trainer_of, place, near, y_devices, x_devices, apart):
    vmem = pl.BlockSpec(memory_space=pltpu.VMEM)
    smem = pl.BlockSpec(memory_space=pltpu.SMEM)
    return pl.pallas_call(
        functools.partial(pick_kernel, y_devices, x_devices, apart),
        out_shape=jax.ShapeDtypeStruct((TCAP, *near[0].shape[1:]), near[0].dtype),
        in_specs=[smem, smem] + [vmem] * len(near),
        out_specs=vmem,
        scratch_shapes=[pltpu.SMEM((2, TCAP), jnp.int32)],
        compiler_params=pltpu.CompilerParams(vmem_limit_bytes=16 * 1024 * 1024),
        name="pick_cubes",
    )(trainer_of, place, *near)


def dot_rows(left, right):
    return jnp.dot(left, right, preferred_element_type=jnp.float32)


def dot_lanes(left, right):
    return lax.dot_general(left, right, (((1,), (1,)), ((), ())), preferred_element_type=jnp.float32)


def exact_parts(values):
    parts = []
    for _ in range(3):
        parts.append(values.astype(jnp.bfloat16))
        values = values - parts[-1].astype(jnp.float32)
    return jnp.concatenate(parts, axis=0)


def patch_masks():
    row = lax.broadcasted_iota(jnp.int32, (8, 128), 0)
    lane = lax.broadcasted_iota(jnp.int32, (8, 128), 1)
    z, y = lane % 8, lane // 8 % 8
    even_z, even_y = row % 2 == 0, row // 2 % 2 == 0
    return {
        "centre": row < 4,
        "even_z": even_z,
        "even_y": even_y,
        "gather_z": jnp.where(even_z, z, 7 - z) < 7,
        "gather_y": jnp.where(even_y, y, 7 - y) < 7,
        "scatter_z": jnp.where(even_z, z, 7 - z) > 0,
        "scatter_y": jnp.where(even_y, y, 7 - y) > 0,
    }


def edge_shift(values, step, even, inside, gather):
    before, after = pltpu.roll(values, step, 1), pltpu.roll(values, 128 - step, 1)
    moved = jnp.where(even, after, before) if gather else jnp.where(even, before, after)
    return jnp.where(inside, moved, 0.0)


def patch_stack(rows, masks):
    both = jnp.where(masks["centre"], rows, pltpu.roll(rows, 4, 0))
    y_edge = edge_shift(both, 8, masks["even_y"], masks["gather_y"], True)
    upper = jnp.where(masks["centre"], both, y_edge)
    return upper, edge_shift(upper, 1, masks["even_z"], masks["gather_z"], True)


def patch_fold(upper, lower, masks):
    line = upper + edge_shift(lower, 1, masks["even_z"], masks["scatter_z"], False)
    return line + pltpu.roll(edge_shift(line, 8, masks["even_y"], masks["scatter_y"], False), 4, 0)


def store_planes(ref, x, channels):
    stacked = jnp.concatenate([part for both in channels for part in both], axis=0).astype(jnp.bfloat16)
    for kx in range(3):
        start = pl.multiple_of((x + 2 - kx) * 128, 128)
        ref[kx * PATCH : (kx + 1) * PATCH, pl.ds(start, 128)] = stacked


def train_kernel(y_devices, x_devices, *refs):
    sources = y_devices + x_devices - 1
    (trainer_of, place, first_ref, last_ref, far_select, far_order) = refs[:6]
    arrived = refs[6 : 6 + sources]
    fields_ref = refs[6 + sources]
    delta_first, delta_last, new_fields_ref = refs[7 + sources : 10 + sources]
    (
        slots,
        picked,
        cubes,
        big_first,
        big_last,
        big_last_t,
        grad_first,
        grad_last,
        now,
        brick,
        select,
        order,
        slot_sems,
        field_sem,
        select_sems,
        *pair_refs,
    ) = refs[10 + sources :]
    targets, tables, inputs, errors, hiddens, pre_grads, slopes, partial_out, raw = [
        pair_refs[kind * PAIRS : (kind + 1) * PAIRS] for kind in range(9)
    ]

    field_in = pltpu.make_async_copy(fields_ref, brick, field_sem)
    field_out = pltpu.make_async_copy(brick, new_fields_ref, field_sem)
    select_copies = [
        pltpu.make_async_copy(far_select, select, select_sems.at[0]),
        pltpu.make_async_copy(far_order, order, select_sems.at[1]),
    ]

    column = place[1] * y_devices + place[2]
    for other in range(x_devices):
        picked[other] = 0
    count = jnp.int32(0)
    groups = trainer_of.shape[0] // (x_devices * y_devices)
    for owner in range(trainer_of.shape[0]):
        group, y_apart, x_apart = owner_apart(owner, groups, place, y_devices, x_devices)
        mine = trainer_of[owner] == column

        @pl.when(mine)
        def _():
            near = x_apart == 0
            slots[0, count] = jnp.where(near, y_apart, y_devices - 1 + x_apart)
            slots[1, count] = jnp.where(near, group, picked[x_apart])
            picked[x_apart] = picked[x_apart] + 1

        count = count + jnp.where(mine, 1, 0)

    def fetch(slot, wait):
        for source in range(sources):

            @pl.when((slot < count) & (slots[0, slot] == source))
            def _():
                copy = pltpu.make_async_copy(
                    arrived[source].at[slots[1, slot]], cubes.at[slot], slot_sems.at[slot]
                )
                copy.wait() if wait else copy.start()

    for slot in range(TCAP):
        fetch(slot, False)

    for copy in select_copies:
        copy.start()
    field_in.start()
    for slot in range(TCAP):

        @pl.when(slot >= count)
        def _():
            cubes[slot] = jnp.zeros(cubes.shape[1:], jnp.bfloat16)

    masks = patch_masks()
    for ref in (*errors, *inputs):
        ref[:PATCH, 128:256] = jnp.zeros((PATCH, 128), jnp.bfloat16)
        ref[2 * PATCH :, COLS - 256 : COLS - 128] = jnp.zeros((PATCH, 128), jnp.bfloat16)
    for ref in partial_out:
        ref[:, :128] = jnp.zeros((STACK, 128), jnp.float32)
        ref[:, COLS - 128 :] = jnp.zeros((STACK, 128), jnp.float32)
    lane = lax.broadcasted_iota(jnp.int32, (8, 128), 1)
    full_weight = 2.0 * (1.0 / (jnp.full((8, 128), count, jnp.int32).astype(jnp.float32) * CELLS))
    weights = [
        jnp.where(lane // 64 + 2 * pair < count, full_weight, 0.0) for pair in range(PAIRS)
    ]
    for slot in range(TCAP):
        fetch(slot, True)

    low_lanes = lax.broadcasted_iota(jnp.int32, (SUB * F * 2, 128), 1) < 64
    for pair in range(PAIRS):
        for kind, ref in enumerate((tables[pair], targets[pair])):
            rows = slice(kind * SUB * F * 2, (kind + 1) * SUB * F * 2)
            even = cubes[2 * pair, rows, :].astype(jnp.float32)
            odd = cubes[2 * pair + 1, rows, :].astype(jnp.float32)
            ref[0] = jnp.where(low_lanes, even, pltpu.roll(odd, 64, 1))
            ref[1] = jnp.where(low_lanes, pltpu.roll(even, 64, 1), odd)

    def patch_cells(ref, quarter, plane, channel):
        start = pl.multiple_of(channel * 32 + quarter % 2 * 16 + plane // 2 * 8, 8)
        rows = ref[quarter // 2, pl.ds(start, 8), :]
        return rows if plane % 2 == 0 else pltpu.roll(rows, 4, 0)

    def stack_planes(quarter, carry):
        for pair in range(PAIRS):
            for plane in range(4):
                x = quarter * 4 + plane
                channels = [
                    patch_stack(patch_cells(tables[pair], quarter, plane, c), masks) for c in range(F)
                ]
                store_planes(inputs[pair], x, channels)
        return carry

    lax.fori_loop(0, 4, stack_planes, 0, unroll=2)

    for copy in select_copies:
        copy.wait()
    start_first = first_ref[...].astype(jnp.bfloat16).astype(jnp.float32)
    start_last = dot_rows(last_ref[...].T.astype(jnp.bfloat16), order[...])
    now[:CH] = start_first
    now[CH:] = start_last
    field_in.wait()
    field_out.start()

    def train_step(step, step_carry):
        rounded = now[...].astype(jnp.bfloat16)
        for cell in range(4):
            rows = slice(cell * CH, (cell + 1) * CH)
            spread = dot_rows(rounded, select[cell])
            big_first[rows, :] = (0.5 * spread[:CH]).astype(jnp.bfloat16)
            big_last[rows, :] = (0.5 * spread[CH:]).astype(jnp.bfloat16)
            big_last_t[:, rows] = spread[CH:].T.astype(jnp.bfloat16)
        grad_first[...] = jnp.zeros(grad_first.shape, jnp.float32)
        grad_last[...] = jnp.zeros(grad_last.shape, jnp.float32)

        def columns_of(quarter):
            return pl.ds(pl.multiple_of(quarter * 512 + 128, 128), 512)

        def first_layer(pair, quarter):
            columns = columns_of(quarter)
            raw[pair][:, columns] = dot_rows(big_first[...], inputs[pair][:, columns])

        def activate(pair, quarter):
            columns = columns_of(quarter)
            for part in range(8):
                rows = slice(part * 32, (part + 1) * 32)
                half = raw[pair][rows, columns]
                curve = jnp.tanh(half)
                above = 1.0 + curve
                value = half * above
                hiddens[pair][rows, columns] = value.astype(jnp.bfloat16)
                slopes[pair][rows, columns] = above + value * (1.0 - curve)

        def last_layer(pair, quarter):
            columns = columns_of(quarter)
            partial_out[pair][:, columns] = dot_rows(big_last_t[...], hiddens[pair][:, columns])

        def find_errors(pair, quarter):
            for plane in range(4):
                x = quarter * 4 + plane
                column = pl.multiple_of((x + 1) * 128, 128)
                total = (
                    partial_out[pair][0:PATCH, pl.ds(pl.multiple_of(column + 128, 128), 128)]
                    + partial_out[pair][PATCH : 2 * PATCH, pl.ds(column, 128)]
                    + partial_out[pair][2 * PATCH :, pl.ds(pl.multiple_of(column - 128, 128), 128)]
                )
                channels = []
                for c in range(F):
                    predicted = patch_fold(
                        total[16 * c : 16 * c + 8], total[16 * c + 8 : 16 * c + 16], masks
                    )
                    wanted = patch_cells(targets[pair], quarter, plane, c)
                    error = weights[pair] * (predicted - wanted)
                    channels.append(patch_stack(error, masks))
                store_planes(errors[pair], x, channels)

        def hidden_layer(pair, quarter):
            columns = columns_of(quarter)
            raw[pair][:, columns] = dot_rows(big_last[...], errors[pair][:, columns])

        def scale(pair, quarter):
            columns = columns_of(quarter)
            for part in range(8):
                rows = slice(part * 32, (part + 1) * 32)
                product = raw[pair][rows, columns] * slopes[pair][rows, columns]
                pre_grads[pair][rows, columns] = product.astype(jnp.bfloat16)

        def gradients(pair, quarter):
            columns = columns_of(quarter)
            grad_first[...] += dot_lanes(pre_grads[pair][:, columns], inputs[pair][:, columns])
            grad_last[...] += dot_lanes(hiddens[pair][:, columns], errors[pair][:, columns])

        stages = (first_layer, activate, last_layer, find_errors, hidden_layer, scale, gradients)
        for turn in range(len(stages) + PAIRS - 1):

            def run(quarter, carry):
                for pair in range(PAIRS):
                    if 0 <= turn - pair < len(stages):
                        stages[turn - pair](pair, quarter)
                return carry

            lax.fori_loop(0, 4, run, 0, unroll=4)

        total = jnp.zeros((6 * CH, 256), jnp.float32)
        for cell in range(4):
            rows = slice(cell * CH, (cell + 1) * CH)
            parts = exact_parts(jnp.concatenate([grad_first[rows, :], grad_last[rows, :]], axis=0))
            total = total + dot_lanes(parts, select[cell])
        both = 2 * CH
        now[...] = now[...] - inner_rate * (total[:both] + total[both : 2 * both] + total[2 * both :])
        return step_carry

    lax.fori_loop(0, INNER, train_step, 0)
    delta_first[...] = start_first - now[:CH]
    ordered = dot_lanes(exact_parts(start_last - now[CH:]), order[...])
    delta_last[...] = (ordered[:CH] + ordered[CH : 2 * CH] + ordered[2 * CH :]).T
    field_out.wait()


def train_cubes(trainer_of, place, first, last, selects, arrived, fields, y_devices, x_devices):
    vmem = pl.BlockSpec(memory_space=pltpu.VMEM)
    smem = pl.BlockSpec(memory_space=pltpu.SMEM)
    anywhere = pl.BlockSpec(memory_space=pl.ANY)
    hbm = pl.BlockSpec(memory_space=pltpu.HBM)
    return pl.pallas_call(
        functools.partial(train_kernel, y_devices, x_devices),
        out_shape=(
            jax.ShapeDtypeStruct((CH, 256), jnp.float32),
            jax.ShapeDtypeStruct((256, CH), jnp.float32),
            jax.ShapeDtypeStruct(fields.shape, fields.dtype),
        ),
        in_specs=[smem] * 2 + [vmem] * 2 + [hbm] * 2 + [anywhere] * len(arrived) + [hbm],
        out_specs=(vmem, vmem, hbm),
        scratch_shapes=[
            pltpu.SMEM((2, TCAP), jnp.int32),
            pltpu.SMEM((x_devices,), jnp.int32),
            pltpu.VMEM((TCAP, 4 * SUB * F, 128), jnp.bfloat16),
            pltpu.VMEM((4 * CH, STACK), jnp.bfloat16),
            pltpu.VMEM((4 * CH, STACK), jnp.bfloat16),
            pltpu.VMEM((STACK, 4 * CH), jnp.bfloat16),
            pltpu.VMEM((4 * CH, STACK), jnp.float32),
            pltpu.VMEM((4 * CH, STACK), jnp.float32),
            pltpu.VMEM((2 * CH, 256), jnp.float32),
            pltpu.VMEM(fields.shape, fields.dtype),
            pltpu.VMEM((4, 256, STACK), jnp.bfloat16),
            pltpu.VMEM((256, 256), jnp.bfloat16),
            pltpu.SemaphoreType.DMA((TCAP,)),
            pltpu.SemaphoreType.DMA,
            pltpu.SemaphoreType.DMA((2,)),
        ]
        + [pltpu.VMEM((2, SUB * F * 2, 128), jnp.float32)] * (2 * PAIRS)
        + [pltpu.VMEM((STACK, COLS), jnp.bfloat16)] * (2 * PAIRS)
        + [pltpu.VMEM((4 * CH, COLS), jnp.bfloat16)] * (2 * PAIRS)
        + [pltpu.VMEM((4 * CH, COLS), jnp.float32)] * PAIRS
        + [pltpu.VMEM((STACK, COLS), jnp.float32)] * PAIRS
        + [pltpu.VMEM((4 * CH, COLS), jnp.float32)] * PAIRS,
        compiler_params=pltpu.CompilerParams(vmem_limit_bytes=52 * 1024 * 1024),
        name="train_cubes",
    )(
        trainer_of,
        place,
        first,
        last,
        *selects,
        *arrived,
        fields,
    )


def viscosity_of(cells, closure):
    def unit(h, total):
        half = closure[F, h] + closure[0, h] * cells[0]
        for f in range(1, F):
            half = half + closure[f, h] * cells[f]
        return total + closure[F + 1, h] * (half * jnp.tanh(half))

    total = closure[F, HID] + closure[0, HID] * cells[0]
    for f in range(1, F):
        total = total + closure[f, HID] * cells[f]
    total = lax.fori_loop(0, HID, unit, total, unroll=8)
    soft = jnp.maximum(total, 0.0) + jnp.log1p(jnp.exp(-jnp.abs(total)))
    return base_viscosity + viscosity_gain * soft


def viscosity_kernel(closure, place, fields, viscosity, x_edges, y_edges, weights, out_column):
    y_cells, z_cells = fields.shape[2:]
    x, x_cells = pl.program_id(0), pl.num_programs(0)
    up_first = lax.rem(place[2], 2) == 0
    for f in range(F):
        low, high = fields[f, 0, 0:1, :], fields[f, 0, y_cells - 1 : y_cells, :]
        y_edges[0, f, pl.ds(x, 1), :] = jnp.where(up_first, high, low)
        y_edges[1, f, pl.ds(x, 1), :] = jnp.where(up_first, low, high)

    @pl.when(x == x_cells - 1)
    def _():
        x_edges[1] = fields[:, 0]

    @pl.when(x == 0)
    def _():
        x_edges[0] = fields[:, 0]
        plain = closure[...]
        high = plain.astype(jnp.bfloat16).astype(jnp.float32)
        low = plain - high
        blank = jnp.zeros((8, 128), jnp.float32)
        for j in range(8):
            turned = [pltpu.roll(part, j, 0) if j else part for part in (high, high, low)]
            stacked = jnp.concatenate([*turned, blank], axis=0)
            weights[j] = stacked.T[: HID + 8].astype(jnp.bfloat16)
        out_column[...] = jnp.broadcast_to(plain.T[:HID, F + 1 : F + 2], (HID, 128))

    sublane = lax.broadcasted_iota(jnp.int32, (8, z_cells), 0)
    wide = z_cells // 128
    tiles = y_cells // 8

    def tile(index, carry):
        rows = pl.ds(pl.multiple_of(index * 8, 8), 8)
        turned = [fields[f, 0, rows, :] for f in range(F)]
        turned = [pltpu.roll(turned[f], f, 0) if f else turned[f] for f in range(F)]
        sums = jnp.zeros((8, z_cells), jnp.float32)
        for j in range(8):
            cells = jnp.where(sublane == (j + F) % 8, 1.0, 0.0)
            for f in range(F):
                cells = jnp.where(sublane == (j + f) % 8, turned[f], cells)
            top = cells.astype(jnp.bfloat16).astype(jnp.float32)
            stacked = jnp.concatenate([top, cells - top, top, jnp.zeros_like(top)], axis=0)
            half = dot_rows(weights[j], stacked.astype(jnp.bfloat16))
            total = half[HID:]
            for group in range(HID // 8):
                part = half[group * 8 : group * 8 + 8]
                column = jnp.concatenate([out_column[group * 8 : group * 8 + 8, :]] * wide, axis=1)
                total = total + column * (part * jnp.tanh(part))
            for step in (4, 2, 1):
                total = total + pltpu.roll(total, step, 0)
            sums = jnp.where(sublane == j, total, sums)
        soft = jnp.maximum(sums, 0.0) + jnp.log1p(jnp.exp(-jnp.abs(sums)))
        viscosity[0, rows, :] = base_viscosity + viscosity_gain * soft
        return carry

    lax.fori_loop(0, tiles, tile, 0)


def brick_viscosity(closure, place, fields):
    count, x_cells, y_cells, z_cells = fields.shape
    return pl.pallas_call(
        viscosity_kernel,
        out_shape=(
            jax.ShapeDtypeStruct(fields.shape[1:], fields.dtype),
            jax.ShapeDtypeStruct((2, count, y_cells, z_cells), fields.dtype),
            jax.ShapeDtypeStruct((2, count, x_cells, z_cells), fields.dtype),
        ),
        grid=(x_cells,),
        in_specs=[
            pl.BlockSpec((8, 128), lambda x: (0, 0)),
            pl.BlockSpec(memory_space=pltpu.SMEM),
            pl.BlockSpec((count, 1, y_cells, z_cells), lambda x: (0, x, 0, 0)),
        ],
        out_specs=(
            pl.BlockSpec((1, y_cells, z_cells), lambda x: (x, 0, 0)),
            pl.BlockSpec((2, count, y_cells, z_cells), lambda x: (0, 0, 0, 0)),
            pl.BlockSpec((2, count, x_cells, z_cells), lambda x: (0, 0, 0, 0)),
        ),
        scratch_shapes=[
            pltpu.VMEM((8, HID + 8, 32), jnp.bfloat16),
            pltpu.VMEM((HID, 128), jnp.float32),
        ],
        compiler_params=pltpu.CompilerParams(vmem_limit_bytes=16 * 1024 * 1024),
        name="brick_viscosity",
    )(closure, place, fields)


def evolve_kernel(place, viscosity, fields, x_halo, y_first, y_second, new_fields):
    up_first = lax.rem(place[2], 2) == 0
    x_cells, y_cells, z_cells = fields.shape[1:]
    row = lax.broadcasted_iota(jnp.int32, (y_cells, z_cells), 0)
    lane = lax.broadcasted_iota(jnp.int32, (y_cells, z_cells), 1)

    def plane(x, carry):
        centre = [fields[f, x] for f in range(F)]
        below = jnp.maximum(x - 1, 0)
        above = jnp.minimum(x + 1, x_cells - 1)
        for f in range(F):
            value = centre[f]
            west = jnp.where(x == 0, x_halo[1, f], fields[f, below])
            east = jnp.where(x == x_cells - 1, x_halo[0, f], fields[f, above])
            first, second = y_first[f, pl.ds(x, 1), :], y_second[f, pl.ds(x, 1), :]
            south = jnp.where(
                row == 0, jnp.where(up_first, second, first), pltpu.roll(value, 1, 0)
            )
            north = jnp.where(
                row == y_cells - 1,
                jnp.where(up_first, first, second),
                pltpu.roll(value, y_cells - 1, 0),
            )
            lower = jnp.where(lane == 0, 0.0, pltpu.roll(value, 1, 1))
            upper = jnp.where(lane == z_cells - 1, 0.0, pltpu.roll(value, z_cells - 1, 1))
            laplacian = east + west + north + south + upper + lower - 6.0 * value
            advection = (
                centre[0] * (east - west) + centre[1] * (north - south) + centre[2] * (upper - lower)
            )
            tendency = viscosity[x] * laplacian - 0.5 * advection
            if f == 2:
                tendency = tendency + buoyancy * centre[3]
            new_fields[f, x] = value + time_step * tendency
        return carry

    lax.fori_loop(0, x_cells, plane, 0)


def evolve(place, viscosity, fields, x_halo, y_first, y_second):
    vmem = pl.BlockSpec(memory_space=pltpu.VMEM)
    return pl.pallas_call(
        evolve_kernel,
        out_shape=jax.ShapeDtypeStruct(fields.shape, fields.dtype),
        in_specs=[pl.BlockSpec(memory_space=pltpu.SMEM)] + [vmem] * 5,
        out_specs=vmem,
        compiler_params=pltpu.CompilerParams(vmem_limit_bytes=16 * 1024 * 1024),
        name="evolve_brick",
    )(place, viscosity, fields, x_halo, y_first, y_second)


def cell_order():
    order = np.zeros((256, 256), np.float32)
    for y in range(SUB):
        for z in range(SUB):
            order[y * SUB + z, (y % 2 * 2 + z % 2) * 64 + y // 2 * 8 + z // 2] = 1.0
    return order


CELL_ORDER = cell_order()


def corner_of(sample_block, place, x_step, y_step, y_cells, z_cells):
    x_devices, y_devices = place[5], place[4]
    gx = lax.rem(place[1] + x_step + x_devices, x_devices)
    gy = lax.rem(place[2] + y_step + y_devices, y_devices)
    group = jnp.minimum(place[0], place[3] - 1)
    block = sample_block[(group * x_devices + gx) * y_devices + gy]
    z_blocks = z_cells // SUB
    return lax.rem(lax.div(block, z_blocks), y_cells // SUB) * SUB, lax.rem(block, z_blocks) * SUB


def thin_kernel(
    y_cells, z_cells, sample_block, place, rows_ref, lines_ref, thin, x_buffer, y_buffer, x_sems, y_sems
):
    def corner(x_step, y_step):
        return corner_of(sample_block, place, x_step, y_step, y_cells, z_cells)

    lane = lax.broadcasted_iota(jnp.int32, (SUB, 128), 1)
    signs = (-1, 1)
    copies = []
    for side, sign in enumerate(signs):
        z_x, z_y = corner(sign, 0)[1], corner(0, sign)[1]
        x, y = side * (SUB - 1), side * (y_cells - 8)
        for field in range(F):
            copies.append(
                pltpu.make_async_copy(
                    rows_ref.at[
                        pl.ds((field * SUB + x) * y_cells, y_cells),
                        pl.ds(pl.multiple_of(lax.div(z_x, 128) * 128, 128), 128),
                    ],
                    x_buffer.at[pl.ds((side * 8 + field) * y_cells, y_cells)],
                    x_sems.at[side, field],
                )
            )
        copies.append(
            pltpu.make_async_copy(
                lines_ref.at[:, pl.ds(y, 8), pl.ds(pl.multiple_of(lax.div(z_y, 128) * 128, 128), 128)],
                y_buffer.at[side],
                y_sems.at[side],
            )
        )
    for copy in copies:
        copy.start()
    thin[...] = jnp.zeros(thin.shape, thin.dtype)
    for copy in copies:
        copy.wait()

    def moved(values, z, lane_start):
        return pltpu.roll(values, lax.rem(lane_start - lax.rem(z, 128) + 256, 128), 1)

    for side, sign in enumerate(signs):
        z = corner(0, sign)[1]
        total = jnp.zeros((SUB, 128), jnp.float32)
        for field in range(F):
            part = y_buffer[side, field * SUB : (field + 1) * SUB, side * 7, :]
            total = jnp.where(lane // SUB == field, moved(part, z, field * SUB), total)
        thin[column_of(place, 0, sign), :, side * 128 : (side + 1) * 128] = total
    for side, sign in enumerate(signs):
        y, z = corner(sign, 0)
        for half in range(2):
            total = jnp.zeros((8, 128), jnp.float32)
            for step in range(8):
                row = side * 8 * y_cells + y + half * 8 + step
                part = moved(x_buffer[pl.ds(row, 8, y_cells), :], z, step * SUB)
                total = jnp.where(lane[:8] // SUB == step, part, total)
            at = (column_of(place, sign, 0), slice(side * 8, side * 8 + 8), slice(half * 128, half * 128 + 128))
            thin[at] = total


def thin_faces(sample_block, place, brick, columns):
    fields, x_cells, y_cells, z_cells = brick.shape
    vmem = pl.BlockSpec(memory_space=pltpu.VMEM)
    smem = pl.BlockSpec(memory_space=pltpu.SMEM)
    hbm = pl.BlockSpec(memory_space=pltpu.HBM)
    return pl.pallas_call(
        functools.partial(thin_kernel, y_cells, z_cells),
        out_shape=jax.ShapeDtypeStruct((columns, SUB, 256), jnp.float32),
        in_specs=[smem, smem, hbm, hbm],
        out_specs=vmem,
        scratch_shapes=[
            pltpu.VMEM((16 * y_cells, 128), jnp.float32),
            pltpu.VMEM((2, fields * x_cells, 8, 128), jnp.float32),
            pltpu.SemaphoreType.DMA((2, fields)),
            pltpu.SemaphoreType.DMA((2,)),
        ],
        compiler_params=pltpu.CompilerParams(vmem_limit_bytes=16 * 1024 * 1024),
        name="thin_faces",
    )(
        sample_block,
        place,
        brick.reshape(fields * x_cells * y_cells, z_cells),
        brick.reshape(fields * x_cells, y_cells, z_cells),
    )


def sample_kernel(
    y_cells,
    z_cells,
    sample_block,
    place,
    brick,
    centre,
    lower,
    upper,
    own_rows,
    windows,
    sems,
):
    rows_of_x = y_cells
    rows_of_field = SUB * y_cells
    window_rows = F * rows_of_field

    def corner(x_step, y_step):
        return corner_of(sample_block, place, x_step, y_step, y_cells, z_cells)

    y_start, z_start = corner(0, 0)
    z_below = jnp.maximum(z_start - 1, 0)
    z_above = jnp.minimum(z_start + SUB, z_cells - 1)
    first_window = lax.div(z_below, 128)
    second_window = jnp.minimum(first_window + 1, z_cells // 128 - 1)
    copies = [
        pltpu.make_async_copy(
            brick.at[:, pl.ds(pl.multiple_of(at * 128, 128), 128)],
            windows.at[pl.ds(slot * window_rows, window_rows)],
            sems.at[slot],
        )
        for slot, at in enumerate((first_window, second_window))
    ]
    for copy in copies:
        copy.start()
    for copy in copies:
        copy.wait()

    def window(row, z):
        slot = lax.div(z, 128) - first_window
        return windows[pl.ds(slot * window_rows + row, SUB, rows_of_x), :]

    lane = lax.broadcasted_iota(jnp.int32, (SUB, 128), 1)
    for field in range(F):
        for half in range(2):
            inside = jnp.zeros((SUB, 128), jnp.float32)
            below = jnp.zeros((SUB, 128), jnp.float32)
            above = jnp.zeros((SUB, 128), jnp.float32)
            for step in range(8):
                row = field * rows_of_field + y_start + half * 8 + step
                first = step * SUB
                values = jnp.where(lane == 127, window(row, z_below), window(row, z_start))
                values = jnp.where(lane == 0, window(row, z_above), values)
                values = pltpu.roll(values, lax.rem(first - lax.rem(z_start, 128) + 256, 128), 1)
                inside = jnp.where(lane // SUB == step, values, inside)
                below = jnp.where(lane == (first - 1) % 128, values, below)
                above = jnp.where(lane == (first + SUB) % 128, values, above)
            below = jnp.where(z_start == 0, 0.0, pltpu.roll(below, 1, 1))
            above = jnp.where(z_start + SUB == z_cells, 0.0, pltpu.roll(above, 127, 1))
            at = (slice(field * SUB, (field + 1) * SUB), slice(half * 128, (half + 1) * 128))
            centre[at] = inside
            lower[at] = jnp.where(lane % SUB == 0, below, pltpu.roll(inside, 1, 1))
            upper[at] = jnp.where(lane % SUB == SUB - 1, above, pltpu.roll(inside, 127, 1))

    def y_row(y, z):
        total = jnp.zeros((SUB, 128), jnp.float32)
        for field in range(F):
            part = window(field * rows_of_field + y, z)
            part = pltpu.roll(part, lax.rem(field * SUB - lax.rem(z, 128) + 256, 128), 1)
            total = jnp.where(lane // SUB == field, part, total)
        return total

    own_rows[0] = y_row(jnp.maximum(y_start - 1, 0), z_start)
    own_rows[1] = y_row(jnp.minimum(y_start + SUB, y_cells - 1), z_start)

def sample_cube(sample_block, place, brick):
    fields, x_cells, y_cells, z_cells = brick.shape
    vmem = pl.BlockSpec(memory_space=pltpu.VMEM)
    smem = pl.BlockSpec(memory_space=pltpu.SMEM)
    hbm = pl.BlockSpec(memory_space=pltpu.HBM)
    rows = fields * x_cells * y_cells
    cube = jax.ShapeDtypeStruct((F * SUB, 256), jnp.float32)
    return pl.pallas_call(
        functools.partial(sample_kernel, y_cells, z_cells),
        out_shape=(
            cube,
            cube,
            cube,
            jax.ShapeDtypeStruct((2, SUB, 128), jnp.float32),
        ),
        in_specs=[smem, smem, hbm],
        out_specs=(vmem,) * 4,
        scratch_shapes=[
            pltpu.VMEM((2 * rows, 128), jnp.float32),
            pltpu.SemaphoreType.DMA((2,)),
        ],
        compiler_params=pltpu.CompilerParams(vmem_limit_bytes=16 * 1024 * 1024),
        cost_estimate=pl.CostEstimate(flops=0, bytes_accessed=16_000_000, transcendentals=0),
        name="sample_cube",
    )(sample_block, place, brick.reshape(rows, z_cells))


def change_kernel(
    y_cells,
    z_cells,
    sample_block,
    place,
    closure,
    order,
    centre,
    lower,
    upper,
    own_rows,
    thin,
    payload,
    table,
):
    y_start = corner_of(sample_block, place, 0, 0, y_cells, z_cells)[0]
    row = lax.broadcasted_iota(jnp.int32, (SUB, 256), 0)
    lane = lax.broadcasted_iota(jnp.int32, (SUB, 256), 1)
    south_row = jnp.where(y_start == 0, thin[column_of(place, 0, -1), :, 128:], own_rows[0])
    north_row = jnp.where(y_start + SUB == y_cells, thin[column_of(place, 0, 1), :, :128], own_rows[1])
    face_low = thin[column_of(place, -1, 0), 8:, :]
    face_high = thin[column_of(place, 1, 0), :8, :]
    cells = [centre[f * SUB : (f + 1) * SUB, :] for f in range(F)]
    viscosity = viscosity_of(cells, closure)
    changes = []
    for f in range(F):
        value = cells[f]
        west = jnp.where(row == 0, face_low[f : f + 1, :], pltpu.roll(value, 1, 0))
        east = jnp.where(row == SUB - 1, face_high[f : f + 1, :], pltpu.roll(value, SUB - 1, 0))
        edge = pltpu.roll(south_row, (128 - f * SUB) % 128, 1)
        south = jnp.where(lane < SUB, jnp.concatenate([edge, edge], 1), pltpu.roll(value, SUB, 1))
        edge = pltpu.roll(north_row, 112 - f * SUB, 1)
        north = jnp.where(
            lane >= 256 - SUB, jnp.concatenate([edge, edge], 1), pltpu.roll(value, 256 - SUB, 1)
        )
        down = lower[f * SUB : (f + 1) * SUB, :]
        up = upper[f * SUB : (f + 1) * SUB, :]
        laplacian = east + west + north + south + up + down - 6.0 * value
        advection = cells[0] * (east - west) + cells[1] * (north - south) + cells[2] * (up - down)
        change = viscosity * laplacian - 0.5 * advection
        if f == 2:
            change = change + buoyancy * cells[3]
        changes.append(change)
    ordered = dot_rows(jnp.concatenate(cells + changes, axis=0).astype(jnp.bfloat16), order[...])
    low_lanes = lane[:8, :128] < 64
    for part in range(2 * F):
        for cell in range(4):
            columns = slice(cell // 2 * 128, cell // 2 * 128 + 128)
            low = ordered[part * SUB : part * SUB + 8, columns]
            high = ordered[part * SUB + 8 : part * SUB + SUB, columns]
            if cell % 2 == 0:
                high = pltpu.roll(high, 64, 1)
            else:
                low = pltpu.roll(low, 64, 1)
            table[pl.ds(part * 32 + cell, 8, 4), :] = jnp.where(low_lanes, low, high)
    payload[...] = table[...].astype(jnp.bfloat16)


def cube_change(sample_block, place, closure, cube, thin, y_cells, z_cells):
    vmem = pl.BlockSpec(memory_space=pltpu.VMEM)
    smem = pl.BlockSpec(memory_space=pltpu.SMEM)
    return pl.pallas_call(
        functools.partial(change_kernel, y_cells, z_cells),
        out_shape=jax.ShapeDtypeStruct((4 * F * SUB, 128), jnp.bfloat16),
        in_specs=[smem] * 3 + [vmem] * 6,
        out_specs=vmem,
        scratch_shapes=[pltpu.VMEM((4 * F * SUB, 128), jnp.float32)],
        compiler_params=pltpu.CompilerParams(vmem_limit_bytes=16 * 1024 * 1024),
        name="cube_change",
    )(sample_block, place, closure, jnp.asarray(CELL_ORDER, jnp.bfloat16), *cube, thin)


def on_device(
    fields, closure_in, closure_bias, closure_out, master, momentum, sample_block, sample_trainer
):
    group_count = lax.axis_size("grp")
    x_devices = lax.axis_size("gx")
    y_devices = lax.axis_size("gy")
    trainers = x_devices * y_devices
    my_group = lax.axis_index("grp")
    my_column = lax.axis_index("gx") * y_devices + lax.axis_index("gy")
    is_trainer = my_group == group_count - 1
    everyone = ("grp", "gx", "gy")
    sim_groups = group_count - 1
    first_trainer = sim_groups * trainers
    brick = fields[0]
    y_cells, z_cells = brick.shape[2:]
    closure = jnp.concatenate(
        [0.5 * closure_in.T, 0.5 * closure_bias[None], closure_out[None]], axis=0
    )
    linear = jnp.sum(closure * closure_out[None], axis=1, keepdims=True)
    closure = jnp.pad(jnp.concatenate([closure, linear], axis=1), ((0, 1), (0, 127 - HID)))
    place = jnp.stack(
        [
            my_group,
            lax.axis_index("gx"),
            lax.axis_index("gy"),
            jnp.int32(sim_groups),
            jnp.int32(y_devices),
            jnp.int32(x_devices),
        ]
    ).astype(jnp.int32)

    def pairs(x_step, even_step):
        found = []
        for g in range(sim_groups):
            for c in range(trainers):
                gx, gy = c // y_devices, c % y_devices
                gx = (gx + x_step) % x_devices
                gy = (gy + (even_step if gy % 2 == 0 else -even_step)) % y_devices
                found.append((g * trainers + c, (g * x_devices + gx) * y_devices + gy))
        return found

    def x_neighbours(edges):
        if x_devices == 2:
            return lax.ppermute(edges, everyone, pairs(1, 0))
        from_high = lax.ppermute(edges[0], everyone, pairs(-1, 0))
        return jnp.stack([from_high, lax.ppermute(edges[1], everyone, pairs(1, 0))])

    def y_neighbours(for_first, for_second):
        return (
            lax.ppermute(for_first, everyone, pairs(0, 1)),
            lax.ppermute(for_second, everyone, pairs(0, -1)),
        )

    def swap(distance):
        return [(first_trainer + c, first_trainer + (c ^ distance)) for c in range(trainers)]

    def to_trainers(payload):
        landed = [
            lax.ppermute(
                payload, everyone, [(g * trainers + c, first_trainer + c) for c in range(trainers)]
            )
            for g in reversed(range(sim_groups))
        ]
        return jnp.stack(landed)

    def from_line(held):
        return [lax.ppermute(held, everyone, swap(apart)) for apart in range(1, y_devices)]

    def across(apart, held):
        return lax.ppermute(held, everyone, swap(apart * y_devices))

    thin = thin_faces(sample_block, place, brick, trainers)
    cube = sample_cube(sample_block, place, brick)
    first_count = CH * TAPS * F
    first = jnp.pad(master[:first_count].reshape(CH, TAPS * F), ((0, 0), (0, 256 - TAPS * F)))
    last = jnp.pad(master[first_count:].reshape(TAPS * F, CH), ((0, 256 - TAPS * F), (0, 0)))

    *cube, first, last = lax.optimization_barrier((*cube, first, last))
    selects = lax.optimization_barrier(
        (jnp.asarray(SELECT, jnp.bfloat16), jnp.asarray(LAST_ORDER, jnp.bfloat16))
    )

    thin = lax.all_to_all(thin, ("gx", "gy"), split_axis=0, concat_axis=0, tiled=True)
    payload = cube_change(sample_block, place, closure, cube, thin, y_cells, z_cells)
    landed = to_trainers(payload)
    closure, landed = lax.optimization_barrier((closure, landed))

    fields_count, x_cells = brick.shape[:2]
    viscosity, x_edges, y_edges = lax.cond(
        is_trainer,
        lambda: (
            jnp.zeros((x_cells, y_cells, z_cells), jnp.float32),
            jnp.zeros((2, fields_count, y_cells, z_cells), jnp.float32),
            jnp.zeros((2, fields_count, x_cells, z_cells), jnp.float32),
        ),
        lambda: brick_viscosity(closure, place, brick),
    )
    share_size = NPARAM // (group_count * trainers)
    share_start = (my_group * trainers + my_column) * share_size
    momentum_share = lax.dynamic_slice_in_dim(momentum, share_start, share_size)
    master_share = lax.dynamic_slice_in_dim(master, share_start, share_size)
    viscosity, momentum_share, master_share = lax.optimization_barrier(
        (viscosity, momentum_share, master_share)
    )
    halo = (x_neighbours(x_edges), *y_neighbours(y_edges[0], y_edges[1]))
    near = [landed, *from_line(landed)]
    far = [
        across(apart, pick_cubes(sample_trainer, place, near, y_devices, x_devices, apart))
        for apart in range(1, x_devices)
    ]
    arrived = [*near, *far]

    def train_here():
        delta_first, delta_last, new_brick = train_cubes(
            sample_trainer, place, first, last, selects, arrived, brick, y_devices, x_devices
        )
        delta = jnp.concatenate(
            [delta_first[:, : TAPS * F].reshape(-1), delta_last[: TAPS * F].reshape(-1)]
        )
        return delta, new_brick

    def evolve_here():
        new_brick = evolve(place, viscosity, brick, *halo)
        return jnp.zeros((NPARAM,), jnp.float32), new_brick

    delta, new_brick = lax.cond(is_trainer, train_here, evolve_here)

    held = delta
    for g in reversed(range(sim_groups)):
        held = held + lax.ppermute(
            delta, everyone, [(first_trainer + c, g * trainers + c) for c in range(trainers)]
        )
    final = delta
    for first_apart in range(1, trainers, group_count):
        meets = [
            (g * trainers + c, g * trainers + (c ^ (first_apart + g)))
            for g in range(group_count)
            for c in range(trainers)
            if first_apart + g < trainers
        ]
        final = final + lax.ppermute(held, everyone, meets)
    for apart in (1, 2):
        final = final + lax.ppermute(
            final,
            everyone,
            [(g * trainers + c, (g ^ apart) * trainers + c) for g in range(group_count) for c in range(trainers)],
        )

    inverse = 1.0 / jnp.sqrt(jnp.sum(final * final) / NPARAM + norm_epsilon)
    delta_share = lax.dynamic_slice_in_dim(final, share_start, share_size)
    new_momentum = momentum_decay * momentum_share + delta_share * inverse
    new_master = master_share - outer_rate * new_momentum
    return (new_brick[None], new_master, new_momentum)


def solution(mesh):
    in_specs = (P("grp", None, "gx", "gy", None), P(), P(), P(), P(), P(), P(), P())
    out_specs = (P("grp", None, "gx", "gy", None), P(("grp", "gx", "gy")), P(("grp", "gx", "gy")))
    return jax.shard_map(
        on_device, mesh=mesh, in_specs=in_specs, out_specs=out_specs, check_vma=False
    )
```

```python
import functools

import jax
import jax.numpy as jnp
import numpy as np
from jax import lax
from jax.experimental import pallas as pl
from jax.experimental.pallas import tpu as pltpu
from jax.sharding import PartitionSpec as P

F = 5
CH = 64
HID = 64
SUB = 16
TCAP = 6
INNER = 3
CELLS = 4096
NPARAM = 17280
TAPS = 27
PAIRS = TCAP // 2
COLS = (SUB + 2) * 128
PATCH = 16 * F
STACK = 3 * PATCH

time_step = 0.1
base_viscosity = 0.02
viscosity_gain = 0.2
buoyancy = 0.5
inner_rate = 0.02
outer_rate = 0.01
momentum_decay = 0.9
norm_epsilon = 1e-06


def patch_position(row):
    group, py, pz = row // 4, row // 2 % 2, row % 2
    ypos = py + 1 if group in (0, 2) else (3 if py == 0 else 0)
    zpos = pz + 1 if group in (0, 1) else (3 if pz == 0 else 0)
    return ypos - 1, zpos - 1


def selections():
    found = np.zeros((4, 256, STACK), np.float32)
    for cell in range(4):
        py, pz = cell // 2, cell % 2
        for kx in range(3):
            for channel in range(F):
                for row in range(16):
                    ypos, zpos = patch_position(row)
                    dy, dz = ypos - py, zpos - pz
                    if abs(dy) <= 1 and abs(dz) <= 1:
                        tap = 9 * kx + 3 * (dy + 1) + dz + 1
                        found[cell, tap * F + channel, kx * PATCH + channel * 16 + row] = 1.0
    return found


def last_order():
    order = np.zeros((256, 256), np.float32)
    for channel in range(F):
        for tap in range(TAPS):
            order[channel * TAPS + tap, (TAPS - 1 - tap) * F + channel] = 1.0
    return order


SELECT, LAST_ORDER = selections(), last_order()


def column_of(place, x_step, y_step):
    gx = lax.rem(place[1] + x_step + place[5], place[5])
    gy = lax.rem(place[2] + y_step + place[4], place[4])
    return gx * place[4] + gy


def owner_apart(owner, groups, place, y_devices, x_devices):
    group, column = divmod(owner, x_devices * y_devices)
    entry = groups - 1 - group
    y_apart = jnp.bitwise_xor(place[2], jnp.int32(column % y_devices))
    return entry, y_apart, jnp.bitwise_xor(place[1], jnp.int32(column // y_devices))


def pick_kernel(y_devices, x_devices, apart, trainer_of, place, *refs):
    near, chosen, owners = refs[:y_devices], refs[y_devices], refs[y_devices + 1]
    wanted = jnp.bitwise_xor(place[1], jnp.int32(apart)) * y_devices + place[2]
    count = jnp.int32(0)
    groups = trainer_of.shape[0] // (x_devices * y_devices)
    for owner in range(trainer_of.shape[0]):
        group, y_apart, x_apart = owner_apart(owner, groups, place, y_devices, x_devices)
        mine = (trainer_of[owner] == wanted) & (x_apart == 0)

        @pl.when(mine)
        def _():
            owners[0, count] = y_apart
            owners[1, count] = group

        count = count + jnp.where(mine, 1, 0)

    def copy_slot(slot, carry):
        for source in range(y_devices):

            @pl.when(owners[0, slot] == source)
            def _():
                chosen[slot] = near[source][owners[1, slot]]

        return carry

    lax.fori_loop(0, count, copy_slot, 0)


def pick_cubes(trainer_of, place, near, y_devices, x_devices, apart):
    vmem = pl.BlockSpec(memory_space=pltpu.VMEM)
    smem = pl.BlockSpec(memory_space=pltpu.SMEM)
    return pl.pallas_call(
        functools.partial(pick_kernel, y_devices, x_devices, apart),
        out_shape=jax.ShapeDtypeStruct((TCAP, *near[0].shape[1:]), near[0].dtype),
        in_specs=[smem, smem] + [vmem] * len(near),
        out_specs=vmem,
        scratch_shapes=[pltpu.SMEM((2, TCAP), jnp.int32)],
        compiler_params=pltpu.CompilerParams(vmem_limit_bytes=16 * 1024 * 1024),
        name="pick_cubes",
    )(trainer_of, place, *near)


def dot_rows(left, right):
    return jnp.dot(left, right, preferred_element_type=jnp.float32)


def dot_lanes(left, right):
    return lax.dot_general(left, right, (((1,), (1,)), ((), ())), preferred_element_type=jnp.float32)


def exact_parts(values):
    parts = []
    for _ in range(3):
        parts.append(values.astype(jnp.bfloat16))
        values = values - parts[-1].astype(jnp.float32)
    return jnp.concatenate(parts, axis=0)


def patch_masks():
    row = lax.broadcasted_iota(jnp.int32, (8, 128), 0)
    lane = lax.broadcasted_iota(jnp.int32, (8, 128), 1)
    z, y = lane % 8, lane // 8 % 8
    even_z, even_y = row % 2 == 0, row // 2 % 2 == 0
    return {
        "centre": row < 4,
        "even_z": even_z,
        "even_y": even_y,
        "gather_z": jnp.where(even_z, z, 7 - z) < 7,
        "gather_y": jnp.where(even_y, y, 7 - y) < 7,
        "scatter_z": jnp.where(even_z, z, 7 - z) > 0,
        "scatter_y": jnp.where(even_y, y, 7 - y) > 0,
    }


def edge_shift(values, step, even, inside, gather):
    before, after = pltpu.roll(values, step, 1), pltpu.roll(values, 128 - step, 1)
    moved = jnp.where(even, after, before) if gather else jnp.where(even, before, after)
    return jnp.where(inside, moved, 0.0)


def patch_stack(rows, masks):
    both = jnp.where(masks["centre"], rows, pltpu.roll(rows, 4, 0))
    y_edge = edge_shift(both, 8, masks["even_y"], masks["gather_y"], True)
    upper = jnp.where(masks["centre"], both, y_edge)
    return upper, edge_shift(upper, 1, masks["even_z"], masks["gather_z"], True)


def patch_fold(upper, lower, masks):
    line = upper + edge_shift(lower, 1, masks["even_z"], masks["scatter_z"], False)
    return line + pltpu.roll(edge_shift(line, 8, masks["even_y"], masks["scatter_y"], False), 4, 0)


def store_planes(ref, x, channels):
    stacked = jnp.concatenate([part for both in channels for part in both], axis=0).astype(jnp.bfloat16)
    for kx in range(3):
        start = pl.multiple_of((x + 2 - kx) * 128, 128)
        ref[kx * PATCH : (kx + 1) * PATCH, pl.ds(start, 128)] = stacked


def train_kernel(y_devices, x_devices, *refs):
    sources = y_devices + x_devices - 1
    (trainer_of, place, first_ref, last_ref, far_select, far_order) = refs[:6]
    arrived = refs[6 : 6 + sources]
    fields_ref = refs[6 + sources]
    delta_first, delta_last, new_fields_ref = refs[7 + sources : 10 + sources]
    (
        slots,
        picked,
        cubes,
        big_first,
        big_last,
        big_last_t,
        grad_first,
        grad_last,
        now,
        brick,
        select,
        order,
        slot_sems,
        field_sem,
        select_sems,
        *pair_refs,
    ) = refs[10 + sources :]
    targets, tables, inputs, errors, hiddens, pre_grads, slopes, partial_out, raw = [
        pair_refs[kind * PAIRS : (kind + 1) * PAIRS] for kind in range(9)
    ]

    field_in = pltpu.make_async_copy(fields_ref, brick, field_sem)
    field_out = pltpu.make_async_copy(brick, new_fields_ref, field_sem)
    select_copies = [
        pltpu.make_async_copy(far_select, select, select_sems.at[0]),
        pltpu.make_async_copy(far_order, order, select_sems.at[1]),
    ]

    column = place[1] * y_devices + place[2]
    for other in range(x_devices):
        picked[other] = 0
    count = jnp.int32(0)
    groups = trainer_of.shape[0] // (x_devices * y_devices)
    for owner in range(trainer_of.shape[0]):
        group, y_apart, x_apart = owner_apart(owner, groups, place, y_devices, x_devices)
        mine = trainer_of[owner] == column

        @pl.when(mine)
        def _():
            near = x_apart == 0
            slots[0, count] = jnp.where(near, y_apart, y_devices - 1 + x_apart)
            slots[1, count] = jnp.where(near, group, picked[x_apart])
            picked[x_apart] = picked[x_apart] + 1

        count = count + jnp.where(mine, 1, 0)

    def fetch(slot, wait):
        for source in range(sources):

            @pl.when((slot < count) & (slots[0, slot] == source))
            def _():
                copy = pltpu.make_async_copy(
                    arrived[source].at[slots[1, slot]], cubes.at[slot], slot_sems.at[slot]
                )
                copy.wait() if wait else copy.start()

    for slot in range(TCAP):
        fetch(slot, False)

    for copy in select_copies:
        copy.start()
    field_in.start()
    for slot in range(TCAP):

        @pl.when(slot >= count)
        def _():
            cubes[slot] = jnp.zeros(cubes.shape[1:], jnp.bfloat16)

    masks = patch_masks()
    for ref in (*errors, *inputs):
        ref[:PATCH, 128:256] = jnp.zeros((PATCH, 128), jnp.bfloat16)
        ref[2 * PATCH :, COLS - 256 : COLS - 128] = jnp.zeros((PATCH, 128), jnp.bfloat16)
    for ref in partial_out:
        ref[:, :128] = jnp.zeros((STACK, 128), jnp.float32)
        ref[:, COLS - 128 :] = jnp.zeros((STACK, 128), jnp.float32)
    lane = lax.broadcasted_iota(jnp.int32, (8, 128), 1)
    full_weight = 2.0 * (1.0 / (jnp.full((8, 128), count, jnp.int32).astype(jnp.float32) * CELLS))
    weights = [
        jnp.where(lane // 64 + 2 * pair < count, full_weight, 0.0) for pair in range(PAIRS)
    ]
    for slot in range(TCAP):
        fetch(slot, True)

    low_lanes = lax.broadcasted_iota(jnp.int32, (SUB * F * 2, 128), 1) < 64
    for pair in range(PAIRS):
        for kind, ref in enumerate((tables[pair], targets[pair])):
            rows = slice(kind * SUB * F * 2, (kind + 1) * SUB * F * 2)
            even = cubes[2 * pair, rows, :].astype(jnp.float32)
            odd = cubes[2 * pair + 1, rows, :].astype(jnp.float32)
            ref[0] = jnp.where(low_lanes, even, pltpu.roll(odd, 64, 1))
            ref[1] = jnp.where(low_lanes, pltpu.roll(even, 64, 1), odd)

    def patch_cells(ref, quarter, plane, channel):
        start = pl.multiple_of(channel * 32 + quarter % 2 * 16 + plane // 2 * 8, 8)
        rows = ref[quarter // 2, pl.ds(start, 8), :]
        return rows if plane % 2 == 0 else pltpu.roll(rows, 4, 0)

    def stack_planes(quarter, carry):
        for pair in range(PAIRS):
            for plane in range(4):
                x = quarter * 4 + plane
                channels = [
                    patch_stack(patch_cells(tables[pair], quarter, plane, c), masks) for c in range(F)
                ]
                store_planes(inputs[pair], x, channels)
        return carry

    lax.fori_loop(0, 4, stack_planes, 0, unroll=2)

    for copy in select_copies:
        copy.wait()
    start_first = first_ref[...].astype(jnp.bfloat16).astype(jnp.float32)
    start_last = dot_rows(last_ref[...].T.astype(jnp.bfloat16), order[...])
    now[:CH] = start_first
    now[CH:] = start_last
    field_in.wait()
    field_out.start()

    def train_step(step, step_carry):
        rounded = now[...].astype(jnp.bfloat16)
        for cell in range(4):
            rows = slice(cell * CH, (cell + 1) * CH)
            spread = dot_rows(rounded, select[cell])
            big_first[rows, :] = (0.5 * spread[:CH]).astype(jnp.bfloat16)
            big_last[rows, :] = (0.5 * spread[CH:]).astype(jnp.bfloat16)
            big_last_t[:, rows] = spread[CH:].T.astype(jnp.bfloat16)
        grad_first[...] = jnp.zeros(grad_first.shape, jnp.float32)
        grad_last[...] = jnp.zeros(grad_last.shape, jnp.float32)

        def columns_of(quarter):
            return pl.ds(pl.multiple_of(quarter * 512 + 128, 128), 512)

        def first_layer(pair, quarter):
            columns = columns_of(quarter)
            raw[pair][:, columns] = dot_rows(big_first[...], inputs[pair][:, columns])

        def activate(pair, quarter):
            columns = columns_of(quarter)
            for part in range(8):
                rows = slice(part * 32, (part + 1) * 32)
                half = raw[pair][rows, columns]
                curve = jnp.tanh(half)
                above = 1.0 + curve
                value = half * above
                hiddens[pair][rows, columns] = value.astype(jnp.bfloat16)
                slopes[pair][rows, columns] = above + value * (1.0 - curve)

        def last_layer(pair, quarter):
            columns = columns_of(quarter)
            partial_out[pair][:, columns] = dot_rows(big_last_t[...], hiddens[pair][:, columns])

        def find_errors(pair, quarter):
            for plane in range(4):
                x = quarter * 4 + plane
                column = pl.multiple_of((x + 1) * 128, 128)
                total = (
                    partial_out[pair][0:PATCH, pl.ds(pl.multiple_of(column + 128, 128), 128)]
                    + partial_out[pair][PATCH : 2 * PATCH, pl.ds(column, 128)]
                    + partial_out[pair][2 * PATCH :, pl.ds(pl.multiple_of(column - 128, 128), 128)]
                )
                channels = []
                for c in range(F):
                    predicted = patch_fold(
                        total[16 * c : 16 * c + 8], total[16 * c + 8 : 16 * c + 16], masks
                    )
                    wanted = patch_cells(targets[pair], quarter, plane, c)
                    error = weights[pair] * (predicted - wanted)
                    channels.append(patch_stack(error, masks))
                store_planes(errors[pair], x, channels)

        def hidden_layer(pair, quarter):
            columns = columns_of(quarter)
            raw[pair][:, columns] = dot_rows(big_last[...], errors[pair][:, columns])

        def scale(pair, quarter):
            columns = columns_of(quarter)
            for part in range(8):
                rows = slice(part * 32, (part + 1) * 32)
                product = raw[pair][rows, columns] * slopes[pair][rows, columns]
                pre_grads[pair][rows, columns] = product.astype(jnp.bfloat16)

        def gradients(pair, quarter):
            columns = columns_of(quarter)
            grad_first[...] += dot_lanes(pre_grads[pair][:, columns], inputs[pair][:, columns])
            grad_last[...] += dot_lanes(hiddens[pair][:, columns], errors[pair][:, columns])

        stages = (first_layer, activate, last_layer, find_errors, hidden_layer, scale, gradients)
        for turn in range(len(stages) + PAIRS - 1):

            def run(quarter, carry):
                for pair in range(PAIRS):
                    if 0 <= turn - pair < len(stages):
                        stages[turn - pair](pair, quarter)
                return carry

            lax.fori_loop(0, 4, run, 0, unroll=4)

        total = jnp.zeros((6 * CH, 256), jnp.float32)
        for cell in range(4):
            rows = slice(cell * CH, (cell + 1) * CH)
            parts = exact_parts(jnp.concatenate([grad_first[rows, :], grad_last[rows, :]], axis=0))
            total = total + dot_lanes(parts, select[cell])
        both = 2 * CH
        now[...] = now[...] - inner_rate * (total[:both] + total[both : 2 * both] + total[2 * both :])
        return step_carry

    lax.fori_loop(0, INNER, train_step, 0)
    delta_first[...] = start_first - now[:CH]
    ordered = dot_lanes(exact_parts(start_last - now[CH:]), order[...])
    delta_last[...] = (ordered[:CH] + ordered[CH : 2 * CH] + ordered[2 * CH :]).T
    field_out.wait()


def train_cubes(trainer_of, place, first, last, selects, arrived, fields, y_devices, x_devices):
    vmem = pl.BlockSpec(memory_space=pltpu.VMEM)
    smem = pl.BlockSpec(memory_space=pltpu.SMEM)
    anywhere = pl.BlockSpec(memory_space=pl.ANY)
    hbm = pl.BlockSpec(memory_space=pltpu.HBM)
    return pl.pallas_call(
        functools.partial(train_kernel, y_devices, x_devices),
        out_shape=(
            jax.ShapeDtypeStruct((CH, 256), jnp.float32),
            jax.ShapeDtypeStruct((256, CH), jnp.float32),
            jax.ShapeDtypeStruct(fields.shape, fields.dtype),
        ),
        in_specs=[smem] * 2 + [vmem] * 2 + [hbm] * 2 + [anywhere] * len(arrived) + [hbm],
        out_specs=(vmem, vmem, hbm),
        scratch_shapes=[
            pltpu.SMEM((2, TCAP), jnp.int32),
            pltpu.SMEM((x_devices,), jnp.int32),
            pltpu.VMEM((TCAP, 4 * SUB * F, 128), jnp.bfloat16),
            pltpu.VMEM((4 * CH, STACK), jnp.bfloat16),
            pltpu.VMEM((4 * CH, STACK), jnp.bfloat16),
            pltpu.VMEM((STACK, 4 * CH), jnp.bfloat16),
            pltpu.VMEM((4 * CH, STACK), jnp.float32),
            pltpu.VMEM((4 * CH, STACK), jnp.float32),
            pltpu.VMEM((2 * CH, 256), jnp.float32),
            pltpu.VMEM(fields.shape, fields.dtype),
            pltpu.VMEM((4, 256, STACK), jnp.bfloat16),
            pltpu.VMEM((256, 256), jnp.bfloat16),
            pltpu.SemaphoreType.DMA((TCAP,)),
            pltpu.SemaphoreType.DMA,
            pltpu.SemaphoreType.DMA((2,)),
        ]
        + [pltpu.VMEM((2, SUB * F * 2, 128), jnp.float32)] * (2 * PAIRS)
        + [pltpu.VMEM((STACK, COLS), jnp.bfloat16)] * (2 * PAIRS)
        + [pltpu.VMEM((4 * CH, COLS), jnp.bfloat16)] * (2 * PAIRS)
        + [pltpu.VMEM((4 * CH, COLS), jnp.float32)] * PAIRS
        + [pltpu.VMEM((STACK, COLS), jnp.float32)] * PAIRS
        + [pltpu.VMEM((4 * CH, COLS), jnp.float32)] * PAIRS,
        compiler_params=pltpu.CompilerParams(vmem_limit_bytes=52 * 1024 * 1024),
        name="train_cubes",
    )(
        trainer_of,
        place,
        first,
        last,
        *selects,
        *arrived,
        fields,
    )


def viscosity_of(cells, closure):
    def unit(h, total):
        half = closure[F, h] + closure[0, h] * cells[0]
        for f in range(1, F):
            half = half + closure[f, h] * cells[f]
        return total + closure[F + 1, h] * (half * jnp.tanh(half))

    total = closure[F, HID] + closure[0, HID] * cells[0]
    for f in range(1, F):
        total = total + closure[f, HID] * cells[f]
    total = lax.fori_loop(0, HID, unit, total, unroll=8)
    soft = jnp.maximum(total, 0.0) + jnp.log1p(jnp.exp(-jnp.abs(total)))
    return base_viscosity + viscosity_gain * soft


def viscosity_kernel(
    closure, place, fields, viscosity, x_edges, y_first, y_second, weights, out_column, masks, ones
):
    y_cells, z_cells = fields.shape[2:]
    x, x_cells = pl.program_id(0), pl.num_programs(0)
    up_first = lax.rem(place[2], 2) == 0
    for f in range(F):
        low, high = fields[f, 0, 0:1, :], fields[f, 0, y_cells - 1 : y_cells, :]
        y_first[f, pl.ds(x, 1), :] = jnp.where(up_first, high, low)
        y_second[f, pl.ds(x, 1), :] = jnp.where(up_first, low, high)

    @pl.when(x == x_cells - 1)
    def _():
        x_edges[1] = fields[:, 0]

    @pl.when(x == 0)
    def _():
        x_edges[0] = fields[:, 0]
        plain = closure[...]
        high = plain.astype(jnp.bfloat16).astype(jnp.float32)
        low = plain - high
        row = lax.broadcasted_iota(jnp.int32, (16, z_cells), 0)
        for j in range(8):
            turned = [pltpu.roll(part, j, 0) if j else part for part in (high, high, low, low)]
            weights[j] = jnp.concatenate(turned, axis=0).T[: HID + 8].astype(jnp.bfloat16)
            masks[j] = jnp.where(row % 8 == j, 1.0, 0.0).astype(jnp.bfloat16)
            ones[j] = jnp.where(row == (j + F) % 8, 1.0, 0.0).astype(jnp.bfloat16)
        out_column[...] = jnp.broadcast_to(plain.T[:HID, F + 1 : F + 2], (HID, 128))

    sublane = lax.broadcasted_iota(jnp.int32, (8, z_cells), 0)
    wide = z_cells // 128

    def tile(index, carry):
        rows = pl.ds(pl.multiple_of(index * 8, 8), 8)
        turned = []
        for f in range(F):
            value = fields[f, 0, rows, :]
            value = pltpu.roll(value, f, 0) if f else value
            top = value.astype(jnp.bfloat16).astype(jnp.float32)
            turned.append(jnp.concatenate([top, value - top], axis=0).astype(jnp.bfloat16))
        sums = jnp.zeros((8, z_cells), jnp.float32)
        for j in range(8):
            cells = ones[j]
            for f in range(F):
                cells = cells + turned[f] * masks[(j + f) % 8]
            half = dot_rows(weights[j], jnp.concatenate([cells, cells], axis=0))
            total = half[HID:]
            for group in range(HID // 8):
                part = half[group * 8 : group * 8 + 8]
                column = jnp.concatenate([out_column[group * 8 : group * 8 + 8, :]] * wide, axis=1)
                total = total + column * (part * jnp.tanh(part))
            for step in (4, 2, 1):
                total = total + pltpu.roll(total, step, 0)
            sums = jnp.where(sublane == j, total, sums)
        soft = jnp.maximum(sums, 0.0) + jnp.log1p(jnp.exp(-jnp.abs(sums)))
        viscosity[0, rows, :] = base_viscosity + viscosity_gain * soft
        return carry

    lax.fori_loop(0, y_cells // 8, tile, 0)


def brick_viscosity(closure, place, fields):
    count, x_cells, y_cells, z_cells = fields.shape
    line = jax.ShapeDtypeStruct((count, x_cells, z_cells), fields.dtype)
    line_spec = pl.BlockSpec(line.shape, lambda x: (0, 0, 0))
    return pl.pallas_call(
        viscosity_kernel,
        out_shape=(
            jax.ShapeDtypeStruct(fields.shape[1:], fields.dtype),
            jax.ShapeDtypeStruct((2, count, y_cells, z_cells), fields.dtype),
            line,
            line,
        ),
        grid=(x_cells,),
        in_specs=[
            pl.BlockSpec((8, 128), lambda x: (0, 0)),
            pl.BlockSpec(memory_space=pltpu.SMEM),
            pl.BlockSpec((count, 1, y_cells, z_cells), lambda x: (0, x, 0, 0)),
        ],
        out_specs=(
            pl.BlockSpec((1, y_cells, z_cells), lambda x: (x, 0, 0)),
            pl.BlockSpec((2, count, y_cells, z_cells), lambda x: (0, 0, 0, 0)),
            line_spec,
            line_spec,
        ),
        scratch_shapes=[
            pltpu.VMEM((8, HID + 8, 32), jnp.bfloat16),
            pltpu.VMEM((HID, 128), jnp.float32),
            pltpu.VMEM((8, 16, z_cells), jnp.bfloat16),
            pltpu.VMEM((8, 16, z_cells), jnp.bfloat16),
        ],
        compiler_params=pltpu.CompilerParams(vmem_limit_bytes=16 * 1024 * 1024),
        name="brick_viscosity",
    )(closure, place, fields)


def evolve_kernel(place, viscosity, fields, x_halo, y_first, y_second, new_fields):
    up_first = lax.rem(place[2], 2) == 0
    x_cells, y_cells, z_cells = fields.shape[1:]
    row = lax.broadcasted_iota(jnp.int32, (y_cells, z_cells), 0)
    lane = lax.broadcasted_iota(jnp.int32, (y_cells, z_cells), 1)

    def plane(x, carry):
        centre = [fields[f, x] for f in range(F)]
        below = jnp.maximum(x - 1, 0)
        above = jnp.minimum(x + 1, x_cells - 1)
        for f in range(F):
            value = centre[f]
            west = jnp.where(x == 0, x_halo[1, f], fields[f, below])
            east = jnp.where(x == x_cells - 1, x_halo[0, f], fields[f, above])
            first, second = y_first[f, pl.ds(x, 1), :], y_second[f, pl.ds(x, 1), :]
            south = jnp.where(
                row == 0, jnp.where(up_first, second, first), pltpu.roll(value, 1, 0)
            )
            north = jnp.where(
                row == y_cells - 1,
                jnp.where(up_first, first, second),
                pltpu.roll(value, y_cells - 1, 0),
            )
            lower = jnp.where(lane == 0, 0.0, pltpu.roll(value, 1, 1))
            upper = jnp.where(lane == z_cells - 1, 0.0, pltpu.roll(value, z_cells - 1, 1))
            laplacian = east + west + north + south + upper + lower - 6.0 * value
            advection = (
                centre[0] * (east - west) + centre[1] * (north - south) + centre[2] * (upper - lower)
            )
            tendency = viscosity[x] * laplacian - 0.5 * advection
            if f == 2:
                tendency = tendency + buoyancy * centre[3]
            new_fields[f, x] = value + time_step * tendency
        return carry

    lax.fori_loop(0, x_cells, plane, 0)


def evolve(place, viscosity, fields, x_halo, y_first, y_second):
    vmem = pl.BlockSpec(memory_space=pltpu.VMEM)
    return pl.pallas_call(
        evolve_kernel,
        out_shape=jax.ShapeDtypeStruct(fields.shape, fields.dtype),
        in_specs=[pl.BlockSpec(memory_space=pltpu.SMEM)] + [vmem] * 5,
        out_specs=vmem,
        compiler_params=pltpu.CompilerParams(vmem_limit_bytes=16 * 1024 * 1024),
        name="evolve_brick",
    )(place, viscosity, fields, x_halo, y_first, y_second)


def cell_order():
    order = np.zeros((256, 256), np.float32)
    for y in range(SUB):
        for z in range(SUB):
            order[y * SUB + z, (y % 2 * 2 + z % 2) * 64 + y // 2 * 8 + z // 2] = 1.0
    return order


CELL_ORDER = cell_order()


def corner_of(sample_block, place, x_step, y_step, y_cells, z_cells):
    x_devices, y_devices = place[5], place[4]
    gx = lax.rem(place[1] + x_step + x_devices, x_devices)
    gy = lax.rem(place[2] + y_step + y_devices, y_devices)
    group = jnp.minimum(place[0], place[3] - 1)
    block = sample_block[(group * x_devices + gx) * y_devices + gy]
    z_blocks = z_cells // SUB
    return lax.rem(lax.div(block, z_blocks), y_cells // SUB) * SUB, lax.rem(block, z_blocks) * SUB


def thin_kernel(
    y_cells, z_cells, sample_block, place, rows_ref, lines_ref, thin, x_buffer, y_buffer, x_sems, y_sems
):
    def corner(x_step, y_step):
        return corner_of(sample_block, place, x_step, y_step, y_cells, z_cells)

    lane = lax.broadcasted_iota(jnp.int32, (SUB, 128), 1)
    signs = (-1, 1)
    copies = []
    for side, sign in enumerate(signs):
        z_x, z_y = corner(sign, 0)[1], corner(0, sign)[1]
        x, y = side * (SUB - 1), side * (y_cells - 8)
        for field in range(F):
            copies.append(
                pltpu.make_async_copy(
                    rows_ref.at[
                        pl.ds((field * SUB + x) * y_cells, y_cells),
                        pl.ds(pl.multiple_of(lax.div(z_x, 128) * 128, 128), 128),
                    ],
                    x_buffer.at[pl.ds((side * 8 + field) * y_cells, y_cells)],
                    x_sems.at[side, field],
                )
            )
        copies.append(
            pltpu.make_async_copy(
                lines_ref.at[:, pl.ds(y, 8), pl.ds(pl.multiple_of(lax.div(z_y, 128) * 128, 128), 128)],
                y_buffer.at[side],
                y_sems.at[side],
            )
        )
    for copy in copies:
        copy.start()
    thin[...] = jnp.zeros(thin.shape, thin.dtype)
    for copy in copies:
        copy.wait()

    def moved(values, z, lane_start):
        return pltpu.roll(values, lax.rem(lane_start - lax.rem(z, 128) + 256, 128), 1)

    for side, sign in enumerate(signs):
        z = corner(0, sign)[1]
        total = jnp.zeros((SUB, 128), jnp.float32)
        for field in range(F):
            part = y_buffer[side, field * SUB : (field + 1) * SUB, side * 7, :]
            total = jnp.where(lane // SUB == field, moved(part, z, field * SUB), total)
        thin[column_of(place, 0, sign), :, side * 128 : (side + 1) * 128] = total
    for side, sign in enumerate(signs):
        y, z = corner(sign, 0)
        for half in range(2):
            total = jnp.zeros((8, 128), jnp.float32)
            for step in range(8):
                row = side * 8 * y_cells + y + half * 8 + step
                part = moved(x_buffer[pl.ds(row, 8, y_cells), :], z, step * SUB)
                total = jnp.where(lane[:8] // SUB == step, part, total)
            at = (column_of(place, sign, 0), slice(side * 8, side * 8 + 8), slice(half * 128, half * 128 + 128))
            thin[at] = total


def thin_faces(sample_block, place, brick, columns):
    fields, x_cells, y_cells, z_cells = brick.shape
    vmem = pl.BlockSpec(memory_space=pltpu.VMEM)
    smem = pl.BlockSpec(memory_space=pltpu.SMEM)
    hbm = pl.BlockSpec(memory_space=pltpu.HBM)
    return pl.pallas_call(
        functools.partial(thin_kernel, y_cells, z_cells),
        out_shape=jax.ShapeDtypeStruct((columns, SUB, 256), jnp.float32),
        in_specs=[smem, smem, hbm, hbm],
        out_specs=vmem,
        scratch_shapes=[
            pltpu.VMEM((16 * y_cells, 128), jnp.float32),
            pltpu.VMEM((2, fields * x_cells, 8, 128), jnp.float32),
            pltpu.SemaphoreType.DMA((2, fields)),
            pltpu.SemaphoreType.DMA((2,)),
        ],
        compiler_params=pltpu.CompilerParams(vmem_limit_bytes=16 * 1024 * 1024),
        name="thin_faces",
    )(
        sample_block,
        place,
        brick.reshape(fields * x_cells * y_cells, z_cells),
        brick.reshape(fields * x_cells, y_cells, z_cells),
    )


def sample_kernel(
    y_cells,
    z_cells,
    sample_block,
    place,
    brick,
    centre,
    lower,
    upper,
    own_rows,
    windows,
    sems,
):
    rows_of_x = y_cells
    rows_of_field = SUB * y_cells
    window_rows = F * rows_of_field

    def corner(x_step, y_step):
        return corner_of(sample_block, place, x_step, y_step, y_cells, z_cells)

    y_start, z_start = corner(0, 0)
    z_below = jnp.maximum(z_start - 1, 0)
    z_above = jnp.minimum(z_start + SUB, z_cells - 1)
    first_window = lax.div(z_below, 128)
    second_window = jnp.minimum(first_window + 1, z_cells // 128 - 1)
    copies = [
        pltpu.make_async_copy(
            brick.at[:, pl.ds(pl.multiple_of(at * 128, 128), 128)],
            windows.at[pl.ds(slot * window_rows, window_rows)],
            sems.at[slot],
        )
        for slot, at in enumerate((first_window, second_window))
    ]
    for copy in copies:
        copy.start()
    for copy in copies:
        copy.wait()

    def window(row, z):
        slot = lax.div(z, 128) - first_window
        return windows[pl.ds(slot * window_rows + row, SUB, rows_of_x), :]

    lane = lax.broadcasted_iota(jnp.int32, (SUB, 128), 1)
    for field in range(F):
        for half in range(2):
            inside = jnp.zeros((SUB, 128), jnp.float32)
            below = jnp.zeros((SUB, 128), jnp.float32)
            above = jnp.zeros((SUB, 128), jnp.float32)
            for step in range(8):
                row = field * rows_of_field + y_start + half * 8 + step
                first = step * SUB
                values = jnp.where(lane == 127, window(row, z_below), window(row, z_start))
                values = jnp.where(lane == 0, window(row, z_above), values)
                values = pltpu.roll(values, lax.rem(first - lax.rem(z_start, 128) + 256, 128), 1)
                inside = jnp.where(lane // SUB == step, values, inside)
                below = jnp.where(lane == (first - 1) % 128, values, below)
                above = jnp.where(lane == (first + SUB) % 128, values, above)
            below = jnp.where(z_start == 0, 0.0, pltpu.roll(below, 1, 1))
            above = jnp.where(z_start + SUB == z_cells, 0.0, pltpu.roll(above, 127, 1))
            at = (slice(field * SUB, (field + 1) * SUB), slice(half * 128, (half + 1) * 128))
            centre[at] = inside
            lower[at] = jnp.where(lane % SUB == 0, below, pltpu.roll(inside, 1, 1))
            upper[at] = jnp.where(lane % SUB == SUB - 1, above, pltpu.roll(inside, 127, 1))

    def y_row(y, z):
        total = jnp.zeros((SUB, 128), jnp.float32)
        for field in range(F):
            part = window(field * rows_of_field + y, z)
            part = pltpu.roll(part, lax.rem(field * SUB - lax.rem(z, 128) + 256, 128), 1)
            total = jnp.where(lane // SUB == field, part, total)
        return total

    own_rows[0] = y_row(jnp.maximum(y_start - 1, 0), z_start)
    own_rows[1] = y_row(jnp.minimum(y_start + SUB, y_cells - 1), z_start)

def sample_cube(sample_block, place, brick):
    fields, x_cells, y_cells, z_cells = brick.shape
    vmem = pl.BlockSpec(memory_space=pltpu.VMEM)
    smem = pl.BlockSpec(memory_space=pltpu.SMEM)
    hbm = pl.BlockSpec(memory_space=pltpu.HBM)
    rows = fields * x_cells * y_cells
    cube = jax.ShapeDtypeStruct((F * SUB, 256), jnp.float32)
    return pl.pallas_call(
        functools.partial(sample_kernel, y_cells, z_cells),
        out_shape=(
            cube,
            cube,
            cube,
            jax.ShapeDtypeStruct((2, SUB, 128), jnp.float32),
        ),
        in_specs=[smem, smem, hbm],
        out_specs=(vmem,) * 4,
        scratch_shapes=[
            pltpu.VMEM((2 * rows, 128), jnp.float32),
            pltpu.SemaphoreType.DMA((2,)),
        ],
        compiler_params=pltpu.CompilerParams(vmem_limit_bytes=16 * 1024 * 1024),
        cost_estimate=pl.CostEstimate(flops=0, bytes_accessed=16_000_000, transcendentals=0),
        name="sample_cube",
    )(sample_block, place, brick.reshape(rows, z_cells))


def change_kernel(
    y_cells,
    z_cells,
    sample_block,
    place,
    closure,
    order,
    centre,
    lower,
    upper,
    own_rows,
    thin,
    payload,
    table,
):
    y_start = corner_of(sample_block, place, 0, 0, y_cells, z_cells)[0]
    row = lax.broadcasted_iota(jnp.int32, (SUB, 256), 0)
    lane = lax.broadcasted_iota(jnp.int32, (SUB, 256), 1)
    south_row = jnp.where(y_start == 0, thin[column_of(place, 0, -1), :, 128:], own_rows[0])
    north_row = jnp.where(y_start + SUB == y_cells, thin[column_of(place, 0, 1), :, :128], own_rows[1])
    face_low = thin[column_of(place, -1, 0), 8:, :]
    face_high = thin[column_of(place, 1, 0), :8, :]
    cells = [centre[f * SUB : (f + 1) * SUB, :] for f in range(F)]
    viscosity = viscosity_of(cells, closure)
    changes = []
    for f in range(F):
        value = cells[f]
        west = jnp.where(row == 0, face_low[f : f + 1, :], pltpu.roll(value, 1, 0))
        east = jnp.where(row == SUB - 1, face_high[f : f + 1, :], pltpu.roll(value, SUB - 1, 0))
        edge = pltpu.roll(south_row, (128 - f * SUB) % 128, 1)
        south = jnp.where(lane < SUB, jnp.concatenate([edge, edge], 1), pltpu.roll(value, SUB, 1))
        edge = pltpu.roll(north_row, 112 - f * SUB, 1)
        north = jnp.where(
            lane >= 256 - SUB, jnp.concatenate([edge, edge], 1), pltpu.roll(value, 256 - SUB, 1)
        )
        down = lower[f * SUB : (f + 1) * SUB, :]
        up = upper[f * SUB : (f + 1) * SUB, :]
        laplacian = east + west + north + south + up + down - 6.0 * value
        advection = cells[0] * (east - west) + cells[1] * (north - south) + cells[2] * (up - down)
        change = viscosity * laplacian - 0.5 * advection
        if f == 2:
            change = change + buoyancy * cells[3]
        changes.append(change)
    ordered = dot_rows(jnp.concatenate(cells + changes, axis=0).astype(jnp.bfloat16), order[...])
    low_lanes = lane[:8, :128] < 64
    for part in range(2 * F):
        for cell in range(4):
            columns = slice(cell // 2 * 128, cell // 2 * 128 + 128)
            low = ordered[part * SUB : part * SUB + 8, columns]
            high = ordered[part * SUB + 8 : part * SUB + SUB, columns]
            if cell % 2 == 0:
                high = pltpu.roll(high, 64, 1)
            else:
                low = pltpu.roll(low, 64, 1)
            table[pl.ds(part * 32 + cell, 8, 4), :] = jnp.where(low_lanes, low, high)
    payload[...] = table[...].astype(jnp.bfloat16)


def cube_change(sample_block, place, closure, cube, thin, y_cells, z_cells):
    vmem = pl.BlockSpec(memory_space=pltpu.VMEM)
    smem = pl.BlockSpec(memory_space=pltpu.SMEM)
    return pl.pallas_call(
        functools.partial(change_kernel, y_cells, z_cells),
        out_shape=jax.ShapeDtypeStruct((4 * F * SUB, 128), jnp.bfloat16),
        in_specs=[smem] * 3 + [vmem] * 6,
        out_specs=vmem,
        scratch_shapes=[pltpu.VMEM((4 * F * SUB, 128), jnp.float32)],
        compiler_params=pltpu.CompilerParams(vmem_limit_bytes=16 * 1024 * 1024),
        name="cube_change",
    )(sample_block, place, closure, jnp.asarray(CELL_ORDER, jnp.bfloat16), *cube, thin)


def on_device(
    fields, closure_in, closure_bias, closure_out, master, momentum, sample_block, sample_trainer
):
    group_count = lax.axis_size("grp")
    x_devices = lax.axis_size("gx")
    y_devices = lax.axis_size("gy")
    trainers = x_devices * y_devices
    my_group = lax.axis_index("grp")
    my_column = lax.axis_index("gx") * y_devices + lax.axis_index("gy")
    is_trainer = my_group == group_count - 1
    everyone = ("grp", "gx", "gy")
    sim_groups = group_count - 1
    first_trainer = sim_groups * trainers
    brick = fields[0]
    y_cells, z_cells = brick.shape[2:]
    closure = jnp.concatenate(
        [0.5 * closure_in.T, 0.5 * closure_bias[None], closure_out[None]], axis=0
    )
    linear = jnp.sum(closure * closure_out[None], axis=1, keepdims=True)
    closure = jnp.pad(jnp.concatenate([closure, linear], axis=1), ((0, 1), (0, 127 - HID)))
    place = jnp.stack(
        [
            my_group,
            lax.axis_index("gx"),
            lax.axis_index("gy"),
            jnp.int32(sim_groups),
            jnp.int32(y_devices),
            jnp.int32(x_devices),
        ]
    ).astype(jnp.int32)

    def pairs(x_step, even_step):
        found = []
        for g in range(sim_groups):
            for c in range(trainers):
                gx, gy = c // y_devices, c % y_devices
                gx = (gx + x_step) % x_devices
                gy = (gy + (even_step if gy % 2 == 0 else -even_step)) % y_devices
                found.append((g * trainers + c, (g * x_devices + gx) * y_devices + gy))
        return found

    def x_neighbours(edges):
        if x_devices == 2:
            return lax.ppermute(edges, everyone, pairs(1, 0))
        from_high = lax.ppermute(edges[0], everyone, pairs(-1, 0))
        return jnp.stack([from_high, lax.ppermute(edges[1], everyone, pairs(1, 0))])

    def y_neighbours(for_first, for_second):
        return (
            lax.ppermute(for_first, everyone, pairs(0, 1)),
            lax.ppermute(for_second, everyone, pairs(0, -1)),
        )

    def swap(distance):
        return [(first_trainer + c, first_trainer + (c ^ distance)) for c in range(trainers)]

    def to_trainers(payload):
        landed = [
            lax.ppermute(
                payload, everyone, [(g * trainers + c, first_trainer + c) for c in range(trainers)]
            )
            for g in reversed(range(sim_groups))
        ]
        return jnp.stack(landed)

    def from_line(held):
        return [lax.ppermute(held, everyone, swap(apart)) for apart in range(1, y_devices)]

    def across(apart, held):
        return lax.ppermute(held, everyone, swap(apart * y_devices))

    thin = thin_faces(sample_block, place, brick, trainers)
    cube = sample_cube(sample_block, place, brick)
    first_count = CH * TAPS * F
    first = jnp.pad(master[:first_count].reshape(CH, TAPS * F), ((0, 0), (0, 256 - TAPS * F)))
    last = jnp.pad(master[first_count:].reshape(TAPS * F, CH), ((0, 256 - TAPS * F), (0, 0)))

    *cube, first, last = lax.optimization_barrier((*cube, first, last))
    selects = lax.optimization_barrier(
        (jnp.asarray(SELECT, jnp.bfloat16), jnp.asarray(LAST_ORDER, jnp.bfloat16))
    )

    thin = lax.all_to_all(thin, ("gx", "gy"), split_axis=0, concat_axis=0, tiled=True)
    payload = cube_change(sample_block, place, closure, cube, thin, y_cells, z_cells)
    landed = to_trainers(payload)
    closure, landed = lax.optimization_barrier((closure, landed))

    fields_count, x_cells = brick.shape[:2]
    viscosity, x_edges, *y_edges = lax.cond(
        is_trainer,
        lambda: (
            jnp.zeros((x_cells, y_cells, z_cells), jnp.float32),
            jnp.zeros((2, fields_count, y_cells, z_cells), jnp.float32),
            jnp.zeros((fields_count, x_cells, z_cells), jnp.float32),
            jnp.zeros((fields_count, x_cells, z_cells), jnp.float32),
        ),
        lambda: brick_viscosity(closure, place, brick),
    )
    share_size = NPARAM // (group_count * trainers)
    share_start = (my_group * trainers + my_column) * share_size
    momentum_share = lax.dynamic_slice_in_dim(momentum, share_start, share_size)
    master_share = lax.dynamic_slice_in_dim(master, share_start, share_size)
    viscosity, momentum_share, master_share = lax.optimization_barrier(
        (viscosity, momentum_share, master_share)
    )
    halo = (x_neighbours(x_edges), *y_neighbours(*y_edges))
    near = [landed, *from_line(landed)]
    far = [
        across(apart, pick_cubes(sample_trainer, place, near, y_devices, x_devices, apart))
        for apart in range(1, x_devices)
    ]
    arrived = [*near, *far]

    def train_here():
        delta_first, delta_last, new_brick = train_cubes(
            sample_trainer, place, first, last, selects, arrived, brick, y_devices, x_devices
        )
        delta = jnp.concatenate(
            [delta_first[:, : TAPS * F].reshape(-1), delta_last[: TAPS * F].reshape(-1)]
        )
        return delta, new_brick

    def evolve_here():
        new_brick = evolve(place, viscosity, brick, *halo)
        return jnp.zeros((NPARAM,), jnp.float32), new_brick

    delta, new_brick = lax.cond(is_trainer, train_here, evolve_here)

    held = delta
    for g in reversed(range(sim_groups)):
        held = held + lax.ppermute(
            delta, everyone, [(first_trainer + c, g * trainers + c) for c in range(trainers)]
        )
    final = delta
    for first_apart in range(1, trainers, group_count):
        meets = [
            (g * trainers + c, g * trainers + (c ^ (first_apart + g)))
            for g in range(group_count)
            for c in range(trainers)
            if first_apart + g < trainers
        ]
        final = final + lax.ppermute(held, everyone, meets)
    for apart in (1, 2):
        final = final + lax.ppermute(
            final,
            everyone,
            [(g * trainers + c, (g ^ apart) * trainers + c) for g in range(group_count) for c in range(trainers)],
        )

    inverse = 1.0 / jnp.sqrt(jnp.sum(final * final) / NPARAM + norm_epsilon)
    delta_share = lax.dynamic_slice_in_dim(final, share_start, share_size)
    new_momentum = momentum_decay * momentum_share + delta_share * inverse
    new_master = master_share - outer_rate * new_momentum
    return (new_brick[None], new_master, new_momentum)


def solution(mesh):
    in_specs = (P("grp", None, "gx", "gy", None), P(), P(), P(), P(), P(), P(), P())
    out_specs = (P("grp", None, "gx", "gy", None), P(("grp", "gx", "gy")), P(("grp", "gx", "gy")))
    return jax.shard_map(
        on_device, mesh=mesh, in_specs=in_specs, out_specs=out_specs, check_vma=False
    )
```

```python
import functools

import jax
import jax.numpy as jnp
import numpy as np
from jax import lax
from jax.experimental import pallas as pl
from jax.experimental.pallas import tpu as pltpu
from jax.sharding import PartitionSpec as P

F = 5
CH = 64
HID = 64
SUB = 16
TCAP = 6
INNER = 3
CELLS = 4096
NPARAM = 17280
TAPS = 27
PAIRS = TCAP // 2
COLS = (SUB + 2) * 128
PATCH = 16 * F
STACK = 3 * PATCH

time_step = 0.1
base_viscosity = 0.02
viscosity_gain = 0.2
buoyancy = 0.5
inner_rate = 0.02
outer_rate = 0.01
momentum_decay = 0.9
norm_epsilon = 1e-06


def patch_position(row):
    group, py, pz = row // 4, row // 2 % 2, row % 2
    ypos = py + 1 if group in (0, 2) else (3 if py == 0 else 0)
    zpos = pz + 1 if group in (0, 1) else (3 if pz == 0 else 0)
    return ypos - 1, zpos - 1


def selections():
    found = np.zeros((4, 256, STACK), np.float32)
    for cell in range(4):
        py, pz = cell // 2, cell % 2
        for kx in range(3):
            for channel in range(F):
                for row in range(16):
                    ypos, zpos = patch_position(row)
                    dy, dz = ypos - py, zpos - pz
                    if abs(dy) <= 1 and abs(dz) <= 1:
                        tap = 9 * kx + 3 * (dy + 1) + dz + 1
                        found[cell, tap * F + channel, kx * PATCH + channel * 16 + row] = 1.0
    return found


def last_order():
    order = np.zeros((256, 256), np.float32)
    for channel in range(F):
        for tap in range(TAPS):
            order[channel * TAPS + tap, (TAPS - 1 - tap) * F + channel] = 1.0
    return order


SELECT, LAST_ORDER = selections(), last_order()


def column_of(place, x_step, y_step):
    gx = lax.rem(place[1] + x_step + place[5], place[5])
    gy = lax.rem(place[2] + y_step + place[4], place[4])
    return gx * place[4] + gy


def owner_apart(owner, groups, place, y_devices, x_devices):
    group, column = divmod(owner, x_devices * y_devices)
    entry = groups - 1 - group
    y_apart = jnp.bitwise_xor(place[2], jnp.int32(column % y_devices))
    return entry, y_apart, jnp.bitwise_xor(place[1], jnp.int32(column // y_devices))


def pick_kernel(y_devices, x_devices, apart, trainer_of, place, *refs):
    near, chosen, owners = refs[:y_devices], refs[y_devices], refs[y_devices + 1]
    wanted = jnp.bitwise_xor(place[1], jnp.int32(apart)) * y_devices + place[2]
    count = jnp.int32(0)
    groups = trainer_of.shape[0] // (x_devices * y_devices)
    for owner in range(trainer_of.shape[0]):
        group, y_apart, x_apart = owner_apart(owner, groups, place, y_devices, x_devices)
        mine = (trainer_of[owner] == wanted) & (x_apart == 0)

        @pl.when(mine)
        def _():
            owners[0, count] = y_apart
            owners[1, count] = group

        count = count + jnp.where(mine, 1, 0)

    def copy_slot(slot, carry):
        for source in range(y_devices):

            @pl.when(owners[0, slot] == source)
            def _():
                chosen[slot] = near[source][owners[1, slot]]

        return carry

    lax.fori_loop(0, count, copy_slot, 0)


def pick_cubes(trainer_of, place, near, y_devices, x_devices, apart):
    vmem = pl.BlockSpec(memory_space=pltpu.VMEM)
    smem = pl.BlockSpec(memory_space=pltpu.SMEM)
    return pl.pallas_call(
        functools.partial(pick_kernel, y_devices, x_devices, apart),
        out_shape=jax.ShapeDtypeStruct((TCAP, *near[0].shape[1:]), near[0].dtype),
        in_specs=[smem, smem] + [vmem] * len(near),
        out_specs=vmem,
        scratch_shapes=[pltpu.SMEM((2, TCAP), jnp.int32)],
        compiler_params=pltpu.CompilerParams(vmem_limit_bytes=16 * 1024 * 1024),
        name="pick_cubes",
    )(trainer_of, place, *near)


def dot_rows(left, right):
    return jnp.dot(left, right, preferred_element_type=jnp.float32)


def dot_lanes(left, right):
    return lax.dot_general(left, right, (((1,), (1,)), ((), ())), preferred_element_type=jnp.float32)


def exact_parts(values):
    parts = []
    for _ in range(3):
        parts.append(values.astype(jnp.bfloat16))
        values = values - parts[-1].astype(jnp.float32)
    return jnp.concatenate(parts, axis=0)


def patch_masks():
    row = lax.broadcasted_iota(jnp.int32, (8, 128), 0)
    lane = lax.broadcasted_iota(jnp.int32, (8, 128), 1)
    z, y = lane % 8, lane // 8 % 8
    even_z, even_y = row % 2 == 0, row // 2 % 2 == 0
    return {
        "centre": row < 4,
        "even_z": even_z,
        "even_y": even_y,
        "gather_z": jnp.where(even_z, z, 7 - z) < 7,
        "gather_y": jnp.where(even_y, y, 7 - y) < 7,
        "scatter_z": jnp.where(even_z, z, 7 - z) > 0,
        "scatter_y": jnp.where(even_y, y, 7 - y) > 0,
    }


def edge_shift(values, step, even, inside, gather):
    before, after = pltpu.roll(values, step, 1), pltpu.roll(values, 128 - step, 1)
    moved = jnp.where(even, after, before) if gather else jnp.where(even, before, after)
    return jnp.where(inside, moved, 0.0)


def patch_stack(rows, masks):
    both = jnp.where(masks["centre"], rows, pltpu.roll(rows, 4, 0))
    y_edge = edge_shift(both, 8, masks["even_y"], masks["gather_y"], True)
    upper = jnp.where(masks["centre"], both, y_edge)
    return upper, edge_shift(upper, 1, masks["even_z"], masks["gather_z"], True)


def patch_fold(upper, lower, masks):
    line = upper + edge_shift(lower, 1, masks["even_z"], masks["scatter_z"], False)
    return line + pltpu.roll(edge_shift(line, 8, masks["even_y"], masks["scatter_y"], False), 4, 0)


def store_planes(ref, x, channels):
    stacked = jnp.concatenate([part for both in channels for part in both], axis=0).astype(jnp.bfloat16)
    for kx in range(3):
        start = pl.multiple_of((x + 2 - kx) * 128, 128)
        ref[kx * PATCH : (kx + 1) * PATCH, pl.ds(start, 128)] = stacked


def train_kernel(y_devices, x_devices, *refs):
    sources = y_devices + x_devices - 1
    (trainer_of, place, first_ref, last_ref, far_select, far_order) = refs[:6]
    arrived = refs[6 : 6 + sources]
    fields_ref = refs[6 + sources]
    delta_first, delta_last, new_fields_ref = refs[7 + sources : 10 + sources]
    (
        slots,
        picked,
        cubes,
        big_first,
        big_last,
        big_last_t,
        grad_first,
        grad_last,
        now,
        brick,
        select,
        order,
        slot_sems,
        field_sem,
        select_sems,
        *pair_refs,
    ) = refs[10 + sources :]
    targets, tables, inputs, errors, hiddens, pre_grads, slopes, partial_out, raw = [
        pair_refs[kind * PAIRS : (kind + 1) * PAIRS] for kind in range(9)
    ]

    field_in = pltpu.make_async_copy(fields_ref, brick, field_sem)
    field_out = pltpu.make_async_copy(brick, new_fields_ref, field_sem)
    select_copies = [
        pltpu.make_async_copy(far_select, select, select_sems.at[0]),
        pltpu.make_async_copy(far_order, order, select_sems.at[1]),
    ]

    column = place[1] * y_devices + place[2]
    for other in range(x_devices):
        picked[other] = 0
    count = jnp.int32(0)
    groups = trainer_of.shape[0] // (x_devices * y_devices)
    for owner in range(trainer_of.shape[0]):
        group, y_apart, x_apart = owner_apart(owner, groups, place, y_devices, x_devices)
        mine = trainer_of[owner] == column

        @pl.when(mine)
        def _():
            near = x_apart == 0
            slots[0, count] = jnp.where(near, y_apart, y_devices - 1 + x_apart)
            slots[1, count] = jnp.where(near, group, picked[x_apart])
            picked[x_apart] = picked[x_apart] + 1

        count = count + jnp.where(mine, 1, 0)

    def fetch(slot, wait):
        for source in range(sources):

            @pl.when((slot < count) & (slots[0, slot] == source))
            def _():
                copy = pltpu.make_async_copy(
                    arrived[source].at[slots[1, slot]], cubes.at[slot], slot_sems.at[slot]
                )
                copy.wait() if wait else copy.start()

    for slot in range(TCAP):
        fetch(slot, False)

    for copy in select_copies:
        copy.start()
    field_in.start()
    for slot in range(TCAP):

        @pl.when(slot >= count)
        def _():
            cubes[slot] = jnp.zeros(cubes.shape[1:], jnp.bfloat16)

    masks = patch_masks()
    for ref in (*errors, *inputs):
        ref[:PATCH, 128:256] = jnp.zeros((PATCH, 128), jnp.bfloat16)
        ref[2 * PATCH :, COLS - 256 : COLS - 128] = jnp.zeros((PATCH, 128), jnp.bfloat16)
    for ref in partial_out:
        ref[:, :128] = jnp.zeros((STACK, 128), jnp.float32)
        ref[:, COLS - 128 :] = jnp.zeros((STACK, 128), jnp.float32)
    lane = lax.broadcasted_iota(jnp.int32, (8, 128), 1)
    full_weight = 2.0 * (1.0 / (jnp.full((8, 128), count, jnp.int32).astype(jnp.float32) * CELLS))
    weights = [
        jnp.where(lane // 64 + 2 * pair < count, full_weight, 0.0) for pair in range(PAIRS)
    ]
    for slot in range(TCAP):
        fetch(slot, True)

    low_lanes = lax.broadcasted_iota(jnp.int32, (SUB * F * 2, 128), 1) < 64
    for pair in range(PAIRS):
        for kind, ref in enumerate((tables[pair], targets[pair])):
            rows = slice(kind * SUB * F * 2, (kind + 1) * SUB * F * 2)
            even = cubes[2 * pair, rows, :].astype(jnp.float32)
            odd = cubes[2 * pair + 1, rows, :].astype(jnp.float32)
            ref[0] = jnp.where(low_lanes, even, pltpu.roll(odd, 64, 1))
            ref[1] = jnp.where(low_lanes, pltpu.roll(even, 64, 1), odd)

    def patch_cells(ref, quarter, plane, channel):
        start = pl.multiple_of(channel * 32 + quarter % 2 * 16 + plane // 2 * 8, 8)
        rows = ref[quarter // 2, pl.ds(start, 8), :]
        return rows if plane % 2 == 0 else pltpu.roll(rows, 4, 0)

    def stack_planes(quarter, carry):
        for pair in range(PAIRS):
            for plane in range(4):
                x = quarter * 4 + plane
                channels = [
                    patch_stack(patch_cells(tables[pair], quarter, plane, c), masks) for c in range(F)
                ]
                store_planes(inputs[pair], x, channels)
        return carry

    lax.fori_loop(0, 4, stack_planes, 0, unroll=2)

    for copy in select_copies:
        copy.wait()
    start_first = first_ref[...].astype(jnp.bfloat16).astype(jnp.float32)
    start_last = dot_rows(last_ref[...].T.astype(jnp.bfloat16), order[...])
    now[:CH] = start_first
    now[CH:] = start_last
    field_in.wait()
    field_out.start()

    def train_step(step, step_carry):
        rounded = now[...].astype(jnp.bfloat16)
        for cell in range(4):
            rows = slice(cell * CH, (cell + 1) * CH)
            spread = dot_rows(rounded, select[cell])
            big_first[rows, :] = (0.5 * spread[:CH]).astype(jnp.bfloat16)
            big_last[rows, :] = (0.5 * spread[CH:]).astype(jnp.bfloat16)
            big_last_t[:, rows] = spread[CH:].T.astype(jnp.bfloat16)
        grad_first[...] = jnp.zeros(grad_first.shape, jnp.float32)
        grad_last[...] = jnp.zeros(grad_last.shape, jnp.float32)

        def columns_of(quarter):
            return pl.ds(pl.multiple_of(quarter * 512 + 128, 128), 512)

        def first_layer(pair, quarter):
            columns = columns_of(quarter)
            raw[pair][:, columns] = dot_rows(big_first[...], inputs[pair][:, columns])

        def activate(pair, quarter):
            columns = columns_of(quarter)
            for part in range(8):
                rows = slice(part * 32, (part + 1) * 32)
                half = raw[pair][rows, columns]
                curve = jnp.tanh(half)
                above = 1.0 + curve
                value = half * above
                hiddens[pair][rows, columns] = value.astype(jnp.bfloat16)
                slopes[pair][rows, columns] = above + value * (1.0 - curve)

        def last_layer(pair, quarter):
            columns = columns_of(quarter)
            partial_out[pair][:, columns] = dot_rows(big_last_t[...], hiddens[pair][:, columns])

        def find_errors(pair, quarter):
            for plane in range(4):
                x = quarter * 4 + plane
                column = pl.multiple_of((x + 1) * 128, 128)
                total = (
                    partial_out[pair][0:PATCH, pl.ds(pl.multiple_of(column + 128, 128), 128)]
                    + partial_out[pair][PATCH : 2 * PATCH, pl.ds(column, 128)]
                    + partial_out[pair][2 * PATCH :, pl.ds(pl.multiple_of(column - 128, 128), 128)]
                )
                channels = []
                for c in range(F):
                    predicted = patch_fold(
                        total[16 * c : 16 * c + 8], total[16 * c + 8 : 16 * c + 16], masks
                    )
                    wanted = patch_cells(targets[pair], quarter, plane, c)
                    error = weights[pair] * (predicted - wanted)
                    channels.append(patch_stack(error, masks))
                store_planes(errors[pair], x, channels)

        def hidden_layer(pair, quarter):
            columns = columns_of(quarter)
            raw[pair][:, columns] = dot_rows(big_last[...], errors[pair][:, columns])

        def scale(pair, quarter):
            columns = columns_of(quarter)
            for part in range(8):
                rows = slice(part * 32, (part + 1) * 32)
                product = raw[pair][rows, columns] * slopes[pair][rows, columns]
                pre_grads[pair][rows, columns] = product.astype(jnp.bfloat16)

        def gradients(pair, quarter):
            columns = columns_of(quarter)
            grad_first[...] += dot_lanes(pre_grads[pair][:, columns], inputs[pair][:, columns])
            grad_last[...] += dot_lanes(hiddens[pair][:, columns], errors[pair][:, columns])

        stages = (first_layer, activate, last_layer, find_errors, hidden_layer, scale, gradients)
        for turn in range(len(stages) + PAIRS - 1):

            def run(quarter, carry):
                for pair in range(PAIRS):
                    if 0 <= turn - pair < len(stages):
                        stages[turn - pair](pair, quarter)
                return carry

            lax.fori_loop(0, 4, run, 0, unroll=4)

        total = jnp.zeros((6 * CH, 256), jnp.float32)
        for cell in range(4):
            rows = slice(cell * CH, (cell + 1) * CH)
            parts = exact_parts(jnp.concatenate([grad_first[rows, :], grad_last[rows, :]], axis=0))
            total = total + dot_lanes(parts, select[cell])
        both = 2 * CH
        now[...] = now[...] - inner_rate * (total[:both] + total[both : 2 * both] + total[2 * both :])
        return step_carry

    lax.fori_loop(0, INNER, train_step, 0)
    delta_first[...] = start_first - now[:CH]
    ordered = dot_lanes(exact_parts(start_last - now[CH:]), order[...])
    delta_last[...] = (ordered[:CH] + ordered[CH : 2 * CH] + ordered[2 * CH :]).T
    field_out.wait()


def train_cubes(trainer_of, place, first, last, selects, arrived, fields, y_devices, x_devices):
    vmem = pl.BlockSpec(memory_space=pltpu.VMEM)
    smem = pl.BlockSpec(memory_space=pltpu.SMEM)
    anywhere = pl.BlockSpec(memory_space=pl.ANY)
    hbm = pl.BlockSpec(memory_space=pltpu.HBM)
    return pl.pallas_call(
        functools.partial(train_kernel, y_devices, x_devices),
        out_shape=(
            jax.ShapeDtypeStruct((CH, 256), jnp.float32),
            jax.ShapeDtypeStruct((256, CH), jnp.float32),
            jax.ShapeDtypeStruct(fields.shape, fields.dtype),
        ),
        in_specs=[smem] * 2 + [vmem] * 2 + [hbm] * 2 + [anywhere] * len(arrived) + [hbm],
        out_specs=(vmem, vmem, hbm),
        scratch_shapes=[
            pltpu.SMEM((2, TCAP), jnp.int32),
            pltpu.SMEM((x_devices,), jnp.int32),
            pltpu.VMEM((TCAP, 4 * SUB * F, 128), jnp.bfloat16),
            pltpu.VMEM((4 * CH, STACK), jnp.bfloat16),
            pltpu.VMEM((4 * CH, STACK), jnp.bfloat16),
            pltpu.VMEM((STACK, 4 * CH), jnp.bfloat16),
            pltpu.VMEM((4 * CH, STACK), jnp.float32),
            pltpu.VMEM((4 * CH, STACK), jnp.float32),
            pltpu.VMEM((2 * CH, 256), jnp.float32),
            pltpu.VMEM(fields.shape, fields.dtype),
            pltpu.VMEM((4, 256, STACK), jnp.bfloat16),
            pltpu.VMEM((256, 256), jnp.bfloat16),
            pltpu.SemaphoreType.DMA((TCAP,)),
            pltpu.SemaphoreType.DMA,
            pltpu.SemaphoreType.DMA((2,)),
        ]
        + [pltpu.VMEM((2, SUB * F * 2, 128), jnp.float32)] * (2 * PAIRS)
        + [pltpu.VMEM((STACK, COLS), jnp.bfloat16)] * (2 * PAIRS)
        + [pltpu.VMEM((4 * CH, COLS), jnp.bfloat16)] * (2 * PAIRS)
        + [pltpu.VMEM((4 * CH, COLS), jnp.float32)] * PAIRS
        + [pltpu.VMEM((STACK, COLS), jnp.float32)] * PAIRS
        + [pltpu.VMEM((4 * CH, COLS), jnp.float32)] * PAIRS,
        compiler_params=pltpu.CompilerParams(vmem_limit_bytes=52 * 1024 * 1024),
        name="train_cubes",
    )(
        trainer_of,
        place,
        first,
        last,
        *selects,
        *arrived,
        fields,
    )


def viscosity_of(cells, closure):
    def unit(h, total):
        half = closure[F, h] + closure[0, h] * cells[0]
        for f in range(1, F):
            half = half + closure[f, h] * cells[f]
        return total + closure[F + 1, h] * (half * jnp.tanh(half))

    total = closure[F, HID] + closure[0, HID] * cells[0]
    for f in range(1, F):
        total = total + closure[f, HID] * cells[f]
    total = lax.fori_loop(0, HID, unit, total, unroll=8)
    soft = jnp.maximum(total, 0.0) + jnp.log1p(jnp.exp(-jnp.abs(total)))
    return base_viscosity + viscosity_gain * soft


def viscosity_kernel(
    closure, place, fields, viscosity, x_edges, y_first, y_second, weights, out_column
):
    y_cells, z_cells = fields.shape[2:]
    x, x_cells = pl.program_id(0), pl.num_programs(0)
    up_first = lax.rem(place[2], 2) == 0
    for f in range(F):
        low, high = fields[f, 0, 0:1, :], fields[f, 0, y_cells - 1 : y_cells, :]
        y_first[f, pl.ds(x, 1), :] = jnp.where(up_first, high, low)
        y_second[f, pl.ds(x, 1), :] = jnp.where(up_first, low, high)

    @pl.when(x == x_cells - 1)
    def _():
        x_edges[1] = fields[:, 0]

    @pl.when(x == 0)
    def _():
        x_edges[0] = fields[:, 0]
        plain = closure[...]
        high = plain.astype(jnp.bfloat16).astype(jnp.float32)
        low = plain - high
        blank = jnp.zeros((8, 128), jnp.float32)
        for j in range(8):
            turned = [pltpu.roll(part, j, 0) if j else part for part in (high, high, low)]
            stacked = jnp.concatenate([*turned, blank], axis=0)
            weights[j] = stacked.T[: HID + 8].astype(jnp.bfloat16)
        out_column[...] = jnp.broadcast_to(plain.T[:HID, F + 1 : F + 2], (HID, 128))

    sublane = lax.broadcasted_iota(jnp.int32, (8, z_cells), 0)
    wide = z_cells // 128

    def tile(index, carry):
        rows = pl.ds(pl.multiple_of(index * 8, 8), 8)
        turned = [fields[f, 0, rows, :] for f in range(F)]
        turned = [pltpu.roll(turned[f], f, 0) if f else turned[f] for f in range(F)]
        sums = jnp.zeros((8, z_cells), jnp.float32)
        for j in range(8):
            cells = jnp.where(sublane == (j + F) % 8, 1.0, 0.0)
            for f in range(F):
                cells = jnp.where(sublane == (j + f) % 8, turned[f], cells)
            top = cells.astype(jnp.bfloat16).astype(jnp.float32)
            stacked = jnp.concatenate([top, cells - top, top, jnp.zeros_like(top)], axis=0)
            half = dot_rows(weights[j], stacked.astype(jnp.bfloat16))
            total = half[HID:]
            for group in range(HID // 8):
                part = half[group * 8 : group * 8 + 8]
                column = jnp.concatenate([out_column[group * 8 : group * 8 + 8, :]] * wide, axis=1)
                total = total + column * (part * jnp.tanh(part))
            for step in (4, 2, 1):
                total = total + pltpu.roll(total, step, 0)
            sums = jnp.where(sublane == j, total, sums)
        soft = jnp.maximum(sums, 0.0) + jnp.log1p(jnp.exp(-jnp.abs(sums)))
        viscosity[0, rows, :] = base_viscosity + viscosity_gain * soft
        return carry

    lax.fori_loop(0, y_cells // 8, tile, 0)


def brick_viscosity(closure, place, fields):
    count, x_cells, y_cells, z_cells = fields.shape
    line = jax.ShapeDtypeStruct((count, x_cells, z_cells), fields.dtype)
    line_spec = pl.BlockSpec(line.shape, lambda x: (0, 0, 0))
    return pl.pallas_call(
        viscosity_kernel,
        out_shape=(
            jax.ShapeDtypeStruct(fields.shape[1:], fields.dtype),
            jax.ShapeDtypeStruct((2, count, y_cells, z_cells), fields.dtype),
            line,
            line,
        ),
        grid=(x_cells,),
        in_specs=[
            pl.BlockSpec((8, 128), lambda x: (0, 0)),
            pl.BlockSpec(memory_space=pltpu.SMEM),
            pl.BlockSpec((count, 1, y_cells, z_cells), lambda x: (0, x, 0, 0)),
        ],
        out_specs=(
            pl.BlockSpec((1, y_cells, z_cells), lambda x: (x, 0, 0)),
            pl.BlockSpec((2, count, y_cells, z_cells), lambda x: (0, 0, 0, 0)),
            line_spec,
            line_spec,
        ),
        scratch_shapes=[
            pltpu.VMEM((8, HID + 8, 32), jnp.bfloat16),
            pltpu.VMEM((HID, 128), jnp.float32),
        ],
        compiler_params=pltpu.CompilerParams(vmem_limit_bytes=16 * 1024 * 1024),
        name="brick_viscosity",
    )(closure, place, fields)


def evolve_kernel(place, viscosity, fields, x_halo, y_first, y_second, new_fields):
    up_first = lax.rem(place[2], 2) == 0
    x_cells, y_cells, z_cells = fields.shape[1:]
    row = lax.broadcasted_iota(jnp.int32, (y_cells, z_cells), 0)
    lane = lax.broadcasted_iota(jnp.int32, (y_cells, z_cells), 1)

    def plane(x, carry):
        centre = [fields[f, x] for f in range(F)]
        below = jnp.maximum(x - 1, 0)
        above = jnp.minimum(x + 1, x_cells - 1)
        for f in range(F):
            value = centre[f]
            west = jnp.where(x == 0, x_halo[1, f], fields[f, below])
            east = jnp.where(x == x_cells - 1, x_halo[0, f], fields[f, above])
            first, second = y_first[f, pl.ds(x, 1), :], y_second[f, pl.ds(x, 1), :]
            south = jnp.where(
                row == 0, jnp.where(up_first, second, first), pltpu.roll(value, 1, 0)
            )
            north = jnp.where(
                row == y_cells - 1,
                jnp.where(up_first, first, second),
                pltpu.roll(value, y_cells - 1, 0),
            )
            lower = jnp.where(lane == 0, 0.0, pltpu.roll(value, 1, 1))
            upper = jnp.where(lane == z_cells - 1, 0.0, pltpu.roll(value, z_cells - 1, 1))
            laplacian = east + west + north + south + upper + lower - 6.0 * value
            advection = (
                centre[0] * (east - west) + centre[1] * (north - south) + centre[2] * (upper - lower)
            )
            tendency = viscosity[x] * laplacian - 0.5 * advection
            if f == 2:
                tendency = tendency + buoyancy * centre[3]
            new_fields[f, x] = value + time_step * tendency
        return carry

    lax.fori_loop(0, x_cells, plane, 0)


def evolve(place, viscosity, fields, x_halo, y_first, y_second):
    vmem = pl.BlockSpec(memory_space=pltpu.VMEM)
    return pl.pallas_call(
        evolve_kernel,
        out_shape=jax.ShapeDtypeStruct(fields.shape, fields.dtype),
        in_specs=[pl.BlockSpec(memory_space=pltpu.SMEM)] + [vmem] * 5,
        out_specs=vmem,
        compiler_params=pltpu.CompilerParams(vmem_limit_bytes=16 * 1024 * 1024),
        name="evolve_brick",
    )(place, viscosity, fields, x_halo, y_first, y_second)


def cell_order():
    order = np.zeros((256, 256), np.float32)
    for y in range(SUB):
        for z in range(SUB):
            order[y * SUB + z, (y % 2 * 2 + z % 2) * 64 + y // 2 * 8 + z // 2] = 1.0
    return order


CELL_ORDER = cell_order()


def corner_of(sample_block, place, x_step, y_step, y_cells, z_cells):
    x_devices, y_devices = place[5], place[4]
    gx = lax.rem(place[1] + x_step + x_devices, x_devices)
    gy = lax.rem(place[2] + y_step + y_devices, y_devices)
    group = jnp.minimum(place[0], place[3] - 1)
    block = sample_block[(group * x_devices + gx) * y_devices + gy]
    z_blocks = z_cells // SUB
    return lax.rem(lax.div(block, z_blocks), y_cells // SUB) * SUB, lax.rem(block, z_blocks) * SUB


def thin_kernel(
    y_cells, z_cells, sample_block, place, rows_ref, lines_ref, thin, x_buffer, y_buffer, x_sems, y_sems
):
    def corner(x_step, y_step):
        return corner_of(sample_block, place, x_step, y_step, y_cells, z_cells)

    lane = lax.broadcasted_iota(jnp.int32, (SUB, 128), 1)
    signs = (-1, 1)
    copies = []
    for side, sign in enumerate(signs):
        z_x, z_y = corner(sign, 0)[1], corner(0, sign)[1]
        x, y = side * (SUB - 1), side * (y_cells - 8)
        for field in range(F):
            copies.append(
                pltpu.make_async_copy(
                    rows_ref.at[
                        pl.ds((field * SUB + x) * y_cells, y_cells),
                        pl.ds(pl.multiple_of(lax.div(z_x, 128) * 128, 128), 128),
                    ],
                    x_buffer.at[pl.ds((side * 8 + field) * y_cells, y_cells)],
                    x_sems.at[side, field],
                )
            )
        copies.append(
            pltpu.make_async_copy(
                lines_ref.at[:, pl.ds(y, 8), pl.ds(pl.multiple_of(lax.div(z_y, 128) * 128, 128), 128)],
                y_buffer.at[side],
                y_sems.at[side],
            )
        )
    for copy in copies:
        copy.start()
    thin[...] = jnp.zeros(thin.shape, thin.dtype)
    for copy in copies:
        copy.wait()

    def moved(values, z, lane_start):
        return pltpu.roll(values, lax.rem(lane_start - lax.rem(z, 128) + 256, 128), 1)

    for side, sign in enumerate(signs):
        z = corner(0, sign)[1]
        total = jnp.zeros((SUB, 128), jnp.float32)
        for field in range(F):
            part = y_buffer[side, field * SUB : (field + 1) * SUB, side * 7, :]
            total = jnp.where(lane // SUB == field, moved(part, z, field * SUB), total)
        thin[column_of(place, 0, sign), :, side * 128 : (side + 1) * 128] = total
    for side, sign in enumerate(signs):
        y, z = corner(sign, 0)
        for half in range(2):
            total = jnp.zeros((8, 128), jnp.float32)
            for step in range(8):
                row = side * 8 * y_cells + y + half * 8 + step
                part = moved(x_buffer[pl.ds(row, 8, y_cells), :], z, step * SUB)
                total = jnp.where(lane[:8] // SUB == step, part, total)
            at = (column_of(place, sign, 0), slice(side * 8, side * 8 + 8), slice(half * 128, half * 128 + 128))
            thin[at] = total


def thin_faces(sample_block, place, brick, columns):
    fields, x_cells, y_cells, z_cells = brick.shape
    vmem = pl.BlockSpec(memory_space=pltpu.VMEM)
    smem = pl.BlockSpec(memory_space=pltpu.SMEM)
    hbm = pl.BlockSpec(memory_space=pltpu.HBM)
    return pl.pallas_call(
        functools.partial(thin_kernel, y_cells, z_cells),
        out_shape=jax.ShapeDtypeStruct((columns, SUB, 256), jnp.float32),
        in_specs=[smem, smem, hbm, hbm],
        out_specs=vmem,
        scratch_shapes=[
            pltpu.VMEM((16 * y_cells, 128), jnp.float32),
            pltpu.VMEM((2, fields * x_cells, 8, 128), jnp.float32),
            pltpu.SemaphoreType.DMA((2, fields)),
            pltpu.SemaphoreType.DMA((2,)),
        ],
        compiler_params=pltpu.CompilerParams(vmem_limit_bytes=16 * 1024 * 1024),
        name="thin_faces",
    )(
        sample_block,
        place,
        brick.reshape(fields * x_cells * y_cells, z_cells),
        brick.reshape(fields * x_cells, y_cells, z_cells),
    )


def sample_kernel(
    y_cells,
    z_cells,
    sample_block,
    place,
    brick,
    centre,
    lower,
    upper,
    own_rows,
    windows,
    sems,
):
    rows_of_x = y_cells
    rows_of_field = SUB * y_cells
    window_rows = F * rows_of_field

    def corner(x_step, y_step):
        return corner_of(sample_block, place, x_step, y_step, y_cells, z_cells)

    y_start, z_start = corner(0, 0)
    z_below = jnp.maximum(z_start - 1, 0)
    z_above = jnp.minimum(z_start + SUB, z_cells - 1)
    first_window = lax.div(z_below, 128)
    second_window = jnp.minimum(first_window + 1, z_cells // 128 - 1)
    copies = [
        pltpu.make_async_copy(
            brick.at[:, pl.ds(pl.multiple_of(at * 128, 128), 128)],
            windows.at[pl.ds(slot * window_rows, window_rows)],
            sems.at[slot],
        )
        for slot, at in enumerate((first_window, second_window))
    ]
    for copy in copies:
        copy.start()
    for copy in copies:
        copy.wait()

    def window(row, z):
        slot = lax.div(z, 128) - first_window
        return windows[pl.ds(slot * window_rows + row, SUB, rows_of_x), :]

    lane = lax.broadcasted_iota(jnp.int32, (SUB, 128), 1)
    for field in range(F):
        for half in range(2):
            inside = jnp.zeros((SUB, 128), jnp.float32)
            below = jnp.zeros((SUB, 128), jnp.float32)
            above = jnp.zeros((SUB, 128), jnp.float32)
            for step in range(8):
                row = field * rows_of_field + y_start + half * 8 + step
                first = step * SUB
                values = jnp.where(lane == 127, window(row, z_below), window(row, z_start))
                values = jnp.where(lane == 0, window(row, z_above), values)
                values = pltpu.roll(values, lax.rem(first - lax.rem(z_start, 128) + 256, 128), 1)
                inside = jnp.where(lane // SUB == step, values, inside)
                below = jnp.where(lane == (first - 1) % 128, values, below)
                above = jnp.where(lane == (first + SUB) % 128, values, above)
            below = jnp.where(z_start == 0, 0.0, pltpu.roll(below, 1, 1))
            above = jnp.where(z_start + SUB == z_cells, 0.0, pltpu.roll(above, 127, 1))
            at = (slice(field * SUB, (field + 1) * SUB), slice(half * 128, (half + 1) * 128))
            centre[at] = inside
            lower[at] = jnp.where(lane % SUB == 0, below, pltpu.roll(inside, 1, 1))
            upper[at] = jnp.where(lane % SUB == SUB - 1, above, pltpu.roll(inside, 127, 1))

    def y_row(y, z):
        total = jnp.zeros((SUB, 128), jnp.float32)
        for field in range(F):
            part = window(field * rows_of_field + y, z)
            part = pltpu.roll(part, lax.rem(field * SUB - lax.rem(z, 128) + 256, 128), 1)
            total = jnp.where(lane // SUB == field, part, total)
        return total

    own_rows[0] = y_row(jnp.maximum(y_start - 1, 0), z_start)
    own_rows[1] = y_row(jnp.minimum(y_start + SUB, y_cells - 1), z_start)

def sample_cube(sample_block, place, brick):
    fields, x_cells, y_cells, z_cells = brick.shape
    vmem = pl.BlockSpec(memory_space=pltpu.VMEM)
    smem = pl.BlockSpec(memory_space=pltpu.SMEM)
    hbm = pl.BlockSpec(memory_space=pltpu.HBM)
    rows = fields * x_cells * y_cells
    cube = jax.ShapeDtypeStruct((F * SUB, 256), jnp.float32)
    return pl.pallas_call(
        functools.partial(sample_kernel, y_cells, z_cells),
        out_shape=(
            cube,
            cube,
            cube,
            jax.ShapeDtypeStruct((2, SUB, 128), jnp.float32),
        ),
        in_specs=[smem, smem, hbm],
        out_specs=(vmem,) * 4,
        scratch_shapes=[
            pltpu.VMEM((2 * rows, 128), jnp.float32),
            pltpu.SemaphoreType.DMA((2,)),
        ],
        compiler_params=pltpu.CompilerParams(vmem_limit_bytes=16 * 1024 * 1024),
        cost_estimate=pl.CostEstimate(flops=0, bytes_accessed=16_000_000, transcendentals=0),
        name="sample_cube",
    )(sample_block, place, brick.reshape(rows, z_cells))


def change_kernel(
    y_cells,
    z_cells,
    sample_block,
    place,
    closure,
    order,
    centre,
    lower,
    upper,
    own_rows,
    thin,
    payload,
    table,
):
    y_start = corner_of(sample_block, place, 0, 0, y_cells, z_cells)[0]
    row = lax.broadcasted_iota(jnp.int32, (SUB, 256), 0)
    lane = lax.broadcasted_iota(jnp.int32, (SUB, 256), 1)
    south_row = jnp.where(y_start == 0, thin[column_of(place, 0, -1), :, 128:], own_rows[0])
    north_row = jnp.where(y_start + SUB == y_cells, thin[column_of(place, 0, 1), :, :128], own_rows[1])
    face_low = thin[column_of(place, -1, 0), 8:, :]
    face_high = thin[column_of(place, 1, 0), :8, :]
    cells = [centre[f * SUB : (f + 1) * SUB, :] for f in range(F)]
    viscosity = viscosity_of(cells, closure)
    changes = []
    for f in range(F):
        value = cells[f]
        west = jnp.where(row == 0, face_low[f : f + 1, :], pltpu.roll(value, 1, 0))
        east = jnp.where(row == SUB - 1, face_high[f : f + 1, :], pltpu.roll(value, SUB - 1, 0))
        edge = pltpu.roll(south_row, (128 - f * SUB) % 128, 1)
        south = jnp.where(lane < SUB, jnp.concatenate([edge, edge], 1), pltpu.roll(value, SUB, 1))
        edge = pltpu.roll(north_row, 112 - f * SUB, 1)
        north = jnp.where(
            lane >= 256 - SUB, jnp.concatenate([edge, edge], 1), pltpu.roll(value, 256 - SUB, 1)
        )
        down = lower[f * SUB : (f + 1) * SUB, :]
        up = upper[f * SUB : (f + 1) * SUB, :]
        laplacian = east + west + north + south + up + down - 6.0 * value
        advection = cells[0] * (east - west) + cells[1] * (north - south) + cells[2] * (up - down)
        change = viscosity * laplacian - 0.5 * advection
        if f == 2:
            change = change + buoyancy * cells[3]
        changes.append(change)
    ordered = dot_rows(jnp.concatenate(cells + changes, axis=0).astype(jnp.bfloat16), order[...])
    low_lanes = lane[:8, :128] < 64
    for part in range(2 * F):
        for cell in range(4):
            columns = slice(cell // 2 * 128, cell // 2 * 128 + 128)
            low = ordered[part * SUB : part * SUB + 8, columns]
            high = ordered[part * SUB + 8 : part * SUB + SUB, columns]
            if cell % 2 == 0:
                high = pltpu.roll(high, 64, 1)
            else:
                low = pltpu.roll(low, 64, 1)
            table[pl.ds(part * 32 + cell, 8, 4), :] = jnp.where(low_lanes, low, high)
    payload[...] = table[...].astype(jnp.bfloat16)


def cube_change(sample_block, place, closure, cube, thin, y_cells, z_cells):
    vmem = pl.BlockSpec(memory_space=pltpu.VMEM)
    smem = pl.BlockSpec(memory_space=pltpu.SMEM)
    return pl.pallas_call(
        functools.partial(change_kernel, y_cells, z_cells),
        out_shape=jax.ShapeDtypeStruct((4 * F * SUB, 128), jnp.bfloat16),
        in_specs=[smem] * 3 + [vmem] * 6,
        out_specs=vmem,
        scratch_shapes=[pltpu.VMEM((4 * F * SUB, 128), jnp.float32)],
        compiler_params=pltpu.CompilerParams(vmem_limit_bytes=16 * 1024 * 1024),
        name="cube_change",
    )(sample_block, place, closure, jnp.asarray(CELL_ORDER, jnp.bfloat16), *cube, thin)


def on_device(
    fields, closure_in, closure_bias, closure_out, master, momentum, sample_block, sample_trainer
):
    group_count = lax.axis_size("grp")
    x_devices = lax.axis_size("gx")
    y_devices = lax.axis_size("gy")
    trainers = x_devices * y_devices
    my_group = lax.axis_index("grp")
    my_column = lax.axis_index("gx") * y_devices + lax.axis_index("gy")
    is_trainer = my_group == group_count - 1
    everyone = ("grp", "gx", "gy")
    sim_groups = group_count - 1
    first_trainer = sim_groups * trainers
    brick = fields[0]
    y_cells, z_cells = brick.shape[2:]
    closure = jnp.concatenate(
        [0.5 * closure_in.T, 0.5 * closure_bias[None], closure_out[None]], axis=0
    )
    linear = jnp.sum(closure * closure_out[None], axis=1, keepdims=True)
    closure = jnp.pad(jnp.concatenate([closure, linear], axis=1), ((0, 1), (0, 127 - HID)))
    place = jnp.stack(
        [
            my_group,
            lax.axis_index("gx"),
            lax.axis_index("gy"),
            jnp.int32(sim_groups),
            jnp.int32(y_devices),
            jnp.int32(x_devices),
        ]
    ).astype(jnp.int32)

    def pairs(x_step, even_step):
        found = []
        for g in range(sim_groups):
            for c in range(trainers):
                gx, gy = c // y_devices, c % y_devices
                gx = (gx + x_step) % x_devices
                gy = (gy + (even_step if gy % 2 == 0 else -even_step)) % y_devices
                found.append((g * trainers + c, (g * x_devices + gx) * y_devices + gy))
        return found

    def x_neighbours(edges):
        if x_devices == 2:
            return lax.ppermute(edges, everyone, pairs(1, 0))
        from_high = lax.ppermute(edges[0], everyone, pairs(-1, 0))
        return jnp.stack([from_high, lax.ppermute(edges[1], everyone, pairs(1, 0))])

    def y_neighbours(for_first, for_second):
        return (
            lax.ppermute(for_first, everyone, pairs(0, 1)),
            lax.ppermute(for_second, everyone, pairs(0, -1)),
        )

    def swap(distance):
        return [(first_trainer + c, first_trainer + (c ^ distance)) for c in range(trainers)]

    def to_trainers(payload):
        landed = [
            lax.ppermute(
                payload, everyone, [(g * trainers + c, first_trainer + c) for c in range(trainers)]
            )
            for g in reversed(range(sim_groups))
        ]
        return jnp.stack(landed)

    def from_line(held):
        return [lax.ppermute(held, everyone, swap(apart)) for apart in range(1, y_devices)]

    def across(apart, held):
        return lax.ppermute(held, everyone, swap(apart * y_devices))

    thin = thin_faces(sample_block, place, brick, trainers)
    cube = sample_cube(sample_block, place, brick)
    first_count = CH * TAPS * F
    first = jnp.pad(master[:first_count].reshape(CH, TAPS * F), ((0, 0), (0, 256 - TAPS * F)))
    last = jnp.pad(master[first_count:].reshape(TAPS * F, CH), ((0, 256 - TAPS * F), (0, 0)))

    *cube, first, last = lax.optimization_barrier((*cube, first, last))
    selects = lax.optimization_barrier(
        (jnp.asarray(SELECT, jnp.bfloat16), jnp.asarray(LAST_ORDER, jnp.bfloat16))
    )

    thin = lax.all_to_all(thin, ("gx", "gy"), split_axis=0, concat_axis=0, tiled=True)
    payload = cube_change(sample_block, place, closure, cube, thin, y_cells, z_cells)
    landed = to_trainers(payload)
    closure, landed = lax.optimization_barrier((closure, landed))

    share_size = NPARAM // (group_count * trainers)
    share_start = (my_group * trainers + my_column) * share_size

    def shares():
        return tuple(
            lax.dynamic_slice_in_dim(array, share_start, share_size) for array in (momentum, master)
        )

    fields_count, x_cells = brick.shape[:2]
    viscosity, x_edges, *y_edges, early_shares = lax.cond(
        is_trainer,
        lambda: (
            jnp.zeros((x_cells, y_cells, z_cells), jnp.float32),
            jnp.zeros((2, fields_count, y_cells, z_cells), jnp.float32),
            jnp.zeros((fields_count, x_cells, z_cells), jnp.float32),
            jnp.zeros((fields_count, x_cells, z_cells), jnp.float32),
            shares(),
        ),
        lambda: (
            *brick_viscosity(closure, place, brick),
            (jnp.zeros((share_size,), jnp.float32),) * 2,
        ),
    )
    halo = (x_neighbours(x_edges), *y_neighbours(*y_edges))
    near = [landed, *from_line(landed)]
    far = [
        across(apart, pick_cubes(sample_trainer, place, near, y_devices, x_devices, apart))
        for apart in range(1, x_devices)
    ]
    arrived = [*near, *far]

    def train_here():
        delta_first, delta_last, new_brick = train_cubes(
            sample_trainer, place, first, last, selects, arrived, brick, y_devices, x_devices
        )
        delta = jnp.concatenate(
            [delta_first[:, : TAPS * F].reshape(-1), delta_last[: TAPS * F].reshape(-1)]
        )
        return delta, new_brick, early_shares

    def evolve_here():
        new_brick = evolve(place, viscosity, brick, *halo)
        return jnp.zeros((NPARAM,), jnp.float32), new_brick, shares()

    delta, new_brick, (momentum_share, master_share) = lax.cond(is_trainer, train_here, evolve_here)

    held = delta
    for g in reversed(range(sim_groups)):
        held = held + lax.ppermute(
            delta, everyone, [(first_trainer + c, g * trainers + c) for c in range(trainers)]
        )
    final = delta
    for first_apart in range(1, trainers, group_count):
        meets = [
            (g * trainers + c, g * trainers + (c ^ (first_apart + g)))
            for g in range(group_count)
            for c in range(trainers)
            if first_apart + g < trainers
        ]
        final = final + lax.ppermute(held, everyone, meets)
    for apart in (1, 2):
        final = final + lax.ppermute(
            final,
            everyone,
            [(g * trainers + c, (g ^ apart) * trainers + c) for g in range(group_count) for c in range(trainers)],
        )

    inverse = 1.0 / jnp.sqrt(jnp.sum(final * final) / NPARAM + norm_epsilon)
    delta_share = lax.dynamic_slice_in_dim(final, share_start, share_size)
    new_momentum = momentum_decay * momentum_share + delta_share * inverse
    new_master = master_share - outer_rate * new_momentum
    return (new_brick[None], new_master, new_momentum)


def solution(mesh):
    in_specs = (P("grp", None, "gx", "gy", None), P(), P(), P(), P(), P(), P(), P())
    out_specs = (P("grp", None, "gx", "gy", None), P(("grp", "gx", "gy")), P(("grp", "gx", "gy")))
    return jax.shard_map(
        on_device, mesh=mesh, in_specs=in_specs, out_specs=out_specs, check_vma=False
    )
```

```python
import functools

import jax
import jax.numpy as jnp
import numpy as np
from jax import lax
from jax.experimental import pallas as pl
from jax.experimental.pallas import tpu as pltpu
from jax.sharding import PartitionSpec as P

F = 5
CH = 64
HID = 64
SUB = 16
TCAP = 6
INNER = 3
CELLS = 4096
NPARAM = 17280
TAPS = 27
PAIRS = TCAP // 2
COLS = (SUB + 2) * 128
PATCH = 16 * F
STACK = 3 * PATCH

time_step = 0.1
base_viscosity = 0.02
viscosity_gain = 0.2
buoyancy = 0.5
inner_rate = 0.02
outer_rate = 0.01
momentum_decay = 0.9
norm_epsilon = 1e-06


def patch_position(row):
    group, py, pz = row // 4, row // 2 % 2, row % 2
    ypos = py + 1 if group in (0, 2) else (3 if py == 0 else 0)
    zpos = pz + 1 if group in (0, 1) else (3 if pz == 0 else 0)
    return ypos - 1, zpos - 1


def selections():
    first = np.zeros((4, 256, STACK), np.float32)
    last = np.zeros((4, 256, STACK), np.float32)
    for cell in range(4):
        py, pz = cell // 2, cell % 2
        for kx in range(3):
            for channel in range(F):
                for row in range(16):
                    ypos, zpos = patch_position(row)
                    column = kx * PATCH + channel * 16 + row
                    dy, dz = ypos - py, zpos - pz
                    if abs(dy) <= 1 and abs(dz) <= 1:
                        tap = 9 * kx + 3 * (dy + 1) + dz + 1
                        first[cell, tap * F + channel, column] = 1.0
                        last[cell, channel * TAPS + 26 - tap, column] = 1.0
    return first, last


SELECT_FIRST, SELECT_LAST = selections()


def column_of(place, x_step, y_step):
    gx = lax.rem(place[1] + x_step + place[5], place[5])
    gy = lax.rem(place[2] + y_step + place[4], place[4])
    return gx * place[4] + gy


def owner_apart(owner, groups, place, y_devices, x_devices):
    group, column = divmod(owner, x_devices * y_devices)
    entry = groups - 1 - group
    y_apart = jnp.bitwise_xor(place[2], jnp.int32(column % y_devices))
    return entry, y_apart, jnp.bitwise_xor(place[1], jnp.int32(column // y_devices))


def pick_kernel(y_devices, x_devices, apart, trainer_of, place, *refs):
    near, chosen, owners = refs[:y_devices], refs[y_devices], refs[y_devices + 1]
    wanted = jnp.bitwise_xor(place[1], jnp.int32(apart)) * y_devices + place[2]
    count = jnp.int32(0)
    groups = trainer_of.shape[0] // (x_devices * y_devices)
    for owner in range(trainer_of.shape[0]):
        group, y_apart, x_apart = owner_apart(owner, groups, place, y_devices, x_devices)
        mine = (trainer_of[owner] == wanted) & (x_apart == 0)

        @pl.when(mine)
        def _():
            owners[0, count] = y_apart
            owners[1, count] = group

        count = count + jnp.where(mine, 1, 0)

    def copy_slot(slot, carry):
        for source in range(y_devices):

            @pl.when(owners[0, slot] == source)
            def _():
                chosen[slot] = near[source][owners[1, slot]]

        return carry

    lax.fori_loop(0, count, copy_slot, 0)


def pick_cubes(trainer_of, place, near, y_devices, x_devices, apart):
    vmem = pl.BlockSpec(memory_space=pltpu.VMEM)
    smem = pl.BlockSpec(memory_space=pltpu.SMEM)
    return pl.pallas_call(
        functools.partial(pick_kernel, y_devices, x_devices, apart),
        out_shape=jax.ShapeDtypeStruct((TCAP, *near[0].shape[1:]), near[0].dtype),
        in_specs=[smem, smem] + [vmem] * len(near),
        out_specs=vmem,
        scratch_shapes=[pltpu.SMEM((2, TCAP), jnp.int32)],
        compiler_params=pltpu.CompilerParams(vmem_limit_bytes=16 * 1024 * 1024),
        name="pick_cubes",
    )(trainer_of, place, *near)


def dot_rows(left, right):
    return jnp.dot(left, right, preferred_element_type=jnp.float32)


def dot_lanes(left, right):
    return lax.dot_general(left, right, (((1,), (1,)), ((), ())), preferred_element_type=jnp.float32)


def patch_masks():
    row = lax.broadcasted_iota(jnp.int32, (8, 128), 0)
    lane = lax.broadcasted_iota(jnp.int32, (8, 128), 1)
    z, y = lane % 8, lane // 8 % 8
    even_z, even_y = row % 2 == 0, row // 2 % 2 == 0
    return {
        "centre": row < 4,
        "even_z": even_z,
        "even_y": even_y,
        "gather_z": jnp.where(even_z, z, 7 - z) < 7,
        "gather_y": jnp.where(even_y, y, 7 - y) < 7,
        "scatter_z": jnp.where(even_z, z, 7 - z) > 0,
        "scatter_y": jnp.where(even_y, y, 7 - y) > 0,
    }


def edge_shift(values, step, even, inside, gather):
    before, after = pltpu.roll(values, step, 1), pltpu.roll(values, 128 - step, 1)
    moved = jnp.where(even, after, before) if gather else jnp.where(even, before, after)
    return jnp.where(inside, moved, 0.0)


def patch_stack(rows, masks):
    both = jnp.where(masks["centre"], rows, pltpu.roll(rows, 4, 0))
    y_edge = edge_shift(both, 8, masks["even_y"], masks["gather_y"], True)
    upper = jnp.where(masks["centre"], both, y_edge)
    return upper, edge_shift(upper, 1, masks["even_z"], masks["gather_z"], True)


def patch_fold(upper, lower, masks):
    line = upper + edge_shift(lower, 1, masks["even_z"], masks["scatter_z"], False)
    return line + pltpu.roll(edge_shift(line, 8, masks["even_y"], masks["scatter_y"], False), 4, 0)


def store_planes(ref, x, channels):
    stacked = jnp.concatenate([part for both in channels for part in both], axis=0).astype(jnp.bfloat16)
    for kx in range(3):
        start = pl.multiple_of((x + 2 - kx) * 128, 128)
        ref[kx * PATCH : (kx + 1) * PATCH, pl.ds(start, 128)] = stacked


def train_kernel(y_devices, x_devices, *refs):
    sources = y_devices + x_devices - 1
    (trainer_of, place, first_ref, last_ref, far_first, far_last) = refs[:6]
    arrived = refs[6 : 6 + sources]
    fields_ref = refs[6 + sources]
    delta_first, delta_last, new_fields_ref = refs[7 + sources : 10 + sources]
    (
        slots,
        picked,
        cubes,
        big_first,
        big_last,
        big_last_t,
        grad_first,
        grad_last,
        now_first,
        now_last,
        brick,
        select_first,
        select_last,
        slot_sems,
        field_sem,
        select_sems,
        *pair_refs,
    ) = refs[10 + sources :]
    targets, tables, inputs, errors, hiddens, pre_grads, slopes, partial_out, raw = [
        pair_refs[kind * PAIRS : (kind + 1) * PAIRS] for kind in range(9)
    ]

    field_in = pltpu.make_async_copy(fields_ref, brick, field_sem)
    field_out = pltpu.make_async_copy(brick, new_fields_ref, field_sem)
    select_copies = [
        pltpu.make_async_copy(far_first, select_first, select_sems.at[0]),
        pltpu.make_async_copy(far_last, select_last, select_sems.at[1]),
    ]

    column = place[1] * y_devices + place[2]
    for other in range(x_devices):
        picked[other] = 0
    count = jnp.int32(0)
    groups = trainer_of.shape[0] // (x_devices * y_devices)
    for owner in range(trainer_of.shape[0]):
        group, y_apart, x_apart = owner_apart(owner, groups, place, y_devices, x_devices)
        mine = trainer_of[owner] == column

        @pl.when(mine)
        def _():
            near = x_apart == 0
            slots[0, count] = jnp.where(near, y_apart, y_devices - 1 + x_apart)
            slots[1, count] = jnp.where(near, group, picked[x_apart])
            picked[x_apart] = picked[x_apart] + 1

        count = count + jnp.where(mine, 1, 0)

    def fetch(slot, wait):
        for source in range(sources):

            @pl.when((slot < count) & (slots[0, slot] == source))
            def _():
                copy = pltpu.make_async_copy(
                    arrived[source].at[slots[1, slot]], cubes.at[slot], slot_sems.at[slot]
                )
                copy.wait() if wait else copy.start()

    for slot in range(TCAP):
        fetch(slot, False)

    for copy in select_copies:
        copy.start()
    field_in.start()
    for slot in range(TCAP):

        @pl.when(slot >= count)
        def _():
            cubes[slot] = jnp.zeros(cubes.shape[1:], jnp.bfloat16)

    masks = patch_masks()
    for ref in (*errors, *inputs):
        ref[:PATCH, 128:256] = jnp.zeros((PATCH, 128), jnp.bfloat16)
        ref[2 * PATCH :, COLS - 256 : COLS - 128] = jnp.zeros((PATCH, 128), jnp.bfloat16)
    for ref in partial_out:
        ref[:, :128] = jnp.zeros((STACK, 128), jnp.float32)
        ref[:, COLS - 128 :] = jnp.zeros((STACK, 128), jnp.float32)
    lane = lax.broadcasted_iota(jnp.int32, (8, 128), 1)
    full_weight = 2.0 * (1.0 / (jnp.full((8, 128), count, jnp.int32).astype(jnp.float32) * CELLS))
    weights = [
        jnp.where(lane // 64 + 2 * pair < count, full_weight, 0.0) for pair in range(PAIRS)
    ]
    start_first = first_ref[...].astype(jnp.bfloat16).astype(jnp.float32)
    start_last = last_ref[...].T.astype(jnp.bfloat16).astype(jnp.float32)
    now_first[...] = start_first
    now_last[...] = start_last

    for slot in range(TCAP):
        fetch(slot, True)

    low_lanes = lax.broadcasted_iota(jnp.int32, (SUB * F * 2, 128), 1) < 64
    for pair in range(PAIRS):
        for kind, ref in enumerate((tables[pair], targets[pair])):
            rows = slice(kind * SUB * F * 2, (kind + 1) * SUB * F * 2)
            even = cubes[2 * pair, rows, :].astype(jnp.float32)
            odd = cubes[2 * pair + 1, rows, :].astype(jnp.float32)
            ref[0] = jnp.where(low_lanes, even, pltpu.roll(odd, 64, 1))
            ref[1] = jnp.where(low_lanes, pltpu.roll(even, 64, 1), odd)

    def patch_cells(ref, quarter, plane, channel):
        start = pl.multiple_of(channel * 32 + quarter % 2 * 16 + plane // 2 * 8, 8)
        rows = ref[quarter // 2, pl.ds(start, 8), :]
        return rows if plane % 2 == 0 else pltpu.roll(rows, 4, 0)

    def stack_planes(quarter, carry):
        for pair in range(PAIRS):
            for plane in range(4):
                x = quarter * 4 + plane
                channels = [
                    patch_stack(patch_cells(tables[pair], quarter, plane, c), masks) for c in range(F)
                ]
                store_planes(inputs[pair], x, channels)
        return carry

    lax.fori_loop(0, 4, stack_planes, 0, unroll=2)

    for copy in select_copies:
        copy.wait()
    field_in.wait()
    field_out.start()

    def train_step(step, step_carry):
        first_now = now_first[...].astype(jnp.bfloat16)
        last_now = now_last[...].astype(jnp.bfloat16)
        for cell in range(4):
            rows = slice(cell * CH, (cell + 1) * CH)
            big_first[rows, :] = (0.5 * dot_rows(first_now, select_first[cell])).astype(jnp.bfloat16)
            spread_last = dot_rows(last_now, select_last[cell])
            big_last[rows, :] = (0.5 * spread_last).astype(jnp.bfloat16)
            big_last_t[:, rows] = spread_last.T.astype(jnp.bfloat16)
        grad_first[...] = jnp.zeros(grad_first.shape, jnp.float32)
        grad_last[...] = jnp.zeros(grad_last.shape, jnp.float32)

        def columns_of(quarter):
            return pl.ds(pl.multiple_of(quarter * 512 + 128, 128), 512)

        def first_layer(pair, quarter):
            columns = columns_of(quarter)
            raw[pair][:, columns] = dot_rows(big_first[...], inputs[pair][:, columns])

        def activate(pair, quarter):
            columns = columns_of(quarter)
            for part in range(8):
                rows = slice(part * 32, (part + 1) * 32)
                half = raw[pair][rows, columns]
                curve = jnp.tanh(half)
                above = 1.0 + curve
                value = half * above
                hiddens[pair][rows, columns] = value.astype(jnp.bfloat16)
                slopes[pair][rows, columns] = above + value * (1.0 - curve)

        def last_layer(pair, quarter):
            columns = columns_of(quarter)
            partial_out[pair][:, columns] = dot_rows(big_last_t[...], hiddens[pair][:, columns])

        def find_errors(pair, quarter):
            for plane in range(4):
                x = quarter * 4 + plane
                column = pl.multiple_of((x + 1) * 128, 128)
                total = (
                    partial_out[pair][0:PATCH, pl.ds(pl.multiple_of(column + 128, 128), 128)]
                    + partial_out[pair][PATCH : 2 * PATCH, pl.ds(column, 128)]
                    + partial_out[pair][2 * PATCH :, pl.ds(pl.multiple_of(column - 128, 128), 128)]
                )
                channels = []
                for c in range(F):
                    predicted = patch_fold(
                        total[16 * c : 16 * c + 8], total[16 * c + 8 : 16 * c + 16], masks
                    )
                    wanted = patch_cells(targets[pair], quarter, plane, c)
                    error = weights[pair] * (predicted - wanted)
                    channels.append(patch_stack(error, masks))
                store_planes(errors[pair], x, channels)

        def hidden_layer(pair, quarter):
            columns = columns_of(quarter)
            raw[pair][:, columns] = dot_rows(big_last[...], errors[pair][:, columns])

        def scale(pair, quarter):
            columns = columns_of(quarter)
            for part in range(8):
                rows = slice(part * 32, (part + 1) * 32)
                product = raw[pair][rows, columns] * slopes[pair][rows, columns]
                pre_grads[pair][rows, columns] = product.astype(jnp.bfloat16)

        def gradients(pair, quarter):
            columns = columns_of(quarter)
            grad_first[...] += dot_lanes(pre_grads[pair][:, columns], inputs[pair][:, columns])
            grad_last[...] += dot_lanes(hiddens[pair][:, columns], errors[pair][:, columns])

        stages = (first_layer, activate, last_layer, find_errors, hidden_layer, scale, gradients)
        for turn in range(len(stages) + PAIRS - 1):

            def run(quarter, carry):
                for pair in range(PAIRS):
                    if 0 <= turn - pair < len(stages):
                        stages[turn - pair](pair, quarter)
                return carry

            lax.fori_loop(0, 4, run, 0, unroll=4)

        def folded(grad, select_ref):
            total = jnp.zeros((3 * CH, 256), jnp.float32)
            for cell in range(4):
                rest = grad[cell * CH : (cell + 1) * CH, :]
                parts = []
                for _ in range(3):
                    parts.append(rest.astype(jnp.bfloat16))
                    rest = rest - parts[-1].astype(jnp.float32)
                total = total + dot_lanes(jnp.concatenate(parts, axis=0), select_ref[cell])
            return total[:CH] + total[CH : 2 * CH] + total[2 * CH :]

        now_first[...] = now_first[...] - inner_rate * folded(grad_first, select_first)
        now_last[...] = now_last[...] - inner_rate * folded(grad_last, select_last)
        return step_carry

    lax.fori_loop(0, INNER, train_step, 0)
    delta_first[...] = start_first - now_first[...]
    delta_last[...] = (start_last - now_last[...]).T
    field_out.wait()


def train_cubes(trainer_of, place, first, last, selects, arrived, fields, y_devices, x_devices):
    vmem = pl.BlockSpec(memory_space=pltpu.VMEM)
    smem = pl.BlockSpec(memory_space=pltpu.SMEM)
    anywhere = pl.BlockSpec(memory_space=pl.ANY)
    hbm = pl.BlockSpec(memory_space=pltpu.HBM)
    return pl.pallas_call(
        functools.partial(train_kernel, y_devices, x_devices),
        out_shape=(
            jax.ShapeDtypeStruct((CH, 256), jnp.float32),
            jax.ShapeDtypeStruct((256, CH), jnp.float32),
            jax.ShapeDtypeStruct(fields.shape, fields.dtype),
        ),
        in_specs=[smem] * 2 + [vmem] * 2 + [hbm] * 2 + [anywhere] * len(arrived) + [hbm],
        out_specs=(vmem, vmem, hbm),
        scratch_shapes=[
            pltpu.SMEM((2, TCAP), jnp.int32),
            pltpu.SMEM((x_devices,), jnp.int32),
            pltpu.VMEM((TCAP, 4 * SUB * F, 128), jnp.bfloat16),
            pltpu.VMEM((4 * CH, STACK), jnp.bfloat16),
            pltpu.VMEM((4 * CH, STACK), jnp.bfloat16),
            pltpu.VMEM((STACK, 4 * CH), jnp.bfloat16),
            pltpu.VMEM((4 * CH, STACK), jnp.float32),
            pltpu.VMEM((4 * CH, STACK), jnp.float32),
            pltpu.VMEM((CH, 256), jnp.float32),
            pltpu.VMEM((CH, 256), jnp.float32),
            pltpu.VMEM(fields.shape, fields.dtype),
            pltpu.VMEM((4, 256, STACK), jnp.bfloat16),
            pltpu.VMEM((4, 256, STACK), jnp.bfloat16),
            pltpu.SemaphoreType.DMA((TCAP,)),
            pltpu.SemaphoreType.DMA,
            pltpu.SemaphoreType.DMA((2,)),
        ]
        + [pltpu.VMEM((2, SUB * F * 2, 128), jnp.float32)] * (2 * PAIRS)
        + [pltpu.VMEM((STACK, COLS), jnp.bfloat16)] * (2 * PAIRS)
        + [pltpu.VMEM((4 * CH, COLS), jnp.bfloat16)] * (2 * PAIRS)
        + [pltpu.VMEM((4 * CH, COLS), jnp.float32)] * PAIRS
        + [pltpu.VMEM((STACK, COLS), jnp.float32)] * PAIRS
        + [pltpu.VMEM((4 * CH, COLS), jnp.float32)] * PAIRS,
        compiler_params=pltpu.CompilerParams(vmem_limit_bytes=52 * 1024 * 1024),
        name="train_cubes",
    )(
        trainer_of,
        place,
        first,
        last,
        *selects,
        *arrived,
        fields,
    )


def viscosity_of(cells, closure):
    def unit(h, total):
        half = closure[F, h] + closure[0, h] * cells[0]
        for f in range(1, F):
            half = half + closure[f, h] * cells[f]
        return total + closure[F + 1, h] * (half * jnp.tanh(half))

    total = closure[F, HID] + closure[0, HID] * cells[0]
    for f in range(1, F):
        total = total + closure[f, HID] * cells[f]
    total = lax.fori_loop(0, HID, unit, total, unroll=8)
    soft = jnp.maximum(total, 0.0) + jnp.log1p(jnp.exp(-jnp.abs(total)))
    return base_viscosity + viscosity_gain * soft


def viscosity_kernel(closure, place, fields, viscosity, x_edges, y_edges, weights, out_column):
    y_cells, z_cells = fields.shape[2:]
    x, x_cells = pl.program_id(0), pl.num_programs(0)
    up_first = lax.rem(place[2], 2) == 0
    for f in range(F):
        low, high = fields[f, 0, 0:1, :], fields[f, 0, y_cells - 1 : y_cells, :]
        y_edges[0, f, pl.ds(x, 1), :] = jnp.where(up_first, high, low)
        y_edges[1, f, pl.ds(x, 1), :] = jnp.where(up_first, low, high)

    @pl.when(x == x_cells - 1)
    def _():
        x_edges[1] = fields[:, 0]

    @pl.when(x == 0)
    def _():
        x_edges[0] = fields[:, 0]
        plain = closure[...]
        high = plain.astype(jnp.bfloat16).astype(jnp.float32)
        low = plain - high
        blank = jnp.zeros((8, 128), jnp.float32)
        for j in range(8):
            turned = [pltpu.roll(part, j, 0) if j else part for part in (high, high, low)]
            stacked = jnp.concatenate([*turned, blank], axis=0)
            weights[j] = stacked.T[: HID + 8].astype(jnp.bfloat16)
        out_column[...] = jnp.broadcast_to(plain.T[:HID, F + 1 : F + 2], (HID, 128))

    sublane = lax.broadcasted_iota(jnp.int32, (8, z_cells), 0)
    wide = z_cells // 128
    tiles = y_cells // 8

    def tile(index, carry):
        rows = pl.ds(pl.multiple_of(index * 8, 8), 8)
        turned = [fields[f, 0, rows, :] for f in range(F)]
        turned = [pltpu.roll(turned[f], f, 0) if f else turned[f] for f in range(F)]
        sums = jnp.zeros((8, z_cells), jnp.float32)
        for j in range(8):
            cells = jnp.where(sublane == (j + F) % 8, 1.0, 0.0)
            for f in range(F):
                cells = jnp.where(sublane == (j + f) % 8, turned[f], cells)
            top = cells.astype(jnp.bfloat16).astype(jnp.float32)
            stacked = jnp.concatenate([top, cells - top, top, jnp.zeros_like(top)], axis=0)
            half = dot_rows(weights[j], stacked.astype(jnp.bfloat16))
            total = half[HID:]
            for group in range(HID // 8):
                part = half[group * 8 : group * 8 + 8]
                column = jnp.concatenate([out_column[group * 8 : group * 8 + 8, :]] * wide, axis=1)
                total = total + column * (part * jnp.tanh(part))
            for step in (4, 2, 1):
                total = total + pltpu.roll(total, step, 0)
            sums = jnp.where(sublane == j, total, sums)
        soft = jnp.maximum(sums, 0.0) + jnp.log1p(jnp.exp(-jnp.abs(sums)))
        viscosity[0, rows, :] = base_viscosity + viscosity_gain * soft
        return carry

    lax.fori_loop(0, tiles, tile, 0)


def brick_viscosity(closure, place, fields):
    count, x_cells, y_cells, z_cells = fields.shape
    return pl.pallas_call(
        viscosity_kernel,
        out_shape=(
            jax.ShapeDtypeStruct(fields.shape[1:], fields.dtype),
            jax.ShapeDtypeStruct((2, count, y_cells, z_cells), fields.dtype),
            jax.ShapeDtypeStruct((2, count, x_cells, z_cells), fields.dtype),
        ),
        grid=(x_cells,),
        in_specs=[
            pl.BlockSpec((8, 128), lambda x: (0, 0)),
            pl.BlockSpec(memory_space=pltpu.SMEM),
            pl.BlockSpec((count, 1, y_cells, z_cells), lambda x: (0, x, 0, 0)),
        ],
        out_specs=(
            pl.BlockSpec((1, y_cells, z_cells), lambda x: (x, 0, 0)),
            pl.BlockSpec((2, count, y_cells, z_cells), lambda x: (0, 0, 0, 0)),
            pl.BlockSpec((2, count, x_cells, z_cells), lambda x: (0, 0, 0, 0)),
        ),
        scratch_shapes=[
            pltpu.VMEM((8, HID + 8, 32), jnp.bfloat16),
            pltpu.VMEM((HID, 128), jnp.float32),
        ],
        compiler_params=pltpu.CompilerParams(vmem_limit_bytes=16 * 1024 * 1024),
        name="brick_viscosity",
    )(closure, place, fields)


def evolve_kernel(place, viscosity, fields, x_halo, y_first, y_second, new_fields):
    up_first = lax.rem(place[2], 2) == 0
    x_cells, y_cells, z_cells = fields.shape[1:]
    row = lax.broadcasted_iota(jnp.int32, (y_cells, z_cells), 0)
    lane = lax.broadcasted_iota(jnp.int32, (y_cells, z_cells), 1)

    def plane(x, carry):
        centre = [fields[f, x] for f in range(F)]
        below = jnp.maximum(x - 1, 0)
        above = jnp.minimum(x + 1, x_cells - 1)
        for f in range(F):
            value = centre[f]
            west = jnp.where(x == 0, x_halo[1, f], fields[f, below])
            east = jnp.where(x == x_cells - 1, x_halo[0, f], fields[f, above])
            first, second = y_first[f, pl.ds(x, 1), :], y_second[f, pl.ds(x, 1), :]
            south = jnp.where(
                row == 0, jnp.where(up_first, second, first), pltpu.roll(value, 1, 0)
            )
            north = jnp.where(
                row == y_cells - 1,
                jnp.where(up_first, first, second),
                pltpu.roll(value, y_cells - 1, 0),
            )
            lower = jnp.where(lane == 0, 0.0, pltpu.roll(value, 1, 1))
            upper = jnp.where(lane == z_cells - 1, 0.0, pltpu.roll(value, z_cells - 1, 1))
            laplacian = east + west + north + south + upper + lower - 6.0 * value
            advection = (
                centre[0] * (east - west) + centre[1] * (north - south) + centre[2] * (upper - lower)
            )
            tendency = viscosity[x] * laplacian - 0.5 * advection
            if f == 2:
                tendency = tendency + buoyancy * centre[3]
            new_fields[f, x] = value + time_step * tendency
        return carry

    lax.fori_loop(0, x_cells, plane, 0)


def evolve(place, viscosity, fields, x_halo, y_first, y_second):
    vmem = pl.BlockSpec(memory_space=pltpu.VMEM)
    return pl.pallas_call(
        evolve_kernel,
        out_shape=jax.ShapeDtypeStruct(fields.shape, fields.dtype),
        in_specs=[pl.BlockSpec(memory_space=pltpu.SMEM)] + [vmem] * 5,
        out_specs=vmem,
        compiler_params=pltpu.CompilerParams(vmem_limit_bytes=16 * 1024 * 1024),
        name="evolve_brick",
    )(place, viscosity, fields, x_halo, y_first, y_second)


def cell_order():
    order = np.zeros((256, 256), np.float32)
    for y in range(SUB):
        for z in range(SUB):
            order[y * SUB + z, (y % 2 * 2 + z % 2) * 64 + y // 2 * 8 + z // 2] = 1.0
    return order


CELL_ORDER = cell_order()


def corner_of(sample_block, place, x_step, y_step, y_cells, z_cells):
    x_devices, y_devices = place[5], place[4]
    gx = lax.rem(place[1] + x_step + x_devices, x_devices)
    gy = lax.rem(place[2] + y_step + y_devices, y_devices)
    group = jnp.minimum(place[0], place[3] - 1)
    block = sample_block[(group * x_devices + gx) * y_devices + gy]
    z_blocks = z_cells // SUB
    return lax.rem(lax.div(block, z_blocks), y_cells // SUB) * SUB, lax.rem(block, z_blocks) * SUB


def thin_kernel(
    y_cells, z_cells, sample_block, place, rows_ref, lines_ref, thin, x_buffer, y_buffer, x_sems, y_sems
):
    def corner(x_step, y_step):
        return corner_of(sample_block, place, x_step, y_step, y_cells, z_cells)

    lane = lax.broadcasted_iota(jnp.int32, (SUB, 128), 1)
    signs = (-1, 1)
    copies = []
    for side, sign in enumerate(signs):
        z_x, z_y = corner(sign, 0)[1], corner(0, sign)[1]
        x, y = side * (SUB - 1), side * (y_cells - 8)
        for field in range(F):
            copies.append(
                pltpu.make_async_copy(
                    rows_ref.at[
                        pl.ds((field * SUB + x) * y_cells, y_cells),
                        pl.ds(pl.multiple_of(lax.div(z_x, 128) * 128, 128), 128),
                    ],
                    x_buffer.at[pl.ds((side * 8 + field) * y_cells, y_cells)],
                    x_sems.at[side, field],
                )
            )
        copies.append(
            pltpu.make_async_copy(
                lines_ref.at[:, pl.ds(y, 8), pl.ds(pl.multiple_of(lax.div(z_y, 128) * 128, 128), 128)],
                y_buffer.at[side],
                y_sems.at[side],
            )
        )
    for copy in copies:
        copy.start()
    thin[...] = jnp.zeros(thin.shape, thin.dtype)
    for copy in copies:
        copy.wait()

    def moved(values, z, lane_start):
        return pltpu.roll(values, lax.rem(lane_start - lax.rem(z, 128) + 256, 128), 1)

    for side, sign in enumerate(signs):
        z = corner(0, sign)[1]
        total = jnp.zeros((SUB, 128), jnp.float32)
        for field in range(F):
            part = y_buffer[side, field * SUB : (field + 1) * SUB, side * 7, :]
            total = jnp.where(lane // SUB == field, moved(part, z, field * SUB), total)
        thin[column_of(place, 0, sign), :, side * 128 : (side + 1) * 128] = total
    for side, sign in enumerate(signs):
        y, z = corner(sign, 0)
        for half in range(2):
            total = jnp.zeros((8, 128), jnp.float32)
            for step in range(8):
                row = side * 8 * y_cells + y + half * 8 + step
                part = moved(x_buffer[pl.ds(row, 8, y_cells), :], z, step * SUB)
                total = jnp.where(lane[:8] // SUB == step, part, total)
            at = (column_of(place, sign, 0), slice(side * 8, side * 8 + 8), slice(half * 128, half * 128 + 128))
            thin[at] = total


def thin_faces(sample_block, place, brick, columns):
    fields, x_cells, y_cells, z_cells = brick.shape
    vmem = pl.BlockSpec(memory_space=pltpu.VMEM)
    smem = pl.BlockSpec(memory_space=pltpu.SMEM)
    hbm = pl.BlockSpec(memory_space=pltpu.HBM)
    return pl.pallas_call(
        functools.partial(thin_kernel, y_cells, z_cells),
        out_shape=jax.ShapeDtypeStruct((columns, SUB, 256), jnp.float32),
        in_specs=[smem, smem, hbm, hbm],
        out_specs=vmem,
        scratch_shapes=[
            pltpu.VMEM((16 * y_cells, 128), jnp.float32),
            pltpu.VMEM((2, fields * x_cells, 8, 128), jnp.float32),
            pltpu.SemaphoreType.DMA((2, fields)),
            pltpu.SemaphoreType.DMA((2,)),
        ],
        compiler_params=pltpu.CompilerParams(vmem_limit_bytes=16 * 1024 * 1024),
        name="thin_faces",
    )(
        sample_block,
        place,
        brick.reshape(fields * x_cells * y_cells, z_cells),
        brick.reshape(fields * x_cells, y_cells, z_cells),
    )


def sample_kernel(
    y_cells,
    z_cells,
    sample_block,
    place,
    brick,
    centre,
    lower,
    upper,
    own_rows,
    windows,
    sems,
):
    rows_of_x = y_cells
    rows_of_field = SUB * y_cells
    window_rows = F * rows_of_field

    def corner(x_step, y_step):
        return corner_of(sample_block, place, x_step, y_step, y_cells, z_cells)

    y_start, z_start = corner(0, 0)
    z_below = jnp.maximum(z_start - 1, 0)
    z_above = jnp.minimum(z_start + SUB, z_cells - 1)
    first_window = lax.div(z_below, 128)
    second_window = jnp.minimum(first_window + 1, z_cells // 128 - 1)
    copies = [
        pltpu.make_async_copy(
            brick.at[:, pl.ds(pl.multiple_of(at * 128, 128), 128)],
            windows.at[pl.ds(slot * window_rows, window_rows)],
            sems.at[slot],
        )
        for slot, at in enumerate((first_window, second_window))
    ]
    for copy in copies:
        copy.start()
    for copy in copies:
        copy.wait()

    def window(row, z):
        slot = lax.div(z, 128) - first_window
        return windows[pl.ds(slot * window_rows + row, SUB, rows_of_x), :]

    lane = lax.broadcasted_iota(jnp.int32, (SUB, 128), 1)
    for field in range(F):
        for half in range(2):
            inside = jnp.zeros((SUB, 128), jnp.float32)
            below = jnp.zeros((SUB, 128), jnp.float32)
            above = jnp.zeros((SUB, 128), jnp.float32)
            for step in range(8):
                row = field * rows_of_field + y_start + half * 8 + step
                first = step * SUB
                values = jnp.where(lane == 127, window(row, z_below), window(row, z_start))
                values = jnp.where(lane == 0, window(row, z_above), values)
                values = pltpu.roll(values, lax.rem(first - lax.rem(z_start, 128) + 256, 128), 1)
                inside = jnp.where(lane // SUB == step, values, inside)
                below = jnp.where(lane == (first - 1) % 128, values, below)
                above = jnp.where(lane == (first + SUB) % 128, values, above)
            below = jnp.where(z_start == 0, 0.0, pltpu.roll(below, 1, 1))
            above = jnp.where(z_start + SUB == z_cells, 0.0, pltpu.roll(above, 127, 1))
            at = (slice(field * SUB, (field + 1) * SUB), slice(half * 128, (half + 1) * 128))
            centre[at] = inside
            lower[at] = jnp.where(lane % SUB == 0, below, pltpu.roll(inside, 1, 1))
            upper[at] = jnp.where(lane % SUB == SUB - 1, above, pltpu.roll(inside, 127, 1))

    def y_row(y, z):
        total = jnp.zeros((SUB, 128), jnp.float32)
        for field in range(F):
            part = window(field * rows_of_field + y, z)
            part = pltpu.roll(part, lax.rem(field * SUB - lax.rem(z, 128) + 256, 128), 1)
            total = jnp.where(lane // SUB == field, part, total)
        return total

    own_rows[0] = y_row(jnp.maximum(y_start - 1, 0), z_start)
    own_rows[1] = y_row(jnp.minimum(y_start + SUB, y_cells - 1), z_start)

def sample_cube(sample_block, place, brick):
    fields, x_cells, y_cells, z_cells = brick.shape
    vmem = pl.BlockSpec(memory_space=pltpu.VMEM)
    smem = pl.BlockSpec(memory_space=pltpu.SMEM)
    hbm = pl.BlockSpec(memory_space=pltpu.HBM)
    rows = fields * x_cells * y_cells
    cube = jax.ShapeDtypeStruct((F * SUB, 256), jnp.float32)
    return pl.pallas_call(
        functools.partial(sample_kernel, y_cells, z_cells),
        out_shape=(
            cube,
            cube,
            cube,
            jax.ShapeDtypeStruct((2, SUB, 128), jnp.float32),
        ),
        in_specs=[smem, smem, hbm],
        out_specs=(vmem,) * 4,
        scratch_shapes=[
            pltpu.VMEM((2 * rows, 128), jnp.float32),
            pltpu.SemaphoreType.DMA((2,)),
        ],
        compiler_params=pltpu.CompilerParams(vmem_limit_bytes=16 * 1024 * 1024),
        cost_estimate=pl.CostEstimate(flops=0, bytes_accessed=16_000_000, transcendentals=0),
        name="sample_cube",
    )(sample_block, place, brick.reshape(rows, z_cells))


def change_kernel(
    y_cells,
    z_cells,
    sample_block,
    place,
    closure,
    order,
    centre,
    lower,
    upper,
    own_rows,
    thin,
    payload,
    table,
):
    y_start = corner_of(sample_block, place, 0, 0, y_cells, z_cells)[0]
    row = lax.broadcasted_iota(jnp.int32, (SUB, 256), 0)
    lane = lax.broadcasted_iota(jnp.int32, (SUB, 256), 1)
    south_row = jnp.where(y_start == 0, thin[column_of(place, 0, -1), :, 128:], own_rows[0])
    north_row = jnp.where(y_start + SUB == y_cells, thin[column_of(place, 0, 1), :, :128], own_rows[1])
    face_low = thin[column_of(place, -1, 0), 8:, :]
    face_high = thin[column_of(place, 1, 0), :8, :]
    cells = [centre[f * SUB : (f + 1) * SUB, :] for f in range(F)]
    viscosity = viscosity_of(cells, closure)
    changes = []
    for f in range(F):
        value = cells[f]
        west = jnp.where(row == 0, face_low[f : f + 1, :], pltpu.roll(value, 1, 0))
        east = jnp.where(row == SUB - 1, face_high[f : f + 1, :], pltpu.roll(value, SUB - 1, 0))
        edge = pltpu.roll(south_row, (128 - f * SUB) % 128, 1)
        south = jnp.where(lane < SUB, jnp.concatenate([edge, edge], 1), pltpu.roll(value, SUB, 1))
        edge = pltpu.roll(north_row, 112 - f * SUB, 1)
        north = jnp.where(
            lane >= 256 - SUB, jnp.concatenate([edge, edge], 1), pltpu.roll(value, 256 - SUB, 1)
        )
        down = lower[f * SUB : (f + 1) * SUB, :]
        up = upper[f * SUB : (f + 1) * SUB, :]
        laplacian = east + west + north + south + up + down - 6.0 * value
        advection = cells[0] * (east - west) + cells[1] * (north - south) + cells[2] * (up - down)
        change = viscosity * laplacian - 0.5 * advection
        if f == 2:
            change = change + buoyancy * cells[3]
        changes.append(change)
    ordered = dot_rows(jnp.concatenate(cells + changes, axis=0).astype(jnp.bfloat16), order[...])
    low_lanes = lane[:8, :128] < 64
    for part in range(2 * F):
        for cell in range(4):
            columns = slice(cell // 2 * 128, cell // 2 * 128 + 128)
            low = ordered[part * SUB : part * SUB + 8, columns]
            high = ordered[part * SUB + 8 : part * SUB + SUB, columns]
            if cell % 2 == 0:
                high = pltpu.roll(high, 64, 1)
            else:
                low = pltpu.roll(low, 64, 1)
            table[pl.ds(part * 32 + cell, 8, 4), :] = jnp.where(low_lanes, low, high)
    payload[...] = table[...].astype(jnp.bfloat16)


def cube_change(sample_block, place, closure, cube, thin, y_cells, z_cells):
    vmem = pl.BlockSpec(memory_space=pltpu.VMEM)
    smem = pl.BlockSpec(memory_space=pltpu.SMEM)
    return pl.pallas_call(
        functools.partial(change_kernel, y_cells, z_cells),
        out_shape=jax.ShapeDtypeStruct((4 * F * SUB, 128), jnp.bfloat16),
        in_specs=[smem] * 3 + [vmem] * 6,
        out_specs=vmem,
        scratch_shapes=[pltpu.VMEM((4 * F * SUB, 128), jnp.float32)],
        compiler_params=pltpu.CompilerParams(vmem_limit_bytes=16 * 1024 * 1024),
        name="cube_change",
    )(sample_block, place, closure, jnp.asarray(CELL_ORDER, jnp.bfloat16), *cube, thin)


def on_device(
    fields, closure_in, closure_bias, closure_out, master, momentum, sample_block, sample_trainer
):
    group_count = lax.axis_size("grp")
    x_devices = lax.axis_size("gx")
    y_devices = lax.axis_size("gy")
    trainers = x_devices * y_devices
    my_group = lax.axis_index("grp")
    my_column = lax.axis_index("gx") * y_devices + lax.axis_index("gy")
    is_trainer = my_group == group_count - 1
    everyone = ("grp", "gx", "gy")
    sim_groups = group_count - 1
    first_trainer = sim_groups * trainers
    brick = fields[0]
    y_cells, z_cells = brick.shape[2:]
    closure = jnp.concatenate(
        [0.5 * closure_in.T, 0.5 * closure_bias[None], closure_out[None]], axis=0
    )
    linear = jnp.sum(closure * closure_out[None], axis=1, keepdims=True)
    closure = jnp.pad(jnp.concatenate([closure, linear], axis=1), ((0, 1), (0, 127 - HID)))
    place = jnp.stack(
        [
            my_group,
            lax.axis_index("gx"),
            lax.axis_index("gy"),
            jnp.int32(sim_groups),
            jnp.int32(y_devices),
            jnp.int32(x_devices),
        ]
    ).astype(jnp.int32)

    def pairs(x_step, even_step):
        found = []
        for g in range(sim_groups):
            for c in range(trainers):
                gx, gy = c // y_devices, c % y_devices
                gx = (gx + x_step) % x_devices
                gy = (gy + (even_step if gy % 2 == 0 else -even_step)) % y_devices
                found.append((g * trainers + c, (g * x_devices + gx) * y_devices + gy))
        return found

    def x_neighbours(edges):
        if x_devices == 2:
            return lax.ppermute(edges, everyone, pairs(1, 0))
        from_high = lax.ppermute(edges[0], everyone, pairs(-1, 0))
        return jnp.stack([from_high, lax.ppermute(edges[1], everyone, pairs(1, 0))])

    def y_neighbours(for_first, for_second):
        return (
            lax.ppermute(for_first, everyone, pairs(0, 1)),
            lax.ppermute(for_second, everyone, pairs(0, -1)),
        )

    def swap(distance):
        return [(first_trainer + c, first_trainer + (c ^ distance)) for c in range(trainers)]

    def to_trainers(payload):
        landed = [
            lax.ppermute(
                payload, everyone, [(g * trainers + c, first_trainer + c) for c in range(trainers)]
            )
            for g in reversed(range(sim_groups))
        ]
        return jnp.stack(landed)

    def from_line(held):
        return [lax.ppermute(held, everyone, swap(apart)) for apart in range(1, y_devices)]

    def across(apart, held):
        return lax.ppermute(held, everyone, swap(apart * y_devices))

    thin = thin_faces(sample_block, place, brick, trainers)
    cube = sample_cube(sample_block, place, brick)
    first_count = CH * TAPS * F
    first = jnp.pad(master[:first_count].reshape(CH, TAPS * F), ((0, 0), (0, 256 - TAPS * F)))
    last = jnp.pad(master[first_count:].reshape(TAPS * F, CH), ((0, 256 - TAPS * F), (0, 0)))

    *cube, first, last = lax.optimization_barrier((*cube, first, last))
    selects = lax.optimization_barrier(
        (jnp.asarray(SELECT_FIRST, jnp.bfloat16), jnp.asarray(SELECT_LAST, jnp.bfloat16))
    )

    thin = lax.all_to_all(thin, ("gx", "gy"), split_axis=0, concat_axis=0, tiled=True)
    payload = cube_change(sample_block, place, closure, cube, thin, y_cells, z_cells)
    landed = to_trainers(payload)
    closure, landed = lax.optimization_barrier((closure, landed))

    fields_count, x_cells = brick.shape[:2]
    viscosity, x_edges, y_edges = lax.cond(
        is_trainer,
        lambda: (
            jnp.zeros((x_cells, y_cells, z_cells), jnp.float32),
            jnp.zeros((2, fields_count, y_cells, z_cells), jnp.float32),
            jnp.zeros((2, fields_count, x_cells, z_cells), jnp.float32),
        ),
        lambda: brick_viscosity(closure, place, brick),
    )
    halo = (x_neighbours(x_edges), *y_neighbours(y_edges[0], y_edges[1]))
    near = [landed, *from_line(landed)]
    far = [
        across(apart, pick_cubes(sample_trainer, place, near, y_devices, x_devices, apart))
        for apart in range(1, x_devices)
    ]
    arrived = [*near, *far]

    def train_here():
        delta_first, delta_last, new_brick = train_cubes(
            sample_trainer, place, first, last, selects, arrived, brick, y_devices, x_devices
        )
        delta = jnp.concatenate(
            [delta_first[:, : TAPS * F].reshape(-1), delta_last[: TAPS * F].reshape(-1)]
        )
        return delta, new_brick

    def evolve_here():
        new_brick = evolve(place, viscosity, brick, *halo)
        return jnp.zeros((NPARAM,), jnp.float32), new_brick

    delta, new_brick = lax.cond(is_trainer, train_here, evolve_here)

    held = delta
    for g in reversed(range(sim_groups)):
        held = held + lax.ppermute(
            delta, everyone, [(first_trainer + c, g * trainers + c) for c in range(trainers)]
        )
    final = delta
    for first_apart in range(1, trainers, group_count):
        meets = [
            (g * trainers + c, g * trainers + (c ^ (first_apart + g)))
            for g in range(group_count)
            for c in range(trainers)
            if first_apart + g < trainers
        ]
        final = final + lax.ppermute(held, everyone, meets)
    for apart in (1, 2):
        final = final + lax.ppermute(
            final,
            everyone,
            [(g * trainers + c, (g ^ apart) * trainers + c) for g in range(group_count) for c in range(trainers)],
        )

    share_size = NPARAM // (group_count * trainers)
    share_start = (my_group * trainers + my_column) * share_size
    momentum_share = lax.dynamic_slice_in_dim(momentum, share_start, share_size)
    master_share = lax.dynamic_slice_in_dim(master, share_start, share_size)
    inverse = 1.0 / jnp.sqrt(jnp.sum(final * final) / NPARAM + norm_epsilon)
    delta_share = lax.dynamic_slice_in_dim(final, share_start, share_size)
    new_momentum = momentum_decay * momentum_share + delta_share * inverse
    new_master = master_share - outer_rate * new_momentum
    return (new_brick[None], new_master, new_momentum)


def solution(mesh):
    in_specs = (P("grp", None, "gx", "gy", None), P(), P(), P(), P(), P(), P(), P())
    out_specs = (P("grp", None, "gx", "gy", None), P(("grp", "gx", "gy")), P(("grp", "gx", "gy")))
    return jax.shard_map(
        on_device, mesh=mesh, in_specs=in_specs, out_specs=out_specs, check_vma=False
    )
```
